32 devices in a mesh: row: 4 (over y, core), seq: 8 (over z, x).
Axes of the slice: x: 2, y: 2, z: 4, core: 2. Of those that a mesh axis runs over, the one named last changes fastest.
Arguments:
- inputs: bfloat16 [4, 1024, 2048], P('row', 'seq'), may hold values from -6 to 6
- lengths: int32 [4, 2], P('row'), may hold values from 352 to 672, as said below
- w_query: bfloat16 [2048, 2048], P(('row', 'seq')), may hold values from -0.1875 to 0.1875
- w_key: bfloat16 [2048, 2048], P(('row', 'seq')), may hold values from -0.1875 to 0.1875
- w_value: bfloat16 [2048, 2048], P(('row', 'seq')), may hold values from -0.125 to 0.125
- w_out: bfloat16 [2048, 2048], P(('row', 'seq')), may hold values from -2.5 to 2.5
- gain_attn: bfloat16 [2048], P(('row', 'seq')), may hold values from 0.5 to 1.5
- w_gate: bfloat16 [2048, 8192], P(('row', 'seq')), may hold values from -0.125 to 0.125
- w_up: bfloat16 [2048, 8192], P(('row', 'seq')), may hold values from -0.125 to 0.125
- w_down: bfloat16 [8192, 2048], P(('row', 'seq')), may hold values from -0.0625 to 0.0625
- gain_mlp: bfloat16 [2048], P(('row', 'seq')), may hold values from 0.5 to 1.5
- cotangent: bfloat16 [4, 1024, 2048], P('row', 'seq'), may hold values from -6 to 6
Outputs:
- output: bfloat16 [4, 1024, 2048], P('row', 'seq')
- input_grad: float32 [4, 1024, 2048], P('row', 'seq')
- grad_query: float32 [2048, 2048], P(('row', 'seq'))
- grad_key: float32 [2048, 2048], P(('row', 'seq'))
- grad_value: float32 [2048, 2048], P(('row', 'seq'))
- grad_out: float32 [2048, 2048], P(('row', 'seq'))
- grad_gain_attn: float32 [2048], P(('row', 'seq'))
- grad_gate: float32 [2048, 8192], P(('row', 'seq'))
- grad_up: float32 [2048, 8192], P(('row', 'seq'))
- grad_down: float32 [8192, 2048], P(('row', 'seq'))
- grad_gain_mlp: float32 [2048], P(('row', 'seq'))
The draws below stay inside these ranges and needn't reach their ends.
Inputs may be any that keep to these rules, and one draw needn't show every extreme that they name: The lengths of a row add up to 1024 and are multiples of 16.
All inputs are finite; a program needn't handle non-finite values.
Results may differ from the reference program's by a relative error of at most 0.012.
The reference program's roundings to bfloat16 on the way count: a program that leaves them out, or rounds other values in their place, can miss the bound.
Values may be sent and summed in bfloat16 or wider, within the bound.
A program may use at most 512 MiB of HBM per device.

```python
import jax
import jax.numpy as jnp
from jax import lax

D = 2048
HEADS = 16
HEAD_DIM = 128
FF = 8192
TOK_DEV = 128
ROWS = 4
ROW_TOKENS = 1024
N_SEQ = 8


def draw_lengths(key, part):
    key = jax.random.fold_in(key, 7)
    unit_total = TOK_DEV // 2
    longest = unit_total * 2 // 3
    pair_units = jnp.array([longest, unit_total - longest], jnp.int32)
    flips = jax.random.randint(key, (ROWS,), 0, 2)
    unit_rows = jnp.where(flips[:, None] == 0, pair_units[None, :], pair_units[None, ::-1])
    return (unit_rows * (2 * N_SEQ)).astype(jnp.int32)


def steps_of(rng, extent, cuts, smallest, largest):
    factor_of, own = 1.0, jax.random.fold_in(rng, 6)
    for dim, parts in cuts:
        steps = jnp.exp(jax.random.uniform(jax.random.fold_in(own, dim), (parts,), jnp.float32, smallest / len(cuts), largest / len(cuts)))
        factor_of = factor_of * jnp.repeat(steps, extent[dim] // parts).reshape([-1 if axis == dim else 1 for axis in range(len(extent))])
    return factor_of


def gaussian(key, dims, spread, most, cuts=(), kind=jnp.bfloat16):
    loudness = steps_of(key, dims, cuts, -0.22, 0.18) if cuts else 1.0
    values = jax.random.normal(key, dims, jnp.float32) * spread * loudness
    return jnp.minimum(jnp.maximum(values, -most), most).astype(kind)


def setup_inputs(seed: int = 0) -> dict:
    key_of = jax.random.split(jax.random.key(seed), 13)
    inputs = gaussian(key_of[0], (ROWS, ROW_TOKENS, D), 1.0, 6.0, ((0, 4), (1, 8)))
    lengths = draw_lengths(jax.random.fold_in(key_of[12], 71), 0)
    w_query = gaussian(key_of[2], (D, D), (D // 2) ** -0.5, 0.1875, ((0, 32),))
    w_key = gaussian(key_of[3], (D, D), (D // 2) ** -0.5, 0.1875, ((0, 32),))
    w_value = gaussian(key_of[4], (D, D), D ** -0.5, 0.125, ((0, 32),))
    w_out = gaussian(key_of[5], (D, D), (max(1, 3 * D // ROW_TOKENS)) ** -0.5, 2.5, ((0, 32),))
    gain_attn = jnp.clip(1.0 + 0.1 * jax.random.normal(key_of[6], (D,), jnp.float32), 0.5, 1.5).astype(jnp.bfloat16)
    w_gate = gaussian(key_of[7], (D, FF), D ** -0.5, 0.125, ((0, 32),))
    w_up = gaussian(key_of[8], (D, FF), D ** -0.5, 0.125, ((0, 32),))
    w_down = gaussian(key_of[9], (FF, D), FF ** -0.5, 0.0625, ((0, 32),))
    gain_mlp = jnp.clip(1.0 + 0.1 * jax.random.normal(key_of[10], (D,), jnp.float32), 0.5, 1.5).astype(jnp.bfloat16)
    cotangent = gaussian(key_of[11], (ROWS, ROW_TOKENS, D), 1.0, 6.0, ((0, 4), (1, 8)))
    return {"inputs": inputs, "lengths": lengths, "w_query": w_query, "w_key": w_key, "w_value": w_value, "w_out": w_out, "gain_attn": gain_attn, "w_gate": w_gate, "w_up": w_up, "w_down": w_down, "gain_mlp": gain_mlp, "cotangent": cotangent}


EPSILON = 1e-05

@jax.custom_vjp
def low(v):
    return lax.optimization_barrier(v.astype(jnp.bfloat16)).astype(jnp.float32)

@jax.custom_vjp
def low_back(v):
    return v

def low_keep(v):
    return (low(v), None)

def low_pass(kept, grad):
    return (grad,)

def back_keep(v):
    return (v, None)

def back_low(kept, grad):
    return (low(grad),)
low.defvjp(low_keep, low_pass)
low_back.defvjp(back_keep, back_low)

def layout(lengths_row, places, block_rows, block_count):
    unit_counts = (lengths_row // (2 * block_count)).astype(jnp.int32)
    span_sizes = 2 * unit_counts
    offsets = (jnp.cumsum(span_sizes) - span_sizes).astype(jnp.int32)
    device = places // block_rows
    within_block = places - device * block_rows
    inside = ((within_block[:, None] >= offsets[None, :]) & (within_block[:, None] < (offsets + span_sizes)[None, :])).astype(jnp.int32)
    numbers = jnp.arange(lengths_row.shape[0], dtype=jnp.int32)
    segment = lax.optimization_barrier(jnp.sum(inside * numbers[None, :], axis=1)).astype(jnp.int32)
    unit_of = lax.optimization_barrier(jnp.sum(inside * unit_counts[None, :], axis=1)).astype(jnp.int32)
    begins = lax.optimization_barrier(jnp.sum(inside * offsets[None, :], axis=1)).astype(jnp.int32)
    length_of = lax.optimization_barrier(jnp.sum(inside * lengths_row[None, :], axis=1)).astype(jnp.int32)
    within = within_block - begins
    position = jnp.where(within < unit_of, device * unit_of + within, (2 * block_count - 1 - device) * unit_of + within - unit_of)
    return (segment, position.astype(jnp.int32), length_of)

def rms_norm(values, gain):
    return values * lax.rsqrt(lax.optimization_barrier(jnp.mean(values * values, axis=-1, keepdims=True)) + EPSILON) * gain

def product(activation, weight):
    return jnp.einsum('rtd,de->rte', activation, weight, precision=lax.Precision.HIGHEST)

def row_attention(queries, key_rows, value_rows, lengths_row):
    places = jnp.arange(ROW_TOKENS, dtype=jnp.int32)
    segment, position, length_of = layout(lengths_row, places, TOK_DEV, N_SEQ)
    key_heads = key_rows.reshape(ROW_TOKENS, HEADS, HEAD_DIM)
    value_heads = value_rows.reshape(ROW_TOKENS, HEADS, HEAD_DIM)

    def one_block(pieces):
        query_block, query_segment, query_position, query_length = pieces
        scores = jnp.einsum('qhd,khd->hqk', query_block.reshape(TOK_DEV, HEADS, HEAD_DIM), key_heads, precision=lax.Precision.HIGHEST) * HEAD_DIM ** (-0.5)
        scores = low_back(scores - jnp.log(query_length.astype(jnp.float32))[None, :, None])
        allowed = (query_segment[:, None] == segment[None, :]) & (position[None, :] <= query_position[:, None])
        sig_terms = low(jnp.where(allowed[None], jax.nn.sigmoid(scores), 0.0))
        attended = jnp.einsum('hqk,khd->qhd', sig_terms, value_heads, precision=lax.Precision.HIGHEST)
        return attended.reshape(TOK_DEV, D)
    blocked = (queries.reshape(N_SEQ, TOK_DEV, D), segment.reshape(N_SEQ, TOK_DEV), position.reshape(N_SEQ, TOK_DEV), length_of.reshape(N_SEQ, TOK_DEV))
    return lax.map(jax.checkpoint(one_block), blocked).reshape(ROW_TOKENS, D)

def forward(residual, w_query, w_key, w_value, w_out, gain_attn, w_gate, w_up, w_down, gain_mlp, lengths):
    normed = low(rms_norm(residual, gain_attn))
    queries = low(low_back(product(normed, w_query)))
    key_rows = low(low_back(product(normed, w_key)))
    value_rows = low(low_back(product(normed, w_value)))
    attended = lax.map(lambda pieces: row_attention(pieces[0], pieces[1], pieces[2], pieces[3]), (queries, key_rows, value_rows, lengths))
    attended = low(low_back(attended))
    middle = residual + low_back(product(attended, w_out))
    normed_mlp = low(rms_norm(middle, gain_mlp))
    gate_vals = low_back(product(normed_mlp, w_gate))
    up_vals = low_back(product(normed_mlp, w_up))
    hidden = low(jax.nn.silu(gate_vals) * up_vals)
    return middle + low_back(product(hidden, w_down))

def reference(inputs, lengths, w_query, w_key, w_value, w_out, gain_attn, w_gate, w_up, w_down, gain_mlp, cotangent):
    params = tuple((member.astype(jnp.float32) for member in (inputs, w_query, w_key, w_value, w_out, gain_attn, w_gate, w_up, w_down, gain_mlp)))

    def closed(*all_values):
        return forward(*all_values, lengths)
    result, pullback = jax.vjp(closed, *params)
    gradients = pullback(cotangent.astype(jnp.float32))
    return (result.astype(jnp.bfloat16), gradients[0], gradients[1], gradients[2], gradients[3], gradients[4], gradients[5], gradients[6], gradients[7], gradients[8], gradients[9])
```

```python
import functools

import jax
import jax.numpy as jnp
from jax import lax
from jax.experimental import pallas as pl
from jax.experimental.pallas import tpu as pltpu
from jax.sharding import PartitionSpec as P

HEADS = 16


EPSILON = 1e-05


def layout(lengths_row, places, block_rows, block_count):
    unit_counts = lengths_row // (2 * block_count)
    span_sizes = 2 * unit_counts
    offsets = jnp.cumsum(span_sizes) - span_sizes
    device = places // block_rows
    within_block = places - device * block_rows
    inside = (
        (within_block[:, None] >= offsets[None, :])
        & (within_block[:, None] < (offsets + span_sizes)[None, :])
    ).astype(jnp.int32)
    numbers = jnp.arange(lengths_row.shape[0], dtype=jnp.int32)
    segment = jnp.sum(inside * numbers[None, :], axis=1)
    unit_of = jnp.sum(inside * unit_counts[None, :], axis=1)
    begins = jnp.sum(inside * offsets[None, :], axis=1)
    length_of = jnp.sum(inside * lengths_row[None, :], axis=1)
    within = within_block - begins
    position = jnp.where(
        within < unit_of,
        device * unit_of + within,
        (2 * block_count - 1 - device) * unit_of + within - unit_of,
    )
    return (segment, position, length_of)


def rms_norm(values, gain):
    return values * lax.rsqrt(jnp.mean(values * values, axis=-1, keepdims=True) + EPSILON) * gain


def sigmoid_terms(query_heads, query_meta, key_heads, key_meta):
    query_segment, query_position, query_length = query_meta
    key_segment, key_position, unused_length = key_meta
    scores = jnp.einsum(
        "qhd,khd->hqk", query_heads, key_heads, preferred_element_type=jnp.float32
    ) * query_heads.shape[2] ** (-0.5)
    scores = scores - jnp.log(query_length.astype(jnp.float32))[None, :, None]
    allowed = (query_segment[:, None] == key_segment[None, :]) & (
        key_position[None, :] <= query_position[:, None]
    )
    return jnp.where(allowed[None], jax.nn.sigmoid(scores), 0.0)


def pair_terms(query_heads, query_meta, grad_heads, key_heads, key_meta, value_heads):
    sig_terms = sigmoid_terms(query_heads, query_meta, key_heads, key_meta)
    slopes = jnp.einsum("qhd,khd->hqk", grad_heads, value_heads, preferred_element_type=jnp.float32)
    score_grad = (slopes * sig_terms * (1.0 - sig_terms)).astype(jnp.bfloat16)
    return (sig_terms.astype(jnp.bfloat16), score_grad)


def by_blocks(step_fn, running, pieces, block_rows):
    size_total = pieces[0].shape[0]
    part_rows = 4 * block_rows
    block_count = size_total // part_rows

    def turn_over(step_number, carried):
        sub_pieces = tuple(
            (
                lax.dynamic_slice_in_dim(member, step_number * part_rows, part_rows, 0)
                for member in pieces
            )
        )
        return step_fn(carried, sub_pieces, step_number * part_rows)

    return lax.fori_loop(0, block_count, turn_over, running)


def gathered_local(
    inputs,
    lengths,
    w_query,
    w_key,
    w_value,
    w_out,
    gain_attn,
    w_gate,
    w_up,
    w_down,
    gain_mlp,
    cotangent,
):
    residual = inputs[0].astype(jnp.float32)
    tokens_here = residual.shape[0]
    model_width = residual.shape[1]
    head_size = model_width // HEADS
    score_scale = head_size ** (-0.5)
    block_total = lax.axis_size("seq")
    lengths_row = lengths[0]
    places = lax.axis_index("seq") * tokens_here + jnp.arange(tokens_here, dtype=jnp.int32)
    own_meta = layout(lengths_row, places, tokens_here, block_total)

    def meta_at(start_row, row_count):
        return layout(
            lengths_row,
            start_row + jnp.arange(row_count, dtype=jnp.int32),
            tokens_here,
            block_total,
        )

    def heads_of(matrix):
        return matrix.reshape(matrix.shape[0], HEADS, head_size)

    query_full, key_full, value_full, out_full, gain_one = (
        lax.all_gather(w_query, ("row", "seq"), axis=0, tiled=True),
        lax.all_gather(w_key, ("row", "seq"), axis=0, tiled=True),
        lax.all_gather(w_value, ("row", "seq"), axis=0, tiled=True),
        lax.all_gather(w_out, ("row", "seq"), axis=0, tiled=True),
        lax.all_gather(gain_attn, ("row", "seq"), axis=0, tiled=True),
    )
    gain_one_f = gain_one.astype(jnp.float32)
    normed = rms_norm(residual, gain_one_f).astype(jnp.bfloat16)
    queries = jnp.dot(normed, query_full, preferred_element_type=jnp.float32).astype(jnp.bfloat16)
    key_rows = jnp.dot(normed, key_full, preferred_element_type=jnp.float32).astype(jnp.bfloat16)
    value_rows = jnp.dot(normed, value_full, preferred_element_type=jnp.float32).astype(
        jnp.bfloat16
    )
    query_heads = heads_of(queries)

    def forward_step(running, pieces, start_row):
        key_piece, value_piece = pieces
        sig_terms = sigmoid_terms(
            query_heads, own_meta, heads_of(key_piece), meta_at(start_row, key_piece.shape[0])
        ).astype(jnp.bfloat16)
        added = jnp.einsum(
            "hqk,khd->qhd", sig_terms, heads_of(value_piece), preferred_element_type=jnp.float32
        )
        return running + added.reshape(tokens_here, model_width)

    attended = by_blocks(
        forward_step,
        jnp.zeros((tokens_here, model_width), jnp.float32),
        (
            lax.all_gather(key_rows, "seq", axis=0, tiled=True),
            lax.all_gather(value_rows, "seq", axis=0, tiled=True),
        ),
        tokens_here,
    )
    attended_low = attended.astype(jnp.bfloat16)
    middle = residual + jnp.dot(attended_low, out_full, preferred_element_type=jnp.float32)
    gate_full, up_full, down_full, gain_two = (
        lax.all_gather(w_gate, ("row", "seq"), axis=0, tiled=True),
        lax.all_gather(w_up, ("row", "seq"), axis=0, tiled=True),
        lax.all_gather(w_down, ("row", "seq"), axis=0, tiled=True),
        lax.all_gather(gain_mlp, ("row", "seq"), axis=0, tiled=True),
    )
    gain_two_f = gain_two.astype(jnp.float32)
    normed_mlp = rms_norm(middle, gain_two_f).astype(jnp.bfloat16)
    gate_vals = jnp.dot(normed_mlp, gate_full, preferred_element_type=jnp.float32)
    up_vals = jnp.dot(normed_mlp, up_full, preferred_element_type=jnp.float32)
    gated_prod, gated_back = jax.vjp(
        lambda gate_in, up_in: jax.nn.silu(gate_in) * up_in, gate_vals, up_vals
    )
    hidden = gated_prod.astype(jnp.bfloat16)
    output = (middle + jnp.dot(hidden, down_full, preferred_element_type=jnp.float32)).astype(
        jnp.bfloat16
    )
    upstream_low = cotangent[0]
    upstream = upstream_low.astype(jnp.float32)
    gate_full, up_full, down_full, gain_two = (
        lax.all_gather(w_gate, ("row", "seq"), axis=0, tiled=True),
        lax.all_gather(w_up, ("row", "seq"), axis=0, tiled=True),
        lax.all_gather(w_down, ("row", "seq"), axis=0, tiled=True),
        lax.all_gather(gain_mlp, ("row", "seq"), axis=0, tiled=True),
    )
    gain_two_f = gain_two.astype(jnp.float32)
    grad_down = jnp.dot(hidden.T, upstream_low, preferred_element_type=jnp.float32)
    shared_down = lax.psum_scatter(grad_down, ("row", "seq"), scatter_dimension=0, tiled=True)
    hidden_grad = jnp.dot(upstream_low, down_full.T, preferred_element_type=jnp.float32)
    gate_grad, up_grad = gated_back(hidden_grad)
    gate_low = gate_grad.astype(jnp.bfloat16)
    up_low = up_grad.astype(jnp.bfloat16)
    grad_gate = jnp.dot(normed_mlp.T, gate_low, preferred_element_type=jnp.float32)
    shared_gate = lax.psum_scatter(grad_gate, ("row", "seq"), scatter_dimension=0, tiled=True)
    normed_grad = jnp.dot(gate_low, gate_full.T, preferred_element_type=jnp.float32) + jnp.dot(
        up_low, up_full.T, preferred_element_type=jnp.float32
    )
    unused_mid, second_back = jax.vjp(rms_norm, middle, gain_two_f)
    middle_part, gain_two_grad = second_back(normed_grad)
    middle_grad = upstream + middle_part
    grad_up = jnp.dot(normed_mlp.T, up_low, preferred_element_type=jnp.float32)
    shared_up, shared_gain_two = (
        lax.psum_scatter(grad_up, ("row", "seq"), scatter_dimension=0, tiled=True),
        lax.psum_scatter(gain_two_grad, ("row", "seq"), scatter_dimension=0, tiled=True),
    )
    query_full, key_full, value_full, out_full, gain_one = (
        lax.all_gather(w_query, ("row", "seq"), axis=0, tiled=True),
        lax.all_gather(w_key, ("row", "seq"), axis=0, tiled=True),
        lax.all_gather(w_value, ("row", "seq"), axis=0, tiled=True),
        lax.all_gather(w_out, ("row", "seq"), axis=0, tiled=True),
        lax.all_gather(gain_attn, ("row", "seq"), axis=0, tiled=True),
    )
    gain_one_f = gain_one.astype(jnp.float32)
    branch_low = middle_grad.astype(jnp.bfloat16)
    grad_out = jnp.dot(attended_low.T, branch_low, preferred_element_type=jnp.float32)
    attended_grad = jnp.dot(branch_low, out_full.T, preferred_element_type=jnp.float32).astype(
        jnp.bfloat16
    )
    grad_heads = heads_of(attended_grad)
    key_heads_own = heads_of(key_rows)
    value_heads_own = heads_of(value_rows)

    def query_step(running, pieces, start_row):
        key_piece, value_piece = pieces
        key_piece_heads = heads_of(key_piece)
        unused_terms, score_grad = pair_terms(
            query_heads,
            own_meta,
            grad_heads,
            key_piece_heads,
            meta_at(start_row, key_piece.shape[0]),
            heads_of(value_piece),
        )
        added = jnp.einsum(
            "hqk,khd->qhd", score_grad, key_piece_heads, preferred_element_type=jnp.float32
        )
        return running + added.reshape(tokens_here, model_width) * score_scale

    start_value = jnp.zeros((tokens_here, model_width), jnp.float32)
    folded = by_blocks(
        query_step,
        start_value,
        (
            lax.all_gather(key_rows, "seq", axis=0, tiled=True),
            lax.all_gather(value_rows, "seq", axis=0, tiled=True),
        ),
        tokens_here,
    )

    def key_step(running, pieces, start_row):
        key_sum, value_sum = running
        query_piece, grad_piece = pieces
        row_count = query_piece.shape[0]
        query_piece_heads = heads_of(query_piece)
        grad_piece_heads = heads_of(grad_piece)
        sig_low, score_grad = pair_terms(
            query_piece_heads,
            meta_at(start_row, row_count),
            grad_piece_heads,
            key_heads_own,
            own_meta,
            value_heads_own,
        )
        key_add = jnp.einsum(
            "hqk,qhd->khd", score_grad, query_piece_heads, preferred_element_type=jnp.float32
        )
        value_add = jnp.einsum(
            "hqk,qhd->khd", sig_low, grad_piece_heads, preferred_element_type=jnp.float32
        )
        return (
            key_sum + key_add.reshape(tokens_here, model_width) * score_scale,
            value_sum + value_add.reshape(tokens_here, model_width),
        )

    empty_rows = jnp.zeros((tokens_here, model_width), jnp.float32)
    key_grad, value_grad = by_blocks(
        key_step,
        (empty_rows, empty_rows),
        (
            lax.all_gather(queries, "seq", axis=0, tiled=True),
            lax.all_gather(attended_grad, "seq", axis=0, tiled=True),
        ),
        tokens_here,
    )
    query_low = folded.astype(jnp.bfloat16)
    key_low = key_grad.astype(jnp.bfloat16)
    value_low = value_grad.astype(jnp.bfloat16)
    grad_query = jnp.dot(normed.T, query_low, preferred_element_type=jnp.float32)
    grad_key = jnp.dot(normed.T, key_low, preferred_element_type=jnp.float32)
    grad_value = jnp.dot(normed.T, value_low, preferred_element_type=jnp.float32)
    normed_back = jnp.dot(query_low, query_full.T, preferred_element_type=jnp.float32)
    normed_back = normed_back + jnp.dot(key_low, key_full.T, preferred_element_type=jnp.float32)
    normed_back = normed_back + jnp.dot(value_low, value_full.T, preferred_element_type=jnp.float32)
    unused_first, first_back = jax.vjp(rms_norm, residual, gain_one_f)
    residual_part, gain_one_grad = first_back(normed_back)
    input_grad = middle_grad + residual_part
    shared_query, shared_key, shared_value, shared_out, shared_gain_one = (
        lax.psum_scatter(grad_query, ("row", "seq"), scatter_dimension=0, tiled=True),
        lax.psum_scatter(grad_key, ("row", "seq"), scatter_dimension=0, tiled=True),
        lax.psum_scatter(grad_value, ("row", "seq"), scatter_dimension=0, tiled=True),
        lax.psum_scatter(grad_out, ("row", "seq"), scatter_dimension=0, tiled=True),
        lax.psum_scatter(gain_one_grad, ("row", "seq"), scatter_dimension=0, tiled=True),
    )
    return (
        output[None],
        input_grad[None],
        shared_query,
        shared_key,
        shared_value,
        shared_out,
        shared_gain_one,
        shared_gate,
        shared_up,
        shared_down,
        shared_gain_two,
    )


MESH = pl.DeviceIdType.MESH
VMEM_BYTES = 60 * 1024 * 1024


class Place:
    def __init__(self, row_count, seq_count):
        self.row_count, self.seq_count = row_count, seq_count
        self.r, self.s = lax.axis_index("row"), lax.axis_index("seq")
        self.n_hi = seq_count // 2
        self.hi, self.lo = self.s // 2, lax.rem(self.s, 2)
        self.r_core = self.r + 1 - 2 * lax.rem(self.r, 2)
        self.r_y = lax.rem(self.r + 2, 4)
        self.r_far = lax.rem(self.r_core + 2, 4)
        self.side = (self.r, self.s + 1 - 2 * self.lo)
        self.up = (self.r, self.s + 2)
        self.down = (self.r, self.s - 2)
        self.core = (self.r_core, self.s)
        self.y = (self.r_y, self.s)
        self.has_up = self.hi < self.n_hi - 1
        self.has_down = self.hi > 0

    def peer(self, step):
        return lax.rem(self.s + step, self.seq_count)

    def chain(self):
        return [(None, self.side), (self.has_up, self.up), (self.has_down, self.down)]

    def peers(self):
        return [(None, (self.r, self.peer(step))) for step in range(1, self.seq_count)]

    def rows(self):
        return [(None, self.core), (None, self.y)]


def greet(devices):
    barrier = pltpu.get_barrier_semaphore()
    total = 0
    for condition, device in devices:
        if condition is None:
            pl.semaphore_signal(barrier, inc=1, device_id=device, device_id_type=MESH)
            total = total + 1
        else:

            @pl.when(condition)
            def _(device=device):
                pl.semaphore_signal(barrier, inc=1, device_id=device, device_id_type=MESH)

            total = total + condition.astype(jnp.int32)
    pl.semaphore_wait(barrier, total)


class Sems:
    def __init__(self, ref):
        self.ref, self.used = ref, 0

    def take(self, count):
        base = self.used
        self.used += count
        assert self.used <= self.ref.shape[0], self.used
        return lambda index: self.ref.at[base + index]


def push(source, target, send, recv, device):
    pltpu.make_async_remote_copy(
        src_ref=source, dst_ref=target, send_sem=send, recv_sem=recv, device_id=device, device_id_type=MESH
    ).start()


def settle(ref, sem):
    pltpu.make_async_copy(ref, ref, sem).wait()


def no_op(block):
    return None


class SeqGather:
    def __init__(self, place, sems, source, at, arrived=no_op):
        self.p, self.source, self.at, self.arrived = place, source, at, arrived
        n = place.n_hi
        self.own, self.up, self.down = sems.take(1), sems.take(n), sems.take(n)
        self.side, self.recv = sems.take(n), sems.take(2 * n)

    def start(self):
        p, s = self.p, self.p.s
        pltpu.make_async_copy(self.source, self.at(s), self.own(0)).start()

        @pl.when(p.has_up)
        def _():
            push(self.source, self.at(s), self.up(0), self.recv(s), p.up)

        @pl.when(p.has_down)
        def _():
            push(self.source, self.at(s), self.down(0), self.recv(s), p.down)

        push(self.source, self.at(s), self.side(p.hi), self.recv(s), p.side)

    def step(self, k):
        p = self.p

        @pl.when(p.hi >= k)
        def _():
            block = p.s - 2 * k
            settle(self.at(block), self.recv(block))

            @pl.when(p.has_up)
            def _():
                push(self.at(block), self.at(block), self.up(k), self.recv(block), p.up)

            push(self.at(block), self.at(block), self.side(p.hi - k), self.recv(block), p.side)
            self.arrived(block)

        @pl.when(p.hi + k < p.n_hi)
        def _():
            block = p.s + 2 * k
            settle(self.at(block), self.recv(block))

            @pl.when(p.has_down)
            def _():
                push(self.at(block), self.at(block), self.down(k), self.recv(block), p.down)

            push(self.at(block), self.at(block), self.side(p.hi + k), self.recv(block), p.side)
            self.arrived(block)

    def aside(self, k):
        p = self.p
        if k == 0:
            block = 2 * p.hi + 1 - p.lo
            settle(self.at(block), self.recv(block))
            self.arrived(block)
            return

        @pl.when(p.hi >= k)
        def _():
            block = 2 * (p.hi - k) + 1 - p.lo
            settle(self.at(block), self.recv(block))
            self.arrived(block)

        @pl.when(p.hi + k < p.n_hi)
        def _():
            block = 2 * (p.hi + k) + 1 - p.lo
            settle(self.at(block), self.recv(block))
            self.arrived(block)

    def finish(self):
        p = self.p
        settle(self.source, self.own(0))
        for k in range(p.n_hi):

            @pl.when(p.has_up & (p.hi >= k))
            def _():
                settle(self.source, self.up(k))

            @pl.when(p.has_down & (p.hi + k < p.n_hi))
            def _():
                settle(self.source, self.down(k))

            settle(self.source, self.side(k))


class SeqExchange:
    def __init__(self, place, sems, piece, at, arrived=no_op):
        self.p, self.piece, self.at, self.arrived = place, piece, at, arrived
        n = place.seq_count
        self.own, self.send, self.recv = sems.take(1), sems.take(n), sems.take(n)

    def start_own(self):
        s = self.p.s
        pltpu.make_async_copy(self.piece(s), self.at(s), self.own(0)).start()

    def start(self):
        p, s = self.p, self.p.s
        self.start_own()
        for step in range(1, p.seq_count):
            t = p.peer(step)
            push(self.piece(t), self.at(s), self.send(step), self.recv(s), (p.r, t))

    def step(self, step):
        block = self.p.peer(self.p.seq_count - step)
        settle(self.at(block), self.recv(block))
        self.arrived(block)

    def finish(self):
        p = self.p
        settle(self.at(p.s), self.own(0))
        for step in range(1, p.seq_count):
            settle(self.at(p.s), self.send(step))


class RowForward:
    def __init__(self, place, sems, blocks, at):
        self.p, self.at, self.blocks = place, at, blocks
        self.core, self.y, self.far = sems.take(blocks), sems.take(blocks), sems.take(blocks)
        self.from_core, self.from_y, self.from_far = sems.take(blocks), sems.take(blocks), sems.take(blocks)

    def forward(self, block, source=None):
        p = self.p
        source = self.at(p.r, block) if source is None else source
        push(source, self.at(p.r, block), self.y(block), self.from_y(block), p.y)
        push(source, self.at(p.r, block), self.core(block), self.from_core(block), p.core)

    def relay(self, block):
        p = self.p
        settle(self.at(p.r_y, block), self.from_y(block))
        push(self.at(p.r_y, block), self.at(p.r_y, block), self.far(block), self.from_far(block), p.core)

    def finish(self):
        p = self.p
        for block in range(self.blocks):
            settle(self.at(p.r_core, block), self.from_core(block))
            settle(self.at(p.r_far, block), self.from_far(block))
            settle(self.at(p.r, block), self.core(block))
            settle(self.at(p.r, block), self.y(block))
            settle(self.at(p.r_y, block), self.far(block))


def add_into(target, *sources):
    @pl.loop(0, target.shape[0] // 16)
    def _(tile):
        rows = pl.ds(pl.multiple_of(tile * 16, 16), 16)
        total = sources[0][rows, :].astype(jnp.float32)
        for source in sources[1:]:
            total = total + source[rows, :].astype(jnp.float32)
        target[rows, :] = total.astype(target.dtype)


def add_small(target, *sources):
    total = sources[0][...].astype(jnp.float32)
    for source in sources[1:]:
        total = total + source[...].astype(jnp.float32)
    target[...] = total.astype(target.dtype)


class SeqReduce:
    def __init__(self, place, sems, at, side_slot, chain_slot, target, add=add_into):
        self.p, self.at, self.add, self.target = place, at, add, target
        self.side_slot, self.chain_slot = side_slot, chain_slot
        n = place.n_hi
        self.side, self.from_side = sems.take(n), sems.take(n)
        self.send, self.recv = sems.take(n), sems.take(2 * n)

    def turn(self, t):
        p = self.p
        n, hi = p.n_hi, p.hi
        low = jnp.where(t < n - 1 - hi, n - 1 - t, t - (n - 1 - hi))
        high = jnp.where(t < hi, t, n - 1 - (t - hi))
        return jnp.where(hi < n // 2, low, high)

    def start(self, t):
        p, block = self.p, self.turn(t)
        push(self.at(2 * block + 1 - p.lo), self.side_slot(block), self.side(block), self.from_side(block), p.side)

    def step(self, t):
        p, n, block = self.p, self.p.n_hi, self.turn(t)
        mine, got = self.at(2 * block + p.lo), self.side_slot(block)
        settle(got, self.from_side(block))
        if t == n - 1:
            return self.close()

        @pl.when(block > p.hi)
        def _():
            @pl.when(p.has_down)
            def _():
                settle(got, self.recv(block))
                self.add(got, mine, got, self.chain_slot(0, block))

            @pl.when(jnp.logical_not(p.has_down))
            def _():
                self.add(got, mine, got)

            push(got, self.chain_slot(0, block), self.send(block), self.recv(block), p.up)

        @pl.when(block < p.hi)
        def _():
            @pl.when(p.has_up)
            def _():
                settle(got, self.recv(n + block))
                self.add(got, mine, got, self.chain_slot(1, block))

            @pl.when(jnp.logical_not(p.has_up))
            def _():
                self.add(got, mine, got)

            push(got, self.chain_slot(1, block), self.send(block), self.recv(n + block), p.down)

    def close(self):
        p, n, hi = self.p, self.p.n_hi, self.p.hi
        mine, got = self.at(p.s), self.side_slot(hi)
        below, above = self.chain_slot(0, hi), self.chain_slot(1, hi)

        @pl.when(p.has_down)
        def _():
            settle(got, self.recv(hi))

        @pl.when(p.has_up)
        def _():
            settle(got, self.recv(n + hi))

        @pl.when(p.has_down & p.has_up)
        def _():
            self.add(self.target, mine, got, below, above)

        @pl.when(p.has_down & jnp.logical_not(p.has_up))
        def _():
            self.add(self.target, mine, got, below)

        @pl.when(jnp.logical_not(p.has_down))
        def _():
            self.add(self.target, mine, got, above)

    def finish(self):
        p = self.p
        for block in range(p.n_hi):
            settle(self.side_slot(block), self.side(block))

            @pl.when(p.hi != block)
            def _():
                settle(self.side_slot(block), self.send(block))


class RowReduce:
    def __init__(self, place, sems, blocks, at, core_slot, y_slot, target, add=add_into):
        self.p, self.at, self.add, self.target = place, at, add, target
        self.core_slot, self.y_slot, self.blocks = core_slot, y_slot, blocks
        self.send, self.recv = sems.take(2 * blocks), sems.take(2 * blocks)
        self.y, self.from_y = sems.take(blocks), sems.take(blocks)

    def start(self, block):
        p, n = self.p, self.blocks
        push(self.at(p.r_far, block), self.core_slot(0, block), self.send(block), self.recv(block), p.core)
        push(self.at(p.r_core, block), self.core_slot(1, block), self.send(n + block), self.recv(n + block), p.core)

    def step(self, block):
        p = self.p
        got = self.core_slot(0, block)
        settle(got, self.recv(block))
        self.add(got, self.at(p.r_y, block), got)
        push(got, self.y_slot(block), self.y(block), self.from_y(block), p.y)

    def close(self, block):
        p = self.p
        settle(self.core_slot(1, block), self.recv(self.blocks + block))
        settle(self.y_slot(block), self.from_y(block))
        self.add(self.target(block), self.at(p.r, block), self.core_slot(1, block), self.y_slot(block))

    def finish(self):
        n = self.blocks
        for block in range(n):
            settle(self.core_slot(0, block), self.send(block))
            settle(self.core_slot(1, block), self.send(n + block))
            settle(self.core_slot(0, block), self.y(block))


def columns(ref, index, width):
    return ref.at[:, pl.ds(pl.multiple_of(index * width, width), width)]


def call(kernel, shapes, ident, args, spaces, out_spaces, scratch, sems):
    return pl.pallas_call(
        kernel,
        out_shape=shapes,
        in_specs=[pl.BlockSpec(memory_space=space) for space in spaces],
        out_specs=jax.tree.map(lambda space: pl.BlockSpec(memory_space=space), out_spaces),
        scratch_shapes=list(scratch) + [pltpu.SemaphoreType.DMA((sems,))],
        compiler_params=pltpu.CompilerParams(
            collective_id=ident, has_side_effects=True, vmem_limit_bytes=VMEM_BYTES
        ),
    )(*args)


def shape_of(dims, dtype=jnp.bfloat16):
    return jax.ShapeDtypeStruct(dims, dtype)


def opening_kernel(rows, seqs, x, g, wqkv, wgu, wdown, wout, gains, xs, gs, vqkv, vgu, vdown, vout, vgains, sems):
    p, pool = Place(rows, seqs), Sems(sems)
    greet(p.peers() + p.rows())
    half = x.shape[0] // 2
    down_blocks, down_rows = vdown.shape[1], vdown.shape[2]

    def part(source, target, c):
        piece = pl.ds(c * half, half)
        return SeqGather(p, pool, source.at[piece], lambda b: target.at[b, piece])

    qkv_rows = RowForward(p, pool, seqs, lambda r, b: vqkv.at[r, b])
    gu_rows = RowForward(p, pool, seqs, lambda r, b: vgu.at[r, b])
    down_fwd = RowForward(p, pool, down_blocks, lambda r, b: vdown.at[r, b])
    out_rows = RowForward(p, pool, seqs, lambda r, b: vout.at[r, b])
    gain_rows = RowForward(p, pool, seqs, lambda r, b: vgains.at[r, b])
    x_parts = [part(x, xs, c) for c in range(2)]
    g_parts = [part(g, gs, c) for c in range(2)]
    qkv = SeqExchange(p, pool, lambda t: wqkv.at[t], lambda b: vqkv.at[p.r, b], qkv_rows.forward)
    gu = SeqExchange(p, pool, lambda t: wgu.at[t], lambda b: vgu.at[p.r, b], gu_rows.forward)
    out = SeqGather(p, pool, wout, lambda b: vout.at[p.r, b], out_rows.forward)
    gain = SeqGather(p, pool, gains, lambda b: vgains.at[p.r, b], gain_rows.forward)
    down_own = pool.take(1)

    gain.start()
    gain_rows.forward(p.s, gains)
    qkv.start()
    qkv_rows.forward(p.s, wqkv.at[p.s])
    for member in x_parts:
        member.start()
    pltpu.make_async_copy(wdown, vdown.at[p.r], down_own(0)).start()
    for block in range(down_blocks):
        down_fwd.forward(block, wdown.at[block])
    gu_rows.forward(p.s, wgu.at[p.s])
    out_rows.forward(p.s, wout)
    gu.start()
    out.start()
    for member in g_parts:
        member.start()
    gathers = [gain] + x_parts + [out] + g_parts
    for k in range(1, p.n_hi):
        for member in gathers:
            member.step(k)
        for step in (2 * k - 1, 2 * k):
            qkv.step(step)
            gu.step(step)
    qkv.step(seqs - 1)
    gu.step(seqs - 1)
    for k in range(p.n_hi):
        for member in gathers:
            member.aside(k)
    for member in (gain_rows, qkv_rows, down_fwd, gu_rows, out_rows):
        for block in range(member.blocks):
            member.relay(block)
    for member in gathers + [qkv, gu, gain_rows, qkv_rows, down_fwd, gu_rows, out_rows]:
        member.finish()
    settle(wdown, down_own(0))


def opening(rows, seqs, x, g, wqkv, wgu, wdown, wout, gains):
    tokens, width = x.shape
    wdown = wdown.reshape(4, wdown.shape[0] // 4, width)
    args = (x, g, wqkv, wgu, wdown, wout, gains)
    shapes = (
        shape_of((seqs, tokens, width)),
        shape_of((seqs, tokens, width)),
        shape_of((rows,) + wqkv.shape),
        shape_of((rows,) + wgu.shape),
        shape_of((rows,) + wdown.shape),
        shape_of((rows, seqs) + wout.shape),
        shape_of((rows, seqs) + gains.shape, jnp.float32),
    )
    return call(
        functools.partial(opening_kernel, rows, seqs), shapes, 1, args, [pl.ANY] * 7, (pl.ANY,) * 7, [], 640
    )


def spread_kernel(rows, seqs, source, target, sems):
    p, pool = Place(rows, seqs), Sems(sems)
    greet(p.chain())
    half = source.shape[0] // 2
    members = []
    for c in range(2):
        piece = pl.ds(c * half, half)
        members.append(SeqGather(p, pool, source.at[piece], lambda b, piece=piece: target.at[b, piece]))
    for member in members:
        member.start()
    for k in range(1, p.n_hi):
        for member in members:
            member.step(k)
    for k in range(p.n_hi):
        for member in members:
            member.aside(k)
    for member in members:
        member.finish()


def spread(rows, seqs, ident, source):
    return call(
        functools.partial(spread_kernel, rows, seqs),
        shape_of((seqs,) + source.shape),
        ident,
        (source,),
        [pltpu.VMEM],
        pltpu.VMEM,
        [],
        128,
    )


def to_tokens_kernel(rows, seqs, source, target, sems):
    p, pool = Place(rows, seqs), Sems(sems)
    greet(p.peers())
    width = source.shape[2]
    member = SeqExchange(p, pool, lambda t: source.at[t], lambda b: columns(target, b, width))
    member.start()
    for step in range(1, seqs):
        member.step(step)
    member.finish()


def to_heads_kernel(rows, seqs, source, target, sems):
    p, pool = Place(rows, seqs), Sems(sems)
    greet(p.peers())
    width = target.shape[2]
    member = SeqExchange(p, pool, lambda t: columns(source, t, width), lambda b: target.at[b])
    member.start()
    for step in range(1, seqs):
        member.step(step)
    member.finish()


def to_tokens(rows, seqs, ident, source):
    tokens = source.shape[0] // seqs
    width = source.shape[1]
    return call(
        functools.partial(to_tokens_kernel, rows, seqs),
        shape_of((tokens, width * seqs)),
        ident,
        (source.reshape(seqs, tokens, width),),
        [pltpu.VMEM],
        pltpu.VMEM,
        [],
        64,
    )


def to_heads(rows, seqs, ident, source):
    tokens, width = source.shape[0], source.shape[1] // seqs
    return call(
        functools.partial(to_heads_kernel, rows, seqs),
        shape_of((seqs, tokens, width)),
        ident,
        (source,),
        [pltpu.VMEM],
        pltpu.VMEM,
        [],
        64,
    ).reshape(seqs * tokens, width)


def reduce_kernel(rows, seqs, count, *refs):
    p = Place(rows, seqs)
    sources, targets = refs[:count], refs[count : 2 * count]
    side, chain, sems = refs[2 * count :]
    pool = Sems(sems)
    greet(p.chain())
    half = targets[0].shape[0] // 2
    members = []
    for number in range(count):
        for c in range(2):
            piece = pl.ds(c * half, half)
            members.append(
                SeqReduce(
                    p,
                    pool,
                    lambda b, n=number, piece=piece: sources[n].at[b, piece],
                    lambda b, n=number, piece=piece: side.at[n, b, piece],
                    lambda w, b, n=number, piece=piece: chain.at[n, w, b, piece],
                    targets[number].at[piece],
                )
            )
    for first in range(0, len(members), 2):
        for t in range(p.n_hi):
            for member in members[first : first + 2]:
                member.start(t)
    for first in range(0, len(members), 2):
        for t in range(p.n_hi):
            for member in members[first : first + 2]:
                member.step(t)
    for member in members:
        member.finish()


def reduced(rows, seqs, ident, sources):
    count = len(sources)
    tokens, width = sources[0].shape[0] // seqs, sources[0].shape[1]
    sources = [source.reshape(seqs, tokens, width) for source in sources]
    return call(
        functools.partial(reduce_kernel, rows, seqs, count),
        (shape_of((tokens, width), jnp.float32),) * count,
        ident,
        sources,
        [pltpu.VMEM] * count,
        (pltpu.VMEM,) * count,
        [
            pltpu.VMEM((count, seqs // 2, tokens, width), jnp.bfloat16),
            pltpu.VMEM((count, 2, seqs // 2, tokens, width), jnp.bfloat16),
        ],
        256,
    )


def closing_kernel(
    rows,
    seqs,
    qkv,
    gu,
    down,
    out,
    gain,
    qkv_got,
    gu_got,
    down_sum,
    out_sum,
    gain_sum,
    qkv_core,
    gu_core,
    down_core,
    out_core,
    gain_core,
    qkv_y,
    gu_y,
    down_y,
    out_y,
    gain_y,
    out_side,
    out_chain,
    gain_side,
    gain_chain,
    sems,
):
    p, pool = Place(rows, seqs), Sems(sems)
    greet(p.peers() + p.rows())

    def over_rows(source, core_slots, y_slots, target, add=add_into):
        return RowReduce(
            p,
            pool,
            source.shape[1],
            lambda r, b: source.at[r, b],
            lambda w, b: core_slots.at[w, b],
            lambda b: y_slots.at[b],
            target,
            add,
        )

    qkv_rows = over_rows(qkv, qkv_core, qkv_y, lambda b: qkv_y.at[b])
    gu_rows = over_rows(gu, gu_core, gu_y, lambda b: gu_y.at[b])
    down_rows = over_rows(down, down_core, down_y, lambda b: down_sum.at[b])
    out_rows = over_rows(out, out_core, out_y, lambda b: out_y.at[b])
    gain_rows = over_rows(gain, gain_core, gain_y, lambda b: gain_y.at[b], add_small)
    qkv_swap = SeqExchange(p, pool, lambda t: qkv_y.at[t], lambda b: qkv_got.at[b])
    gu_swap = SeqExchange(p, pool, lambda t: gu_y.at[t], lambda b: gu_got.at[b])
    out_seq = SeqReduce(
        p,
        pool,
        lambda b: out_y.at[b],
        lambda b: out_side.at[b],
        lambda w, b: out_chain.at[w, b],
        out_sum,
    )
    gain_seq = SeqReduce(
        p,
        pool,
        lambda b: gain_y.at[b],
        lambda b: gain_side.at[b],
        lambda w, b: gain_chain.at[w, b],
        gain_sum,
        add_small,
    )
    members = (gain_rows, gu_rows, qkv_rows, out_rows, down_rows)
    for member in members:
        for block in range(member.blocks):
            member.start(block)
    for member in members:
        for block in range(member.blocks):
            member.step(block)
    for block in range(seqs):
        gain_rows.close(block)
    for t in range(p.n_hi):
        gain_seq.start(t)
    for block in range(seqs):
        gu_rows.close(block)
    gu_swap.start()
    for block in range(seqs):
        qkv_rows.close(block)
    qkv_swap.start()
    for block in range(seqs):
        out_rows.close(block)
    for t in range(p.n_hi):
        out_seq.start(t)
    for block in range(down_rows.blocks):
        down_rows.close(block)
    for t in range(p.n_hi):
        gain_seq.step(t)
        out_seq.step(t)
    for step in range(1, seqs):
        gu_swap.step(step)
        qkv_swap.step(step)
    for member in members + (gu_swap, qkv_swap, out_seq, gain_seq):
        member.finish()


def closing(rows, seqs, qkv, gu, down, out, gain):
    def blocks_of(array, count):
        return array.reshape(rows, count, array.shape[0] // (rows * count), array.shape[1])

    qkv, gu, out, gain = (blocks_of(array, seqs) for array in (qkv, gu, out, gain))
    down = blocks_of(down, 4)
    args = (qkv, gu, down, out, gain)

    def slots(array, copies):
        return pltpu.VMEM(copies + array.shape[1:], array.dtype)

    half = seqs // 2
    shapes = (
        shape_of(qkv.shape[1:]),
        shape_of(gu.shape[1:]),
        shape_of(down.shape[1:], jnp.float32),
        shape_of(out.shape[2:], jnp.float32),
        shape_of(gain.shape[2:], jnp.float32),
    )
    scratch = [slots(array, (2,)) for array in args] + [slots(array, ()) for array in args]
    for array in (out, gain):
        scratch.append(pltpu.VMEM((half,) + array.shape[2:], array.dtype))
        scratch.append(pltpu.VMEM((2, half) + array.shape[2:], array.dtype))
    return call(
        functools.partial(closing_kernel, rows, seqs),
        shapes,
        9,
        args,
        [pltpu.VMEM] * 5,
        (pl.ANY, pl.ANY, pltpu.VMEM, pltpu.VMEM, pltpu.VMEM),
        scratch,
        480,
    )


def dot(left, right, left_axis=1, right_axis=0):
    return lax.dot_general(
        left, right, (((left_axis,), (right_axis,)), ((), ())), preferred_element_type=jnp.float32
    )


def split_local(
    rows,
    seqs,
    inputs,
    lengths,
    w_query,
    w_key,
    w_value,
    w_out,
    gain_attn,
    w_gate,
    w_up,
    w_down,
    gain_mlp,
    cotangent,
):
    low, f32 = jnp.bfloat16, jnp.float32
    tokens, width = inputs.shape[1], inputs.shape[2]
    deep = w_query.shape[0]
    row_tokens = tokens * seqs
    head_size = width // HEADS
    scale = head_size ** (-0.5)
    own_width = width // seqs
    hidden_own = w_gate.shape[1] // seqs
    heads_own = HEADS // seqs
    hidden_block = hidden_own // rows

    def by_heads(weight):
        return weight.reshape(deep, seqs, own_width).transpose(1, 0, 2)

    def by_hidden(weight):
        return (
            weight.reshape(deep, rows, seqs, hidden_block).transpose(2, 0, 1, 3).reshape(seqs, deep, hidden_own)
        )

    wqkv = jnp.concatenate([by_heads(w_query), by_heads(w_key), by_heads(w_value)], axis=2)
    wgu = jnp.concatenate([by_hidden(w_gate), by_hidden(w_up)], axis=2)
    gains_own = jnp.concatenate([gain_attn, gain_mlp]).astype(f32)[None, :]
    gains_own = jnp.broadcast_to(gains_own, (8, 2 * deep))
    x_low, g_low = inputs[0], cotangent[0]
    x_all, g_all, wqkv, wgu, wdown, wout, gains = opening(
        rows, seqs, x_low, g_low, wqkv, wgu, w_down, w_out, gains_own
    )
    gains = gains[:, :, 0, :].reshape(rows * seqs, 2, deep)
    gain_one, gain_two = gains[:, 0].reshape(width), gains[:, 1].reshape(width)
    wqkv = wqkv.reshape(width, 3 * own_width)
    wgu = wgu.reshape(width, 2 * hidden_own)
    wdown = wdown.reshape(hidden_own, width)
    wout = wout.reshape(width, width)
    g_all = g_all.reshape(row_tokens, width)

    x_full = x_all.reshape(row_tokens, width).astype(f32)
    hn = rms_norm(x_full, gain_one).astype(low)
    qkv = dot(hn, wqkv).astype(low)
    queries, keys, values = (
        qkv[:, n * own_width : (n + 1) * own_width].reshape(row_tokens, heads_own, head_size) for n in range(3)
    )
    meta = layout(lengths[0], jnp.arange(row_tokens, dtype=jnp.int32), tokens, seqs)
    segment, position, length_of = meta
    allowed = (segment[:, None] == segment[None, :]) & (position[None, :] <= position[:, None])
    shift = jnp.log(length_of.astype(f32))[None, :, None]

    def sigmoids():
        scores = jnp.einsum("qhd,khd->hqk", queries, keys, preferred_element_type=f32) * scale
        return jnp.where(allowed[None], jax.nn.sigmoid(scores - shift), 0.0)

    sig_low = sigmoids().astype(low)
    attended = jnp.einsum("hqk,khd->qhd", sig_low, values, preferred_element_type=f32)
    attended = to_tokens(rows, seqs, 2, attended.reshape(row_tokens, own_width).astype(low))

    residual = x_low.astype(f32)
    middle = residual + dot(attended, wout)
    h2 = spread(rows, seqs, 3, rms_norm(middle, gain_two).astype(low)).reshape(row_tokens, width)
    gate_up = dot(h2, wgu)
    gate, up = gate_up[:, :hidden_own], gate_up[:, hidden_own:]
    gated, gated_back = jax.vjp(lambda a, b: jax.nn.silu(a) * b, gate, up)
    hidden = gated.astype(low)
    out_part = dot(hidden, wdown).astype(low)
    gate_grad, up_grad = gated_back(dot(g_all, wdown, 1, 1))
    gu_grad = jnp.concatenate([gate_grad.astype(low), up_grad.astype(low)], axis=1)
    h2_part = dot(gu_grad, wgu, 1, 1).astype(low)
    grad_down = dot(hidden, g_all, 0, 0).astype(low)
    grad_gu = dot(h2, gu_grad, 0, 0).astype(low)
    h2_grad, out_sum = reduced(rows, seqs, 4, [h2_part, out_part])
    output = (middle + out_sum).astype(low)

    unused_two, second_back = jax.vjp(rms_norm, middle, gain_two)
    middle_part, gain_two_grad = second_back(h2_grad)
    middle_grad = g_low.astype(f32) + middle_part
    branch = middle_grad.astype(low)
    grad_out = dot(attended, branch, 0, 0).astype(low)
    o_grad = to_heads(rows, seqs, 5, dot(branch, wout, 1, 1).astype(low))
    o_grad = o_grad.reshape(row_tokens, heads_own, head_size)

    sig = sigmoids()
    slopes = jnp.einsum("qhd,khd->hqk", o_grad, values, preferred_element_type=f32)
    score_grad = (slopes * sig * (1.0 - sig)).astype(low)
    q_grad = jnp.einsum("hqk,khd->qhd", score_grad, keys, preferred_element_type=f32) * scale
    k_grad = jnp.einsum("hqk,qhd->khd", score_grad, queries, preferred_element_type=f32) * scale
    v_grad = jnp.einsum("hqk,qhd->khd", sig.astype(low), o_grad, preferred_element_type=f32)
    qkv_grad = jnp.concatenate(
        [member.reshape(row_tokens, own_width).astype(low) for member in (q_grad, k_grad, v_grad)], axis=1
    )
    grad_qkv = dot(hn, qkv_grad, 0, 0).astype(low)
    (hn_grad,) = reduced(rows, seqs, 6, [dot(qkv_grad, wqkv, 1, 1).astype(low)])
    unused_one, first_back = jax.vjp(rms_norm, residual, gain_one)
    residual_part, gain_one_grad = first_back(hn_grad)
    input_grad = middle_grad + residual_part

    gain_grads = jnp.concatenate(
        [gain_one_grad.reshape(rows * seqs, deep), gain_two_grad.reshape(rows * seqs, deep)], axis=1
    )
    gain_grads = jnp.broadcast_to(gain_grads[:, None, :], (rows * seqs, 8, 2 * deep)).reshape(-1, 2 * deep)
    got_qkv, got_gu, sum_down, sum_out, sum_gain = closing(
        rows, seqs, grad_qkv, grad_gu, grad_down, grad_out, gain_grads
    )
    got_qkv = got_qkv.reshape(seqs, deep, 3, own_width).transpose(2, 1, 0, 3).reshape(3, deep, width).astype(f32)
    got_gu = (
        got_gu.reshape(seqs, deep, 2, rows, hidden_block)
        .transpose(2, 1, 3, 0, 4)
        .reshape(2, deep, w_gate.shape[1])
        .astype(f32)
    )
    return (
        output[None],
        input_grad[None],
        got_qkv[0],
        got_qkv[1],
        got_qkv[2],
        sum_out,
        sum_gain[0, :deep],
        got_gu[0],
        got_gu[1],
        sum_down.reshape(w_down.shape),
        sum_gain[0, deep:],
    )


def solution(mesh):
    placed = (
        P("row", "seq", None),
        P("row", None),
        P(("row", "seq"), None),
        P(("row", "seq"), None),
        P(("row", "seq"), None),
        P(("row", "seq"), None),
        P(("row", "seq")),
        P(("row", "seq"), None),
        P(("row", "seq"), None),
        P(("row", "seq"), None),
        P(("row", "seq")),
        P("row", "seq", None),
    )
    row_count, seq_count = mesh.shape["row"], mesh.shape["seq"]
    if row_count == 4 and seq_count % 2 == 0 and HEADS % seq_count == 0:
        local = functools.partial(split_local, row_count, seq_count)
    else:
        local = gathered_local
    return jax.shard_map(
        local,
        mesh=mesh,
        in_specs=placed,
        out_specs=(
            P("row", "seq", None),
            P("row", "seq", None),
            P(("row", "seq"), None),
            P(("row", "seq"), None),
            P(("row", "seq"), None),
            P(("row", "seq"), None),
            P(("row", "seq")),
            P(("row", "seq"), None),
            P(("row", "seq"), None),
            P(("row", "seq"), None),
            P(("row", "seq")),
        ),
        check_vma=False,
    )
```

```python
import functools

import jax
import jax.numpy as jnp
from jax import lax
from jax.experimental import pallas as pl
from jax.experimental.pallas import tpu as pltpu
from jax.sharding import PartitionSpec as P

HEADS = 16


EPSILON = 1e-05


def layout(lengths_row, places, block_rows, block_count):
    unit_counts = lengths_row // (2 * block_count)
    span_sizes = 2 * unit_counts
    offsets = jnp.cumsum(span_sizes) - span_sizes
    device = places // block_rows
    within_block = places - device * block_rows
    inside = (
        (within_block[:, None] >= offsets[None, :])
        & (within_block[:, None] < (offsets + span_sizes)[None, :])
    ).astype(jnp.int32)
    numbers = jnp.arange(lengths_row.shape[0], dtype=jnp.int32)
    segment = jnp.sum(inside * numbers[None, :], axis=1)
    unit_of = jnp.sum(inside * unit_counts[None, :], axis=1)
    begins = jnp.sum(inside * offsets[None, :], axis=1)
    length_of = jnp.sum(inside * lengths_row[None, :], axis=1)
    within = within_block - begins
    position = jnp.where(
        within < unit_of,
        device * unit_of + within,
        (2 * block_count - 1 - device) * unit_of + within - unit_of,
    )
    return (segment, position, length_of)


def rms_norm(values, gain):
    return values * lax.rsqrt(jnp.mean(values * values, axis=-1, keepdims=True) + EPSILON) * gain


def sigmoid_terms(query_heads, query_meta, key_heads, key_meta):
    query_segment, query_position, query_length = query_meta
    key_segment, key_position, unused_length = key_meta
    scores = jnp.einsum(
        "qhd,khd->hqk", query_heads, key_heads, preferred_element_type=jnp.float32
    ) * query_heads.shape[2] ** (-0.5)
    scores = scores - jnp.log(query_length.astype(jnp.float32))[None, :, None]
    allowed = (query_segment[:, None] == key_segment[None, :]) & (
        key_position[None, :] <= query_position[:, None]
    )
    return jnp.where(allowed[None], jax.nn.sigmoid(scores), 0.0)


def pair_terms(query_heads, query_meta, grad_heads, key_heads, key_meta, value_heads):
    sig_terms = sigmoid_terms(query_heads, query_meta, key_heads, key_meta)
    slopes = jnp.einsum("qhd,khd->hqk", grad_heads, value_heads, preferred_element_type=jnp.float32)
    score_grad = (slopes * sig_terms * (1.0 - sig_terms)).astype(jnp.bfloat16)
    return (sig_terms.astype(jnp.bfloat16), score_grad)


def by_blocks(step_fn, running, pieces, block_rows):
    size_total = pieces[0].shape[0]
    part_rows = 4 * block_rows
    block_count = size_total // part_rows

    def turn_over(step_number, carried):
        sub_pieces = tuple(
            (
                lax.dynamic_slice_in_dim(member, step_number * part_rows, part_rows, 0)
                for member in pieces
            )
        )
        return step_fn(carried, sub_pieces, step_number * part_rows)

    return lax.fori_loop(0, block_count, turn_over, running)


def gathered_local(
    inputs,
    lengths,
    w_query,
    w_key,
    w_value,
    w_out,
    gain_attn,
    w_gate,
    w_up,
    w_down,
    gain_mlp,
    cotangent,
):
    residual = inputs[0].astype(jnp.float32)
    tokens_here = residual.shape[0]
    model_width = residual.shape[1]
    head_size = model_width // HEADS
    score_scale = head_size ** (-0.5)
    block_total = lax.axis_size("seq")
    lengths_row = lengths[0]
    places = lax.axis_index("seq") * tokens_here + jnp.arange(tokens_here, dtype=jnp.int32)
    own_meta = layout(lengths_row, places, tokens_here, block_total)

    def meta_at(start_row, row_count):
        return layout(
            lengths_row,
            start_row + jnp.arange(row_count, dtype=jnp.int32),
            tokens_here,
            block_total,
        )

    def heads_of(matrix):
        return matrix.reshape(matrix.shape[0], HEADS, head_size)

    query_full, key_full, value_full, out_full, gain_one = (
        lax.all_gather(w_query, ("row", "seq"), axis=0, tiled=True),
        lax.all_gather(w_key, ("row", "seq"), axis=0, tiled=True),
        lax.all_gather(w_value, ("row", "seq"), axis=0, tiled=True),
        lax.all_gather(w_out, ("row", "seq"), axis=0, tiled=True),
        lax.all_gather(gain_attn, ("row", "seq"), axis=0, tiled=True),
    )
    gain_one_f = gain_one.astype(jnp.float32)
    normed = rms_norm(residual, gain_one_f).astype(jnp.bfloat16)
    queries = jnp.dot(normed, query_full, preferred_element_type=jnp.float32).astype(jnp.bfloat16)
    key_rows = jnp.dot(normed, key_full, preferred_element_type=jnp.float32).astype(jnp.bfloat16)
    value_rows = jnp.dot(normed, value_full, preferred_element_type=jnp.float32).astype(
        jnp.bfloat16
    )
    query_heads = heads_of(queries)

    def forward_step(running, pieces, start_row):
        key_piece, value_piece = pieces
        sig_terms = sigmoid_terms(
            query_heads, own_meta, heads_of(key_piece), meta_at(start_row, key_piece.shape[0])
        ).astype(jnp.bfloat16)
        added = jnp.einsum(
            "hqk,khd->qhd", sig_terms, heads_of(value_piece), preferred_element_type=jnp.float32
        )
        return running + added.reshape(tokens_here, model_width)

    attended = by_blocks(
        forward_step,
        jnp.zeros((tokens_here, model_width), jnp.float32),
        (
            lax.all_gather(key_rows, "seq", axis=0, tiled=True),
            lax.all_gather(value_rows, "seq", axis=0, tiled=True),
        ),
        tokens_here,
    )
    attended_low = attended.astype(jnp.bfloat16)
    middle = residual + jnp.dot(attended_low, out_full, preferred_element_type=jnp.float32)
    gate_full, up_full, down_full, gain_two = (
        lax.all_gather(w_gate, ("row", "seq"), axis=0, tiled=True),
        lax.all_gather(w_up, ("row", "seq"), axis=0, tiled=True),
        lax.all_gather(w_down, ("row", "seq"), axis=0, tiled=True),
        lax.all_gather(gain_mlp, ("row", "seq"), axis=0, tiled=True),
    )
    gain_two_f = gain_two.astype(jnp.float32)
    normed_mlp = rms_norm(middle, gain_two_f).astype(jnp.bfloat16)
    gate_vals = jnp.dot(normed_mlp, gate_full, preferred_element_type=jnp.float32)
    up_vals = jnp.dot(normed_mlp, up_full, preferred_element_type=jnp.float32)
    gated_prod, gated_back = jax.vjp(
        lambda gate_in, up_in: jax.nn.silu(gate_in) * up_in, gate_vals, up_vals
    )
    hidden = gated_prod.astype(jnp.bfloat16)
    output = (middle + jnp.dot(hidden, down_full, preferred_element_type=jnp.float32)).astype(
        jnp.bfloat16
    )
    upstream_low = cotangent[0]
    upstream = upstream_low.astype(jnp.float32)
    gate_full, up_full, down_full, gain_two = (
        lax.all_gather(w_gate, ("row", "seq"), axis=0, tiled=True),
        lax.all_gather(w_up, ("row", "seq"), axis=0, tiled=True),
        lax.all_gather(w_down, ("row", "seq"), axis=0, tiled=True),
        lax.all_gather(gain_mlp, ("row", "seq"), axis=0, tiled=True),
    )
    gain_two_f = gain_two.astype(jnp.float32)
    grad_down = jnp.dot(hidden.T, upstream_low, preferred_element_type=jnp.float32)
    shared_down = lax.psum_scatter(grad_down, ("row", "seq"), scatter_dimension=0, tiled=True)
    hidden_grad = jnp.dot(upstream_low, down_full.T, preferred_element_type=jnp.float32)
    gate_grad, up_grad = gated_back(hidden_grad)
    gate_low = gate_grad.astype(jnp.bfloat16)
    up_low = up_grad.astype(jnp.bfloat16)
    grad_gate = jnp.dot(normed_mlp.T, gate_low, preferred_element_type=jnp.float32)
    shared_gate = lax.psum_scatter(grad_gate, ("row", "seq"), scatter_dimension=0, tiled=True)
    normed_grad = jnp.dot(gate_low, gate_full.T, preferred_element_type=jnp.float32) + jnp.dot(
        up_low, up_full.T, preferred_element_type=jnp.float32
    )
    unused_mid, second_back = jax.vjp(rms_norm, middle, gain_two_f)
    middle_part, gain_two_grad = second_back(normed_grad)
    middle_grad = upstream + middle_part
    grad_up = jnp.dot(normed_mlp.T, up_low, preferred_element_type=jnp.float32)
    shared_up, shared_gain_two = (
        lax.psum_scatter(grad_up, ("row", "seq"), scatter_dimension=0, tiled=True),
        lax.psum_scatter(gain_two_grad, ("row", "seq"), scatter_dimension=0, tiled=True),
    )
    query_full, key_full, value_full, out_full, gain_one = (
        lax.all_gather(w_query, ("row", "seq"), axis=0, tiled=True),
        lax.all_gather(w_key, ("row", "seq"), axis=0, tiled=True),
        lax.all_gather(w_value, ("row", "seq"), axis=0, tiled=True),
        lax.all_gather(w_out, ("row", "seq"), axis=0, tiled=True),
        lax.all_gather(gain_attn, ("row", "seq"), axis=0, tiled=True),
    )
    gain_one_f = gain_one.astype(jnp.float32)
    branch_low = middle_grad.astype(jnp.bfloat16)
    grad_out = jnp.dot(attended_low.T, branch_low, preferred_element_type=jnp.float32)
    attended_grad = jnp.dot(branch_low, out_full.T, preferred_element_type=jnp.float32).astype(
        jnp.bfloat16
    )
    grad_heads = heads_of(attended_grad)
    key_heads_own = heads_of(key_rows)
    value_heads_own = heads_of(value_rows)

    def query_step(running, pieces, start_row):
        key_piece, value_piece = pieces
        key_piece_heads = heads_of(key_piece)
        unused_terms, score_grad = pair_terms(
            query_heads,
            own_meta,
            grad_heads,
            key_piece_heads,
            meta_at(start_row, key_piece.shape[0]),
            heads_of(value_piece),
        )
        added = jnp.einsum(
            "hqk,khd->qhd", score_grad, key_piece_heads, preferred_element_type=jnp.float32
        )
        return running + added.reshape(tokens_here, model_width) * score_scale

    start_value = jnp.zeros((tokens_here, model_width), jnp.float32)
    folded = by_blocks(
        query_step,
        start_value,
        (
            lax.all_gather(key_rows, "seq", axis=0, tiled=True),
            lax.all_gather(value_rows, "seq", axis=0, tiled=True),
        ),
        tokens_here,
    )

    def key_step(running, pieces, start_row):
        key_sum, value_sum = running
        query_piece, grad_piece = pieces
        row_count = query_piece.shape[0]
        query_piece_heads = heads_of(query_piece)
        grad_piece_heads = heads_of(grad_piece)
        sig_low, score_grad = pair_terms(
            query_piece_heads,
            meta_at(start_row, row_count),
            grad_piece_heads,
            key_heads_own,
            own_meta,
            value_heads_own,
        )
        key_add = jnp.einsum(
            "hqk,qhd->khd", score_grad, query_piece_heads, preferred_element_type=jnp.float32
        )
        value_add = jnp.einsum(
            "hqk,qhd->khd", sig_low, grad_piece_heads, preferred_element_type=jnp.float32
        )
        return (
            key_sum + key_add.reshape(tokens_here, model_width) * score_scale,
            value_sum + value_add.reshape(tokens_here, model_width),
        )

    empty_rows = jnp.zeros((tokens_here, model_width), jnp.float32)
    key_grad, value_grad = by_blocks(
        key_step,
        (empty_rows, empty_rows),
        (
            lax.all_gather(queries, "seq", axis=0, tiled=True),
            lax.all_gather(attended_grad, "seq", axis=0, tiled=True),
        ),
        tokens_here,
    )
    query_low = folded.astype(jnp.bfloat16)
    key_low = key_grad.astype(jnp.bfloat16)
    value_low = value_grad.astype(jnp.bfloat16)
    grad_query = jnp.dot(normed.T, query_low, preferred_element_type=jnp.float32)
    grad_key = jnp.dot(normed.T, key_low, preferred_element_type=jnp.float32)
    grad_value = jnp.dot(normed.T, value_low, preferred_element_type=jnp.float32)
    normed_back = jnp.dot(query_low, query_full.T, preferred_element_type=jnp.float32)
    normed_back = normed_back + jnp.dot(key_low, key_full.T, preferred_element_type=jnp.float32)
    normed_back = normed_back + jnp.dot(value_low, value_full.T, preferred_element_type=jnp.float32)
    unused_first, first_back = jax.vjp(rms_norm, residual, gain_one_f)
    residual_part, gain_one_grad = first_back(normed_back)
    input_grad = middle_grad + residual_part
    shared_query, shared_key, shared_value, shared_out, shared_gain_one = (
        lax.psum_scatter(grad_query, ("row", "seq"), scatter_dimension=0, tiled=True),
        lax.psum_scatter(grad_key, ("row", "seq"), scatter_dimension=0, tiled=True),
        lax.psum_scatter(grad_value, ("row", "seq"), scatter_dimension=0, tiled=True),
        lax.psum_scatter(grad_out, ("row", "seq"), scatter_dimension=0, tiled=True),
        lax.psum_scatter(gain_one_grad, ("row", "seq"), scatter_dimension=0, tiled=True),
    )
    return (
        output[None],
        input_grad[None],
        shared_query,
        shared_key,
        shared_value,
        shared_out,
        shared_gain_one,
        shared_gate,
        shared_up,
        shared_down,
        shared_gain_two,
    )


MESH = pl.DeviceIdType.MESH
VMEM_BYTES = 60 * 1024 * 1024


class Place:
    def __init__(self, row_count, seq_count):
        self.row_count, self.seq_count = row_count, seq_count
        self.r, self.s = lax.axis_index("row"), lax.axis_index("seq")
        self.n_hi = seq_count // 2
        self.hi, self.lo = self.s // 2, lax.rem(self.s, 2)
        self.r_core = self.r + 1 - 2 * lax.rem(self.r, 2)
        self.r_y = lax.rem(self.r + 2, 4)
        self.r_far = lax.rem(self.r_core + 2, 4)
        self.side = (self.r, self.s + 1 - 2 * self.lo)
        self.up = (self.r, self.s + 2)
        self.down = (self.r, self.s - 2)
        self.core = (self.r_core, self.s)
        self.y = (self.r_y, self.s)
        self.has_up = self.hi < self.n_hi - 1
        self.has_down = self.hi > 0

    def peer(self, step):
        return lax.rem(self.s + step, self.seq_count)

    def chain(self):
        return [(None, self.side), (self.has_up, self.up), (self.has_down, self.down)]

    def peers(self):
        return [(None, (self.r, self.peer(step))) for step in range(1, self.seq_count)]

    def rows(self):
        return [(None, self.core), (None, self.y)]


def greet(devices):
    barrier = pltpu.get_barrier_semaphore()
    total = 0
    for condition, device in devices:
        if condition is None:
            pl.semaphore_signal(barrier, inc=1, device_id=device, device_id_type=MESH)
            total = total + 1
        else:

            @pl.when(condition)
            def _(device=device):
                pl.semaphore_signal(barrier, inc=1, device_id=device, device_id_type=MESH)

            total = total + condition.astype(jnp.int32)
    pl.semaphore_wait(barrier, total)


class Sems:
    def __init__(self, ref):
        self.ref, self.used = ref, 0

    def take(self, count):
        base = self.used
        self.used += count
        assert self.used <= self.ref.shape[0], self.used
        return lambda index: self.ref.at[base + index]


def push(source, target, send, recv, device):
    pltpu.make_async_remote_copy(
        src_ref=source, dst_ref=target, send_sem=send, recv_sem=recv, device_id=device, device_id_type=MESH
    ).start()


def settle(ref, sem):
    pltpu.make_async_copy(ref, ref, sem).wait()


def no_op(block):
    return None


class SeqGather:
    def __init__(self, place, sems, source, at, arrived=no_op):
        self.p, self.source, self.at, self.arrived = place, source, at, arrived
        n = place.n_hi
        self.own, self.up, self.down = sems.take(1), sems.take(n), sems.take(n)
        self.side, self.recv = sems.take(n), sems.take(2 * n)

    def start(self):
        p, s = self.p, self.p.s
        pltpu.make_async_copy(self.source, self.at(s), self.own(0)).start()

        @pl.when(p.has_up)
        def _():
            push(self.source, self.at(s), self.up(0), self.recv(s), p.up)

        @pl.when(p.has_down)
        def _():
            push(self.source, self.at(s), self.down(0), self.recv(s), p.down)

        push(self.source, self.at(s), self.side(p.hi), self.recv(s), p.side)

    def step(self, k):
        p = self.p

        @pl.when(p.hi >= k)
        def _():
            block = p.s - 2 * k
            settle(self.at(block), self.recv(block))

            @pl.when(p.has_up)
            def _():
                push(self.at(block), self.at(block), self.up(k), self.recv(block), p.up)

            push(self.at(block), self.at(block), self.side(p.hi - k), self.recv(block), p.side)
            self.arrived(block)

        @pl.when(p.hi + k < p.n_hi)
        def _():
            block = p.s + 2 * k
            settle(self.at(block), self.recv(block))

            @pl.when(p.has_down)
            def _():
                push(self.at(block), self.at(block), self.down(k), self.recv(block), p.down)

            push(self.at(block), self.at(block), self.side(p.hi + k), self.recv(block), p.side)
            self.arrived(block)

    def aside(self, k):
        p = self.p
        if k == 0:
            block = 2 * p.hi + 1 - p.lo
            settle(self.at(block), self.recv(block))
            self.arrived(block)
            return

        @pl.when(p.hi >= k)
        def _():
            block = 2 * (p.hi - k) + 1 - p.lo
            settle(self.at(block), self.recv(block))
            self.arrived(block)

        @pl.when(p.hi + k < p.n_hi)
        def _():
            block = 2 * (p.hi + k) + 1 - p.lo
            settle(self.at(block), self.recv(block))
            self.arrived(block)

    def finish(self):
        p = self.p
        settle(self.source, self.own(0))
        for k in range(p.n_hi):

            @pl.when(p.has_up & (p.hi >= k))
            def _():
                settle(self.source, self.up(k))

            @pl.when(p.has_down & (p.hi + k < p.n_hi))
            def _():
                settle(self.source, self.down(k))

            settle(self.source, self.side(k))


class SeqExchange:
    def __init__(self, place, sems, piece, at, arrived=no_op):
        self.p, self.piece, self.at, self.arrived = place, piece, at, arrived
        n = place.seq_count
        self.own, self.send, self.recv = sems.take(1), sems.take(n), sems.take(n)

    def start_own(self):
        s = self.p.s
        pltpu.make_async_copy(self.piece(s), self.at(s), self.own(0)).start()

    def start(self):
        p, s = self.p, self.p.s
        self.start_own()
        for step in range(1, p.seq_count):
            t = p.peer(step)
            push(self.piece(t), self.at(s), self.send(step), self.recv(s), (p.r, t))

    def step(self, step):
        block = self.p.peer(self.p.seq_count - step)
        settle(self.at(block), self.recv(block))
        self.arrived(block)

    def finish(self):
        p = self.p
        settle(self.at(p.s), self.own(0))
        for step in range(1, p.seq_count):
            settle(self.at(p.s), self.send(step))


class RowForward:
    def __init__(self, place, sems, blocks, at):
        self.p, self.at, self.blocks = place, at, blocks
        self.core, self.y, self.far = sems.take(blocks), sems.take(blocks), sems.take(blocks)
        self.from_core, self.from_y, self.from_far = sems.take(blocks), sems.take(blocks), sems.take(blocks)

    def forward(self, block, source=None):
        p = self.p
        source = self.at(p.r, block) if source is None else source
        push(source, self.at(p.r, block), self.y(block), self.from_y(block), p.y)
        push(source, self.at(p.r, block), self.core(block), self.from_core(block), p.core)

    def relay(self, block):
        p = self.p
        settle(self.at(p.r_y, block), self.from_y(block))
        push(self.at(p.r_y, block), self.at(p.r_y, block), self.far(block), self.from_far(block), p.core)

    def finish(self):
        p = self.p
        for block in range(self.blocks):
            settle(self.at(p.r_core, block), self.from_core(block))
            settle(self.at(p.r_far, block), self.from_far(block))
            settle(self.at(p.r, block), self.core(block))
            settle(self.at(p.r, block), self.y(block))
            settle(self.at(p.r_y, block), self.far(block))


def add_into(target, *sources):
    @pl.loop(0, target.shape[0] // 16)
    def _(tile):
        rows = pl.ds(pl.multiple_of(tile * 16, 16), 16)
        total = sources[0][rows, :].astype(jnp.float32)
        for source in sources[1:]:
            total = total + source[rows, :].astype(jnp.float32)
        target[rows, :] = total.astype(target.dtype)


def add_small(target, *sources):
    total = sources[0][...].astype(jnp.float32)
    for source in sources[1:]:
        total = total + source[...].astype(jnp.float32)
    target[...] = total.astype(target.dtype)


class SeqReduce:
    def __init__(self, place, sems, at, side_slot, chain_slot, target, add=add_into):
        self.p, self.at, self.add, self.target = place, at, add, target
        self.side_slot, self.chain_slot = side_slot, chain_slot
        n = place.n_hi
        self.side, self.from_side = sems.take(n), sems.take(n)
        self.send, self.recv = sems.take(n), sems.take(2 * n)

    def turn(self, t):
        p = self.p
        n, hi = p.n_hi, p.hi
        low = jnp.where(t < n - 1 - hi, n - 1 - t, t - (n - 1 - hi))
        high = jnp.where(t < hi, t, n - 1 - (t - hi))
        return jnp.where(hi < n // 2, low, high)

    def start(self, t):
        p, block = self.p, self.turn(t)
        push(self.at(2 * block + 1 - p.lo), self.side_slot(block), self.side(block), self.from_side(block), p.side)

    def step(self, t):
        p, n, block = self.p, self.p.n_hi, self.turn(t)
        mine, got = self.at(2 * block + p.lo), self.side_slot(block)
        settle(got, self.from_side(block))
        if t == n - 1:
            return self.close()

        @pl.when(block > p.hi)
        def _():
            @pl.when(p.has_down)
            def _():
                settle(got, self.recv(block))
                self.add(got, mine, got, self.chain_slot(0, block))

            @pl.when(jnp.logical_not(p.has_down))
            def _():
                self.add(got, mine, got)

            push(got, self.chain_slot(0, block), self.send(block), self.recv(block), p.up)

        @pl.when(block < p.hi)
        def _():
            @pl.when(p.has_up)
            def _():
                settle(got, self.recv(n + block))
                self.add(got, mine, got, self.chain_slot(1, block))

            @pl.when(jnp.logical_not(p.has_up))
            def _():
                self.add(got, mine, got)

            push(got, self.chain_slot(1, block), self.send(block), self.recv(n + block), p.down)

    def close(self):
        p, n, hi = self.p, self.p.n_hi, self.p.hi
        mine, got = self.at(p.s), self.side_slot(hi)
        below, above = self.chain_slot(0, hi), self.chain_slot(1, hi)

        @pl.when(p.has_down)
        def _():
            settle(got, self.recv(hi))

        @pl.when(p.has_up)
        def _():
            settle(got, self.recv(n + hi))

        @pl.when(p.has_down & p.has_up)
        def _():
            self.add(self.target, mine, got, below, above)

        @pl.when(p.has_down & jnp.logical_not(p.has_up))
        def _():
            self.add(self.target, mine, got, below)

        @pl.when(jnp.logical_not(p.has_down))
        def _():
            self.add(self.target, mine, got, above)

    def finish(self):
        p = self.p
        for block in range(p.n_hi):
            settle(self.side_slot(block), self.side(block))

            @pl.when(p.hi != block)
            def _():
                settle(self.side_slot(block), self.send(block))


class RowReduce:
    def __init__(self, place, sems, blocks, at, core_slot, y_slot, target, add=add_into):
        self.p, self.at, self.add, self.target = place, at, add, target
        self.core_slot, self.y_slot, self.blocks = core_slot, y_slot, blocks
        self.send, self.recv = sems.take(2 * blocks), sems.take(2 * blocks)
        self.y, self.from_y = sems.take(blocks), sems.take(blocks)

    def start(self, block):
        p, n = self.p, self.blocks
        push(self.at(p.r_far, block), self.core_slot(0, block), self.send(block), self.recv(block), p.core)
        push(self.at(p.r_core, block), self.core_slot(1, block), self.send(n + block), self.recv(n + block), p.core)

    def step(self, block):
        p = self.p
        got = self.core_slot(0, block)
        settle(got, self.recv(block))
        self.add(got, self.at(p.r_y, block), got)
        push(got, self.y_slot(block), self.y(block), self.from_y(block), p.y)

    def close(self, block):
        p = self.p
        settle(self.core_slot(1, block), self.recv(self.blocks + block))
        settle(self.y_slot(block), self.from_y(block))
        self.add(self.target(block), self.at(p.r, block), self.core_slot(1, block), self.y_slot(block))

    def finish(self):
        n = self.blocks
        for block in range(n):
            settle(self.core_slot(0, block), self.send(block))
            settle(self.core_slot(1, block), self.send(n + block))
            settle(self.core_slot(0, block), self.y(block))


def columns(ref, index, width):
    return ref.at[:, pl.ds(pl.multiple_of(index * width, width), width)]


def call(kernel, shapes, ident, args, spaces, out_spaces, scratch, sems):
    return pl.pallas_call(
        kernel,
        out_shape=shapes,
        in_specs=[pl.BlockSpec(memory_space=space) for space in spaces],
        out_specs=jax.tree.map(lambda space: pl.BlockSpec(memory_space=space), out_spaces),
        scratch_shapes=list(scratch) + [pltpu.SemaphoreType.DMA((sems,))],
        compiler_params=pltpu.CompilerParams(
            collective_id=ident, has_side_effects=True, vmem_limit_bytes=VMEM_BYTES
        ),
    )(*args)


def shape_of(dims, dtype=jnp.bfloat16):
    return jax.ShapeDtypeStruct(dims, dtype)


def opening_kernel(rows, seqs, x, g, wqkv, wgu, wdown, wout, gains, xs, gs, vqkv, vgu, vdown, vout, vgains, sems):
    p, pool = Place(rows, seqs), Sems(sems)
    greet(p.peers() + p.rows())
    half = x.shape[0] // 2
    down_blocks, down_rows = vdown.shape[1], vdown.shape[2]

    def part(source, target, c):
        piece = pl.ds(c * half, half)
        return SeqGather(p, pool, source.at[piece], lambda b: target.at[b, piece])

    qkv_rows = RowForward(p, pool, seqs, lambda r, b: vqkv.at[r, b])
    gu_rows = RowForward(p, pool, seqs, lambda r, b: vgu.at[r, b])
    down_fwd = RowForward(p, pool, down_blocks, lambda r, b: vdown.at[r, b])
    out_rows = RowForward(p, pool, seqs, lambda r, b: vout.at[r, b])
    gain_rows = RowForward(p, pool, seqs, lambda r, b: vgains.at[r, b])
    x_parts = [part(x, xs, c) for c in range(2)]
    g_parts = [part(g, gs, c) for c in range(2)]
    qkv = SeqExchange(p, pool, lambda t: wqkv.at[t], lambda b: vqkv.at[p.r, b], qkv_rows.forward)
    gu = SeqExchange(p, pool, lambda t: wgu.at[t], lambda b: vgu.at[p.r, b], gu_rows.forward)
    out = SeqGather(p, pool, wout, lambda b: vout.at[p.r, b], out_rows.forward)
    gain = SeqGather(p, pool, gains, lambda b: vgains.at[p.r, b], gain_rows.forward)
    down_own = pool.take(1)

    gain.start()
    gain_rows.forward(p.s, gains)
    qkv.start()
    qkv_rows.forward(p.s, wqkv.at[p.s])
    for member in x_parts:
        member.start()
    pltpu.make_async_copy(wdown, vdown.at[p.r], down_own(0)).start()
    for block in range(down_blocks):
        down_fwd.forward(block, wdown.at[block])
    gu_rows.forward(p.s, wgu.at[p.s])
    out_rows.forward(p.s, wout)
    gu.start()
    out.start()
    for member in g_parts:
        member.start()
    gathers = [gain] + x_parts + [out] + g_parts
    for k in range(1, p.n_hi):
        for member in gathers:
            member.step(k)
        for step in (2 * k - 1, 2 * k):
            qkv.step(step)
            gu.step(step)
    qkv.step(seqs - 1)
    gu.step(seqs - 1)
    for k in range(p.n_hi):
        for member in gathers:
            member.aside(k)
    for member in (gain_rows, qkv_rows, down_fwd, gu_rows, out_rows):
        for block in range(member.blocks):
            member.relay(block)
    for member in gathers + [qkv, gu, gain_rows, qkv_rows, down_fwd, gu_rows, out_rows]:
        member.finish()
    settle(wdown, down_own(0))


def opening(rows, seqs, x, g, wqkv, wgu, wdown, wout, gains):
    tokens, width = x.shape
    wdown = wdown.reshape(4, wdown.shape[0] // 4, width)
    args = (x, g, wqkv, wgu, wdown, wout, gains)
    shapes = (
        shape_of((seqs, tokens, width)),
        shape_of((seqs, tokens, width)),
        shape_of((rows,) + wqkv.shape),
        shape_of((rows,) + wgu.shape),
        shape_of((rows,) + wdown.shape),
        shape_of((rows, seqs) + wout.shape),
        shape_of((rows, seqs) + gains.shape, jnp.float32),
    )
    return call(
        functools.partial(opening_kernel, rows, seqs), shapes, 1, args, [pl.ANY] * 7, (pl.ANY,) * 7, [], 640
    )


def spread_kernel(rows, seqs, source, target, sems):
    p, pool = Place(rows, seqs), Sems(sems)
    greet(p.chain())
    half = source.shape[0] // 2
    members = []
    for c in range(2):
        piece = pl.ds(c * half, half)
        members.append(SeqGather(p, pool, source.at[piece], lambda b, piece=piece: target.at[b, piece]))
    for member in members:
        member.start()
    for k in range(1, p.n_hi):
        for member in members:
            member.step(k)
    for k in range(p.n_hi):
        for member in members:
            member.aside(k)
    for member in members:
        member.finish()


def spread(rows, seqs, ident, source):
    return call(
        functools.partial(spread_kernel, rows, seqs),
        shape_of((seqs,) + source.shape),
        ident,
        (source,),
        [pltpu.VMEM],
        pltpu.VMEM,
        [],
        128,
    )


def to_tokens_kernel(rows, seqs, source, target, sems):
    p, pool = Place(rows, seqs), Sems(sems)
    greet(p.peers())
    width = source.shape[2]
    member = SeqExchange(p, pool, lambda t: source.at[t], lambda b: columns(target, b, width))
    member.start()
    for step in range(1, seqs):
        member.step(step)
    member.finish()


def to_heads_kernel(rows, seqs, source, target, sems):
    p, pool = Place(rows, seqs), Sems(sems)
    greet(p.peers())
    width = target.shape[2]
    member = SeqExchange(p, pool, lambda t: columns(source, t, width), lambda b: target.at[b])
    member.start()
    for step in range(1, seqs):
        member.step(step)
    member.finish()


def to_tokens(rows, seqs, ident, source):
    tokens = source.shape[0] // seqs
    width = source.shape[1]
    return call(
        functools.partial(to_tokens_kernel, rows, seqs),
        shape_of((tokens, width * seqs)),
        ident,
        (source.reshape(seqs, tokens, width),),
        [pltpu.VMEM],
        pltpu.VMEM,
        [],
        64,
    )


def to_heads(rows, seqs, ident, source):
    tokens, width = source.shape[0], source.shape[1] // seqs
    return call(
        functools.partial(to_heads_kernel, rows, seqs),
        shape_of((seqs, tokens, width)),
        ident,
        (source,),
        [pltpu.VMEM],
        pltpu.VMEM,
        [],
        64,
    ).reshape(seqs * tokens, width)


def seq_reducers(place, pool, source, side, chain, target):
    half = target.shape[0] // 2
    members = []
    for c in range(2):
        piece = pl.ds(c * half, half)
        members.append(
            SeqReduce(
                place,
                pool,
                lambda b, piece=piece: source.at[b, piece],
                lambda b, piece=piece: side.at[b, piece],
                lambda w, b, piece=piece: chain.at[w, b, piece],
                target.at[piece],
            )
        )
    return members


def row_reducer(place, pool, source, core_slots, y_slots, target, add=add_into):
    return RowReduce(
        place,
        pool,
        source.shape[1],
        lambda r, b: source.at[r, b],
        lambda w, b: core_slots.at[w, b],
        lambda b: y_slots.at[b],
        lambda b: target.at[b],
        add,
    )


def middle_kernel(
    rows,
    seqs,
    h2,
    out,
    gu,
    down,
    h2_sum,
    out_sum,
    gu_sum,
    down_sum,
    h2_side,
    h2_chain,
    out_side,
    out_chain,
    gu_core,
    gu_y,
    down_core,
    down_y,
    sems,
):
    p, pool = Place(rows, seqs), Sems(sems)
    greet(p.chain() + p.rows())
    h2_parts = seq_reducers(p, pool, h2, h2_side, h2_chain, h2_sum)
    out_parts = seq_reducers(p, pool, out, out_side, out_chain, out_sum)
    gu_rows = row_reducer(p, pool, gu, gu_core, gu_y, gu_sum)
    down_rows = row_reducer(p, pool, down, down_core, down_y, down_sum)
    row_work = [(gu_rows, b) for b in range(gu_rows.blocks)] + [(down_rows, b) for b in range(down_rows.blocks)]
    for t in range(p.n_hi):
        for member in h2_parts:
            member.start(t)
    for member, block in row_work:
        member.start(block)
    for t in range(p.n_hi):
        for member in out_parts:
            member.start(t)
    turns = [(member, t) for parts in (h2_parts, out_parts) for t in range(p.n_hi) for member in parts]
    first = p.n_hi
    share = -(-len(row_work) // first)
    for number in range(first):
        for member, t in turns[2 * number : 2 * number + 2]:
            member.step(t)
        for member, block in row_work[number * share : (number + 1) * share]:
            member.step(block)
    for member, t in turns[2 * first :]:
        member.step(t)
    for member, block in row_work:
        member.close(block)
    for member in h2_parts + out_parts + [gu_rows, down_rows]:
        member.finish()


def slots(array, copies=()):
    return pltpu.VMEM(copies + array.shape[1:], array.dtype)


def seq_slots(array):
    half = array.shape[0] // 2
    return [
        pltpu.VMEM((half,) + array.shape[1:], array.dtype),
        pltpu.VMEM((2, half) + array.shape[1:], array.dtype),
    ]


def row_slots(array):
    return [slots(array, (2,)), slots(array)]


def row_blocks(rows, array, count):
    return array.reshape(rows, count, array.shape[0] // (rows * count), array.shape[1])


def middle_sums(rows, seqs, h2, out, gu, down):
    h2, out = (array.reshape(seqs, array.shape[0] // seqs, array.shape[1]) for array in (h2, out))
    gu, down = row_blocks(rows, gu, seqs), row_blocks(rows, down, 4)
    shapes = (
        shape_of(h2.shape[1:], jnp.float32),
        shape_of(out.shape[1:], jnp.float32),
        shape_of(gu.shape[1:]),
        shape_of(down.shape[1:]),
    )
    return call(
        functools.partial(middle_kernel, rows, seqs),
        shapes,
        4,
        (h2, out, gu, down),
        [pltpu.VMEM] * 4,
        (pltpu.VMEM,) * 4,
        seq_slots(h2) + seq_slots(out) + row_slots(gu) + row_slots(down),
        320,
    )


class ColumnExchange:
    def __init__(self, place, sems, piece, parts):
        self.p, self.piece, self.parts = place, piece, parts
        n = place.seq_count
        self.own, self.send, self.recv = sems.take(1), sems.take(n), sems.take(n)

    def start(self):
        p, s = self.p, self.p.s
        for step in range(p.seq_count):
            t = p.peer(step)
            piece = self.piece(t)
            for offset, width, target in self.parts(s):
                source = piece.at[:, pl.ds(offset, width)]
                if step == 0:
                    pltpu.make_async_copy(source, target, self.own(0)).start()
                else:
                    push(source, target, self.send(step), self.recv(s), (p.r, t))

    def finish(self):
        p = self.p
        settle(self.piece(p.s), self.own(0))
        for step in range(1, p.seq_count):
            settle(self.piece(p.s), self.send(step))
            settle(self.piece(p.s), self.recv(p.peer(step)))


def late_kernel(
    rows,
    seqs,
    hn,
    out,
    qkv,
    gu,
    hn_sum,
    out_sum,
    qkv_sum,
    gate_got,
    up_got,
    hn_side,
    hn_chain,
    out_core,
    out_y,
    qkv_core,
    qkv_y,
    sems,
):
    p, pool = Place(rows, seqs), Sems(sems)
    greet(p.peers() + p.rows())
    hn_parts = seq_reducers(p, pool, hn, hn_side, hn_chain, hn_sum)
    out_rows = row_reducer(p, pool, out, out_core, out_y, out_sum)
    qkv_rows = row_reducer(p, pool, qkv, qkv_core, qkv_y, qkv_sum)
    hidden_own = gu.shape[2] // 2
    block = hidden_own // rows

    def gu_parts(s):
        for n, target in ((0, gate_got), (1, up_got)):
            for r in range(rows):
                yield n * hidden_own + r * block, block, columns(target, r * seqs + s, block)

    swap = ColumnExchange(p, pool, lambda t: gu.at[t], gu_parts)
    for t in range(p.n_hi):
        for member in hn_parts:
            member.start(t)
    row_work = [(member, b) for member in (out_rows, qkv_rows) for b in range(member.blocks)]
    for member, b in row_work:
        member.start(b)
    swap.start()
    share = -(-len(row_work) // p.n_hi)
    for t in range(p.n_hi):
        for member in hn_parts:
            member.step(t)
        for member, b in row_work[t * share : (t + 1) * share]:
            member.step(b)
    for member, b in row_work:
        member.close(b)
    for member in hn_parts + [out_rows, qkv_rows, swap]:
        member.finish()


def late_sums(rows, seqs, hn, out, qkv, gu):
    hn = hn.reshape(seqs, hn.shape[0] // seqs, hn.shape[1])
    out, qkv = row_blocks(rows, out, seqs), row_blocks(rows, qkv, seqs)
    got = shape_of((gu.shape[1], gu.shape[2] // 2 * seqs))
    shapes = (
        shape_of(hn.shape[1:], jnp.float32),
        shape_of(out.shape[1:]),
        shape_of(qkv.shape[1:]),
        got,
        got,
    )
    return call(
        functools.partial(late_kernel, rows, seqs),
        shapes,
        6,
        (hn, out, qkv, gu),
        [pltpu.VMEM] * 4,
        (pltpu.VMEM,) * 3 + (pl.ANY,) * 2,
        seq_slots(hn) + row_slots(out) + row_slots(qkv),
        320,
    )


def closing_kernel(
    rows,
    seqs,
    out,
    qkv,
    gain,
    out_sum,
    query_got,
    key_got,
    value_got,
    gain_sum,
    out_side,
    out_chain,
    gain_side,
    gain_chain,
    gain_core,
    gain_y,
    sems,
):
    p, pool = Place(rows, seqs), Sems(sems)
    greet(p.peers() + p.rows())
    own_width = qkv.shape[2] // 3

    def qkv_parts(s):
        for n, target in enumerate((query_got, key_got, value_got)):
            yield n * own_width, own_width, columns(target, s, own_width)

    swap = ColumnExchange(p, pool, lambda t: qkv.at[t], qkv_parts)
    out_seq = SeqReduce(
        p, pool, lambda b: out.at[b], lambda b: out_side.at[b], lambda w, b: out_chain.at[w, b], out_sum
    )
    gain_rows = row_reducer(p, pool, gain, gain_core, gain_y, gain_y, add_small)
    gain_seq = SeqReduce(
        p,
        pool,
        lambda b: gain_y.at[b],
        lambda b: gain_side.at[b],
        lambda w, b: gain_chain.at[w, b],
        gain_sum,
        add_small,
    )
    for block in range(seqs):
        gain_rows.start(block)
    for t in range(p.n_hi):
        out_seq.start(t)
    swap.start()
    for block in range(seqs):
        gain_rows.step(block)
    for block in range(seqs):
        gain_rows.close(block)
    for t in range(p.n_hi):
        gain_seq.start(t)
    for t in range(p.n_hi):
        out_seq.step(t)
        gain_seq.step(t)
    for member in (gain_rows, swap, out_seq, gain_seq):
        member.finish()


def closing(rows, seqs, out, qkv, gain):
    gain = row_blocks(rows, gain, seqs)
    got = shape_of((qkv.shape[1], qkv.shape[2] // 3 * seqs))
    shapes = (shape_of(out.shape[1:]), got, got, got, shape_of(gain.shape[2:], jnp.float32))
    return call(
        functools.partial(closing_kernel, rows, seqs),
        shapes,
        9,
        (out, qkv, gain),
        [pltpu.VMEM] * 3,
        (pltpu.VMEM,) * 5,
        seq_slots(out) + seq_slots(gain[0]) + row_slots(gain),
        320,
    )


def dot(left, right, left_axis=1, right_axis=0):
    return lax.dot_general(
        left, right, (((left_axis,), (right_axis,)), ((), ())), preferred_element_type=jnp.float32
    )


def split_local(
    rows,
    seqs,
    inputs,
    lengths,
    w_query,
    w_key,
    w_value,
    w_out,
    gain_attn,
    w_gate,
    w_up,
    w_down,
    gain_mlp,
    cotangent,
):
    low, f32 = jnp.bfloat16, jnp.float32
    tokens, width = inputs.shape[1], inputs.shape[2]
    deep = w_query.shape[0]
    row_tokens = tokens * seqs
    head_size = width // HEADS
    scale = head_size ** (-0.5)
    own_width = width // seqs
    hidden_own = w_gate.shape[1] // seqs
    heads_own = HEADS // seqs
    hidden_block = hidden_own // rows

    def by_heads(weight):
        return weight.reshape(deep, seqs, own_width).transpose(1, 0, 2)

    def by_hidden(weight):
        return (
            weight.reshape(deep, rows, seqs, hidden_block).transpose(2, 0, 1, 3).reshape(seqs, deep, hidden_own)
        )

    wqkv = jnp.concatenate([by_heads(w_query), by_heads(w_key), by_heads(w_value)], axis=2)
    wgu = jnp.concatenate([by_hidden(w_gate), by_hidden(w_up)], axis=2)
    gains_own = jnp.concatenate([gain_attn, gain_mlp]).astype(f32)[None, :]
    gains_own = jnp.broadcast_to(gains_own, (8, 2 * deep))
    x_low, g_low = inputs[0], cotangent[0]
    x_all, g_all, wqkv, wgu, wdown, wout, gains = opening(
        rows, seqs, x_low, g_low, wqkv, wgu, w_down, w_out, gains_own
    )
    gains = gains[:, :, 0, :].reshape(rows * seqs, 2, deep)
    gain_one, gain_two = gains[:, 0].reshape(width), gains[:, 1].reshape(width)
    wqkv = wqkv.reshape(width, 3 * own_width)
    wgu = wgu.reshape(width, 2 * hidden_own)
    wdown = wdown.reshape(hidden_own, width)
    wout = wout.reshape(width, width)
    g_all = g_all.reshape(row_tokens, width)

    x_full = x_all.reshape(row_tokens, width).astype(f32)
    hn = rms_norm(x_full, gain_one).astype(low)
    qkv = dot(hn, wqkv).astype(low)
    queries, keys, values = (
        qkv[:, n * own_width : (n + 1) * own_width].reshape(row_tokens, heads_own, head_size) for n in range(3)
    )
    meta = layout(lengths[0], jnp.arange(row_tokens, dtype=jnp.int32), tokens, seqs)
    segment, position, length_of = meta
    allowed = (segment[:, None] == segment[None, :]) & (position[None, :] <= position[:, None])
    shift = jnp.log(length_of.astype(f32))[None, :, None]

    def sigmoids():
        scores = jnp.einsum("qhd,khd->hqk", queries, keys, preferred_element_type=f32) * scale
        return jnp.where(allowed[None], jax.nn.sigmoid(scores - shift), 0.0)

    sig_low = sigmoids().astype(low)
    attended = jnp.einsum("hqk,khd->qhd", sig_low, values, preferred_element_type=f32)
    attended = to_tokens(rows, seqs, 2, attended.reshape(row_tokens, own_width).astype(low))

    residual = x_low.astype(f32)
    middle = residual + dot(attended, wout)
    h2 = spread(rows, seqs, 3, rms_norm(middle, gain_two).astype(low)).reshape(row_tokens, width)
    gate_up = dot(h2, wgu)
    gate, up = gate_up[:, :hidden_own], gate_up[:, hidden_own:]
    gated, gated_back = jax.vjp(lambda a, b: jax.nn.silu(a) * b, gate, up)
    hidden = gated.astype(low)
    out_part = dot(hidden, wdown).astype(low)
    gate_grad, up_grad = gated_back(dot(g_all, wdown, 1, 1))
    gu_grad = jnp.concatenate([gate_grad.astype(low), up_grad.astype(low)], axis=1)
    h2_part = dot(gu_grad, wgu, 1, 1).astype(low)
    grad_down = dot(hidden, g_all, 0, 0).astype(low)
    grad_gu = dot(h2, gu_grad, 0, 0).astype(low)
    h2_grad, out_sum, sum_gu, sum_down = middle_sums(rows, seqs, h2_part, out_part, grad_gu, grad_down)
    output = (middle + out_sum).astype(low)

    unused_two, second_back = jax.vjp(rms_norm, middle, gain_two)
    middle_part, gain_two_grad = second_back(h2_grad)
    middle_grad = g_low.astype(f32) + middle_part
    branch = middle_grad.astype(low)
    grad_out = dot(attended, branch, 0, 0).astype(low)
    o_grad = to_heads(rows, seqs, 5, dot(branch, wout, 1, 1).astype(low))
    o_grad = o_grad.reshape(row_tokens, heads_own, head_size)

    sig = sigmoids()
    slopes = jnp.einsum("qhd,khd->hqk", o_grad, values, preferred_element_type=f32)
    score_grad = (slopes * sig * (1.0 - sig)).astype(low)
    q_grad = jnp.einsum("hqk,khd->qhd", score_grad, keys, preferred_element_type=f32) * scale
    k_grad = jnp.einsum("hqk,qhd->khd", score_grad, queries, preferred_element_type=f32) * scale
    v_grad = jnp.einsum("hqk,qhd->khd", sig.astype(low), o_grad, preferred_element_type=f32)
    qkv_grad = jnp.concatenate(
        [member.reshape(row_tokens, own_width).astype(low) for member in (q_grad, k_grad, v_grad)], axis=1
    )
    grad_qkv = dot(hn, qkv_grad, 0, 0).astype(low)
    hn_part = dot(qkv_grad, wqkv, 1, 1).astype(low)
    hn_grad, sum_out, sum_qkv, got_gate, got_up = late_sums(rows, seqs, hn_part, grad_out, grad_qkv, sum_gu)
    unused_one, first_back = jax.vjp(rms_norm, residual, gain_one)
    residual_part, gain_one_grad = first_back(hn_grad)
    input_grad = middle_grad + residual_part

    gain_grads = jnp.concatenate(
        [gain_one_grad.reshape(rows * seqs, deep), gain_two_grad.reshape(rows * seqs, deep)], axis=1
    )
    gain_grads = jnp.broadcast_to(gain_grads[:, None, :], (rows * seqs, 8, 2 * deep)).reshape(-1, 2 * deep)
    sum_out, got_query, got_key, got_value, sum_gain = closing(rows, seqs, sum_out, sum_qkv, gain_grads)
    return (
        output[None],
        input_grad[None],
        got_query.astype(f32),
        got_key.astype(f32),
        got_value.astype(f32),
        sum_out.astype(f32),
        sum_gain[0, :deep],
        got_gate.astype(f32),
        got_up.astype(f32),
        sum_down.reshape(w_down.shape).astype(f32),
        sum_gain[0, deep:],
    )


def solution(mesh):
    placed = (
        P("row", "seq", None),
        P("row", None),
        P(("row", "seq"), None),
        P(("row", "seq"), None),
        P(("row", "seq"), None),
        P(("row", "seq"), None),
        P(("row", "seq")),
        P(("row", "seq"), None),
        P(("row", "seq"), None),
        P(("row", "seq"), None),
        P(("row", "seq")),
        P("row", "seq", None),
    )
    row_count, seq_count = mesh.shape["row"], mesh.shape["seq"]
    if row_count == 4 and seq_count % 2 == 0 and HEADS % seq_count == 0:
        local = functools.partial(split_local, row_count, seq_count)
    else:
        local = gathered_local
    return jax.shard_map(
        local,
        mesh=mesh,
        in_specs=placed,
        out_specs=(
            P("row", "seq", None),
            P("row", "seq", None),
            P(("row", "seq"), None),
            P(("row", "seq"), None),
            P(("row", "seq"), None),
            P(("row", "seq"), None),
            P(("row", "seq")),
            P(("row", "seq"), None),
            P(("row", "seq"), None),
            P(("row", "seq"), None),
            P(("row", "seq")),
        ),
        check_vma=False,
    )
```

```python
import functools

import jax
import jax.numpy as jnp
from jax import lax
from jax.experimental import pallas as pl
from jax.experimental.pallas import tpu as pltpu
from jax.sharding import PartitionSpec as P

HEADS = 16


EPSILON = 1e-05


def layout(lengths_row, places, block_rows, block_count):
    unit_counts = lengths_row // (2 * block_count)
    span_sizes = 2 * unit_counts
    offsets = jnp.cumsum(span_sizes) - span_sizes
    device = places // block_rows
    within_block = places - device * block_rows
    inside = (
        (within_block[:, None] >= offsets[None, :])
        & (within_block[:, None] < (offsets + span_sizes)[None, :])
    ).astype(jnp.int32)
    numbers = jnp.arange(lengths_row.shape[0], dtype=jnp.int32)
    segment = jnp.sum(inside * numbers[None, :], axis=1)
    unit_of = jnp.sum(inside * unit_counts[None, :], axis=1)
    begins = jnp.sum(inside * offsets[None, :], axis=1)
    length_of = jnp.sum(inside * lengths_row[None, :], axis=1)
    within = within_block - begins
    position = jnp.where(
        within < unit_of,
        device * unit_of + within,
        (2 * block_count - 1 - device) * unit_of + within - unit_of,
    )
    return (segment, position, length_of)


def rms_norm(values, gain):
    return values * lax.rsqrt(jnp.mean(values * values, axis=-1, keepdims=True) + EPSILON) * gain


def sigmoid_terms(query_heads, query_meta, key_heads, key_meta):
    query_segment, query_position, query_length = query_meta
    key_segment, key_position, unused_length = key_meta
    scores = jnp.einsum(
        "qhd,khd->hqk", query_heads, key_heads, preferred_element_type=jnp.float32
    ) * query_heads.shape[2] ** (-0.5)
    scores = scores - jnp.log(query_length.astype(jnp.float32))[None, :, None]
    allowed = (query_segment[:, None] == key_segment[None, :]) & (
        key_position[None, :] <= query_position[:, None]
    )
    return jnp.where(allowed[None], jax.nn.sigmoid(scores), 0.0)


def pair_terms(query_heads, query_meta, grad_heads, key_heads, key_meta, value_heads):
    sig_terms = sigmoid_terms(query_heads, query_meta, key_heads, key_meta)
    slopes = jnp.einsum("qhd,khd->hqk", grad_heads, value_heads, preferred_element_type=jnp.float32)
    score_grad = (slopes * sig_terms * (1.0 - sig_terms)).astype(jnp.bfloat16)
    return (sig_terms.astype(jnp.bfloat16), score_grad)


def by_blocks(step_fn, running, pieces, block_rows):
    size_total = pieces[0].shape[0]
    part_rows = 4 * block_rows
    block_count = size_total // part_rows

    def turn_over(step_number, carried):
        sub_pieces = tuple(
            (
                lax.dynamic_slice_in_dim(member, step_number * part_rows, part_rows, 0)
                for member in pieces
            )
        )
        return step_fn(carried, sub_pieces, step_number * part_rows)

    return lax.fori_loop(0, block_count, turn_over, running)


def gathered_local(
    inputs,
    lengths,
    w_query,
    w_key,
    w_value,
    w_out,
    gain_attn,
    w_gate,
    w_up,
    w_down,
    gain_mlp,
    cotangent,
):
    residual = inputs[0].astype(jnp.float32)
    tokens_here = residual.shape[0]
    model_width = residual.shape[1]
    head_size = model_width // HEADS
    score_scale = head_size ** (-0.5)
    block_total = lax.axis_size("seq")
    lengths_row = lengths[0]
    places = lax.axis_index("seq") * tokens_here + jnp.arange(tokens_here, dtype=jnp.int32)
    own_meta = layout(lengths_row, places, tokens_here, block_total)

    def meta_at(start_row, row_count):
        return layout(
            lengths_row,
            start_row + jnp.arange(row_count, dtype=jnp.int32),
            tokens_here,
            block_total,
        )

    def heads_of(matrix):
        return matrix.reshape(matrix.shape[0], HEADS, head_size)

    query_full, key_full, value_full, out_full, gain_one = (
        lax.all_gather(w_query, ("row", "seq"), axis=0, tiled=True),
        lax.all_gather(w_key, ("row", "seq"), axis=0, tiled=True),
        lax.all_gather(w_value, ("row", "seq"), axis=0, tiled=True),
        lax.all_gather(w_out, ("row", "seq"), axis=0, tiled=True),
        lax.all_gather(gain_attn, ("row", "seq"), axis=0, tiled=True),
    )
    gain_one_f = gain_one.astype(jnp.float32)
    normed = rms_norm(residual, gain_one_f).astype(jnp.bfloat16)
    queries = jnp.dot(normed, query_full, preferred_element_type=jnp.float32).astype(jnp.bfloat16)
    key_rows = jnp.dot(normed, key_full, preferred_element_type=jnp.float32).astype(jnp.bfloat16)
    value_rows = jnp.dot(normed, value_full, preferred_element_type=jnp.float32).astype(
        jnp.bfloat16
    )
    query_heads = heads_of(queries)

    def forward_step(running, pieces, start_row):
        key_piece, value_piece = pieces
        sig_terms = sigmoid_terms(
            query_heads, own_meta, heads_of(key_piece), meta_at(start_row, key_piece.shape[0])
        ).astype(jnp.bfloat16)
        added = jnp.einsum(
            "hqk,khd->qhd", sig_terms, heads_of(value_piece), preferred_element_type=jnp.float32
        )
        return running + added.reshape(tokens_here, model_width)

    attended = by_blocks(
        forward_step,
        jnp.zeros((tokens_here, model_width), jnp.float32),
        (
            lax.all_gather(key_rows, "seq", axis=0, tiled=True),
            lax.all_gather(value_rows, "seq", axis=0, tiled=True),
        ),
        tokens_here,
    )
    attended_low = attended.astype(jnp.bfloat16)
    middle = residual + jnp.dot(attended_low, out_full, preferred_element_type=jnp.float32)
    gate_full, up_full, down_full, gain_two = (
        lax.all_gather(w_gate, ("row", "seq"), axis=0, tiled=True),
        lax.all_gather(w_up, ("row", "seq"), axis=0, tiled=True),
        lax.all_gather(w_down, ("row", "seq"), axis=0, tiled=True),
        lax.all_gather(gain_mlp, ("row", "seq"), axis=0, tiled=True),
    )
    gain_two_f = gain_two.astype(jnp.float32)
    normed_mlp = rms_norm(middle, gain_two_f).astype(jnp.bfloat16)
    gate_vals = jnp.dot(normed_mlp, gate_full, preferred_element_type=jnp.float32)
    up_vals = jnp.dot(normed_mlp, up_full, preferred_element_type=jnp.float32)
    gated_prod, gated_back = jax.vjp(
        lambda gate_in, up_in: jax.nn.silu(gate_in) * up_in, gate_vals, up_vals
    )
    hidden = gated_prod.astype(jnp.bfloat16)
    output = (middle + jnp.dot(hidden, down_full, preferred_element_type=jnp.float32)).astype(
        jnp.bfloat16
    )
    upstream_low = cotangent[0]
    upstream = upstream_low.astype(jnp.float32)
    gate_full, up_full, down_full, gain_two = (
        lax.all_gather(w_gate, ("row", "seq"), axis=0, tiled=True),
        lax.all_gather(w_up, ("row", "seq"), axis=0, tiled=True),
        lax.all_gather(w_down, ("row", "seq"), axis=0, tiled=True),
        lax.all_gather(gain_mlp, ("row", "seq"), axis=0, tiled=True),
    )
    gain_two_f = gain_two.astype(jnp.float32)
    grad_down = jnp.dot(hidden.T, upstream_low, preferred_element_type=jnp.float32)
    shared_down = lax.psum_scatter(grad_down, ("row", "seq"), scatter_dimension=0, tiled=True)
    hidden_grad = jnp.dot(upstream_low, down_full.T, preferred_element_type=jnp.float32)
    gate_grad, up_grad = gated_back(hidden_grad)
    gate_low = gate_grad.astype(jnp.bfloat16)
    up_low = up_grad.astype(jnp.bfloat16)
    grad_gate = jnp.dot(normed_mlp.T, gate_low, preferred_element_type=jnp.float32)
    shared_gate = lax.psum_scatter(grad_gate, ("row", "seq"), scatter_dimension=0, tiled=True)
    normed_grad = jnp.dot(gate_low, gate_full.T, preferred_element_type=jnp.float32) + jnp.dot(
        up_low, up_full.T, preferred_element_type=jnp.float32
    )
    unused_mid, second_back = jax.vjp(rms_norm, middle, gain_two_f)
    middle_part, gain_two_grad = second_back(normed_grad)
    middle_grad = upstream + middle_part
    grad_up = jnp.dot(normed_mlp.T, up_low, preferred_element_type=jnp.float32)
    shared_up, shared_gain_two = (
        lax.psum_scatter(grad_up, ("row", "seq"), scatter_dimension=0, tiled=True),
        lax.psum_scatter(gain_two_grad, ("row", "seq"), scatter_dimension=0, tiled=True),
    )
    query_full, key_full, value_full, out_full, gain_one = (
        lax.all_gather(w_query, ("row", "seq"), axis=0, tiled=True),
        lax.all_gather(w_key, ("row", "seq"), axis=0, tiled=True),
        lax.all_gather(w_value, ("row", "seq"), axis=0, tiled=True),
        lax.all_gather(w_out, ("row", "seq"), axis=0, tiled=True),
        lax.all_gather(gain_attn, ("row", "seq"), axis=0, tiled=True),
    )
    gain_one_f = gain_one.astype(jnp.float32)
    branch_low = middle_grad.astype(jnp.bfloat16)
    grad_out = jnp.dot(attended_low.T, branch_low, preferred_element_type=jnp.float32)
    attended_grad = jnp.dot(branch_low, out_full.T, preferred_element_type=jnp.float32).astype(
        jnp.bfloat16
    )
    grad_heads = heads_of(attended_grad)
    key_heads_own = heads_of(key_rows)
    value_heads_own = heads_of(value_rows)

    def query_step(running, pieces, start_row):
        key_piece, value_piece = pieces
        key_piece_heads = heads_of(key_piece)
        unused_terms, score_grad = pair_terms(
            query_heads,
            own_meta,
            grad_heads,
            key_piece_heads,
            meta_at(start_row, key_piece.shape[0]),
            heads_of(value_piece),
        )
        added = jnp.einsum(
            "hqk,khd->qhd", score_grad, key_piece_heads, preferred_element_type=jnp.float32
        )
        return running + added.reshape(tokens_here, model_width) * score_scale

    start_value = jnp.zeros((tokens_here, model_width), jnp.float32)
    folded = by_blocks(
        query_step,
        start_value,
        (
            lax.all_gather(key_rows, "seq", axis=0, tiled=True),
            lax.all_gather(value_rows, "seq", axis=0, tiled=True),
        ),
        tokens_here,
    )

    def key_step(running, pieces, start_row):
        key_sum, value_sum = running
        query_piece, grad_piece = pieces
        row_count = query_piece.shape[0]
        query_piece_heads = heads_of(query_piece)
        grad_piece_heads = heads_of(grad_piece)
        sig_low, score_grad = pair_terms(
            query_piece_heads,
            meta_at(start_row, row_count),
            grad_piece_heads,
            key_heads_own,
            own_meta,
            value_heads_own,
        )
        key_add = jnp.einsum(
            "hqk,qhd->khd", score_grad, query_piece_heads, preferred_element_type=jnp.float32
        )
        value_add = jnp.einsum(
            "hqk,qhd->khd", sig_low, grad_piece_heads, preferred_element_type=jnp.float32
        )
        return (
            key_sum + key_add.reshape(tokens_here, model_width) * score_scale,
            value_sum + value_add.reshape(tokens_here, model_width),
        )

    empty_rows = jnp.zeros((tokens_here, model_width), jnp.float32)
    key_grad, value_grad = by_blocks(
        key_step,
        (empty_rows, empty_rows),
        (
            lax.all_gather(queries, "seq", axis=0, tiled=True),
            lax.all_gather(attended_grad, "seq", axis=0, tiled=True),
        ),
        tokens_here,
    )
    query_low = folded.astype(jnp.bfloat16)
    key_low = key_grad.astype(jnp.bfloat16)
    value_low = value_grad.astype(jnp.bfloat16)
    grad_query = jnp.dot(normed.T, query_low, preferred_element_type=jnp.float32)
    grad_key = jnp.dot(normed.T, key_low, preferred_element_type=jnp.float32)
    grad_value = jnp.dot(normed.T, value_low, preferred_element_type=jnp.float32)
    normed_back = jnp.dot(query_low, query_full.T, preferred_element_type=jnp.float32)
    normed_back = normed_back + jnp.dot(key_low, key_full.T, preferred_element_type=jnp.float32)
    normed_back = normed_back + jnp.dot(value_low, value_full.T, preferred_element_type=jnp.float32)
    unused_first, first_back = jax.vjp(rms_norm, residual, gain_one_f)
    residual_part, gain_one_grad = first_back(normed_back)
    input_grad = middle_grad + residual_part
    shared_query, shared_key, shared_value, shared_out, shared_gain_one = (
        lax.psum_scatter(grad_query, ("row", "seq"), scatter_dimension=0, tiled=True),
        lax.psum_scatter(grad_key, ("row", "seq"), scatter_dimension=0, tiled=True),
        lax.psum_scatter(grad_value, ("row", "seq"), scatter_dimension=0, tiled=True),
        lax.psum_scatter(grad_out, ("row", "seq"), scatter_dimension=0, tiled=True),
        lax.psum_scatter(gain_one_grad, ("row", "seq"), scatter_dimension=0, tiled=True),
    )
    return (
        output[None],
        input_grad[None],
        shared_query,
        shared_key,
        shared_value,
        shared_out,
        shared_gain_one,
        shared_gate,
        shared_up,
        shared_down,
        shared_gain_two,
    )


MESH = pl.DeviceIdType.MESH
VMEM_BYTES = 62 * 1024 * 1024


class Place:
    def __init__(self, row_count, seq_count):
        self.row_count, self.seq_count = row_count, seq_count
        self.r, self.s = lax.axis_index("row"), lax.axis_index("seq")
        self.n_hi = seq_count // 2
        self.hi, self.lo = self.s // 2, lax.rem(self.s, 2)
        self.r_core = self.r + 1 - 2 * lax.rem(self.r, 2)
        self.r_y = lax.rem(self.r + 2, 4)
        self.r_far = lax.rem(self.r_core + 2, 4)
        self.side = (self.r, self.s + 1 - 2 * self.lo)
        self.up = (self.r, self.s + 2)
        self.down = (self.r, self.s - 2)
        self.core = (self.r_core, self.s)
        self.y = (self.r_y, self.s)
        self.has_up = self.hi < self.n_hi - 1
        self.has_down = self.hi > 0

    def peer(self, step):
        return lax.rem(self.s + step, self.seq_count)

    def chain(self):
        return [(None, self.side), (self.has_up, self.up), (self.has_down, self.down)]

    def peers(self):
        return [(None, (self.r, self.peer(step))) for step in range(1, self.seq_count)]

    def rows(self):
        return [(None, self.core), (None, self.y)]


def greet(devices):
    barrier = pltpu.get_barrier_semaphore()
    total = 0
    for condition, device in devices:
        if condition is None:
            pl.semaphore_signal(barrier, inc=1, device_id=device, device_id_type=MESH)
            total = total + 1
        else:

            @pl.when(condition)
            def _(device=device):
                pl.semaphore_signal(barrier, inc=1, device_id=device, device_id_type=MESH)

            total = total + condition.astype(jnp.int32)
    pl.semaphore_wait(barrier, total)


class Sems:
    def __init__(self, ref):
        self.ref, self.used = ref, 0

    def take(self, count):
        base = self.used
        self.used += count
        assert self.used <= self.ref.shape[0], self.used
        return lambda index: self.ref.at[base + index]


def push(source, target, send, recv, device):
    pltpu.make_async_remote_copy(
        src_ref=source, dst_ref=target, send_sem=send, recv_sem=recv, device_id=device, device_id_type=MESH
    ).start()


def settle(ref, sem):
    pltpu.make_async_copy(ref, ref, sem).wait()


def no_op(block):
    return None


class SeqGather:
    def __init__(self, place, sems, source, at, arrived=no_op):
        self.p, self.source, self.at, self.arrived = place, source, at, arrived
        n = place.n_hi
        self.own, self.up, self.down = sems.take(1), sems.take(n), sems.take(n)
        self.side, self.recv = sems.take(n), sems.take(2 * n)

    def start(self):
        p, s = self.p, self.p.s
        pltpu.make_async_copy(self.source, self.at(s), self.own(0)).start()

        @pl.when(p.has_up)
        def _():
            push(self.source, self.at(s), self.up(0), self.recv(s), p.up)

        @pl.when(p.has_down)
        def _():
            push(self.source, self.at(s), self.down(0), self.recv(s), p.down)

        push(self.source, self.at(s), self.side(p.hi), self.recv(s), p.side)

    def step(self, k):
        p = self.p

        @pl.when(p.hi >= k)
        def _():
            block = p.s - 2 * k
            settle(self.at(block), self.recv(block))

            @pl.when(p.has_up)
            def _():
                push(self.at(block), self.at(block), self.up(k), self.recv(block), p.up)

            push(self.at(block), self.at(block), self.side(p.hi - k), self.recv(block), p.side)
            self.arrived(block)

        @pl.when(p.hi + k < p.n_hi)
        def _():
            block = p.s + 2 * k
            settle(self.at(block), self.recv(block))

            @pl.when(p.has_down)
            def _():
                push(self.at(block), self.at(block), self.down(k), self.recv(block), p.down)

            push(self.at(block), self.at(block), self.side(p.hi + k), self.recv(block), p.side)
            self.arrived(block)

    def aside(self, k):
        p = self.p
        if k == 0:
            block = 2 * p.hi + 1 - p.lo
            settle(self.at(block), self.recv(block))
            self.arrived(block)
            return

        @pl.when(p.hi >= k)
        def _():
            block = 2 * (p.hi - k) + 1 - p.lo
            settle(self.at(block), self.recv(block))
            self.arrived(block)

        @pl.when(p.hi + k < p.n_hi)
        def _():
            block = 2 * (p.hi + k) + 1 - p.lo
            settle(self.at(block), self.recv(block))
            self.arrived(block)

    def finish(self):
        p = self.p
        settle(self.source, self.own(0))
        for k in range(p.n_hi):

            @pl.when(p.has_up & (p.hi >= k))
            def _():
                settle(self.source, self.up(k))

            @pl.when(p.has_down & (p.hi + k < p.n_hi))
            def _():
                settle(self.source, self.down(k))

            settle(self.source, self.side(k))


class SeqExchange:
    def __init__(self, place, sems, piece, at, arrived=no_op):
        self.p, self.piece, self.at, self.arrived = place, piece, at, arrived
        n = place.seq_count
        self.own, self.send, self.recv = sems.take(1), sems.take(n), sems.take(n)

    def start_own(self):
        s = self.p.s
        pltpu.make_async_copy(self.piece(s), self.at(s), self.own(0)).start()

    def start(self):
        p, s = self.p, self.p.s
        self.start_own()
        for step in range(1, p.seq_count):
            t = p.peer(step)
            push(self.piece(t), self.at(s), self.send(step), self.recv(s), (p.r, t))

    def step(self, step):
        block = self.p.peer(self.p.seq_count - step)
        settle(self.at(block), self.recv(block))
        self.arrived(block)

    def finish(self):
        p = self.p
        settle(self.at(p.s), self.own(0))
        for step in range(1, p.seq_count):
            settle(self.at(p.s), self.send(step))


class RowForward:
    def __init__(self, place, sems, blocks, at):
        self.p, self.at, self.blocks = place, at, blocks
        self.core, self.y, self.far = sems.take(blocks), sems.take(blocks), sems.take(blocks)
        self.from_core, self.from_y, self.from_far = sems.take(blocks), sems.take(blocks), sems.take(blocks)

    def forward(self, block, source=None):
        p = self.p
        source = self.at(p.r, block) if source is None else source
        push(source, self.at(p.r, block), self.y(block), self.from_y(block), p.y)
        push(source, self.at(p.r, block), self.core(block), self.from_core(block), p.core)

    def relay(self, block):
        p = self.p
        settle(self.at(p.r_y, block), self.from_y(block))
        push(self.at(p.r_y, block), self.at(p.r_y, block), self.far(block), self.from_far(block), p.core)

    def finish(self):
        p = self.p
        for block in range(self.blocks):
            settle(self.at(p.r_core, block), self.from_core(block))
            settle(self.at(p.r_far, block), self.from_far(block))
            settle(self.at(p.r, block), self.core(block))
            settle(self.at(p.r, block), self.y(block))
            settle(self.at(p.r_y, block), self.far(block))


def add_into(target, *sources):
    @pl.loop(0, target.shape[0] // 16)
    def _(tile):
        rows = pl.ds(pl.multiple_of(tile * 16, 16), 16)
        total = sources[0][rows, :].astype(jnp.float32)
        for source in sources[1:]:
            total = total + source[rows, :].astype(jnp.float32)
        target[rows, :] = total.astype(target.dtype)


def add_small(target, *sources):
    total = sources[0][...].astype(jnp.float32)
    for source in sources[1:]:
        total = total + source[...].astype(jnp.float32)
    target[...] = total.astype(target.dtype)


class SeqReduce:
    def __init__(self, place, sems, at, side_slot, chain_slot, target, add=add_into):
        self.p, self.at, self.add, self.target = place, at, add, target
        self.side_slot, self.chain_slot = side_slot, chain_slot
        n = place.n_hi
        self.side, self.from_side = sems.take(n), sems.take(n)
        self.send, self.recv = sems.take(n), sems.take(2 * n)

    def turn(self, t):
        p = self.p
        n, hi = p.n_hi, p.hi
        low = jnp.where(t < n - 1 - hi, n - 1 - t, t - (n - 1 - hi))
        high = jnp.where(t < hi, t, n - 1 - (t - hi))
        return jnp.where(hi < n // 2, low, high)

    def start(self, t):
        p, block = self.p, self.turn(t)
        push(self.at(2 * block + 1 - p.lo), self.side_slot(block), self.side(block), self.from_side(block), p.side)

    def step(self, t):
        p, n, block = self.p, self.p.n_hi, self.turn(t)
        mine, got = self.at(2 * block + p.lo), self.side_slot(block)
        settle(got, self.from_side(block))
        if t == n - 1:
            return self.close()

        @pl.when(block > p.hi)
        def _():
            @pl.when(p.has_down)
            def _():
                settle(got, self.recv(block))
                self.add(got, mine, got, self.chain_slot(0, block))

            @pl.when(jnp.logical_not(p.has_down))
            def _():
                self.add(got, mine, got)

            push(got, self.chain_slot(0, block), self.send(block), self.recv(block), p.up)

        @pl.when(block < p.hi)
        def _():
            @pl.when(p.has_up)
            def _():
                settle(got, self.recv(n + block))
                self.add(got, mine, got, self.chain_slot(1, block))

            @pl.when(jnp.logical_not(p.has_up))
            def _():
                self.add(got, mine, got)

            push(got, self.chain_slot(1, block), self.send(block), self.recv(n + block), p.down)

    def close(self):
        p, n, hi = self.p, self.p.n_hi, self.p.hi
        mine, got = self.at(p.s), self.side_slot(hi)
        below, above = self.chain_slot(0, hi), self.chain_slot(1, hi)

        @pl.when(p.has_down)
        def _():
            settle(got, self.recv(hi))

        @pl.when(p.has_up)
        def _():
            settle(got, self.recv(n + hi))

        @pl.when(p.has_down & p.has_up)
        def _():
            self.add(self.target, mine, got, below, above)

        @pl.when(p.has_down & jnp.logical_not(p.has_up))
        def _():
            self.add(self.target, mine, got, below)

        @pl.when(jnp.logical_not(p.has_down))
        def _():
            self.add(self.target, mine, got, above)

    def finish(self):
        p = self.p
        for block in range(p.n_hi):
            settle(self.side_slot(block), self.side(block))

            @pl.when(p.hi != block)
            def _():
                settle(self.side_slot(block), self.send(block))


class RowReduce:
    def __init__(self, place, sems, blocks, at, core_slot, y_slot, target, add=add_into):
        self.p, self.at, self.add, self.target = place, at, add, target
        self.core_slot, self.y_slot, self.blocks = core_slot, y_slot, blocks
        self.send, self.recv = sems.take(2 * blocks), sems.take(2 * blocks)
        self.y, self.from_y = sems.take(blocks), sems.take(blocks)

    def start(self, block):
        p, n = self.p, self.blocks
        push(self.at(p.r_far, block), self.core_slot(0, block), self.send(block), self.recv(block), p.core)
        push(self.at(p.r_core, block), self.core_slot(1, block), self.send(n + block), self.recv(n + block), p.core)

    def step(self, block):
        p = self.p
        got = self.core_slot(0, block)
        settle(got, self.recv(block))
        self.add(got, self.at(p.r_y, block), got)
        push(got, self.y_slot(block), self.y(block), self.from_y(block), p.y)

    def close(self, block):
        p = self.p
        settle(self.core_slot(1, block), self.recv(self.blocks + block))
        settle(self.y_slot(block), self.from_y(block))
        self.add(self.target(block), self.at(p.r, block), self.core_slot(1, block), self.y_slot(block))

    def finish(self):
        n = self.blocks
        for block in range(n):
            settle(self.core_slot(0, block), self.send(block))
            settle(self.core_slot(1, block), self.send(n + block))
            settle(self.core_slot(0, block), self.y(block))


def columns(ref, index, width):
    return ref.at[:, pl.ds(pl.multiple_of(index * width, width), width)]


def call(kernel, shapes, ident, args, spaces, out_spaces, scratch, sems):
    return pl.pallas_call(
        kernel,
        out_shape=shapes,
        in_specs=[pl.BlockSpec(memory_space=space) for space in spaces],
        out_specs=jax.tree.map(lambda space: pl.BlockSpec(memory_space=space), out_spaces),
        scratch_shapes=list(scratch) + [pltpu.SemaphoreType.DMA((sems,))],
        compiler_params=pltpu.CompilerParams(
            collective_id=ident, has_side_effects=True, vmem_limit_bytes=VMEM_BYTES
        ),
    )(*args)


def shape_of(dims, dtype=jnp.bfloat16):
    return jax.ShapeDtypeStruct(dims, dtype)


def opening_kernel(rows, seqs, x, g, wqkv, wgu, wdown, wout, gains, xs, gs, vqkv, vgu, vdown, vout, vgains, sems):
    p, pool = Place(rows, seqs), Sems(sems)
    greet(p.peers() + p.rows())
    half = x.shape[0] // 2
    down_blocks, down_rows = vdown.shape[1], vdown.shape[2]

    def part(source, target, c):
        piece = pl.ds(c * half, half)
        return SeqGather(p, pool, source.at[piece], lambda b: target.at[b, piece])

    qkv_rows = RowForward(p, pool, seqs, lambda r, b: vqkv.at[r, b])
    gu_rows = RowForward(p, pool, seqs, lambda r, b: vgu.at[r, b])
    down_fwd = RowForward(p, pool, down_blocks, lambda r, b: vdown.at[r, b])
    out_rows = RowForward(p, pool, seqs, lambda r, b: vout.at[r, b])
    gain_rows = RowForward(p, pool, seqs, lambda r, b: vgains.at[r, b])
    x_parts = [part(x, xs, c) for c in range(2)]
    g_parts = [part(g, gs, c) for c in range(2)]
    qkv = SeqExchange(p, pool, lambda t: wqkv.at[t], lambda b: vqkv.at[p.r, b], qkv_rows.forward)
    gu = SeqExchange(p, pool, lambda t: wgu.at[t], lambda b: vgu.at[p.r, b], gu_rows.forward)
    out = SeqGather(p, pool, wout, lambda b: vout.at[p.r, b], out_rows.forward)
    gain = SeqGather(p, pool, gains, lambda b: vgains.at[p.r, b], gain_rows.forward)
    down_own = pool.take(1)

    gain.start()
    gain_rows.forward(p.s, gains)
    qkv.start()
    qkv_rows.forward(p.s, wqkv.at[p.s])
    for member in x_parts:
        member.start()
    pltpu.make_async_copy(wdown, vdown.at[p.r], down_own(0)).start()
    for block in range(down_blocks):
        down_fwd.forward(block, wdown.at[block])
    gu_rows.forward(p.s, wgu.at[p.s])
    out_rows.forward(p.s, wout)
    gu.start()
    out.start()
    for member in g_parts:
        member.start()
    gathers = [gain] + x_parts + [out] + g_parts
    for k in range(1, p.n_hi):
        for member in gathers:
            member.step(k)
        for step in (2 * k - 1, 2 * k):
            qkv.step(step)
            gu.step(step)
    qkv.step(seqs - 1)
    gu.step(seqs - 1)
    for k in range(p.n_hi):
        for member in gathers:
            member.aside(k)
    for member in (gain_rows, qkv_rows, down_fwd, gu_rows, out_rows):
        for block in range(member.blocks):
            member.relay(block)
    for member in gathers + [qkv, gu, gain_rows, qkv_rows, down_fwd, gu_rows, out_rows]:
        member.finish()
    settle(wdown, down_own(0))


def opening(rows, seqs, x, g, wqkv, wgu, wdown, wout, gains):
    tokens, width = x.shape
    wdown = wdown.reshape(4, wdown.shape[0] // 4, width)
    args = (x, g, wqkv, wgu, wdown, wout, gains)
    shapes = (
        shape_of((seqs, tokens, width)),
        shape_of((seqs, tokens, width)),
        shape_of((rows,) + wqkv.shape),
        shape_of((rows,) + wgu.shape),
        shape_of((rows,) + wdown.shape),
        shape_of((rows, seqs) + wout.shape),
        shape_of((rows, seqs) + gains.shape, jnp.float32),
    )
    return call(
        functools.partial(opening_kernel, rows, seqs), shapes, 1, args, [pl.ANY] * 7, (pl.ANY,) * 7, [], 640
    )


def spread_kernel(rows, seqs, source, target, sems):
    p, pool = Place(rows, seqs), Sems(sems)
    greet(p.chain())
    half = source.shape[0] // 2
    members = []
    for c in range(2):
        piece = pl.ds(c * half, half)
        members.append(SeqGather(p, pool, source.at[piece], lambda b, piece=piece: target.at[b, piece]))
    for member in members:
        member.start()
    for k in range(1, p.n_hi):
        for member in members:
            member.step(k)
    for k in range(p.n_hi):
        for member in members:
            member.aside(k)
    for member in members:
        member.finish()


def spread(rows, seqs, ident, source):
    return call(
        functools.partial(spread_kernel, rows, seqs),
        shape_of((seqs,) + source.shape),
        ident,
        (source,),
        [pltpu.VMEM],
        pltpu.VMEM,
        [],
        128,
    )


def to_tokens_kernel(rows, seqs, source, target, sems):
    p, pool = Place(rows, seqs), Sems(sems)
    greet(p.peers())
    width = source.shape[2]
    member = SeqExchange(p, pool, lambda t: source.at[t], lambda b: columns(target, b, width))
    member.start()
    for step in range(1, seqs):
        member.step(step)
    member.finish()


def to_heads_kernel(rows, seqs, source, target, sems):
    p, pool = Place(rows, seqs), Sems(sems)
    greet(p.peers())
    width = target.shape[2]
    member = SeqExchange(p, pool, lambda t: columns(source, t, width), lambda b: target.at[b])
    member.start()
    for step in range(1, seqs):
        member.step(step)
    member.finish()


def to_tokens(rows, seqs, ident, source):
    tokens = source.shape[0] // seqs
    width = source.shape[1]
    return call(
        functools.partial(to_tokens_kernel, rows, seqs),
        shape_of((tokens, width * seqs)),
        ident,
        (source.reshape(seqs, tokens, width),),
        [pltpu.VMEM],
        pltpu.VMEM,
        [],
        64,
    )


def to_heads(rows, seqs, ident, source):
    tokens, width = source.shape[0], source.shape[1] // seqs
    return call(
        functools.partial(to_heads_kernel, rows, seqs),
        shape_of((seqs, tokens, width)),
        ident,
        (source,),
        [pltpu.VMEM],
        pltpu.VMEM,
        [],
        64,
    ).reshape(seqs * tokens, width)


def seq_reducers(place, pool, source, side, chain, target):
    half = target.shape[0] // 2
    members = []
    for c in range(2):
        piece = pl.ds(c * half, half)
        members.append(
            SeqReduce(
                place,
                pool,
                lambda b, piece=piece: source.at[b, piece],
                lambda b, piece=piece: side.at[b, piece],
                lambda w, b, piece=piece: chain.at[w, b, piece],
                target.at[piece],
            )
        )
    return members


def row_reducer(place, pool, source, core_slots, y_slots, target, add=add_into):
    return RowReduce(
        place,
        pool,
        source.shape[1],
        lambda r, b: source.at[r, b],
        lambda w, b: core_slots.at[w, b],
        lambda b: y_slots.at[b],
        lambda b: target.at[b],
        add,
    )


def middle_kernel(
    rows,
    seqs,
    h2,
    out,
    gu,
    down,
    h2_sum,
    out_sum,
    gu_sum,
    down_sum,
    h2_side,
    h2_chain,
    out_side,
    out_chain,
    gu_core,
    gu_y,
    down_core,
    down_y,
    sems,
):
    p, pool = Place(rows, seqs), Sems(sems)
    greet(p.chain() + p.rows())
    h2_parts = seq_reducers(p, pool, h2, h2_side, h2_chain, h2_sum)
    out_parts = seq_reducers(p, pool, out, out_side, out_chain, out_sum)
    gu_rows = row_reducer(p, pool, gu, gu_core, gu_y, gu_sum)
    down_rows = row_reducer(p, pool, down, down_core, down_y, down_sum)
    row_work = [(gu_rows, b) for b in range(gu_rows.blocks)] + [(down_rows, b) for b in range(down_rows.blocks)]
    for t in range(p.n_hi):
        for member in h2_parts:
            member.start(t)
    for member, block in row_work:
        member.start(block)
    for t in range(p.n_hi):
        for member in out_parts:
            member.start(t)
    turns = [(member, t) for parts in (h2_parts, out_parts) for t in range(p.n_hi) for member in parts]
    first = p.n_hi
    share = -(-len(row_work) // first)
    for number in range(first):
        for member, t in turns[2 * number : 2 * number + 2]:
            member.step(t)
        for member, block in row_work[number * share : (number + 1) * share]:
            member.step(block)
    for member, t in turns[2 * first :]:
        member.step(t)
    for member, block in row_work:
        member.close(block)
    for member in h2_parts + out_parts + [gu_rows, down_rows]:
        member.finish()


def slots(array, copies=()):
    return pltpu.VMEM(copies + array.shape[1:], array.dtype)


def seq_slots(array):
    half = array.shape[0] // 2
    return [
        pltpu.VMEM((half,) + array.shape[1:], array.dtype),
        pltpu.VMEM((2, half) + array.shape[1:], array.dtype),
    ]


def row_slots(array):
    return [slots(array, (2,)), slots(array)]


def row_blocks(rows, array, count):
    return array.reshape(rows, count, array.shape[0] // (rows * count), array.shape[1])


def middle_sums(rows, seqs, h2, out, gu, down):
    h2, out = (array.reshape(seqs, array.shape[0] // seqs, array.shape[1]) for array in (h2, out))
    gu, down = row_blocks(rows, gu, seqs), row_blocks(rows, down, 4)
    shapes = (
        shape_of(h2.shape[1:], jnp.float32),
        shape_of(out.shape[1:], jnp.float32),
        shape_of(gu.shape[1:]),
        shape_of(down.shape[1:]),
    )
    return call(
        functools.partial(middle_kernel, rows, seqs),
        shapes,
        4,
        (h2, out, gu, down),
        [pltpu.VMEM] * 4,
        (pltpu.VMEM,) * 4,
        seq_slots(h2) + seq_slots(out) + row_slots(gu) + row_slots(down),
        320,
    )


class ColumnExchange:
    def __init__(self, place, sems, piece, parts):
        self.p, self.piece, self.parts = place, piece, parts
        n = place.seq_count
        self.own, self.send, self.recv = sems.take(1), sems.take(n), sems.take(n)

    def start(self):
        p, s = self.p, self.p.s
        for step in range(p.seq_count):
            t = p.peer(step)
            piece = self.piece(t)
            for offset, width, target in self.parts(s):
                source = piece.at[:, pl.ds(offset, width)]
                if step == 0:
                    pltpu.make_async_copy(source, target, self.own(0)).start()
                else:
                    push(source, target, self.send(step), self.recv(s), (p.r, t))

    def finish(self):
        p = self.p
        settle(self.piece(p.s), self.own(0))
        for step in range(1, p.seq_count):
            settle(self.piece(p.s), self.send(step))
            settle(self.piece(p.s), self.recv(p.peer(step)))


def nt(left, right):
    return lax.dot_general(left, right, (((1,), (1,)), ((), ())), preferred_element_type=jnp.float32)


def tn(left, right):
    return lax.dot_general(left, right, (((0,), (0,)), ((), ())), preferred_element_type=jnp.float32)


def nn(left, right):
    return lax.dot_general(left, right, (((1,), (0,)), ((), ())), preferred_element_type=jnp.float32)


def attention_back(qkv, do, dqkv, key_place, query_low, query_high, shift, dq_turned, head_size):
    tokens, own_width = do.shape
    scale = head_size ** (-0.5)
    keys_step = 256
    for head in range(own_width // head_size):
        lanes = pl.ds(head * head_size, head_size)
        key_lanes = pl.ds(own_width + head * head_size, head_size)
        value_lanes = pl.ds(2 * own_width + head * head_size, head_size)
        dq_turned[...] = jnp.zeros_like(dq_turned)

        @pl.loop(0, tokens // keys_step)
        def _(step):
            rows = pl.ds(pl.multiple_of(step * keys_step, keys_step), keys_step)
            key, value = qkv[rows, key_lanes], qkv[rows, value_lanes]
            queries, grads = qkv[:, lanes], do[:, lanes]
            places = key_place[rows, :]
            allowed = (places >= query_low[...]) & (places <= query_high[...])
            scores = nt(key, queries) * scale - shift[...]
            sig = jnp.where(allowed, jax.nn.sigmoid(scores), 0.0)
            score_grad = (nt(value, grads) * sig * (1.0 - sig)).astype(jnp.bfloat16)
            dqkv[rows, value_lanes] = nn(sig.astype(jnp.bfloat16), grads).astype(jnp.bfloat16)
            dqkv[rows, key_lanes] = (nn(score_grad, queries) * scale).astype(jnp.bfloat16)
            dq_turned[...] += nn(key.T, score_grad)

        dqkv[:, lanes] = (dq_turned[...].T * scale).astype(jnp.bfloat16)


def back_kernel(
    rows,
    seqs,
    head_size,
    do_own,
    qkv,
    hn,
    wqkv,
    out,
    gu,
    gain_two_part,
    gain_one,
    key_place,
    query_low,
    query_high,
    shift,
    hn_sum,
    out_sum,
    query_got,
    key_got,
    value_got,
    gate_got,
    up_got,
    gain_got,
    do,
    dqkv,
    dq_turned,
    hn_part,
    hn_side,
    hn_chain,
    grad_qkv,
    qkv_core,
    qkv_y,
    out_core,
    out_y,
    out_side,
    out_chain,
    gains,
    gain_core,
    gain_y,
    sems,
):
    p, pool = Place(rows, seqs), Sems(sems)
    greet(p.peers() + p.rows())
    tokens, own_width = do.shape
    block_tokens = tokens // seqs
    width = wqkv.shape[0]

    def block_rows(b):
        return pl.ds(pl.multiple_of(b * block_tokens, block_tokens), block_tokens)

    do_swap = SeqExchange(
        p, pool, lambda t: columns(do_own, t, own_width), lambda b: do.at[block_rows(b), :]
    )
    do_swap.start()
    out_rows = row_reducer(p, pool, out, out_core, out_y, out_y)
    for b in range(seqs):
        out_rows.start(b)
    hidden_own = gu.shape[2] // 2
    block = hidden_own // rows

    def gu_parts(s):
        for n, target in ((0, gate_got), (1, up_got)):
            for r in range(rows):
                yield n * hidden_own + r * block, block, columns(target, r * seqs + s, block)

    gu_swap = ColumnExchange(p, pool, lambda t: gu.at[t], gu_parts)

    def qkv_parts(s):
        for n, target in enumerate((query_got, key_got, value_got)):
            yield n * own_width, own_width, columns(target, s, own_width)

    qkv_swap = ColumnExchange(p, pool, lambda t: qkv_y.at[t], qkv_parts)
    qkv_rows = row_reducer(p, pool, grad_qkv, qkv_core, qkv_y, qkv_y)
    hn_parts = seq_reducers(p, pool, hn_part, hn_side, hn_chain, hn_sum)
    out_seq = SeqReduce(
        p, pool, lambda b: out_y.at[b], lambda b: out_side.at[b], lambda w, b: out_chain.at[w, b], out_sum
    )
    quarter = width // rows
    gain_rows = RowReduce(
        p,
        pool,
        1,
        lambda r, b: columns(gains, r, quarter),
        lambda w, b: gain_core.at[w],
        lambda b: gain_y,
        lambda b: gain_y,
        add_small,
    )
    gain_width = 2 * quarter // seqs
    gain_swap = SeqExchange(
        p, pool, lambda t: columns(gain_y, t // 2, gain_width), lambda b: gain_got.at[b]
    )

    for step in range(1, seqs):
        do_swap.step(step)
    settle(do.at[block_rows(p.s), :], do_swap.own(0))
    gu_swap.start()
    for b in range(seqs):
        out_rows.step(b)
    attention_back(qkv, do, dqkv, key_place, query_low, query_high, shift, dq_turned, head_size)

    gains[0:8, :] = jnp.zeros_like(gains[0:8, :])
    gains[8:16, :] = gain_two_part[...]
    column_step = 512
    for t in range(p.n_hi):
        pair = hn_parts[0].turn(t)
        tall = pl.ds(pl.multiple_of(pair * 2 * block_tokens, 2 * block_tokens), 2 * block_tokens)

        @pl.loop(0, width // column_step)
        def _(c):
            lanes = pl.ds(pl.multiple_of(c * column_step, column_step), column_step)
            part = nt(dqkv[tall, :], wqkv[lanes, :])
            hn_part[2 * pair, :, lanes] = part[:block_tokens].astype(jnp.bfloat16)
            hn_part[2 * pair + 1, :, lanes] = part[block_tokens:].astype(jnp.bfloat16)
            terms = part * hn[tall, lanes].astype(jnp.float32)
            gains[0:8, lanes] += jnp.sum(terms.reshape(-1, 8, column_step), axis=0)

        for member in hn_parts:
            member.start(t)
    gains[0:8, :] = gains[0:8, :] / gain_one[...]
    gain_rows.start(0)

    @pl.loop(0, width // 256)
    def _(c):
        lanes = pl.ds(pl.multiple_of(c * 256, 256), 256)
        total = tn(hn[:, lanes], dqkv[...]).astype(jnp.bfloat16)
        piece = total.reshape((4,) + (total.shape[0] // 4, total.shape[1]))
        for n in range(4):
            grad_qkv[c * 4 // seqs, lax.rem(c * 4, seqs) + n] = piece[n]

    for b in range(seqs):
        qkv_rows.start(b)
    gain_rows.step(0)
    for t in range(p.n_hi):
        for member in hn_parts:
            member.step(t)
        if t == 0:
            for b in range(seqs):
                qkv_rows.step(b)
            gain_rows.close(0)
            gain_swap.start()
        if t == 1:
            for b in range(seqs):
                out_rows.close(b)
            for k in range(p.n_hi):
                out_seq.start(k)
        if t == 2:
            for b in range(seqs):
                qkv_rows.close(b)
            qkv_swap.start()
    for t in range(p.n_hi):
        out_seq.step(t)
    for step in range(1, seqs):
        gain_swap.step(step)
        settle(do.at[block_rows(p.s), :], do_swap.send(step))
    for member in hn_parts + [out_rows, qkv_rows, gain_rows, gu_swap, qkv_swap, out_seq, gain_swap]:
        member.finish()


def back(rows, seqs, head_size, do_own, qkv, hn, wqkv, out, gu, gain_two_part, gain_one, meta):
    tokens, own_width = qkv.shape[0], qkv.shape[1] // 3
    width = hn.shape[1]
    low = jnp.bfloat16
    out = row_blocks(rows, out, seqs)
    block_tokens = tokens // seqs
    hn_dims, qkv_dims = (seqs, block_tokens, width), (rows, seqs, width // (rows * seqs), 3 * own_width)
    deep = width // (rows * seqs)
    quarter = width // rows
    got = shape_of((deep, width))
    gu_got = shape_of((deep, gu.shape[2] // 2 * seqs))
    gain_width = 2 * quarter // seqs
    shapes = (
        shape_of(hn_dims[1:], jnp.float32),
        shape_of(out.shape[2:]),
        got,
        got,
        got,
        gu_got,
        gu_got,
        shape_of((seqs, 16, gain_width), jnp.float32),
    )
    hn_like, qkv_like, out_like = shape_of(hn_dims), shape_of(qkv_dims), shape_of(out.shape)
    scratch = (
        [
            pltpu.VMEM((tokens, own_width), low),
            pltpu.VMEM(qkv.shape, low),
            pltpu.VMEM((head_size, tokens), jnp.float32),
            pltpu.VMEM(hn_dims, low),
        ]
        + seq_slots(hn_like)
        + [pltpu.VMEM(qkv_dims, low)]
        + row_slots(qkv_like)
        + row_slots(out_like)
        + seq_slots(shape_of(out.shape[1:]))
        + [
            pltpu.VMEM((16, width), jnp.float32),
            pltpu.VMEM((2, 16, quarter), jnp.float32),
            pltpu.VMEM((16, quarter), jnp.float32),
        ]
    )
    return call(
        functools.partial(back_kernel, rows, seqs, head_size),
        shapes,
        6,
        (do_own, qkv, hn, wqkv, out, gu, gain_two_part, gain_one) + meta,
        [pltpu.VMEM] * 12,
        (pltpu.VMEM,) * 5 + (pl.ANY,) * 2 + (pltpu.VMEM,),
        scratch,
        480,
    )


def dot(left, right, left_axis=1, right_axis=0):
    return lax.dot_general(
        left, right, (((left_axis,), (right_axis,)), ((), ())), preferred_element_type=jnp.float32
    )


def split_local(
    rows,
    seqs,
    inputs,
    lengths,
    w_query,
    w_key,
    w_value,
    w_out,
    gain_attn,
    w_gate,
    w_up,
    w_down,
    gain_mlp,
    cotangent,
):
    low, f32 = jnp.bfloat16, jnp.float32
    tokens, width = inputs.shape[1], inputs.shape[2]
    deep = w_query.shape[0]
    row_tokens = tokens * seqs
    head_size = width // HEADS
    scale = head_size ** (-0.5)
    own_width = width // seqs
    hidden_own = w_gate.shape[1] // seqs
    heads_own = HEADS // seqs
    hidden_block = hidden_own // rows

    def by_heads(weight):
        return weight.reshape(deep, seqs, own_width).transpose(1, 0, 2)

    def by_hidden(weight):
        return (
            weight.reshape(deep, rows, seqs, hidden_block).transpose(2, 0, 1, 3).reshape(seqs, deep, hidden_own)
        )

    wqkv = jnp.concatenate([by_heads(w_query), by_heads(w_key), by_heads(w_value)], axis=2)
    wgu = jnp.concatenate([by_hidden(w_gate), by_hidden(w_up)], axis=2)
    gains_own = jnp.concatenate([gain_attn, gain_mlp]).astype(f32)[None, :]
    gains_own = jnp.broadcast_to(gains_own, (8, 2 * deep))
    x_low, g_low = inputs[0], cotangent[0]
    x_all, g_all, wqkv, wgu, wdown, wout, gains = opening(
        rows, seqs, x_low, g_low, wqkv, wgu, w_down, w_out, gains_own
    )
    gains = gains[:, :, 0, :].reshape(rows * seqs, 2, deep)
    gain_one, gain_two = gains[:, 0].reshape(width), gains[:, 1].reshape(width)
    wqkv = wqkv.reshape(width, 3 * own_width)
    wgu = wgu.reshape(width, 2 * hidden_own)
    wdown = wdown.reshape(hidden_own, width)
    wout = wout.reshape(width, width)
    g_all = g_all.reshape(row_tokens, width)

    x_full = x_all.reshape(row_tokens, width).astype(f32)
    hn = rms_norm(x_full, gain_one).astype(low)
    qkv = dot(hn, wqkv).astype(low)
    queries, keys, values = (
        qkv[:, n * own_width : (n + 1) * own_width].reshape(row_tokens, heads_own, head_size) for n in range(3)
    )
    meta = layout(lengths[0], jnp.arange(row_tokens, dtype=jnp.int32), tokens, seqs)
    segment, position, length_of = meta
    allowed = (segment[:, None] == segment[None, :]) & (position[None, :] <= position[:, None])
    shift = jnp.log(length_of.astype(f32))[None, :, None]

    def sigmoids():
        scores = jnp.einsum("qhd,khd->hqk", queries, keys, preferred_element_type=f32) * scale
        return jnp.where(allowed[None], jax.nn.sigmoid(scores - shift), 0.0)

    sig_low = sigmoids().astype(low)
    attended = jnp.einsum("hqk,khd->qhd", sig_low, values, preferred_element_type=f32)
    attended = to_tokens(rows, seqs, 2, attended.reshape(row_tokens, own_width).astype(low))

    residual = x_low.astype(f32)
    middle = residual + dot(attended, wout)
    h2 = spread(rows, seqs, 3, rms_norm(middle, gain_two).astype(low)).reshape(row_tokens, width)
    gate_up = dot(h2, wgu)
    gate, up = gate_up[:, :hidden_own], gate_up[:, hidden_own:]
    gated, gated_back = jax.vjp(lambda a, b: jax.nn.silu(a) * b, gate, up)
    hidden = gated.astype(low)
    out_part = dot(hidden, wdown).astype(low)
    gate_grad, up_grad = gated_back(dot(g_all, wdown, 1, 1))
    gu_grad = jnp.concatenate([gate_grad.astype(low), up_grad.astype(low)], axis=1)
    h2_part = dot(gu_grad, wgu, 1, 1).astype(low)
    grad_down = dot(hidden, g_all, 0, 0).astype(low)
    grad_gu = dot(h2, gu_grad, 0, 0).astype(low)
    h2_grad, out_sum, sum_gu, sum_down = middle_sums(rows, seqs, h2_part, out_part, grad_gu, grad_down)
    output = (middle + out_sum).astype(low)

    inverse = lax.rsqrt(jnp.mean(middle * middle, axis=-1, keepdims=True) + EPSILON)
    scaled_grad = gain_two * h2_grad
    gain_two_part = jnp.sum((h2_grad * middle * inverse).reshape(-1, 8, width), axis=0)
    middle_grad = (
        g_low.astype(f32)
        + inverse * scaled_grad
        - middle * inverse**3 * jnp.mean(scaled_grad * middle, axis=-1, keepdims=True)
    )
    branch = middle_grad.astype(low)
    grad_out = dot(attended, branch, 0, 0).astype(low)
    do_own = dot(branch, wout, 1, 1).astype(low)
    place = segment * row_tokens + position
    back_meta = (
        place[:, None],
        (segment * row_tokens)[None, :],
        place[None, :],
        jnp.log(length_of.astype(f32))[None, :],
    )
    hn_grad, sum_out, got_query, got_key, got_value, got_gate, got_up, got_gain = back(
        rows, seqs, head_size, do_own, qkv, hn, wqkv, grad_out, sum_gu, gain_two_part, gain_one[None, :], back_meta
    )
    spread_inverse = lax.rsqrt(jnp.mean(residual * residual, axis=-1, keepdims=True) + EPSILON)
    scaled_grad = gain_one * hn_grad
    input_grad = (
        middle_grad
        + spread_inverse * scaled_grad
        - residual * spread_inverse**3 * jnp.mean(scaled_grad * residual, axis=-1, keepdims=True)
    )
    gain_sums = jnp.sum(got_gain, axis=0).reshape(2, 8, 2, deep).sum(axis=1)
    gain_sums = lax.dynamic_index_in_dim(gain_sums, lax.rem(lax.axis_index("seq"), 2), 1, keepdims=False)
    return (
        output[None],
        input_grad[None],
        got_query.astype(f32),
        got_key.astype(f32),
        got_value.astype(f32),
        sum_out.astype(f32),
        gain_sums[0],
        got_gate.astype(f32),
        got_up.astype(f32),
        sum_down.reshape(w_down.shape).astype(f32),
        gain_sums[1],
    )


def solution(mesh):
    placed = (
        P("row", "seq", None),
        P("row", None),
        P(("row", "seq"), None),
        P(("row", "seq"), None),
        P(("row", "seq"), None),
        P(("row", "seq"), None),
        P(("row", "seq")),
        P(("row", "seq"), None),
        P(("row", "seq"), None),
        P(("row", "seq"), None),
        P(("row", "seq")),
        P("row", "seq", None),
    )
    row_count, seq_count = mesh.shape["row"], mesh.shape["seq"]
    if row_count == 4 and seq_count % 2 == 0 and HEADS % seq_count == 0:
        local = functools.partial(split_local, row_count, seq_count)
    else:
        local = gathered_local
    return jax.shard_map(
        local,
        mesh=mesh,
        in_specs=placed,
        out_specs=(
            P("row", "seq", None),
            P("row", "seq", None),
            P(("row", "seq"), None),
            P(("row", "seq"), None),
            P(("row", "seq"), None),
            P(("row", "seq"), None),
            P(("row", "seq")),
            P(("row", "seq"), None),
            P(("row", "seq"), None),
            P(("row", "seq"), None),
            P(("row", "seq")),
        ),
        check_vma=False,
    )
```

```python
import functools

import jax
import jax.numpy as jnp
from jax import lax
from jax.experimental import pallas as pl
from jax.experimental.pallas import tpu as pltpu
from jax.sharding import PartitionSpec as P

HEADS = 16


EPSILON = 1e-05


def layout(lengths_row, places, block_rows, block_count):
    unit_counts = lengths_row // (2 * block_count)
    span_sizes = 2 * unit_counts
    offsets = jnp.cumsum(span_sizes) - span_sizes
    device = places // block_rows
    within_block = places - device * block_rows
    inside = (
        (within_block[:, None] >= offsets[None, :])
        & (within_block[:, None] < (offsets + span_sizes)[None, :])
    ).astype(jnp.int32)
    numbers = jnp.arange(lengths_row.shape[0], dtype=jnp.int32)
    segment = jnp.sum(inside * numbers[None, :], axis=1)
    unit_of = jnp.sum(inside * unit_counts[None, :], axis=1)
    begins = jnp.sum(inside * offsets[None, :], axis=1)
    length_of = jnp.sum(inside * lengths_row[None, :], axis=1)
    within = within_block - begins
    position = jnp.where(
        within < unit_of,
        device * unit_of + within,
        (2 * block_count - 1 - device) * unit_of + within - unit_of,
    )
    return (segment, position, length_of)


def rms_norm(values, gain):
    return values * lax.rsqrt(jnp.mean(values * values, axis=-1, keepdims=True) + EPSILON) * gain


def sigmoid_terms(query_heads, query_meta, key_heads, key_meta):
    query_segment, query_position, query_length = query_meta
    key_segment, key_position, unused_length = key_meta
    scores = jnp.einsum(
        "qhd,khd->hqk", query_heads, key_heads, preferred_element_type=jnp.float32
    ) * query_heads.shape[2] ** (-0.5)
    scores = scores - jnp.log(query_length.astype(jnp.float32))[None, :, None]
    allowed = (query_segment[:, None] == key_segment[None, :]) & (
        key_position[None, :] <= query_position[:, None]
    )
    return jnp.where(allowed[None], jax.nn.sigmoid(scores), 0.0)


def pair_terms(query_heads, query_meta, grad_heads, key_heads, key_meta, value_heads):
    sig_terms = sigmoid_terms(query_heads, query_meta, key_heads, key_meta)
    slopes = jnp.einsum("qhd,khd->hqk", grad_heads, value_heads, preferred_element_type=jnp.float32)
    score_grad = (slopes * sig_terms * (1.0 - sig_terms)).astype(jnp.bfloat16)
    return (sig_terms.astype(jnp.bfloat16), score_grad)


def by_blocks(step_fn, running, pieces, block_rows):
    size_total = pieces[0].shape[0]
    part_rows = 4 * block_rows
    block_count = size_total // part_rows

    def turn_over(step_number, carried):
        sub_pieces = tuple(
            (
                lax.dynamic_slice_in_dim(member, step_number * part_rows, part_rows, 0)
                for member in pieces
            )
        )
        return step_fn(carried, sub_pieces, step_number * part_rows)

    return lax.fori_loop(0, block_count, turn_over, running)


def gathered_local(
    inputs,
    lengths,
    w_query,
    w_key,
    w_value,
    w_out,
    gain_attn,
    w_gate,
    w_up,
    w_down,
    gain_mlp,
    cotangent,
):
    residual = inputs[0].astype(jnp.float32)
    tokens_here = residual.shape[0]
    model_width = residual.shape[1]
    head_size = model_width // HEADS
    score_scale = head_size ** (-0.5)
    block_total = lax.axis_size("seq")
    lengths_row = lengths[0]
    places = lax.axis_index("seq") * tokens_here + jnp.arange(tokens_here, dtype=jnp.int32)
    own_meta = layout(lengths_row, places, tokens_here, block_total)

    def meta_at(start_row, row_count):
        return layout(
            lengths_row,
            start_row + jnp.arange(row_count, dtype=jnp.int32),
            tokens_here,
            block_total,
        )

    def heads_of(matrix):
        return matrix.reshape(matrix.shape[0], HEADS, head_size)

    query_full, key_full, value_full, out_full, gain_one = (
        lax.all_gather(w_query, ("row", "seq"), axis=0, tiled=True),
        lax.all_gather(w_key, ("row", "seq"), axis=0, tiled=True),
        lax.all_gather(w_value, ("row", "seq"), axis=0, tiled=True),
        lax.all_gather(w_out, ("row", "seq"), axis=0, tiled=True),
        lax.all_gather(gain_attn, ("row", "seq"), axis=0, tiled=True),
    )
    gain_one_f = gain_one.astype(jnp.float32)
    normed = rms_norm(residual, gain_one_f).astype(jnp.bfloat16)
    queries = jnp.dot(normed, query_full, preferred_element_type=jnp.float32).astype(jnp.bfloat16)
    key_rows = jnp.dot(normed, key_full, preferred_element_type=jnp.float32).astype(jnp.bfloat16)
    value_rows = jnp.dot(normed, value_full, preferred_element_type=jnp.float32).astype(
        jnp.bfloat16
    )
    query_heads = heads_of(queries)

    def forward_step(running, pieces, start_row):
        key_piece, value_piece = pieces
        sig_terms = sigmoid_terms(
            query_heads, own_meta, heads_of(key_piece), meta_at(start_row, key_piece.shape[0])
        ).astype(jnp.bfloat16)
        added = jnp.einsum(
            "hqk,khd->qhd", sig_terms, heads_of(value_piece), preferred_element_type=jnp.float32
        )
        return running + added.reshape(tokens_here, model_width)

    attended = by_blocks(
        forward_step,
        jnp.zeros((tokens_here, model_width), jnp.float32),
        (
            lax.all_gather(key_rows, "seq", axis=0, tiled=True),
            lax.all_gather(value_rows, "seq", axis=0, tiled=True),
        ),
        tokens_here,
    )
    attended_low = attended.astype(jnp.bfloat16)
    middle = residual + jnp.dot(attended_low, out_full, preferred_element_type=jnp.float32)
    gate_full, up_full, down_full, gain_two = (
        lax.all_gather(w_gate, ("row", "seq"), axis=0, tiled=True),
        lax.all_gather(w_up, ("row", "seq"), axis=0, tiled=True),
        lax.all_gather(w_down, ("row", "seq"), axis=0, tiled=True),
        lax.all_gather(gain_mlp, ("row", "seq"), axis=0, tiled=True),
    )
    gain_two_f = gain_two.astype(jnp.float32)
    normed_mlp = rms_norm(middle, gain_two_f).astype(jnp.bfloat16)
    gate_vals = jnp.dot(normed_mlp, gate_full, preferred_element_type=jnp.float32)
    up_vals = jnp.dot(normed_mlp, up_full, preferred_element_type=jnp.float32)
    gated_prod, gated_back = jax.vjp(
        lambda gate_in, up_in: jax.nn.silu(gate_in) * up_in, gate_vals, up_vals
    )
    hidden = gated_prod.astype(jnp.bfloat16)
    output = (middle + jnp.dot(hidden, down_full, preferred_element_type=jnp.float32)).astype(
        jnp.bfloat16
    )
    upstream_low = cotangent[0]
    upstream = upstream_low.astype(jnp.float32)
    gate_full, up_full, down_full, gain_two = (
        lax.all_gather(w_gate, ("row", "seq"), axis=0, tiled=True),
        lax.all_gather(w_up, ("row", "seq"), axis=0, tiled=True),
        lax.all_gather(w_down, ("row", "seq"), axis=0, tiled=True),
        lax.all_gather(gain_mlp, ("row", "seq"), axis=0, tiled=True),
    )
    gain_two_f = gain_two.astype(jnp.float32)
    grad_down = jnp.dot(hidden.T, upstream_low, preferred_element_type=jnp.float32)
    shared_down = lax.psum_scatter(grad_down, ("row", "seq"), scatter_dimension=0, tiled=True)
    hidden_grad = jnp.dot(upstream_low, down_full.T, preferred_element_type=jnp.float32)
    gate_grad, up_grad = gated_back(hidden_grad)
    gate_low = gate_grad.astype(jnp.bfloat16)
    up_low = up_grad.astype(jnp.bfloat16)
    grad_gate = jnp.dot(normed_mlp.T, gate_low, preferred_element_type=jnp.float32)
    shared_gate = lax.psum_scatter(grad_gate, ("row", "seq"), scatter_dimension=0, tiled=True)
    normed_grad = jnp.dot(gate_low, gate_full.T, preferred_element_type=jnp.float32) + jnp.dot(
        up_low, up_full.T, preferred_element_type=jnp.float32
    )
    unused_mid, second_back = jax.vjp(rms_norm, middle, gain_two_f)
    middle_part, gain_two_grad = second_back(normed_grad)
    middle_grad = upstream + middle_part
    grad_up = jnp.dot(normed_mlp.T, up_low, preferred_element_type=jnp.float32)
    shared_up, shared_gain_two = (
        lax.psum_scatter(grad_up, ("row", "seq"), scatter_dimension=0, tiled=True),
        lax.psum_scatter(gain_two_grad, ("row", "seq"), scatter_dimension=0, tiled=True),
    )
    query_full, key_full, value_full, out_full, gain_one = (
        lax.all_gather(w_query, ("row", "seq"), axis=0, tiled=True),
        lax.all_gather(w_key, ("row", "seq"), axis=0, tiled=True),
        lax.all_gather(w_value, ("row", "seq"), axis=0, tiled=True),
        lax.all_gather(w_out, ("row", "seq"), axis=0, tiled=True),
        lax.all_gather(gain_attn, ("row", "seq"), axis=0, tiled=True),
    )
    gain_one_f = gain_one.astype(jnp.float32)
    branch_low = middle_grad.astype(jnp.bfloat16)
    grad_out = jnp.dot(attended_low.T, branch_low, preferred_element_type=jnp.float32)
    attended_grad = jnp.dot(branch_low, out_full.T, preferred_element_type=jnp.float32).astype(
        jnp.bfloat16
    )
    grad_heads = heads_of(attended_grad)
    key_heads_own = heads_of(key_rows)
    value_heads_own = heads_of(value_rows)

    def query_step(running, pieces, start_row):
        key_piece, value_piece = pieces
        key_piece_heads = heads_of(key_piece)
        unused_terms, score_grad = pair_terms(
            query_heads,
            own_meta,
            grad_heads,
            key_piece_heads,
            meta_at(start_row, key_piece.shape[0]),
            heads_of(value_piece),
        )
        added = jnp.einsum(
            "hqk,khd->qhd", score_grad, key_piece_heads, preferred_element_type=jnp.float32
        )
        return running + added.reshape(tokens_here, model_width) * score_scale

    start_value = jnp.zeros((tokens_here, model_width), jnp.float32)
    folded = by_blocks(
        query_step,
        start_value,
        (
            lax.all_gather(key_rows, "seq", axis=0, tiled=True),
            lax.all_gather(value_rows, "seq", axis=0, tiled=True),
        ),
        tokens_here,
    )

    def key_step(running, pieces, start_row):
        key_sum, value_sum = running
        query_piece, grad_piece = pieces
        row_count = query_piece.shape[0]
        query_piece_heads = heads_of(query_piece)
        grad_piece_heads = heads_of(grad_piece)
        sig_low, score_grad = pair_terms(
            query_piece_heads,
            meta_at(start_row, row_count),
            grad_piece_heads,
            key_heads_own,
            own_meta,
            value_heads_own,
        )
        key_add = jnp.einsum(
            "hqk,qhd->khd", score_grad, query_piece_heads, preferred_element_type=jnp.float32
        )
        value_add = jnp.einsum(
            "hqk,qhd->khd", sig_low, grad_piece_heads, preferred_element_type=jnp.float32
        )
        return (
            key_sum + key_add.reshape(tokens_here, model_width) * score_scale,
            value_sum + value_add.reshape(tokens_here, model_width),
        )

    empty_rows = jnp.zeros((tokens_here, model_width), jnp.float32)
    key_grad, value_grad = by_blocks(
        key_step,
        (empty_rows, empty_rows),
        (
            lax.all_gather(queries, "seq", axis=0, tiled=True),
            lax.all_gather(attended_grad, "seq", axis=0, tiled=True),
        ),
        tokens_here,
    )
    query_low = folded.astype(jnp.bfloat16)
    key_low = key_grad.astype(jnp.bfloat16)
    value_low = value_grad.astype(jnp.bfloat16)
    grad_query = jnp.dot(normed.T, query_low, preferred_element_type=jnp.float32)
    grad_key = jnp.dot(normed.T, key_low, preferred_element_type=jnp.float32)
    grad_value = jnp.dot(normed.T, value_low, preferred_element_type=jnp.float32)
    normed_back = jnp.dot(query_low, query_full.T, preferred_element_type=jnp.float32)
    normed_back = normed_back + jnp.dot(key_low, key_full.T, preferred_element_type=jnp.float32)
    normed_back = normed_back + jnp.dot(value_low, value_full.T, preferred_element_type=jnp.float32)
    unused_first, first_back = jax.vjp(rms_norm, residual, gain_one_f)
    residual_part, gain_one_grad = first_back(normed_back)
    input_grad = middle_grad + residual_part
    shared_query, shared_key, shared_value, shared_out, shared_gain_one = (
        lax.psum_scatter(grad_query, ("row", "seq"), scatter_dimension=0, tiled=True),
        lax.psum_scatter(grad_key, ("row", "seq"), scatter_dimension=0, tiled=True),
        lax.psum_scatter(grad_value, ("row", "seq"), scatter_dimension=0, tiled=True),
        lax.psum_scatter(grad_out, ("row", "seq"), scatter_dimension=0, tiled=True),
        lax.psum_scatter(gain_one_grad, ("row", "seq"), scatter_dimension=0, tiled=True),
    )
    return (
        output[None],
        input_grad[None],
        shared_query,
        shared_key,
        shared_value,
        shared_out,
        shared_gain_one,
        shared_gate,
        shared_up,
        shared_down,
        shared_gain_two,
    )


MESH = pl.DeviceIdType.MESH
VMEM_BYTES = 62 * 1024 * 1024


class Place:
    def __init__(self, row_count, seq_count):
        self.row_count, self.seq_count = row_count, seq_count
        self.r, self.s = lax.axis_index("row"), lax.axis_index("seq")
        self.n_hi = seq_count // 2
        self.hi, self.lo = self.s // 2, lax.rem(self.s, 2)
        self.r_core = self.r + 1 - 2 * lax.rem(self.r, 2)
        self.r_y = lax.rem(self.r + 2, 4)
        self.r_far = lax.rem(self.r_core + 2, 4)
        self.side = (self.r, self.s + 1 - 2 * self.lo)
        self.up = (self.r, self.s + 2)
        self.down = (self.r, self.s - 2)
        self.core = (self.r_core, self.s)
        self.y = (self.r_y, self.s)
        self.has_up = self.hi < self.n_hi - 1
        self.has_down = self.hi > 0

    def peer(self, step):
        return lax.rem(self.s + step, self.seq_count)

    def chain(self):
        return [(None, self.side), (self.has_up, self.up), (self.has_down, self.down)]

    def peers(self):
        return [(None, (self.r, self.peer(step))) for step in range(1, self.seq_count)]

    def rows(self):
        return [(None, self.core), (None, self.y)]


def greet(devices):
    barrier = pltpu.get_barrier_semaphore()
    total = 0
    for condition, device in devices:
        if condition is None:
            pl.semaphore_signal(barrier, inc=1, device_id=device, device_id_type=MESH)
            total = total + 1
        else:

            @pl.when(condition)
            def _(device=device):
                pl.semaphore_signal(barrier, inc=1, device_id=device, device_id_type=MESH)

            total = total + condition.astype(jnp.int32)
    pl.semaphore_wait(barrier, total)


class Sems:
    def __init__(self, ref):
        self.ref, self.used = ref, 0

    def take(self, count):
        base = self.used
        self.used += count
        assert self.used <= self.ref.shape[0], self.used
        return lambda index: self.ref.at[base + index]


def push(source, target, send, recv, device):
    pltpu.make_async_remote_copy(
        src_ref=source, dst_ref=target, send_sem=send, recv_sem=recv, device_id=device, device_id_type=MESH
    ).start()


def settle(ref, sem):
    pltpu.make_async_copy(ref, ref, sem).wait()


def no_op(block):
    return None


class SeqGather:
    def __init__(self, place, sems, source, at, arrived=no_op):
        self.p, self.source, self.at, self.arrived = place, source, at, arrived
        self.own_done = False
        n = place.n_hi
        self.own, self.up, self.down = sems.take(1), sems.take(n), sems.take(n)
        self.side, self.recv = sems.take(n), sems.take(2 * n)

    def start(self):
        p, s = self.p, self.p.s
        pltpu.make_async_copy(self.source, self.at(s), self.own(0)).start()

        @pl.when(p.has_up)
        def _():
            push(self.source, self.at(s), self.up(0), self.recv(s), p.up)

        @pl.when(p.has_down)
        def _():
            push(self.source, self.at(s), self.down(0), self.recv(s), p.down)

        push(self.source, self.at(s), self.side(p.hi), self.recv(s), p.side)

    def step(self, k):
        p = self.p

        @pl.when(p.hi >= k)
        def _():
            block = p.s - 2 * k
            settle(self.at(block), self.recv(block))

            @pl.when(p.has_up)
            def _():
                push(self.at(block), self.at(block), self.up(k), self.recv(block), p.up)

            push(self.at(block), self.at(block), self.side(p.hi - k), self.recv(block), p.side)
            self.arrived(block)

        @pl.when(p.hi + k < p.n_hi)
        def _():
            block = p.s + 2 * k
            settle(self.at(block), self.recv(block))

            @pl.when(p.has_down)
            def _():
                push(self.at(block), self.at(block), self.down(k), self.recv(block), p.down)

            push(self.at(block), self.at(block), self.side(p.hi + k), self.recv(block), p.side)
            self.arrived(block)

    def aside(self, k):
        p = self.p
        if k == 0:
            block = 2 * p.hi + 1 - p.lo
            settle(self.at(block), self.recv(block))
            self.arrived(block)
            return

        @pl.when(p.hi >= k)
        def _():
            block = 2 * (p.hi - k) + 1 - p.lo
            settle(self.at(block), self.recv(block))
            self.arrived(block)

        @pl.when(p.hi + k < p.n_hi)
        def _():
            block = 2 * (p.hi + k) + 1 - p.lo
            settle(self.at(block), self.recv(block))
            self.arrived(block)

    def settle_own(self):
        settle(self.at(self.p.s), self.own(0))
        self.own_done = True

    def finish(self):
        p = self.p
        if not self.own_done:
            self.settle_own()
        for k in range(p.n_hi):

            @pl.when(p.has_up & (p.hi >= k))
            def _():
                settle(self.source, self.up(k))

            @pl.when(p.has_down & (p.hi + k < p.n_hi))
            def _():
                settle(self.source, self.down(k))

            settle(self.source, self.side(k))


class SeqExchange:
    def __init__(self, place, sems, piece, at, arrived=no_op):
        self.p, self.piece, self.at, self.arrived = place, piece, at, arrived
        n = place.seq_count
        self.own, self.send, self.recv = sems.take(1), sems.take(n), sems.take(n)

    def start_own(self):
        s = self.p.s
        pltpu.make_async_copy(self.piece(s), self.at(s), self.own(0)).start()

    def start(self):
        p, s = self.p, self.p.s
        self.start_own()
        for step in range(1, p.seq_count):
            t = p.peer(step)
            push(self.piece(t), self.at(s), self.send(step), self.recv(s), (p.r, t))

    def step(self, step):
        block = self.p.peer(self.p.seq_count - step)
        settle(self.at(block), self.recv(block))
        self.arrived(block)

    def finish(self):
        p = self.p
        settle(self.at(p.s), self.own(0))
        for step in range(1, p.seq_count):
            settle(self.at(p.s), self.send(step))


class RowForward:
    def __init__(self, place, sems, blocks, at):
        self.p, self.at, self.blocks = place, at, blocks
        self.core, self.y, self.far = sems.take(blocks), sems.take(blocks), sems.take(blocks)
        self.from_core, self.from_y, self.from_far = sems.take(blocks), sems.take(blocks), sems.take(blocks)

    def forward(self, block, source=None):
        p = self.p
        source = self.at(p.r, block) if source is None else source
        push(source, self.at(p.r, block), self.y(block), self.from_y(block), p.y)
        push(source, self.at(p.r, block), self.core(block), self.from_core(block), p.core)

    def relay(self, block):
        p = self.p
        settle(self.at(p.r_y, block), self.from_y(block))
        push(self.at(p.r_y, block), self.at(p.r_y, block), self.far(block), self.from_far(block), p.core)

    def finish(self):
        p = self.p
        for block in range(self.blocks):
            settle(self.at(p.r_core, block), self.from_core(block))
            settle(self.at(p.r_far, block), self.from_far(block))
            settle(self.at(p.r, block), self.core(block))
            settle(self.at(p.r, block), self.y(block))
            settle(self.at(p.r_y, block), self.far(block))


def add_into(target, *sources):
    @pl.loop(0, target.shape[0] // 16)
    def _(tile):
        rows = pl.ds(pl.multiple_of(tile * 16, 16), 16)
        total = sources[0][rows, :].astype(jnp.float32)
        for source in sources[1:]:
            total = total + source[rows, :].astype(jnp.float32)
        target[rows, :] = total.astype(target.dtype)


def add_small(target, *sources):
    total = sources[0][...].astype(jnp.float32)
    for source in sources[1:]:
        total = total + source[...].astype(jnp.float32)
    target[...] = total.astype(target.dtype)


class SeqReduce:
    def __init__(self, place, sems, at, side_slot, chain_slot, target, add=add_into):
        self.p, self.at, self.add, self.target = place, at, add, target
        self.side_slot, self.chain_slot = side_slot, chain_slot
        n = place.n_hi
        self.side, self.from_side = sems.take(n), sems.take(n)
        self.send, self.recv = sems.take(n), sems.take(2 * n)

    def turn(self, t):
        p = self.p
        n, hi = p.n_hi, p.hi
        low = jnp.where(t < n - 1 - hi, n - 1 - t, t - (n - 1 - hi))
        high = jnp.where(t < hi, t, n - 1 - (t - hi))
        return jnp.where(hi < n // 2, low, high)

    def start(self, t):
        p, block = self.p, self.turn(t)
        push(self.at(2 * block + 1 - p.lo), self.side_slot(block), self.side(block), self.from_side(block), p.side)

    def step(self, t):
        p, n, block = self.p, self.p.n_hi, self.turn(t)
        mine, got = self.at(2 * block + p.lo), self.side_slot(block)
        settle(got, self.from_side(block))
        if t == n - 1:
            return self.close()

        @pl.when(block > p.hi)
        def _():
            @pl.when(p.has_down)
            def _():
                settle(got, self.recv(block))
                self.add(got, mine, got, self.chain_slot(0, block))

            @pl.when(jnp.logical_not(p.has_down))
            def _():
                self.add(got, mine, got)

            push(got, self.chain_slot(0, block), self.send(block), self.recv(block), p.up)

        @pl.when(block < p.hi)
        def _():
            @pl.when(p.has_up)
            def _():
                settle(got, self.recv(n + block))
                self.add(got, mine, got, self.chain_slot(1, block))

            @pl.when(jnp.logical_not(p.has_up))
            def _():
                self.add(got, mine, got)

            push(got, self.chain_slot(1, block), self.send(block), self.recv(n + block), p.down)

    def close(self):
        p, n, hi = self.p, self.p.n_hi, self.p.hi
        mine, got = self.at(p.s), self.side_slot(hi)
        below, above = self.chain_slot(0, hi), self.chain_slot(1, hi)

        @pl.when(p.has_down)
        def _():
            settle(got, self.recv(hi))

        @pl.when(p.has_up)
        def _():
            settle(got, self.recv(n + hi))

        @pl.when(p.has_down & p.has_up)
        def _():
            self.add(self.target, mine, got, below, above)

        @pl.when(p.has_down & jnp.logical_not(p.has_up))
        def _():
            self.add(self.target, mine, got, below)

        @pl.when(jnp.logical_not(p.has_down))
        def _():
            self.add(self.target, mine, got, above)

    def finish(self):
        p = self.p
        for block in range(p.n_hi):
            settle(self.side_slot(block), self.side(block))

            @pl.when(p.hi != block)
            def _():
                settle(self.side_slot(block), self.send(block))


class RowReduce:
    def __init__(self, place, sems, blocks, at, core_slot, y_slot, target, add=add_into):
        self.p, self.at, self.add, self.target = place, at, add, target
        self.core_slot, self.y_slot, self.blocks = core_slot, y_slot, blocks
        self.send, self.recv = sems.take(2 * blocks), sems.take(2 * blocks)
        self.y, self.from_y = sems.take(blocks), sems.take(blocks)

    def start(self, block):
        p, n = self.p, self.blocks
        push(self.at(p.r_far, block), self.core_slot(0, block), self.send(block), self.recv(block), p.core)
        push(self.at(p.r_core, block), self.core_slot(1, block), self.send(n + block), self.recv(n + block), p.core)

    def step(self, block):
        p = self.p
        got = self.core_slot(0, block)
        settle(got, self.recv(block))
        self.add(got, self.at(p.r_y, block), got)
        push(got, self.y_slot(block), self.y(block), self.from_y(block), p.y)

    def close(self, block):
        p = self.p
        settle(self.core_slot(1, block), self.recv(self.blocks + block))
        settle(self.y_slot(block), self.from_y(block))
        self.add(self.target(block), self.at(p.r, block), self.core_slot(1, block), self.y_slot(block))

    def finish(self):
        n = self.blocks
        for block in range(n):
            settle(self.core_slot(0, block), self.send(block))
            settle(self.core_slot(1, block), self.send(n + block))
            settle(self.core_slot(0, block), self.y(block))


def columns(ref, index, width):
    return ref.at[:, pl.ds(pl.multiple_of(index * width, width), width)]


def call(kernel, shapes, ident, args, spaces, out_spaces, scratch, sems):
    return pl.pallas_call(
        kernel,
        out_shape=shapes,
        in_specs=[pl.BlockSpec(memory_space=space) for space in spaces],
        out_specs=jax.tree.map(lambda space: pl.BlockSpec(memory_space=space), out_spaces),
        scratch_shapes=list(scratch) + [pltpu.SemaphoreType.DMA((sems,))],
        compiler_params=pltpu.CompilerParams(
            collective_id=ident, has_side_effects=True, vmem_limit_bytes=VMEM_BYTES
        ),
    )(*args)


def shape_of(dims, dtype=jnp.bfloat16):
    return jax.ShapeDtypeStruct(dims, dtype)


def nt(left, right):
    return lax.dot_general(left, right, (((1,), (1,)), ((), ())), preferred_element_type=jnp.float32)


def tn(left, right):
    return lax.dot_general(left, right, (((0,), (0,)), ((), ())), preferred_element_type=jnp.float32)


def nn(left, right):
    return lax.dot_general(left, right, (((1,), (0,)), ((), ())), preferred_element_type=jnp.float32)


def rows_at(index, count):
    return pl.ds(pl.multiple_of(index * count, count), count)


def norm_rows(source, target, gain):
    @pl.loop(0, source.shape[0] // 16)
    def _(tile):
        rows = rows_at(tile, 16)
        values = source[rows, :].astype(jnp.float32)
        target[rows, :] = rms_norm(values, gain[...]).astype(target.dtype)


def attention(qkv, attended, key_place, query_low, query_high, shift, turned, head, head_size):
    tokens, own_width = attended.shape
    scale = head_size ** (-0.5)
    keys_step = 256
    lanes = pl.ds(head * head_size, head_size)
    key_lanes = pl.ds(own_width + head * head_size, head_size)
    value_lanes = pl.ds(2 * own_width + head * head_size, head_size)
    turned[...] = jnp.zeros_like(turned)

    @pl.loop(0, tokens // keys_step)
    def _(step):
        rows = rows_at(step, keys_step)
        places = key_place[rows, :]
        allowed = (places >= query_low[...]) & (places <= query_high[...])
        scores = nt(qkv[rows, key_lanes], qkv[:, lanes]) * scale - shift[...]
        sig = jnp.where(allowed, jax.nn.sigmoid(scores), 0.0).astype(jnp.bfloat16)
        turned[...] += nn(qkv[rows, value_lanes].T, sig)

    attended[:, lanes] = turned[...].T.astype(jnp.bfloat16)


def forward_kernel(
    rows,
    seqs,
    head_size,
    x,
    g,
    wqkv,
    wgu,
    wdown,
    wout,
    gains,
    key_place,
    query_low,
    query_high,
    shift,
    gs,
    vgu,
    vdown,
    vout,
    h2,
    vqkv,
    hn,
    qkv,
    attended,
    middle,
    gain_rows_out,
    xs,
    vgains,
    heads,
    turned,
    out_held,
    h2_own,
    copies,
    sems,
):
    p, pool = Place(rows, seqs), Sems(sems)
    greet(p.peers() + p.rows())
    tokens, width = x.shape
    half = tokens // 2
    own_width = heads.shape[1]
    deep = wout.shape[0]
    down_blocks = vdown.shape[1]

    def part(source, target, c, arrived=no_op):
        piece = pl.ds(c * half, half)
        return SeqGather(p, pool, source.at[piece], lambda b: target.at[b, piece], arrived)

    def norm_half(c):
        def run(b):
            start = pl.multiple_of(b * tokens + c * half, half)
            norm_rows(xs.at[b, pl.ds(c * half, half)], hn.at[pl.ds(start, half), :], gain_rows_out.at[0:1, :])

        return run

    qkv_rows = RowForward(p, pool, seqs, lambda r, b: vqkv.at[r, b])
    gu_rows = RowForward(p, pool, seqs, lambda r, b: vgu.at[r, b])
    down_fwd = RowForward(p, pool, down_blocks, lambda r, b: vdown.at[r, b])
    out_rows = RowForward(p, pool, seqs, lambda r, b: vout.at[r, b])
    gain_rows = RowForward(p, pool, seqs, lambda r, b: vgains.at[r, b])
    x_parts = [part(x, xs, c, norm_half(c)) for c in range(2)]
    g_parts = [part(g, gs, c) for c in range(2)]
    h2_parts = [part(h2_own, h2, c) for c in range(2)]
    qkv_swap = SeqExchange(p, pool, lambda t: wqkv.at[t], lambda b: vqkv.at[p.r, b], qkv_rows.forward)
    gu_swap = SeqExchange(p, pool, lambda t: wgu.at[t], lambda b: vgu.at[p.r, b], gu_rows.forward)
    out = SeqGather(p, pool, wout, lambda b: vout.at[p.r, b], out_rows.forward)
    gain = SeqGather(p, pool, gains, lambda b: vgains.at[p.r, b], gain_rows.forward)
    heads_swap = SeqExchange(
        p, pool, lambda t: heads.at[rows_at(t, tokens), :], lambda b: columns(attended, b, own_width)
    )
    down_own = pool.take(1)

    gain.start()
    gain_rows.forward(p.s, gains)
    for member in x_parts:
        member.start()
    qkv_swap.start()
    qkv_rows.forward(p.s, wqkv.at[p.s])
    pltpu.make_async_copy(wdown, vdown.at[p.r], down_own(0)).start()
    for block in range(down_blocks):
        down_fwd.forward(block, wdown.at[block])

    for k in range(1, p.n_hi):
        gain.step(k)
    for k in range(p.n_hi):
        gain.aside(k)
    for block in range(seqs):
        gain_rows.relay(block)
    gain.finish()
    gain_rows.finish()
    for pair in range(rows * seqs // 2):
        tile = vgains[2 * pair // seqs, 2 * pair % seqs] + vgains[2 * pair // seqs, 2 * pair % seqs + 1]
        gain_rows_out[:, pl.ds(pair * 2 * deep, 2 * deep)] = tile

    out_rows.forward(p.s, wout)
    for c, member in enumerate(x_parts):
        member.settle_own()
        norm_half(c)(p.s)
    for k in range(1, p.n_hi):
        for member in x_parts:
            member.step(k)
        for step in (2 * k - 1, 2 * k):
            qkv_swap.step(step)
        if k == p.n_hi - 1:
            out.start()
    qkv_swap.step(seqs - 1)
    gu_rows.forward(p.s, wgu.at[p.s])
    for k in range(p.n_hi):
        if k > 0:
            out.step(k)
        for member in x_parts:
            member.aside(k)
    gu_swap.start()
    for block in range(seqs):
        qkv_rows.relay(block)
    qkv_swap.finish()
    qkv_rows.finish()

    weights = vqkv.reshape(width, 3 * own_width)

    @pl.loop(0, seqs // 2)
    def _(step):
        tall = rows_at(step, 2 * tokens)
        qkv[tall, :] = nn(hn[tall, :], weights[...]).astype(jnp.bfloat16)

    for k in range(p.n_hi):
        out.aside(k)
    for member in g_parts:
        member.start()
    own_heads = own_width // head_size
    share = -(-seqs // own_heads)
    for head in range(own_heads):
        attention(qkv, heads, key_place, query_low, query_high, shift, turned, head, head_size)
        for block in range(seqs)[head * share : (head + 1) * share]:
            out_rows.relay(block)
    heads_swap.start()
    for step in range(1, seqs):
        gu_swap.step(step)
    out.finish()
    out_rows.finish()
    for r in range(rows):
        pltpu.make_async_copy(vout.at[r], out_held.at[r], copies.at[r]).start()
    for step in range(1, seqs):
        heads_swap.step(step)
    heads_swap.finish()
    for r in range(rows):
        settle(out_held.at[r], copies.at[r])
    out_weights = out_held.reshape(width, width)
    for member in g_parts:
        member.step(1)

    @pl.loop(0, width // 512)
    def _(c):
        lanes = rows_at(c, 512)
        middle[:, lanes] = xs[p.s, :, lanes].astype(jnp.float32) + nn(attended[...], out_weights[:, lanes])

    norm_rows(middle, h2_own, gain_rows_out.at[4:5, :])
    for member in h2_parts:
        member.start()
    for k in range(1, p.n_hi):
        for member in h2_parts:
            member.step(k)
        if k > 1:
            for member in g_parts:
                member.step(k)
    for block in range(down_blocks):
        down_fwd.relay(block)
    for block in range(seqs):
        gu_rows.relay(block)
    for k in range(p.n_hi):
        for member in h2_parts + g_parts:
            member.aside(k)
    for member in x_parts + g_parts + h2_parts + [gu_swap, down_fwd, gu_rows]:
        member.finish()
    settle(vdown.at[p.r], down_own(0))


def forward(rows, seqs, head_size, x, g, wqkv, wgu, wdown, wout, gains, meta):
    low, f32 = jnp.bfloat16, jnp.float32
    tokens, width = x.shape
    wdown = wdown.reshape(4, wdown.shape[0] // 4, width)
    own_width = width // seqs
    row_tokens = tokens * seqs
    shapes = (
        shape_of((seqs, tokens, width)),
        shape_of((rows,) + wgu.shape),
        shape_of((rows,) + wdown.shape),
        shape_of((rows, seqs) + wout.shape),
        shape_of((seqs, tokens, width)),
        shape_of((rows,) + wqkv.shape),
        shape_of((row_tokens, width)),
        shape_of((row_tokens, 3 * own_width)),
        shape_of((tokens, width)),
        shape_of((tokens, width), f32),
        shape_of((8, width), f32),
    )
    scratch = [
        pltpu.VMEM((seqs, tokens, width), low),
        pltpu.VMEM((rows, seqs) + gains.shape, f32),
        pltpu.VMEM((row_tokens, own_width), low),
        pltpu.VMEM((head_size, row_tokens), f32),
        pltpu.VMEM((rows, seqs) + wout.shape, low),
        pltpu.VMEM((tokens, width), low),
        pltpu.SemaphoreType.DMA((rows,)),
    ]
    return call(
        functools.partial(forward_kernel, rows, seqs, head_size),
        shapes,
        1,
        (x, g, wqkv, wgu, wdown, wout, gains) + meta,
        [pl.ANY] * 7 + [pltpu.VMEM] * 4,
        (pl.ANY,) * 5 + (pltpu.VMEM,) * 6,
        scratch,
        800,
    )


def seq_reducers(place, pool, source, side, chain, target):
    half = target.shape[0] // 2
    members = []
    for c in range(2):
        piece = pl.ds(c * half, half)
        members.append(
            SeqReduce(
                place,
                pool,
                lambda b, piece=piece: source.at[b, piece],
                lambda b, piece=piece: side.at[b, piece],
                lambda w, b, piece=piece: chain.at[w, b, piece],
                target.at[piece],
            )
        )
    return members


def row_reducer(place, pool, source, core_slots, y_slots, target, add=add_into):
    return RowReduce(
        place,
        pool,
        source.shape[1],
        lambda r, b: source.at[r, b],
        lambda w, b: core_slots.at[w, b],
        lambda b: y_slots.at[b],
        lambda b: target.at[b],
        add,
    )


def middle_kernel(
    rows,
    seqs,
    h2,
    out,
    gu,
    down,
    h2_sum,
    out_sum,
    gu_sum,
    down_sum,
    h2_side,
    h2_chain,
    out_side,
    out_chain,
    gu_core,
    gu_y,
    down_core,
    down_y,
    sems,
):
    p, pool = Place(rows, seqs), Sems(sems)
    greet(p.chain() + p.rows())
    h2_parts = seq_reducers(p, pool, h2, h2_side, h2_chain, h2_sum)
    out_parts = seq_reducers(p, pool, out, out_side, out_chain, out_sum)
    gu_rows = row_reducer(p, pool, gu, gu_core, gu_y, gu_sum)
    down_rows = row_reducer(p, pool, down, down_core, down_y, down_sum)
    row_work = [(gu_rows, b) for b in range(gu_rows.blocks)] + [(down_rows, b) for b in range(down_rows.blocks)]
    for t in range(p.n_hi):
        for member in h2_parts:
            member.start(t)
    for member, block in row_work:
        member.start(block)
    for t in range(p.n_hi):
        for member in out_parts:
            member.start(t)
    turns = [(member, t) for parts in (h2_parts, out_parts) for t in range(p.n_hi) for member in parts]
    first = p.n_hi
    share = -(-len(row_work) // first)
    for number in range(first):
        for member, t in turns[2 * number : 2 * number + 2]:
            member.step(t)
        for member, block in row_work[number * share : (number + 1) * share]:
            member.step(block)
    for member, t in turns[2 * first :]:
        member.step(t)
    for member, block in row_work:
        member.close(block)
    for member in h2_parts + out_parts + [gu_rows, down_rows]:
        member.finish()


def slots(array, copies=()):
    return pltpu.VMEM(copies + array.shape[1:], array.dtype)


def seq_slots(array):
    half = array.shape[0] // 2
    return [
        pltpu.VMEM((half,) + array.shape[1:], array.dtype),
        pltpu.VMEM((2, half) + array.shape[1:], array.dtype),
    ]


def row_slots(array):
    return [slots(array, (2,)), slots(array)]


def row_blocks(rows, array, count):
    return array.reshape(rows, count, array.shape[0] // (rows * count), array.shape[1])


def middle_sums(rows, seqs, h2, out, gu, down):
    h2, out = (array.reshape(seqs, array.shape[0] // seqs, array.shape[1]) for array in (h2, out))
    gu, down = row_blocks(rows, gu, seqs), row_blocks(rows, down, 4)
    shapes = (
        shape_of(h2.shape[1:], jnp.float32),
        shape_of(out.shape[1:], jnp.float32),
        shape_of(gu.shape[1:]),
        shape_of(down.shape[1:]),
    )
    return call(
        functools.partial(middle_kernel, rows, seqs),
        shapes,
        4,
        (h2, out, gu, down),
        [pltpu.VMEM] * 4,
        (pltpu.VMEM,) * 4,
        seq_slots(h2) + seq_slots(out) + row_slots(gu) + row_slots(down),
        320,
    )


class ColumnExchange:
    def __init__(self, place, sems, piece, parts):
        self.p, self.piece, self.parts = place, piece, parts
        n = place.seq_count
        self.own, self.send, self.recv = sems.take(1), sems.take(n), sems.take(n)

    def start(self):
        p, s = self.p, self.p.s
        for step in range(p.seq_count):
            t = p.peer(step)
            piece = self.piece(t)
            for offset, width, target in self.parts(s):
                source = piece.at[:, pl.ds(offset, width)]
                if step == 0:
                    pltpu.make_async_copy(source, target, self.own(0)).start()
                else:
                    push(source, target, self.send(step), self.recv(s), (p.r, t))

    def finish(self):
        p = self.p
        settle(self.piece(p.s), self.own(0))
        for step in range(1, p.seq_count):
            settle(self.piece(p.s), self.send(step))
            settle(self.piece(p.s), self.recv(p.peer(step)))


def attention_back(qkv, do, dqkv, key_place, query_low, query_high, shift, dq_turned, head_size):
    tokens, own_width = do.shape
    scale = head_size ** (-0.5)
    keys_step = 256
    for head in range(own_width // head_size):
        lanes = pl.ds(head * head_size, head_size)
        key_lanes = pl.ds(own_width + head * head_size, head_size)
        value_lanes = pl.ds(2 * own_width + head * head_size, head_size)
        dq_turned[...] = jnp.zeros_like(dq_turned)

        @pl.loop(0, tokens // keys_step)
        def _(step):
            rows = pl.ds(pl.multiple_of(step * keys_step, keys_step), keys_step)
            key, value = qkv[rows, key_lanes], qkv[rows, value_lanes]
            queries, grads = qkv[:, lanes], do[:, lanes]
            places = key_place[rows, :]
            allowed = (places >= query_low[...]) & (places <= query_high[...])
            scores = nt(key, queries) * scale - shift[...]
            sig = jnp.where(allowed, jax.nn.sigmoid(scores), 0.0)
            score_grad = (nt(value, grads) * sig * (1.0 - sig)).astype(jnp.bfloat16)
            dqkv[rows, value_lanes] = nn(sig.astype(jnp.bfloat16), grads).astype(jnp.bfloat16)
            dqkv[rows, key_lanes] = (nn(score_grad, queries) * scale).astype(jnp.bfloat16)
            dq_turned[...] += nn(key.T, score_grad)

        dqkv[:, lanes] = (dq_turned[...].T * scale).astype(jnp.bfloat16)


def back_kernel(
    rows,
    seqs,
    head_size,
    do_own,
    qkv,
    hn,
    wqkv,
    out,
    gu,
    gain_two_part,
    gain_one,
    key_place,
    query_low,
    query_high,
    shift,
    hn_sum,
    out_sum,
    query_got,
    key_got,
    value_got,
    gate_got,
    up_got,
    gain_got,
    do,
    dqkv,
    dq_turned,
    hn_part,
    hn_side,
    hn_chain,
    grad_qkv,
    qkv_core,
    qkv_y,
    out_core,
    out_y,
    out_side,
    out_chain,
    gains,
    gain_core,
    gain_y,
    sems,
):
    p, pool = Place(rows, seqs), Sems(sems)
    greet(p.peers() + p.rows())
    tokens, own_width = do.shape
    block_tokens = tokens // seqs
    width = wqkv.shape[0]

    def block_rows(b):
        return pl.ds(pl.multiple_of(b * block_tokens, block_tokens), block_tokens)

    do_swap = SeqExchange(
        p, pool, lambda t: columns(do_own, t, own_width), lambda b: do.at[block_rows(b), :]
    )
    do_swap.start()
    out_rows = row_reducer(p, pool, out, out_core, out_y, out_y)
    for b in range(seqs):
        out_rows.start(b)
    hidden_own = gu.shape[2] // 2
    block = hidden_own // rows

    def gu_parts(s):
        for n, target in ((0, gate_got), (1, up_got)):
            for r in range(rows):
                yield n * hidden_own + r * block, block, columns(target, r * seqs + s, block)

    gu_swap = ColumnExchange(p, pool, lambda t: gu.at[t], gu_parts)

    def qkv_parts(s):
        for n, target in enumerate((query_got, key_got, value_got)):
            yield n * own_width, own_width, columns(target, s, own_width)

    qkv_swap = ColumnExchange(p, pool, lambda t: qkv_y.at[t], qkv_parts)
    qkv_rows = row_reducer(p, pool, grad_qkv, qkv_core, qkv_y, qkv_y)
    hn_parts = seq_reducers(p, pool, hn_part, hn_side, hn_chain, hn_sum)
    out_seq = SeqReduce(
        p, pool, lambda b: out_y.at[b], lambda b: out_side.at[b], lambda w, b: out_chain.at[w, b], out_sum
    )
    quarter = width // rows
    gain_rows = RowReduce(
        p,
        pool,
        1,
        lambda r, b: columns(gains, r, quarter),
        lambda w, b: gain_core.at[w],
        lambda b: gain_y,
        lambda b: gain_y,
        add_small,
    )
    gain_width = 2 * quarter // seqs
    gain_swap = SeqExchange(
        p, pool, lambda t: columns(gain_y, t // 2, gain_width), lambda b: gain_got.at[b]
    )

    for step in range(1, seqs):
        do_swap.step(step)
    settle(do.at[block_rows(p.s), :], do_swap.own(0))
    gu_swap.start()
    for b in range(seqs):
        out_rows.step(b)
    attention_back(qkv, do, dqkv, key_place, query_low, query_high, shift, dq_turned, head_size)

    gains[0:8, :] = jnp.zeros_like(gains[0:8, :])
    gains[8:16, :] = gain_two_part[...]
    column_step = 512
    for t in range(p.n_hi):
        pair = hn_parts[0].turn(t)
        tall = pl.ds(pl.multiple_of(pair * 2 * block_tokens, 2 * block_tokens), 2 * block_tokens)

        @pl.loop(0, width // column_step)
        def _(c):
            lanes = pl.ds(pl.multiple_of(c * column_step, column_step), column_step)
            part = nt(dqkv[tall, :], wqkv[lanes, :])
            hn_part[2 * pair, :, lanes] = part[:block_tokens].astype(jnp.bfloat16)
            hn_part[2 * pair + 1, :, lanes] = part[block_tokens:].astype(jnp.bfloat16)
            terms = part * hn[tall, lanes].astype(jnp.float32)
            gains[0:8, lanes] += jnp.sum(terms.reshape(-1, 8, column_step), axis=0)

        for member in hn_parts:
            member.start(t)
    gains[0:8, :] = gains[0:8, :] / gain_one[...]
    gain_rows.start(0)

    @pl.loop(0, width // 256)
    def _(c):
        lanes = pl.ds(pl.multiple_of(c * 256, 256), 256)
        total = tn(hn[:, lanes], dqkv[...]).astype(jnp.bfloat16)
        piece = total.reshape((4,) + (total.shape[0] // 4, total.shape[1]))
        for n in range(4):
            grad_qkv[c * 4 // seqs, lax.rem(c * 4, seqs) + n] = piece[n]

    for b in range(seqs):
        qkv_rows.start(b)
    gain_rows.step(0)
    for t in range(p.n_hi):
        for member in hn_parts:
            member.step(t)
        if t == 0:
            for b in range(seqs):
                qkv_rows.step(b)
            gain_rows.close(0)
            gain_swap.start()
        if t == 1:
            for b in range(seqs):
                out_rows.close(b)
            for k in range(p.n_hi):
                out_seq.start(k)
        if t == 2:
            for b in range(seqs):
                qkv_rows.close(b)
            qkv_swap.start()
    for t in range(p.n_hi):
        out_seq.step(t)
    for step in range(1, seqs):
        gain_swap.step(step)
        settle(do.at[block_rows(p.s), :], do_swap.send(step))
    for member in hn_parts + [out_rows, qkv_rows, gain_rows, gu_swap, qkv_swap, out_seq, gain_swap]:
        member.finish()


def back(rows, seqs, head_size, do_own, qkv, hn, wqkv, out, gu, gain_two_part, gain_one, meta):
    tokens, own_width = qkv.shape[0], qkv.shape[1] // 3
    width = hn.shape[1]
    low = jnp.bfloat16
    out = row_blocks(rows, out, seqs)
    block_tokens = tokens // seqs
    hn_dims, qkv_dims = (seqs, block_tokens, width), (rows, seqs, width // (rows * seqs), 3 * own_width)
    deep = width // (rows * seqs)
    quarter = width // rows
    got = shape_of((deep, width))
    gu_got = shape_of((deep, gu.shape[2] // 2 * seqs))
    gain_width = 2 * quarter // seqs
    shapes = (
        shape_of(hn_dims[1:], jnp.float32),
        shape_of(out.shape[2:]),
        got,
        got,
        got,
        gu_got,
        gu_got,
        shape_of((seqs, 16, gain_width), jnp.float32),
    )
    hn_like, qkv_like, out_like = shape_of(hn_dims), shape_of(qkv_dims), shape_of(out.shape)
    scratch = (
        [
            pltpu.VMEM((tokens, own_width), low),
            pltpu.VMEM(qkv.shape, low),
            pltpu.VMEM((head_size, tokens), jnp.float32),
            pltpu.VMEM(hn_dims, low),
        ]
        + seq_slots(hn_like)
        + [pltpu.VMEM(qkv_dims, low)]
        + row_slots(qkv_like)
        + row_slots(out_like)
        + seq_slots(shape_of(out.shape[1:]))
        + [
            pltpu.VMEM((16, width), jnp.float32),
            pltpu.VMEM((2, 16, quarter), jnp.float32),
            pltpu.VMEM((16, quarter), jnp.float32),
        ]
    )
    return call(
        functools.partial(back_kernel, rows, seqs, head_size),
        shapes,
        6,
        (do_own, qkv, hn, wqkv, out, gu, gain_two_part, gain_one) + meta,
        [pltpu.VMEM] * 12,
        (pltpu.VMEM,) * 5 + (pl.ANY,) * 2 + (pltpu.VMEM,),
        scratch,
        480,
    )


def dot(left, right, left_axis=1, right_axis=0):
    return lax.dot_general(
        left, right, (((left_axis,), (right_axis,)), ((), ())), preferred_element_type=jnp.float32
    )


def split_local(
    rows,
    seqs,
    inputs,
    lengths,
    w_query,
    w_key,
    w_value,
    w_out,
    gain_attn,
    w_gate,
    w_up,
    w_down,
    gain_mlp,
    cotangent,
):
    low, f32 = jnp.bfloat16, jnp.float32
    tokens, width = inputs.shape[1], inputs.shape[2]
    deep = w_query.shape[0]
    row_tokens = tokens * seqs
    head_size = width // HEADS
    own_width = width // seqs
    hidden_own = w_gate.shape[1] // seqs
    hidden_block = hidden_own // rows

    def by_heads(weight):
        return weight.reshape(deep, seqs, own_width).transpose(1, 0, 2)

    def by_hidden(weight):
        return (
            weight.reshape(deep, rows, seqs, hidden_block).transpose(2, 0, 1, 3).reshape(seqs, deep, hidden_own)
        )

    wqkv = jnp.concatenate([by_heads(w_query), by_heads(w_key), by_heads(w_value)], axis=2)
    wgu = jnp.concatenate([by_hidden(w_gate), by_hidden(w_up)], axis=2)
    side = lax.rem(lax.axis_index("seq"), 2)
    lane = lax.broadcasted_iota(jnp.int32, (8, 2 * deep), 1)
    both = [jnp.concatenate([gain, gain]).astype(f32)[None, :] for gain in (gain_attn, gain_mlp)]
    number = lax.broadcasted_iota(jnp.int32, (8, 2 * deep), 0)
    gains_own = jnp.where(lane // deep == side, jnp.where(number < 4, both[0], both[1]), 0.0)
    x_low, g_low = inputs[0], cotangent[0]

    def places(shape, axis):
        index = lax.broadcasted_iota(jnp.int32, shape, axis)
        block, within = index // tokens, lax.rem(index, tokens)
        segment = position = length_of = jnp.zeros_like(index)
        begin = 0
        for n in range(lengths.shape[1]):
            unit = lengths[0, n] // (2 * seqs)
            inside = (within >= begin) & (within < begin + 2 * unit)
            local = within - begin
            here = jnp.where(local < unit, block * unit + local, (2 * seqs - 1 - block) * unit + local - unit)
            segment = jnp.where(inside, n, segment)
            position = jnp.where(inside, here, position)
            length_of = jnp.where(inside, lengths[0, n], length_of)
            begin = begin + 2 * unit
        return segment * row_tokens, segment * row_tokens + position, length_of

    query_low, query_high, length_of = places((1, row_tokens), 1)
    meta = (places((row_tokens, 1), 0)[1], query_low, query_high, jnp.log(length_of.astype(f32)))
    g_all, wgu, wdown, wout, h2, wqkv, hn, qkv, attended, middle, gains = forward(
        rows, seqs, head_size, x_low, g_low, wqkv, wgu, w_down, w_out, gains_own, meta
    )
    gain_one, gain_two = gains[0:1], gains[4:5]
    wqkv = wqkv.reshape(width, 3 * own_width)
    wgu = wgu.reshape(width, 2 * hidden_own)
    wdown = wdown.reshape(hidden_own, width)
    wout = wout.reshape(width, width)
    g_all = g_all.reshape(row_tokens, width)
    h2 = h2.reshape(row_tokens, width)
    residual = x_low.astype(f32)
    gate_up = dot(h2, wgu)
    gate, up = gate_up[:, :hidden_own], gate_up[:, hidden_own:]
    gated, gated_back = jax.vjp(lambda a, b: jax.nn.silu(a) * b, gate, up)
    hidden = gated.astype(low)
    out_part = dot(hidden, wdown).astype(low)
    gate_grad, up_grad = gated_back(dot(g_all, wdown, 1, 1))
    gu_grad = jnp.concatenate([gate_grad.astype(low), up_grad.astype(low)], axis=1)
    h2_part = dot(gu_grad, wgu, 1, 1).astype(low)
    grad_down = dot(hidden, g_all, 0, 0).astype(low)
    grad_gu = dot(h2, gu_grad, 0, 0).astype(low)
    h2_grad, out_sum, sum_gu, sum_down = middle_sums(rows, seqs, h2_part, out_part, grad_gu, grad_down)
    output = (middle + out_sum).astype(low)

    inverse = lax.rsqrt(jnp.mean(middle * middle, axis=-1, keepdims=True) + EPSILON)
    scaled_grad = gain_two * h2_grad
    gain_two_part = jnp.sum((h2_grad * middle * inverse).reshape(-1, 8, width), axis=0)
    middle_grad = (
        g_low.astype(f32)
        + inverse * scaled_grad
        - middle * inverse**3 * jnp.mean(scaled_grad * middle, axis=-1, keepdims=True)
    )
    branch = middle_grad.astype(low)
    grad_out = dot(attended, branch, 0, 0).astype(low)
    do_own = dot(branch, wout, 1, 1).astype(low)
    hn_grad, sum_out, got_query, got_key, got_value, got_gate, got_up, got_gain = back(
        rows, seqs, head_size, do_own, qkv, hn, wqkv, grad_out, sum_gu, gain_two_part, gain_one, meta
    )
    spread_inverse = lax.rsqrt(jnp.mean(residual * residual, axis=-1, keepdims=True) + EPSILON)
    scaled_grad = gain_one * hn_grad
    input_grad = (
        middle_grad
        + spread_inverse * scaled_grad
        - residual * spread_inverse**3 * jnp.mean(scaled_grad * residual, axis=-1, keepdims=True)
    )
    gain_sums = jnp.sum(got_gain, axis=0).reshape(2, 8, 2, deep).sum(axis=1)
    gain_sums = lax.dynamic_index_in_dim(gain_sums, lax.rem(lax.axis_index("seq"), 2), 1, keepdims=False)
    return (
        output[None],
        input_grad[None],
        got_query.astype(f32),
        got_key.astype(f32),
        got_value.astype(f32),
        sum_out.astype(f32),
        gain_sums[0],
        got_gate.astype(f32),
        got_up.astype(f32),
        sum_down.reshape(w_down.shape).astype(f32),
        gain_sums[1],
    )


def solution(mesh):
    placed = (
        P("row", "seq", None),
        P("row", None),
        P(("row", "seq"), None),
        P(("row", "seq"), None),
        P(("row", "seq"), None),
        P(("row", "seq"), None),
        P(("row", "seq")),
        P(("row", "seq"), None),
        P(("row", "seq"), None),
        P(("row", "seq"), None),
        P(("row", "seq")),
        P("row", "seq", None),
    )
    row_count, seq_count = mesh.shape["row"], mesh.shape["seq"]
    if row_count == 4 and seq_count % 2 == 0 and HEADS % seq_count == 0:
        local = functools.partial(split_local, row_count, seq_count)
    else:
        local = gathered_local
    return jax.shard_map(
        local,
        mesh=mesh,
        in_specs=placed,
        out_specs=(
            P("row", "seq", None),
            P("row", "seq", None),
            P(("row", "seq"), None),
            P(("row", "seq"), None),
            P(("row", "seq"), None),
            P(("row", "seq"), None),
            P(("row", "seq")),
            P(("row", "seq"), None),
            P(("row", "seq"), None),
            P(("row", "seq"), None),
            P(("row", "seq")),
        ),
        check_vma=False,
    )
```

```python
import functools

import jax
import jax.numpy as jnp
from jax import lax
from jax.experimental import pallas as pl
from jax.experimental.pallas import tpu as pltpu
from jax.sharding import PartitionSpec as P

HEADS = 16


EPSILON = 1e-05


def layout(lengths_row, places, block_rows, block_count):
    unit_counts = lengths_row // (2 * block_count)
    span_sizes = 2 * unit_counts
    offsets = jnp.cumsum(span_sizes) - span_sizes
    device = places // block_rows
    within_block = places - device * block_rows
    inside = (
        (within_block[:, None] >= offsets[None, :])
        & (within_block[:, None] < (offsets + span_sizes)[None, :])
    ).astype(jnp.int32)
    numbers = jnp.arange(lengths_row.shape[0], dtype=jnp.int32)
    segment = jnp.sum(inside * numbers[None, :], axis=1)
    unit_of = jnp.sum(inside * unit_counts[None, :], axis=1)
    begins = jnp.sum(inside * offsets[None, :], axis=1)
    length_of = jnp.sum(inside * lengths_row[None, :], axis=1)
    within = within_block - begins
    position = jnp.where(
        within < unit_of,
        device * unit_of + within,
        (2 * block_count - 1 - device) * unit_of + within - unit_of,
    )
    return (segment, position, length_of)


def rms_norm(values, gain):
    return values * lax.rsqrt(jnp.mean(values * values, axis=-1, keepdims=True) + EPSILON) * gain


def sigmoid_terms(query_heads, query_meta, key_heads, key_meta):
    query_segment, query_position, query_length = query_meta
    key_segment, key_position, unused_length = key_meta
    scores = jnp.einsum(
        "qhd,khd->hqk", query_heads, key_heads, preferred_element_type=jnp.float32
    ) * query_heads.shape[2] ** (-0.5)
    scores = scores - jnp.log(query_length.astype(jnp.float32))[None, :, None]
    allowed = (query_segment[:, None] == key_segment[None, :]) & (
        key_position[None, :] <= query_position[:, None]
    )
    return jnp.where(allowed[None], jax.nn.sigmoid(scores), 0.0)


def pair_terms(query_heads, query_meta, grad_heads, key_heads, key_meta, value_heads):
    sig_terms = sigmoid_terms(query_heads, query_meta, key_heads, key_meta)
    slopes = jnp.einsum("qhd,khd->hqk", grad_heads, value_heads, preferred_element_type=jnp.float32)
    score_grad = (slopes * sig_terms * (1.0 - sig_terms)).astype(jnp.bfloat16)
    return (sig_terms.astype(jnp.bfloat16), score_grad)


def by_blocks(step_fn, running, pieces, block_rows):
    size_total = pieces[0].shape[0]
    part_rows = 4 * block_rows
    block_count = size_total // part_rows

    def turn_over(step_number, carried):
        sub_pieces = tuple(
            (
                lax.dynamic_slice_in_dim(member, step_number * part_rows, part_rows, 0)
                for member in pieces
            )
        )
        return step_fn(carried, sub_pieces, step_number * part_rows)

    return lax.fori_loop(0, block_count, turn_over, running)


def gathered_local(
    inputs,
    lengths,
    w_query,
    w_key,
    w_value,
    w_out,
    gain_attn,
    w_gate,
    w_up,
    w_down,
    gain_mlp,
    cotangent,
):
    residual = inputs[0].astype(jnp.float32)
    tokens_here = residual.shape[0]
    model_width = residual.shape[1]
    head_size = model_width // HEADS
    score_scale = head_size ** (-0.5)
    block_total = lax.axis_size("seq")
    lengths_row = lengths[0]
    places = lax.axis_index("seq") * tokens_here + jnp.arange(tokens_here, dtype=jnp.int32)
    own_meta = layout(lengths_row, places, tokens_here, block_total)

    def meta_at(start_row, row_count):
        return layout(
            lengths_row,
            start_row + jnp.arange(row_count, dtype=jnp.int32),
            tokens_here,
            block_total,
        )

    def heads_of(matrix):
        return matrix.reshape(matrix.shape[0], HEADS, head_size)

    query_full, key_full, value_full, out_full, gain_one = (
        lax.all_gather(w_query, ("row", "seq"), axis=0, tiled=True),
        lax.all_gather(w_key, ("row", "seq"), axis=0, tiled=True),
        lax.all_gather(w_value, ("row", "seq"), axis=0, tiled=True),
        lax.all_gather(w_out, ("row", "seq"), axis=0, tiled=True),
        lax.all_gather(gain_attn, ("row", "seq"), axis=0, tiled=True),
    )
    gain_one_f = gain_one.astype(jnp.float32)
    normed = rms_norm(residual, gain_one_f).astype(jnp.bfloat16)
    queries = jnp.dot(normed, query_full, preferred_element_type=jnp.float32).astype(jnp.bfloat16)
    key_rows = jnp.dot(normed, key_full, preferred_element_type=jnp.float32).astype(jnp.bfloat16)
    value_rows = jnp.dot(normed, value_full, preferred_element_type=jnp.float32).astype(
        jnp.bfloat16
    )
    query_heads = heads_of(queries)

    def forward_step(running, pieces, start_row):
        key_piece, value_piece = pieces
        sig_terms = sigmoid_terms(
            query_heads, own_meta, heads_of(key_piece), meta_at(start_row, key_piece.shape[0])
        ).astype(jnp.bfloat16)
        added = jnp.einsum(
            "hqk,khd->qhd", sig_terms, heads_of(value_piece), preferred_element_type=jnp.float32
        )
        return running + added.reshape(tokens_here, model_width)

    attended = by_blocks(
        forward_step,
        jnp.zeros((tokens_here, model_width), jnp.float32),
        (
            lax.all_gather(key_rows, "seq", axis=0, tiled=True),
            lax.all_gather(value_rows, "seq", axis=0, tiled=True),
        ),
        tokens_here,
    )
    attended_low = attended.astype(jnp.bfloat16)
    middle = residual + jnp.dot(attended_low, out_full, preferred_element_type=jnp.float32)
    gate_full, up_full, down_full, gain_two = (
        lax.all_gather(w_gate, ("row", "seq"), axis=0, tiled=True),
        lax.all_gather(w_up, ("row", "seq"), axis=0, tiled=True),
        lax.all_gather(w_down, ("row", "seq"), axis=0, tiled=True),
        lax.all_gather(gain_mlp, ("row", "seq"), axis=0, tiled=True),
    )
    gain_two_f = gain_two.astype(jnp.float32)
    normed_mlp = rms_norm(middle, gain_two_f).astype(jnp.bfloat16)
    gate_vals = jnp.dot(normed_mlp, gate_full, preferred_element_type=jnp.float32)
    up_vals = jnp.dot(normed_mlp, up_full, preferred_element_type=jnp.float32)
    gated_prod, gated_back = jax.vjp(
        lambda gate_in, up_in: jax.nn.silu(gate_in) * up_in, gate_vals, up_vals
    )
    hidden = gated_prod.astype(jnp.bfloat16)
    output = (middle + jnp.dot(hidden, down_full, preferred_element_type=jnp.float32)).astype(
        jnp.bfloat16
    )
    upstream_low = cotangent[0]
    upstream = upstream_low.astype(jnp.float32)
    gate_full, up_full, down_full, gain_two = (
        lax.all_gather(w_gate, ("row", "seq"), axis=0, tiled=True),
        lax.all_gather(w_up, ("row", "seq"), axis=0, tiled=True),
        lax.all_gather(w_down, ("row", "seq"), axis=0, tiled=True),
        lax.all_gather(gain_mlp, ("row", "seq"), axis=0, tiled=True),
    )
    gain_two_f = gain_two.astype(jnp.float32)
    grad_down = jnp.dot(hidden.T, upstream_low, preferred_element_type=jnp.float32)
    shared_down = lax.psum_scatter(grad_down, ("row", "seq"), scatter_dimension=0, tiled=True)
    hidden_grad = jnp.dot(upstream_low, down_full.T, preferred_element_type=jnp.float32)
    gate_grad, up_grad = gated_back(hidden_grad)
    gate_low = gate_grad.astype(jnp.bfloat16)
    up_low = up_grad.astype(jnp.bfloat16)
    grad_gate = jnp.dot(normed_mlp.T, gate_low, preferred_element_type=jnp.float32)
    shared_gate = lax.psum_scatter(grad_gate, ("row", "seq"), scatter_dimension=0, tiled=True)
    normed_grad = jnp.dot(gate_low, gate_full.T, preferred_element_type=jnp.float32) + jnp.dot(
        up_low, up_full.T, preferred_element_type=jnp.float32
    )
    unused_mid, second_back = jax.vjp(rms_norm, middle, gain_two_f)
    middle_part, gain_two_grad = second_back(normed_grad)
    middle_grad = upstream + middle_part
    grad_up = jnp.dot(normed_mlp.T, up_low, preferred_element_type=jnp.float32)
    shared_up, shared_gain_two = (
        lax.psum_scatter(grad_up, ("row", "seq"), scatter_dimension=0, tiled=True),
        lax.psum_scatter(gain_two_grad, ("row", "seq"), scatter_dimension=0, tiled=True),
    )
    query_full, key_full, value_full, out_full, gain_one = (
        lax.all_gather(w_query, ("row", "seq"), axis=0, tiled=True),
        lax.all_gather(w_key, ("row", "seq"), axis=0, tiled=True),
        lax.all_gather(w_value, ("row", "seq"), axis=0, tiled=True),
        lax.all_gather(w_out, ("row", "seq"), axis=0, tiled=True),
        lax.all_gather(gain_attn, ("row", "seq"), axis=0, tiled=True),
    )
    gain_one_f = gain_one.astype(jnp.float32)
    branch_low = middle_grad.astype(jnp.bfloat16)
    grad_out = jnp.dot(attended_low.T, branch_low, preferred_element_type=jnp.float32)
    attended_grad = jnp.dot(branch_low, out_full.T, preferred_element_type=jnp.float32).astype(
        jnp.bfloat16
    )
    grad_heads = heads_of(attended_grad)
    key_heads_own = heads_of(key_rows)
    value_heads_own = heads_of(value_rows)

    def query_step(running, pieces, start_row):
        key_piece, value_piece = pieces
        key_piece_heads = heads_of(key_piece)
        unused_terms, score_grad = pair_terms(
            query_heads,
            own_meta,
            grad_heads,
            key_piece_heads,
            meta_at(start_row, key_piece.shape[0]),
            heads_of(value_piece),
        )
        added = jnp.einsum(
            "hqk,khd->qhd", score_grad, key_piece_heads, preferred_element_type=jnp.float32
        )
        return running + added.reshape(tokens_here, model_width) * score_scale

    start_value = jnp.zeros((tokens_here, model_width), jnp.float32)
    folded = by_blocks(
        query_step,
        start_value,
        (
            lax.all_gather(key_rows, "seq", axis=0, tiled=True),
            lax.all_gather(value_rows, "seq", axis=0, tiled=True),
        ),
        tokens_here,
    )

    def key_step(running, pieces, start_row):
        key_sum, value_sum = running
        query_piece, grad_piece = pieces
        row_count = query_piece.shape[0]
        query_piece_heads = heads_of(query_piece)
        grad_piece_heads = heads_of(grad_piece)
        sig_low, score_grad = pair_terms(
            query_piece_heads,
            meta_at(start_row, row_count),
            grad_piece_heads,
            key_heads_own,
            own_meta,
            value_heads_own,
        )
        key_add = jnp.einsum(
            "hqk,qhd->khd", score_grad, query_piece_heads, preferred_element_type=jnp.float32
        )
        value_add = jnp.einsum(
            "hqk,qhd->khd", sig_low, grad_piece_heads, preferred_element_type=jnp.float32
        )
        return (
            key_sum + key_add.reshape(tokens_here, model_width) * score_scale,
            value_sum + value_add.reshape(tokens_here, model_width),
        )

    empty_rows = jnp.zeros((tokens_here, model_width), jnp.float32)
    key_grad, value_grad = by_blocks(
        key_step,
        (empty_rows, empty_rows),
        (
            lax.all_gather(queries, "seq", axis=0, tiled=True),
            lax.all_gather(attended_grad, "seq", axis=0, tiled=True),
        ),
        tokens_here,
    )
    query_low = folded.astype(jnp.bfloat16)
    key_low = key_grad.astype(jnp.bfloat16)
    value_low = value_grad.astype(jnp.bfloat16)
    grad_query = jnp.dot(normed.T, query_low, preferred_element_type=jnp.float32)
    grad_key = jnp.dot(normed.T, key_low, preferred_element_type=jnp.float32)
    grad_value = jnp.dot(normed.T, value_low, preferred_element_type=jnp.float32)
    normed_back = jnp.dot(query_low, query_full.T, preferred_element_type=jnp.float32)
    normed_back = normed_back + jnp.dot(key_low, key_full.T, preferred_element_type=jnp.float32)
    normed_back = normed_back + jnp.dot(value_low, value_full.T, preferred_element_type=jnp.float32)
    unused_first, first_back = jax.vjp(rms_norm, residual, gain_one_f)
    residual_part, gain_one_grad = first_back(normed_back)
    input_grad = middle_grad + residual_part
    shared_query, shared_key, shared_value, shared_out, shared_gain_one = (
        lax.psum_scatter(grad_query, ("row", "seq"), scatter_dimension=0, tiled=True),
        lax.psum_scatter(grad_key, ("row", "seq"), scatter_dimension=0, tiled=True),
        lax.psum_scatter(grad_value, ("row", "seq"), scatter_dimension=0, tiled=True),
        lax.psum_scatter(grad_out, ("row", "seq"), scatter_dimension=0, tiled=True),
        lax.psum_scatter(gain_one_grad, ("row", "seq"), scatter_dimension=0, tiled=True),
    )
    return (
        output[None],
        input_grad[None],
        shared_query,
        shared_key,
        shared_value,
        shared_out,
        shared_gain_one,
        shared_gate,
        shared_up,
        shared_down,
        shared_gain_two,
    )


MESH = pl.DeviceIdType.MESH
VMEM_BYTES = 62 * 1024 * 1024


class Place:
    def __init__(self, row_count, seq_count):
        self.row_count, self.seq_count = row_count, seq_count
        self.r, self.s = lax.axis_index("row"), lax.axis_index("seq")
        self.n_hi = seq_count // 2
        self.hi, self.lo = self.s // 2, lax.rem(self.s, 2)
        self.r_core = self.r + 1 - 2 * lax.rem(self.r, 2)
        self.r_y = lax.rem(self.r + 2, 4)
        self.r_far = lax.rem(self.r_core + 2, 4)
        self.side = (self.r, self.s + 1 - 2 * self.lo)
        self.up = (self.r, self.s + 2)
        self.down = (self.r, self.s - 2)
        self.core = (self.r_core, self.s)
        self.y = (self.r_y, self.s)
        self.has_up = self.hi < self.n_hi - 1
        self.has_down = self.hi > 0

    def peer(self, step):
        return lax.rem(self.s + step, self.seq_count)

    def chain(self):
        return [(None, self.side), (self.has_up, self.up), (self.has_down, self.down)]

    def peers(self):
        return [(None, (self.r, self.peer(step))) for step in range(1, self.seq_count)]

    def rows(self):
        return [(None, self.core), (None, self.y)]


def greet(devices):
    barrier = pltpu.get_barrier_semaphore()
    total = 0
    for condition, device in devices:
        if condition is None:
            pl.semaphore_signal(barrier, inc=1, device_id=device, device_id_type=MESH)
            total = total + 1
        else:

            @pl.when(condition)
            def _(device=device):
                pl.semaphore_signal(barrier, inc=1, device_id=device, device_id_type=MESH)

            total = total + condition.astype(jnp.int32)
    pl.semaphore_wait(barrier, total)


class Sems:
    def __init__(self, ref):
        self.ref, self.used = ref, 0

    def take(self, count):
        base = self.used
        self.used += count
        assert self.used <= self.ref.shape[0], self.used
        return lambda index: self.ref.at[base + index]


def push(source, target, send, recv, device):
    pltpu.make_async_remote_copy(
        src_ref=source, dst_ref=target, send_sem=send, recv_sem=recv, device_id=device, device_id_type=MESH
    ).start()


def settle(ref, sem):
    pltpu.make_async_copy(ref, ref, sem).wait()


def no_op(block):
    return None


class SeqGather:
    def __init__(self, place, sems, source, at, arrived=no_op):
        self.p, self.source, self.at, self.arrived = place, source, at, arrived
        self.own_done = False
        n = place.n_hi
        self.own, self.up, self.down = sems.take(1), sems.take(n), sems.take(n)
        self.side, self.recv = sems.take(n), sems.take(2 * n)

    def start(self):
        p, s = self.p, self.p.s
        pltpu.make_async_copy(self.source, self.at(s), self.own(0)).start()

        @pl.when(p.has_up)
        def _():
            push(self.source, self.at(s), self.up(0), self.recv(s), p.up)

        @pl.when(p.has_down)
        def _():
            push(self.source, self.at(s), self.down(0), self.recv(s), p.down)

        push(self.source, self.at(s), self.side(p.hi), self.recv(s), p.side)

    def step(self, k):
        p = self.p

        @pl.when(p.hi >= k)
        def _():
            block = p.s - 2 * k
            settle(self.at(block), self.recv(block))

            @pl.when(p.has_up)
            def _():
                push(self.at(block), self.at(block), self.up(k), self.recv(block), p.up)

            push(self.at(block), self.at(block), self.side(p.hi - k), self.recv(block), p.side)
            self.arrived(block)

        @pl.when(p.hi + k < p.n_hi)
        def _():
            block = p.s + 2 * k
            settle(self.at(block), self.recv(block))

            @pl.when(p.has_down)
            def _():
                push(self.at(block), self.at(block), self.down(k), self.recv(block), p.down)

            push(self.at(block), self.at(block), self.side(p.hi + k), self.recv(block), p.side)
            self.arrived(block)

    def aside(self, k):
        p = self.p
        if k == 0:
            block = 2 * p.hi + 1 - p.lo
            settle(self.at(block), self.recv(block))
            self.arrived(block)
            return

        @pl.when(p.hi >= k)
        def _():
            block = 2 * (p.hi - k) + 1 - p.lo
            settle(self.at(block), self.recv(block))
            self.arrived(block)

        @pl.when(p.hi + k < p.n_hi)
        def _():
            block = 2 * (p.hi + k) + 1 - p.lo
            settle(self.at(block), self.recv(block))
            self.arrived(block)

    def settle_own(self):
        settle(self.at(self.p.s), self.own(0))
        self.own_done = True

    def finish(self):
        p = self.p
        if not self.own_done:
            self.settle_own()
        for k in range(p.n_hi):

            @pl.when(p.has_up & (p.hi >= k))
            def _():
                settle(self.source, self.up(k))

            @pl.when(p.has_down & (p.hi + k < p.n_hi))
            def _():
                settle(self.source, self.down(k))

            settle(self.source, self.side(k))


class SeqExchange:
    def __init__(self, place, sems, piece, at, arrived=no_op):
        self.p, self.piece, self.at, self.arrived = place, piece, at, arrived
        n = place.seq_count
        self.own, self.send, self.recv = sems.take(1), sems.take(n), sems.take(n)

    def start_own(self):
        s = self.p.s
        pltpu.make_async_copy(self.piece(s), self.at(s), self.own(0)).start()

    def start(self):
        p, s = self.p, self.p.s
        self.start_own()
        for step in range(1, p.seq_count):
            t = p.peer(step)
            push(self.piece(t), self.at(s), self.send(step), self.recv(s), (p.r, t))

    def step(self, step):
        block = self.p.peer(self.p.seq_count - step)
        settle(self.at(block), self.recv(block))
        self.arrived(block)

    def finish(self):
        p = self.p
        settle(self.at(p.s), self.own(0))
        for step in range(1, p.seq_count):
            settle(self.at(p.s), self.send(step))


class RowForward:
    def __init__(self, place, sems, blocks, at):
        self.p, self.at, self.blocks = place, at, blocks
        self.core, self.y, self.far = sems.take(blocks), sems.take(blocks), sems.take(blocks)
        self.from_core, self.from_y, self.from_far = sems.take(blocks), sems.take(blocks), sems.take(blocks)

    def forward(self, block, source=None):
        p = self.p
        source = self.at(p.r, block) if source is None else source
        push(source, self.at(p.r, block), self.y(block), self.from_y(block), p.y)
        push(source, self.at(p.r, block), self.core(block), self.from_core(block), p.core)

    def relay(self, block):
        p = self.p
        settle(self.at(p.r_y, block), self.from_y(block))
        push(self.at(p.r_y, block), self.at(p.r_y, block), self.far(block), self.from_far(block), p.core)

    def finish(self):
        p = self.p
        for block in range(self.blocks):
            settle(self.at(p.r_core, block), self.from_core(block))
            settle(self.at(p.r_far, block), self.from_far(block))
            settle(self.at(p.r, block), self.core(block))
            settle(self.at(p.r, block), self.y(block))
            settle(self.at(p.r_y, block), self.far(block))


def add_into(target, *sources):
    @pl.loop(0, target.shape[0] // 16)
    def _(tile):
        rows = pl.ds(pl.multiple_of(tile * 16, 16), 16)
        total = sources[0][rows, :].astype(jnp.float32)
        for source in sources[1:]:
            total = total + source[rows, :].astype(jnp.float32)
        target[rows, :] = total.astype(target.dtype)


def add_small(target, *sources):
    total = sources[0][...].astype(jnp.float32)
    for source in sources[1:]:
        total = total + source[...].astype(jnp.float32)
    target[...] = total.astype(target.dtype)


class SeqReduce:
    def __init__(self, place, sems, at, side_slot, chain_slot, target, add=add_into):
        self.p, self.at, self.add, self.target = place, at, add, target
        self.side_slot, self.chain_slot = side_slot, chain_slot
        n = place.n_hi
        self.side, self.from_side = sems.take(n), sems.take(n)
        self.send, self.recv = sems.take(n), sems.take(2 * n)

    def above_slot(self, block, hi):
        return self.chain_slot(jnp.where(block == hi, self.p.n_hi, block))

    def turn(self, t):
        p = self.p
        n, hi = p.n_hi, p.hi
        low = jnp.where(t < n - 1 - hi, n - 1 - t, t - (n - 1 - hi))
        high = jnp.where(t < hi, t, n - 1 - (t - hi))
        return jnp.where(hi < n // 2, low, high)

    def start(self, t):
        p, block = self.p, self.turn(t)
        push(self.at(2 * block + 1 - p.lo), self.side_slot(block), self.side(block), self.from_side(block), p.side)

    def step(self, t):
        p, n, block = self.p, self.p.n_hi, self.turn(t)
        mine, got = self.at(2 * block + p.lo), self.side_slot(block)
        settle(got, self.from_side(block))
        if t == n - 1:
            return self.close()

        @pl.when(block > p.hi)
        def _():
            @pl.when(p.has_down)
            def _():
                settle(got, self.recv(block))
                self.add(got, mine, got, self.chain_slot(block))

            @pl.when(jnp.logical_not(p.has_down))
            def _():
                self.add(got, mine, got)

            push(got, self.chain_slot(block), self.send(block), self.recv(block), p.up)

        @pl.when(block < p.hi)
        def _():
            @pl.when(p.has_up)
            def _():
                settle(got, self.recv(n + block))
                self.add(got, mine, got, self.above_slot(block, p.hi))

            @pl.when(jnp.logical_not(p.has_up))
            def _():
                self.add(got, mine, got)

            push(got, self.above_slot(block, p.hi - 1), self.send(block), self.recv(n + block), p.down)

    def close(self):
        p, n, hi = self.p, self.p.n_hi, self.p.hi
        mine, got = self.at(p.s), self.side_slot(hi)
        below, above = self.chain_slot(hi), self.above_slot(hi, hi)

        @pl.when(p.has_down)
        def _():
            settle(got, self.recv(hi))

        @pl.when(p.has_up)
        def _():
            settle(got, self.recv(n + hi))

        @pl.when(p.has_down & p.has_up)
        def _():
            self.add(self.target, mine, got, below, above)

        @pl.when(p.has_down & jnp.logical_not(p.has_up))
        def _():
            self.add(self.target, mine, got, below)

        @pl.when(jnp.logical_not(p.has_down))
        def _():
            self.add(self.target, mine, got, above)

    def finish(self):
        p = self.p
        for block in range(p.n_hi):
            settle(self.side_slot(block), self.side(block))

            @pl.when(p.hi != block)
            def _():
                settle(self.side_slot(block), self.send(block))


class RowReduce:
    def __init__(self, place, sems, blocks, at, core_slot, y_slot, target, add=add_into):
        self.p, self.at, self.add, self.target = place, at, add, target
        self.core_slot, self.y_slot, self.blocks = core_slot, y_slot, blocks
        self.send, self.recv = sems.take(2 * blocks), sems.take(2 * blocks)
        self.y, self.from_y = sems.take(blocks), sems.take(blocks)

    def start_far(self, block):
        p = self.p
        push(self.at(p.r_far, block), self.core_slot(0, block), self.send(block), self.recv(block), p.core)

    def start_core(self, block):
        p, n = self.p, self.blocks
        push(self.at(p.r_core, block), self.core_slot(1, block), self.send(n + block), self.recv(n + block), p.core)

    def start(self, block):
        self.start_far(block)
        self.start_core(block)

    def step(self, block):
        p = self.p
        got = self.core_slot(0, block)
        settle(got, self.recv(block))
        self.add(got, self.at(p.r_y, block), got)
        push(got, self.y_slot(block), self.y(block), self.from_y(block), p.y)

    def close(self, block):
        p = self.p
        settle(self.core_slot(1, block), self.recv(self.blocks + block))
        settle(self.y_slot(block), self.from_y(block))
        self.add(self.target(block), self.at(p.r, block), self.core_slot(1, block), self.y_slot(block))

    def finish(self):
        n = self.blocks
        for block in range(n):
            settle(self.core_slot(0, block), self.send(block))
            settle(self.core_slot(1, block), self.send(n + block))
            settle(self.core_slot(0, block), self.y(block))


def columns(ref, index, width):
    return ref.at[:, pl.ds(pl.multiple_of(index * width, width), width)]


def call(kernel, shapes, ident, args, spaces, out_spaces, scratch, sems):
    return pl.pallas_call(
        kernel,
        out_shape=shapes,
        in_specs=[pl.BlockSpec(memory_space=space) for space in spaces],
        out_specs=jax.tree.map(lambda space: pl.BlockSpec(memory_space=space), out_spaces),
        scratch_shapes=list(scratch) + [pltpu.SemaphoreType.DMA((sems,))],
        compiler_params=pltpu.CompilerParams(
            collective_id=ident, has_side_effects=True, vmem_limit_bytes=VMEM_BYTES
        ),
    )(*args)


def shape_of(dims, dtype=jnp.bfloat16):
    return jax.ShapeDtypeStruct(dims, dtype)


def nt(left, right):
    return lax.dot_general(left, right, (((1,), (1,)), ((), ())), preferred_element_type=jnp.float32)


def tn(left, right):
    return lax.dot_general(left, right, (((0,), (0,)), ((), ())), preferred_element_type=jnp.float32)


def nn(left, right):
    return lax.dot_general(left, right, (((1,), (0,)), ((), ())), preferred_element_type=jnp.float32)


def rows_at(index, count):
    return pl.ds(pl.multiple_of(index * count, count), count)


def norm_rows(source, target, gain):
    @pl.loop(0, source.shape[0] // 16)
    def _(tile):
        rows = rows_at(tile, 16)
        values = source[rows, :].astype(jnp.float32)
        target[rows, :] = rms_norm(values, gain[...]).astype(target.dtype)


def attention(qkv, attended, key_place, query_low, query_high, shift, turned, head, head_size):
    tokens, own_width = attended.shape
    scale = head_size ** (-0.5)
    keys_step = 256
    lanes = pl.ds(head * head_size, head_size)
    key_lanes = pl.ds(own_width + head * head_size, head_size)
    value_lanes = pl.ds(2 * own_width + head * head_size, head_size)
    turned[...] = jnp.zeros_like(turned)

    @pl.loop(0, tokens // keys_step)
    def _(step):
        rows = rows_at(step, keys_step)
        places = key_place[rows, :]
        allowed = (places >= query_low[...]) & (places <= query_high[...])
        scores = nt(qkv[rows, key_lanes], qkv[:, lanes]) * scale - shift[...]
        sig = jnp.where(allowed, jax.nn.sigmoid(scores), 0.0).astype(jnp.bfloat16)
        turned[...] += nn(qkv[rows, value_lanes].T, sig)

    attended[:, lanes] = turned[...].T.astype(jnp.bfloat16)


def forward_kernel(
    rows,
    seqs,
    head_size,
    x,
    g,
    wqkv,
    wgu,
    wdown,
    wout,
    gains,
    key_place,
    query_low,
    query_high,
    shift,
    gs,
    vgu,
    vdown,
    vout,
    h2,
    vqkv,
    hn,
    qkv,
    attended,
    middle,
    gain_rows_out,
    xs,
    vgains,
    heads,
    turned,
    out_held,
    h2_own,
    copies,
    sems,
):
    p, pool = Place(rows, seqs), Sems(sems)
    greet(p.peers() + p.rows())
    tokens, width = x.shape
    half = tokens // 2
    own_width = heads.shape[1]
    deep = wout.shape[0]
    down_blocks = vdown.shape[1]

    def part(source, target, c, arrived=no_op):
        piece = pl.ds(c * half, half)
        return SeqGather(p, pool, source.at[piece], lambda b: target.at[b, piece], arrived)

    def norm_half(c):
        def run(b):
            start = pl.multiple_of(b * tokens + c * half, half)
            norm_rows(xs.at[b, pl.ds(c * half, half)], hn.at[pl.ds(start, half), :], gain_rows_out.at[0:1, :])

        return run

    qkv_rows = RowForward(p, pool, seqs, lambda r, b: vqkv.at[r, b])
    gu_rows = RowForward(p, pool, seqs, lambda r, b: vgu.at[r, b])
    down_fwd = RowForward(p, pool, down_blocks, lambda r, b: vdown.at[r, b])
    out_rows = RowForward(p, pool, seqs, lambda r, b: vout.at[r, b])
    gain_rows = RowForward(p, pool, seqs, lambda r, b: vgains.at[r, b])
    x_parts = [part(x, xs, c, norm_half(c)) for c in range(2)]
    g_parts = [part(g, gs, c) for c in range(2)]
    h2_parts = [part(h2_own, h2, c) for c in range(2)]
    qkv_swap = SeqExchange(p, pool, lambda t: wqkv.at[t], lambda b: vqkv.at[p.r, b], qkv_rows.forward)
    gu_swap = SeqExchange(p, pool, lambda t: wgu.at[t], lambda b: vgu.at[p.r, b], gu_rows.forward)
    out = SeqGather(p, pool, wout, lambda b: vout.at[p.r, b], out_rows.forward)
    gain = SeqGather(p, pool, gains, lambda b: vgains.at[p.r, b], gain_rows.forward)
    heads_swap = SeqExchange(
        p, pool, lambda t: heads.at[rows_at(t, tokens), :], lambda b: columns(attended, b, own_width)
    )
    down_own = pool.take(1)

    gain.start()
    gain_rows.forward(p.s, gains)
    for member in x_parts:
        member.start()
    qkv_swap.start()
    qkv_rows.forward(p.s, wqkv.at[p.s])
    pltpu.make_async_copy(wdown, vdown.at[p.r], down_own(0)).start()
    for block in range(down_blocks):
        down_fwd.forward(block, wdown.at[block])

    for k in range(1, p.n_hi):
        gain.step(k)
    for k in range(p.n_hi):
        gain.aside(k)
    for block in range(seqs):
        gain_rows.relay(block)
    gain.finish()
    gain_rows.finish()
    for pair in range(rows * seqs // 2):
        tile = vgains[2 * pair // seqs, 2 * pair % seqs] + vgains[2 * pair // seqs, 2 * pair % seqs + 1]
        gain_rows_out[:, pl.ds(pair * 2 * deep, 2 * deep)] = tile

    out_rows.forward(p.s, wout)
    for c, member in enumerate(x_parts):
        member.settle_own()
        norm_half(c)(p.s)
    for k in range(1, p.n_hi):
        for member in x_parts:
            member.step(k)
        for step in (2 * k - 1, 2 * k):
            qkv_swap.step(step)
        if k == p.n_hi - 1:
            out.start()
    qkv_swap.step(seqs - 1)
    gu_rows.forward(p.s, wgu.at[p.s])
    for k in range(p.n_hi):
        if k > 0:
            out.step(k)
        for member in x_parts:
            member.aside(k)
    gu_swap.start()
    for block in range(seqs):
        qkv_rows.relay(block)
    qkv_swap.finish()
    qkv_rows.finish()

    weights = vqkv.reshape(width, 3 * own_width)

    @pl.loop(0, seqs // 2)
    def _(step):
        tall = rows_at(step, 2 * tokens)
        qkv[tall, :] = nn(hn[tall, :], weights[...]).astype(jnp.bfloat16)

    for k in range(p.n_hi):
        out.aside(k)
    for member in g_parts:
        member.start()
    own_heads = own_width // head_size
    share = -(-seqs // own_heads)
    for head in range(own_heads):
        attention(qkv, heads, key_place, query_low, query_high, shift, turned, head, head_size)
        for block in range(seqs)[head * share : (head + 1) * share]:
            out_rows.relay(block)
    heads_swap.start()
    for step in range(1, seqs):
        gu_swap.step(step)
    out.finish()
    out_rows.finish()
    for r in range(rows):
        pltpu.make_async_copy(vout.at[r], out_held.at[r], copies.at[r]).start()
    for step in range(1, seqs):
        heads_swap.step(step)
    heads_swap.finish()
    for r in range(rows):
        settle(out_held.at[r], copies.at[r])
    out_weights = out_held.reshape(width, width)
    for member in g_parts:
        member.step(1)

    @pl.loop(0, width // 512)
    def _(c):
        lanes = rows_at(c, 512)
        middle[:, lanes] = xs[p.s, :, lanes].astype(jnp.float32) + nn(attended[...], out_weights[:, lanes])

    norm_rows(middle, h2_own, gain_rows_out.at[4:5, :])
    for member in h2_parts:
        member.start()
    for k in range(1, p.n_hi):
        for member in h2_parts:
            member.step(k)
        if k > 1:
            for member in g_parts:
                member.step(k)
    for block in range(down_blocks):
        down_fwd.relay(block)
    for block in range(seqs):
        gu_rows.relay(block)
    for k in range(p.n_hi):
        for member in h2_parts + g_parts:
            member.aside(k)
    for member in x_parts + g_parts + h2_parts + [gu_swap, down_fwd, gu_rows]:
        member.finish()
    settle(vdown.at[p.r], down_own(0))


def forward(rows, seqs, head_size, x, g, wqkv, wgu, wdown, wout, gains, meta):
    low, f32 = jnp.bfloat16, jnp.float32
    tokens, width = x.shape
    wdown = wdown.reshape(4, wdown.shape[0] // 4, width)
    own_width = width // seqs
    row_tokens = tokens * seqs
    shapes = (
        shape_of((seqs, tokens, width)),
        shape_of((rows,) + wgu.shape),
        shape_of((rows,) + wdown.shape),
        shape_of((rows, seqs) + wout.shape),
        shape_of((seqs, tokens, width)),
        shape_of((rows,) + wqkv.shape),
        shape_of((row_tokens, width)),
        shape_of((row_tokens, 3 * own_width)),
        shape_of((tokens, width)),
        shape_of((tokens, width), f32),
        shape_of((8, width), f32),
    )
    scratch = [
        pltpu.VMEM((seqs, tokens, width), low),
        pltpu.VMEM((rows, seqs) + gains.shape, f32),
        pltpu.VMEM((row_tokens, own_width), low),
        pltpu.VMEM((head_size, row_tokens), f32),
        pltpu.VMEM((rows, seqs) + wout.shape, low),
        pltpu.VMEM((tokens, width), low),
        pltpu.SemaphoreType.DMA((rows,)),
    ]
    return call(
        functools.partial(forward_kernel, rows, seqs, head_size),
        shapes,
        1,
        (x, g, wqkv, wgu, wdown, wout, gains) + meta,
        [pl.ANY] * 7 + [pltpu.VMEM] * 4,
        (pl.ANY,) * 5 + (pltpu.VMEM,) * 6,
        scratch,
        800,
    )


def seq_reducers(place, pool, source, side, chain, target):
    half = target.shape[0] // 2
    members = []
    for c in range(2):
        piece = pl.ds(c * half, half)
        members.append(
            SeqReduce(
                place,
                pool,
                lambda b, piece=piece: source.at[b, piece],
                lambda b, piece=piece: side.at[b, piece],
                lambda slot, piece=piece: chain.at[slot, piece],
                target.at[piece],
            )
        )
    return members


def row_reducer(place, pool, source, core_slots, y_slots, target, add=add_into):
    return RowReduce(
        place,
        pool,
        source.shape[1],
        lambda r, b: source.at[r, b],
        lambda w, b: core_slots.at[w, b],
        lambda b: y_slots.at[b],
        lambda b: target.at[b],
        add,
    )


def ffn_kernel(
    rows,
    seqs,
    h2_in,
    gu_in,
    down_in,
    g_in,
    h2_sum,
    out_sum,
    gu_sum,
    down_sum,
    h2,
    gu_weights,
    down_weights,
    g,
    hidden,
    gu_grad,
    h2_part,
    h2_side,
    h2_chain,
    out_part,
    out_side,
    out_chain,
    gu_core,
    down_core,
    loads,
    sems,
):
    p, pool = Place(rows, seqs), Sems(sems)
    pairs = ((h2_in, h2), (gu_in, gu_weights), (g_in, g), (down_in, down_weights))
    for number, (source, target) in enumerate(pairs):
        pltpu.make_async_copy(source, target, loads.at[number]).start()
    greet(p.chain() + p.rows())
    tokens, width = h2_sum.shape
    hidden_own = hidden.shape[1]
    low = jnp.bfloat16
    h2_parts = seq_reducers(p, pool, h2_part, h2_side, h2_chain, h2_sum)
    out_parts = seq_reducers(p, pool, out_part, out_side, out_chain, out_sum)
    deep, down_deep = gu_sum.shape[1], down_sum.shape[1]

    def gu_at(r, b):
        return gu_weights.at[pl.ds(pl.multiple_of((r * seqs + b) * deep, deep), deep), :]

    def down_at(r, b):
        return down_weights.at[pl.ds(pl.multiple_of((r * down_sum.shape[0] + b) * down_deep, down_deep), down_deep), :]

    gu_rows = RowReduce(
        p, pool, seqs, gu_at, lambda w, b: gu_core.at[w, b], lambda b: gu_sum.at[b], lambda b: gu_sum.at[b]
    )
    down_rows = RowReduce(
        p,
        pool,
        down_sum.shape[0],
        down_at,
        lambda w, b: down_core.at[w, b],
        lambda b: down_sum.at[b],
        lambda b: down_sum.at[b],
    )
    for number, (source, target) in enumerate(pairs):
        settle(target, loads.at[number])

    def block(t):
        pair = h2_parts[0].turn(t)
        tall = rows_at(pair, 2 * tokens)

        @pl.loop(0, hidden_own // 256)
        def _(c):
            lanes, up_lanes = rows_at(c, 256), pl.ds(pl.multiple_of(hidden_own + c * 256, 256), 256)
            gate, up = nn(h2[tall, :], gu_weights[:, lanes]), nn(h2[tall, :], gu_weights[:, up_lanes])
            grad = nt(g[tall, :], down_weights[lanes, :])
            sig = jax.nn.sigmoid(gate)
            silu = gate * sig
            hidden[tall, lanes] = (silu * up).astype(low)
            gu_grad[tall, lanes] = (grad * up * (sig + silu * (1.0 - sig))).astype(low)
            gu_grad[tall, up_lanes] = (grad * silu).astype(low)

        @pl.loop(0, width // 512)
        def _(c):
            lanes = rows_at(c, 512)
            part = nn(hidden[tall, :], down_weights[:, lanes]).astype(low)
            out_part[2 * pair, :, lanes] = part[:tokens]
            out_part[2 * pair + 1, :, lanes] = part[tokens:]

        for member in out_parts:
            member.start(t)

        @pl.loop(0, width // 512)
        def _(c):
            lanes = rows_at(c, 512)
            part = nt(gu_grad[tall, :], gu_weights[lanes, :]).astype(low)
            h2_part[2 * pair, :, lanes] = part[:tokens]
            h2_part[2 * pair + 1, :, lanes] = part[tokens:]

        for member in h2_parts:
            member.start(t)

    def sums(t):
        for member in out_parts + h2_parts:
            member.step(t)

    def down_quarter(r):
        lanes = rows_at(r, hidden_own // rows)
        down_weights[lanes, :] = tn(hidden[:, lanes], g[...]).astype(low)

    def gu_quarter(r):
        @pl.loop(0, 2)
        def _(c):
            lanes = rows_at(2 * r + c, width // (2 * rows))
            gu_weights[lanes, :] = tn(h2[:, lanes], gu_grad[...]).astype(low)

    for t in range(p.n_hi):
        if t == p.n_hi - 1:
            sums(0)
        block(t)
    down_blocks, gu_blocks = range(down_sum.shape[0]), range(seqs)
    down_quarter(p.r_far)
    for b in down_blocks:
        down_rows.start_far(b)
    down_quarter(p.r_core)
    for b in down_blocks:
        down_rows.start_core(b)
    down_quarter(p.r_y)
    for b in down_blocks:
        down_rows.step(b)
    gu_quarter(p.r_far)
    for b in gu_blocks:
        gu_rows.start_far(b)
    if p.n_hi > 2:
        sums(1)
    gu_quarter(p.r_core)
    for b in gu_blocks:
        gu_rows.start_core(b)
    gu_quarter(p.r_y)
    for b in gu_blocks:
        gu_rows.step(b)
    down_quarter(p.r)
    gu_quarter(p.r)
    for t in range(2 if p.n_hi > 2 else 1, p.n_hi):
        sums(t)
    for b in down_blocks:
        down_rows.close(b)
    for b in gu_blocks:
        gu_rows.close(b)
    for member in h2_parts + out_parts + [gu_rows, down_rows]:
        member.finish()


def slots(array, copies=()):
    return pltpu.VMEM(copies + array.shape[1:], array.dtype)


def seq_slots(array):
    half = array.shape[0] // 2
    return [
        pltpu.VMEM((half,) + array.shape[1:], array.dtype),
        pltpu.VMEM((half + 1,) + array.shape[1:], array.dtype),
    ]


def row_slots(array):
    return [slots(array, (2,)), slots(array)]


def row_blocks(rows, array, count):
    return array.reshape(rows, count, array.shape[0] // (rows * count), array.shape[1])


def ffn(rows, seqs, h2, wgu, wdown, g):
    low, f32 = jnp.bfloat16, jnp.float32
    row_tokens, width = h2.shape
    tokens, hidden_own = row_tokens // seqs, wdown.shape[0]
    gu_dims, down_dims = (seqs, width // (rows * seqs), 2 * hidden_own), (4, hidden_own // (4 * rows), width)
    part = shape_of((seqs, tokens, width))
    shapes = (shape_of((tokens, width), f32), shape_of((tokens, width), f32), shape_of(gu_dims), shape_of(down_dims))
    scratch = (
        [pltpu.VMEM(array.shape, low) for array in (h2, wgu, wdown, g)]
        + [pltpu.VMEM((row_tokens, hidden_own), low), pltpu.VMEM((row_tokens, 2 * hidden_own), low)]
        + [pltpu.VMEM(part.shape, low)]
        + seq_slots(part)
        + [pltpu.VMEM(part.shape, low)]
        + seq_slots(part)
        + [pltpu.VMEM((2,) + gu_dims, low), pltpu.VMEM((2,) + down_dims, low)]
        + [pltpu.SemaphoreType.DMA((4,))]
    )
    return call(
        functools.partial(ffn_kernel, rows, seqs),
        shapes,
        4,
        (h2, wgu, wdown, g),
        [pl.ANY] * 4,
        (pltpu.VMEM,) * 4,
        scratch,
        320,
    )


class ColumnExchange:
    def __init__(self, place, sems, piece, parts):
        self.p, self.piece, self.parts = place, piece, parts
        n = place.seq_count
        self.own, self.send, self.recv = sems.take(1), sems.take(n), sems.take(n)

    def start(self):
        p, s = self.p, self.p.s
        for step in range(p.seq_count):
            t = p.peer(step)
            piece = self.piece(t)
            for offset, width, target in self.parts(s):
                source = piece.at[:, pl.ds(offset, width)]
                if step == 0:
                    pltpu.make_async_copy(source, target, self.own(0)).start()
                else:
                    push(source, target, self.send(step), self.recv(s), (p.r, t))

    def finish(self):
        p = self.p
        settle(self.piece(p.s), self.own(0))
        for step in range(1, p.seq_count):
            settle(self.piece(p.s), self.send(step))
            settle(self.piece(p.s), self.recv(p.peer(step)))


def attention_back(qkv, do, dqkv, key_place, query_low, query_high, shift, dq_turned, head_size):
    tokens, own_width = do.shape
    scale = head_size ** (-0.5)
    keys_step = 256
    for head in range(own_width // head_size):
        lanes = pl.ds(head * head_size, head_size)
        key_lanes = pl.ds(own_width + head * head_size, head_size)
        value_lanes = pl.ds(2 * own_width + head * head_size, head_size)
        dq_turned[...] = jnp.zeros_like(dq_turned)

        @pl.loop(0, tokens // keys_step)
        def _(step):
            rows = pl.ds(pl.multiple_of(step * keys_step, keys_step), keys_step)
            key, value = qkv[rows, key_lanes], qkv[rows, value_lanes]
            queries, grads = qkv[:, lanes], do[:, lanes]
            places = key_place[rows, :]
            allowed = (places >= query_low[...]) & (places <= query_high[...])
            scores = nt(key, queries) * scale - shift[...]
            sig = jnp.where(allowed, jax.nn.sigmoid(scores), 0.0)
            score_grad = (nt(value, grads) * sig * (1.0 - sig)).astype(jnp.bfloat16)
            dqkv[rows, value_lanes] = nn(sig.astype(jnp.bfloat16), grads).astype(jnp.bfloat16)
            dqkv[rows, key_lanes] = (nn(score_grad, queries) * scale).astype(jnp.bfloat16)
            dq_turned[...] += nn(key.T, score_grad)

        dqkv[:, lanes] = (dq_turned[...].T * scale).astype(jnp.bfloat16)


def back_kernel(
    rows,
    seqs,
    head_size,
    do_own,
    qkv,
    hn,
    wqkv,
    out,
    gu,
    gain_two_part,
    gain_one,
    key_place,
    query_low,
    query_high,
    shift,
    hn_sum,
    out_sum,
    query_got,
    key_got,
    value_got,
    gate_got,
    up_got,
    gain_got,
    do,
    dqkv,
    dq_turned,
    hn_part,
    hn_side,
    hn_chain,
    grad_qkv,
    qkv_core,
    qkv_y,
    out_core,
    out_y,
    out_side,
    out_chain,
    gains,
    gain_core,
    gain_y,
    sems,
):
    p, pool = Place(rows, seqs), Sems(sems)
    greet(p.peers() + p.rows())
    tokens, own_width = do.shape
    block_tokens = tokens // seqs
    width = wqkv.shape[0]

    def block_rows(b):
        return pl.ds(pl.multiple_of(b * block_tokens, block_tokens), block_tokens)

    do_swap = SeqExchange(
        p, pool, lambda t: columns(do_own, t, own_width), lambda b: do.at[block_rows(b), :]
    )
    do_swap.start()
    out_rows = row_reducer(p, pool, out, out_core, out_y, out_y)
    for b in range(seqs):
        out_rows.start(b)
    hidden_own = gu.shape[2] // 2
    block = hidden_own // rows

    def gu_parts(s):
        for n, target in ((0, gate_got), (1, up_got)):
            for r in range(rows):
                yield n * hidden_own + r * block, block, columns(target, r * seqs + s, block)

    gu_swap = ColumnExchange(p, pool, lambda t: gu.at[t], gu_parts)

    def qkv_parts(s):
        for n, target in enumerate((query_got, key_got, value_got)):
            yield n * own_width, own_width, columns(target, s, own_width)

    qkv_swap = ColumnExchange(p, pool, lambda t: qkv_y.at[t], qkv_parts)
    qkv_rows = row_reducer(p, pool, grad_qkv, qkv_core, qkv_y, qkv_y)
    hn_parts = seq_reducers(p, pool, hn_part, hn_side, hn_chain, hn_sum)
    out_seq = SeqReduce(
        p, pool, lambda b: out_y.at[b], lambda b: out_side.at[b], lambda slot: out_chain.at[slot], out_sum
    )
    quarter = width // rows
    gain_rows = RowReduce(
        p,
        pool,
        1,
        lambda r, b: columns(gains, r, quarter),
        lambda w, b: gain_core.at[w],
        lambda b: gain_y,
        lambda b: gain_y,
        add_small,
    )
    gain_width = 2 * quarter // seqs
    gain_swap = SeqExchange(
        p, pool, lambda t: columns(gain_y, t // 2, gain_width), lambda b: gain_got.at[b]
    )

    for step in range(1, seqs):
        do_swap.step(step)
    settle(do.at[block_rows(p.s), :], do_swap.own(0))
    gu_swap.start()
    for b in range(seqs):
        out_rows.step(b)
    attention_back(qkv, do, dqkv, key_place, query_low, query_high, shift, dq_turned, head_size)

    gains[0:8, :] = jnp.zeros_like(gains[0:8, :])
    gains[8:16, :] = gain_two_part[...]
    column_step = 512
    for t in range(p.n_hi):
        pair = hn_parts[0].turn(t)
        tall = pl.ds(pl.multiple_of(pair * 2 * block_tokens, 2 * block_tokens), 2 * block_tokens)

        @pl.loop(0, width // column_step)
        def _(c):
            lanes = pl.ds(pl.multiple_of(c * column_step, column_step), column_step)
            part = nt(dqkv[tall, :], wqkv[lanes, :])
            hn_part[2 * pair, :, lanes] = part[:block_tokens].astype(jnp.bfloat16)
            hn_part[2 * pair + 1, :, lanes] = part[block_tokens:].astype(jnp.bfloat16)
            terms = part * hn[tall, lanes].astype(jnp.float32)
            gains[0:8, lanes] += jnp.sum(terms.reshape(-1, 8, column_step), axis=0)

        for member in hn_parts:
            member.start(t)
    gains[0:8, :] = gains[0:8, :] / gain_one[...]
    gain_rows.start(0)

    @pl.loop(0, width // 256)
    def _(c):
        lanes = pl.ds(pl.multiple_of(c * 256, 256), 256)
        total = tn(hn[:, lanes], dqkv[...]).astype(jnp.bfloat16)
        piece = total.reshape((4,) + (total.shape[0] // 4, total.shape[1]))
        for n in range(4):
            grad_qkv[c * 4 // seqs, lax.rem(c * 4, seqs) + n] = piece[n]

    for b in range(seqs):
        qkv_rows.start(b)
    gain_rows.step(0)
    for t in range(p.n_hi):
        for member in hn_parts:
            member.step(t)
        if t == 0:
            for b in range(seqs):
                qkv_rows.step(b)
            gain_rows.close(0)
            gain_swap.start()
        if t == 1:
            for b in range(seqs):
                out_rows.close(b)
            for k in range(p.n_hi):
                out_seq.start(k)
        if t == 2:
            for b in range(seqs):
                qkv_rows.close(b)
            qkv_swap.start()
    for t in range(p.n_hi):
        out_seq.step(t)
    for step in range(1, seqs):
        gain_swap.step(step)
        settle(do.at[block_rows(p.s), :], do_swap.send(step))
    for member in hn_parts + [out_rows, qkv_rows, gain_rows, gu_swap, qkv_swap, out_seq, gain_swap]:
        member.finish()


def back(rows, seqs, head_size, do_own, qkv, hn, wqkv, out, gu, gain_two_part, gain_one, meta):
    tokens, own_width = qkv.shape[0], qkv.shape[1] // 3
    width = hn.shape[1]
    low = jnp.bfloat16
    out = row_blocks(rows, out, seqs)
    block_tokens = tokens // seqs
    hn_dims, qkv_dims = (seqs, block_tokens, width), (rows, seqs, width // (rows * seqs), 3 * own_width)
    deep = width // (rows * seqs)
    quarter = width // rows
    got = shape_of((deep, width))
    gu_got = shape_of((deep, gu.shape[2] // 2 * seqs))
    gain_width = 2 * quarter // seqs
    shapes = (
        shape_of(hn_dims[1:], jnp.float32),
        shape_of(out.shape[2:]),
        got,
        got,
        got,
        gu_got,
        gu_got,
        shape_of((seqs, 16, gain_width), jnp.float32),
    )
    hn_like, qkv_like, out_like = shape_of(hn_dims), shape_of(qkv_dims), shape_of(out.shape)
    scratch = (
        [
            pltpu.VMEM((tokens, own_width), low),
            pltpu.VMEM(qkv.shape, low),
            pltpu.VMEM((head_size, tokens), jnp.float32),
            pltpu.VMEM(hn_dims, low),
        ]
        + seq_slots(hn_like)
        + [pltpu.VMEM(qkv_dims, low)]
        + row_slots(qkv_like)
        + row_slots(out_like)
        + seq_slots(shape_of(out.shape[1:]))
        + [
            pltpu.VMEM((16, width), jnp.float32),
            pltpu.VMEM((2, 16, quarter), jnp.float32),
            pltpu.VMEM((16, quarter), jnp.float32),
        ]
    )
    return call(
        functools.partial(back_kernel, rows, seqs, head_size),
        shapes,
        6,
        (do_own, qkv, hn, wqkv, out, gu, gain_two_part, gain_one) + meta,
        [pltpu.VMEM] * 12,
        (pltpu.VMEM,) * 5 + (pl.ANY,) * 2 + (pltpu.VMEM,),
        scratch,
        480,
    )


def dot(left, right, left_axis=1, right_axis=0):
    return lax.dot_general(
        left, right, (((left_axis,), (right_axis,)), ((), ())), preferred_element_type=jnp.float32
    )


def split_local(
    rows,
    seqs,
    inputs,
    lengths,
    w_query,
    w_key,
    w_value,
    w_out,
    gain_attn,
    w_gate,
    w_up,
    w_down,
    gain_mlp,
    cotangent,
):
    low, f32 = jnp.bfloat16, jnp.float32
    tokens, width = inputs.shape[1], inputs.shape[2]
    deep = w_query.shape[0]
    row_tokens = tokens * seqs
    head_size = width // HEADS
    own_width = width // seqs
    hidden_own = w_gate.shape[1] // seqs
    hidden_block = hidden_own // rows

    def by_heads(weight):
        return weight.reshape(deep, seqs, own_width).transpose(1, 0, 2)

    def by_hidden(weight):
        return (
            weight.reshape(deep, rows, seqs, hidden_block).transpose(2, 0, 1, 3).reshape(seqs, deep, hidden_own)
        )

    wqkv = jnp.concatenate([by_heads(w_query), by_heads(w_key), by_heads(w_value)], axis=2)
    wgu = jnp.concatenate([by_hidden(w_gate), by_hidden(w_up)], axis=2)
    side = lax.rem(lax.axis_index("seq"), 2)
    lane = lax.broadcasted_iota(jnp.int32, (8, 2 * deep), 1)
    both = [jnp.concatenate([gain, gain]).astype(f32)[None, :] for gain in (gain_attn, gain_mlp)]
    number = lax.broadcasted_iota(jnp.int32, (8, 2 * deep), 0)
    gains_own = jnp.where(lane // deep == side, jnp.where(number < 4, both[0], both[1]), 0.0)
    x_low, g_low = inputs[0], cotangent[0]

    def places(shape, axis):
        index = lax.broadcasted_iota(jnp.int32, shape, axis)
        block, within = index // tokens, lax.rem(index, tokens)
        segment = position = length_of = jnp.zeros_like(index)
        begin = 0
        for n in range(lengths.shape[1]):
            unit = lengths[0, n] // (2 * seqs)
            inside = (within >= begin) & (within < begin + 2 * unit)
            local = within - begin
            here = jnp.where(local < unit, block * unit + local, (2 * seqs - 1 - block) * unit + local - unit)
            segment = jnp.where(inside, n, segment)
            position = jnp.where(inside, here, position)
            length_of = jnp.where(inside, lengths[0, n], length_of)
            begin = begin + 2 * unit
        return segment * row_tokens, segment * row_tokens + position, length_of

    query_low, query_high, length_of = places((1, row_tokens), 1)
    meta = (places((row_tokens, 1), 0)[1], query_low, query_high, jnp.log(length_of.astype(f32)))
    g_all, wgu, wdown, wout, h2, wqkv, hn, qkv, attended, middle, gains = forward(
        rows, seqs, head_size, x_low, g_low, wqkv, wgu, w_down, w_out, gains_own, meta
    )
    gain_one, gain_two = gains[0:1], gains[4:5]
    wqkv = wqkv.reshape(width, 3 * own_width)
    wgu = wgu.reshape(width, 2 * hidden_own)
    wdown = wdown.reshape(hidden_own, width)
    wout = wout.reshape(width, width)
    g_all = g_all.reshape(row_tokens, width)
    h2 = h2.reshape(row_tokens, width)
    residual = x_low.astype(f32)
    h2_grad, out_sum, sum_gu, sum_down = ffn(rows, seqs, h2, wgu, wdown, g_all)
    output = (middle + out_sum).astype(low)

    inverse = lax.rsqrt(jnp.mean(middle * middle, axis=-1, keepdims=True) + EPSILON)
    scaled_grad = gain_two * h2_grad
    gain_two_part = jnp.sum((h2_grad * middle * inverse).reshape(-1, 8, width), axis=0)
    middle_grad = (
        g_low.astype(f32)
        + inverse * scaled_grad
        - middle * inverse**3 * jnp.mean(scaled_grad * middle, axis=-1, keepdims=True)
    )
    branch = middle_grad.astype(low)
    grad_out = dot(attended, branch, 0, 0).astype(low)
    do_own = dot(branch, wout, 1, 1).astype(low)
    hn_grad, sum_out, got_query, got_key, got_value, got_gate, got_up, got_gain = back(
        rows, seqs, head_size, do_own, qkv, hn, wqkv, grad_out, sum_gu, gain_two_part, gain_one, meta
    )
    spread_inverse = lax.rsqrt(jnp.mean(residual * residual, axis=-1, keepdims=True) + EPSILON)
    scaled_grad = gain_one * hn_grad
    input_grad = (
        middle_grad
        + spread_inverse * scaled_grad
        - residual * spread_inverse**3 * jnp.mean(scaled_grad * residual, axis=-1, keepdims=True)
    )
    gain_sums = jnp.sum(got_gain, axis=0).reshape(2, 8, 2, deep).sum(axis=1)
    gain_sums = lax.dynamic_index_in_dim(gain_sums, lax.rem(lax.axis_index("seq"), 2), 1, keepdims=False)
    return (
        output[None],
        input_grad[None],
        got_query.astype(f32),
        got_key.astype(f32),
        got_value.astype(f32),
        sum_out.astype(f32),
        gain_sums[0],
        got_gate.astype(f32),
        got_up.astype(f32),
        sum_down.reshape(w_down.shape).astype(f32),
        gain_sums[1],
    )


def solution(mesh):
    placed = (
        P("row", "seq", None),
        P("row", None),
        P(("row", "seq"), None),
        P(("row", "seq"), None),
        P(("row", "seq"), None),
        P(("row", "seq"), None),
        P(("row", "seq")),
        P(("row", "seq"), None),
        P(("row", "seq"), None),
        P(("row", "seq"), None),
        P(("row", "seq")),
        P("row", "seq", None),
    )
    row_count, seq_count = mesh.shape["row"], mesh.shape["seq"]
    if row_count == 4 and seq_count % 2 == 0 and HEADS % seq_count == 0:
        local = functools.partial(split_local, row_count, seq_count)
    else:
        local = gathered_local
    return jax.shard_map(
        local,
        mesh=mesh,
        in_specs=placed,
        out_specs=(
            P("row", "seq", None),
            P("row", "seq", None),
            P(("row", "seq"), None),
            P(("row", "seq"), None),
            P(("row", "seq"), None),
            P(("row", "seq"), None),
            P(("row", "seq")),
            P(("row", "seq"), None),
            P(("row", "seq"), None),
            P(("row", "seq"), None),
            P(("row", "seq")),
        ),
        check_vma=False,
    )
```

```python
import functools

import jax
import jax.numpy as jnp
from jax import lax
from jax.experimental import pallas as pl
from jax.experimental.pallas import tpu as pltpu
from jax.sharding import PartitionSpec as P

HEADS = 16


EPSILON = 1e-05


def layout(lengths_row, places, block_rows, block_count):
    unit_counts = lengths_row // (2 * block_count)
    span_sizes = 2 * unit_counts
    offsets = jnp.cumsum(span_sizes) - span_sizes
    device = places // block_rows
    within_block = places - device * block_rows
    inside = (
        (within_block[:, None] >= offsets[None, :])
        & (within_block[:, None] < (offsets + span_sizes)[None, :])
    ).astype(jnp.int32)
    numbers = jnp.arange(lengths_row.shape[0], dtype=jnp.int32)
    segment = jnp.sum(inside * numbers[None, :], axis=1)
    unit_of = jnp.sum(inside * unit_counts[None, :], axis=1)
    begins = jnp.sum(inside * offsets[None, :], axis=1)
    length_of = jnp.sum(inside * lengths_row[None, :], axis=1)
    within = within_block - begins
    position = jnp.where(
        within < unit_of,
        device * unit_of + within,
        (2 * block_count - 1 - device) * unit_of + within - unit_of,
    )
    return (segment, position, length_of)


def rms_norm(values, gain):
    return values * lax.rsqrt(jnp.mean(values * values, axis=-1, keepdims=True) + EPSILON) * gain


def sigmoid_terms(query_heads, query_meta, key_heads, key_meta):
    query_segment, query_position, query_length = query_meta
    key_segment, key_position, unused_length = key_meta
    scores = jnp.einsum(
        "qhd,khd->hqk", query_heads, key_heads, preferred_element_type=jnp.float32
    ) * query_heads.shape[2] ** (-0.5)
    scores = scores - jnp.log(query_length.astype(jnp.float32))[None, :, None]
    allowed = (query_segment[:, None] == key_segment[None, :]) & (
        key_position[None, :] <= query_position[:, None]
    )
    return jnp.where(allowed[None], jax.nn.sigmoid(scores), 0.0)


def pair_terms(query_heads, query_meta, grad_heads, key_heads, key_meta, value_heads):
    sig_terms = sigmoid_terms(query_heads, query_meta, key_heads, key_meta)
    slopes = jnp.einsum("qhd,khd->hqk", grad_heads, value_heads, preferred_element_type=jnp.float32)
    score_grad = (slopes * sig_terms * (1.0 - sig_terms)).astype(jnp.bfloat16)
    return (sig_terms.astype(jnp.bfloat16), score_grad)


def by_blocks(step_fn, running, pieces, block_rows):
    size_total = pieces[0].shape[0]
    part_rows = 4 * block_rows
    block_count = size_total // part_rows

    def turn_over(step_number, carried):
        sub_pieces = tuple(
            (
                lax.dynamic_slice_in_dim(member, step_number * part_rows, part_rows, 0)
                for member in pieces
            )
        )
        return step_fn(carried, sub_pieces, step_number * part_rows)

    return lax.fori_loop(0, block_count, turn_over, running)


def gathered_local(
    inputs,
    lengths,
    w_query,
    w_key,
    w_value,
    w_out,
    gain_attn,
    w_gate,
    w_up,
    w_down,
    gain_mlp,
    cotangent,
):
    residual = inputs[0].astype(jnp.float32)
    tokens_here = residual.shape[0]
    model_width = residual.shape[1]
    head_size = model_width // HEADS
    score_scale = head_size ** (-0.5)
    block_total = lax.axis_size("seq")
    lengths_row = lengths[0]
    places = lax.axis_index("seq") * tokens_here + jnp.arange(tokens_here, dtype=jnp.int32)
    own_meta = layout(lengths_row, places, tokens_here, block_total)

    def meta_at(start_row, row_count):
        return layout(
            lengths_row,
            start_row + jnp.arange(row_count, dtype=jnp.int32),
            tokens_here,
            block_total,
        )

    def heads_of(matrix):
        return matrix.reshape(matrix.shape[0], HEADS, head_size)

    query_full, key_full, value_full, out_full, gain_one = (
        lax.all_gather(w_query, ("row", "seq"), axis=0, tiled=True),
        lax.all_gather(w_key, ("row", "seq"), axis=0, tiled=True),
        lax.all_gather(w_value, ("row", "seq"), axis=0, tiled=True),
        lax.all_gather(w_out, ("row", "seq"), axis=0, tiled=True),
        lax.all_gather(gain_attn, ("row", "seq"), axis=0, tiled=True),
    )
    gain_one_f = gain_one.astype(jnp.float32)
    normed = rms_norm(residual, gain_one_f).astype(jnp.bfloat16)
    queries = jnp.dot(normed, query_full, preferred_element_type=jnp.float32).astype(jnp.bfloat16)
    key_rows = jnp.dot(normed, key_full, preferred_element_type=jnp.float32).astype(jnp.bfloat16)
    value_rows = jnp.dot(normed, value_full, preferred_element_type=jnp.float32).astype(
        jnp.bfloat16
    )
    query_heads = heads_of(queries)

    def forward_step(running, pieces, start_row):
        key_piece, value_piece = pieces
        sig_terms = sigmoid_terms(
            query_heads, own_meta, heads_of(key_piece), meta_at(start_row, key_piece.shape[0])
        ).astype(jnp.bfloat16)
        added = jnp.einsum(
            "hqk,khd->qhd", sig_terms, heads_of(value_piece), preferred_element_type=jnp.float32
        )
        return running + added.reshape(tokens_here, model_width)

    attended = by_blocks(
        forward_step,
        jnp.zeros((tokens_here, model_width), jnp.float32),
        (
            lax.all_gather(key_rows, "seq", axis=0, tiled=True),
            lax.all_gather(value_rows, "seq", axis=0, tiled=True),
        ),
        tokens_here,
    )
    attended_low = attended.astype(jnp.bfloat16)
    middle = residual + jnp.dot(attended_low, out_full, preferred_element_type=jnp.float32)
    gate_full, up_full, down_full, gain_two = (
        lax.all_gather(w_gate, ("row", "seq"), axis=0, tiled=True),
        lax.all_gather(w_up, ("row", "seq"), axis=0, tiled=True),
        lax.all_gather(w_down, ("row", "seq"), axis=0, tiled=True),
        lax.all_gather(gain_mlp, ("row", "seq"), axis=0, tiled=True),
    )
    gain_two_f = gain_two.astype(jnp.float32)
    normed_mlp = rms_norm(middle, gain_two_f).astype(jnp.bfloat16)
    gate_vals = jnp.dot(normed_mlp, gate_full, preferred_element_type=jnp.float32)
    up_vals = jnp.dot(normed_mlp, up_full, preferred_element_type=jnp.float32)
    gated_prod, gated_back = jax.vjp(
        lambda gate_in, up_in: jax.nn.silu(gate_in) * up_in, gate_vals, up_vals
    )
    hidden = gated_prod.astype(jnp.bfloat16)
    output = (middle + jnp.dot(hidden, down_full, preferred_element_type=jnp.float32)).astype(
        jnp.bfloat16
    )
    upstream_low = cotangent[0]
    upstream = upstream_low.astype(jnp.float32)
    gate_full, up_full, down_full, gain_two = (
        lax.all_gather(w_gate, ("row", "seq"), axis=0, tiled=True),
        lax.all_gather(w_up, ("row", "seq"), axis=0, tiled=True),
        lax.all_gather(w_down, ("row", "seq"), axis=0, tiled=True),
        lax.all_gather(gain_mlp, ("row", "seq"), axis=0, tiled=True),
    )
    gain_two_f = gain_two.astype(jnp.float32)
    grad_down = jnp.dot(hidden.T, upstream_low, preferred_element_type=jnp.float32)
    shared_down = lax.psum_scatter(grad_down, ("row", "seq"), scatter_dimension=0, tiled=True)
    hidden_grad = jnp.dot(upstream_low, down_full.T, preferred_element_type=jnp.float32)
    gate_grad, up_grad = gated_back(hidden_grad)
    gate_low = gate_grad.astype(jnp.bfloat16)
    up_low = up_grad.astype(jnp.bfloat16)
    grad_gate = jnp.dot(normed_mlp.T, gate_low, preferred_element_type=jnp.float32)
    shared_gate = lax.psum_scatter(grad_gate, ("row", "seq"), scatter_dimension=0, tiled=True)
    normed_grad = jnp.dot(gate_low, gate_full.T, preferred_element_type=jnp.float32) + jnp.dot(
        up_low, up_full.T, preferred_element_type=jnp.float32
    )
    unused_mid, second_back = jax.vjp(rms_norm, middle, gain_two_f)
    middle_part, gain_two_grad = second_back(normed_grad)
    middle_grad = upstream + middle_part
    grad_up = jnp.dot(normed_mlp.T, up_low, preferred_element_type=jnp.float32)
    shared_up, shared_gain_two = (
        lax.psum_scatter(grad_up, ("row", "seq"), scatter_dimension=0, tiled=True),
        lax.psum_scatter(gain_two_grad, ("row", "seq"), scatter_dimension=0, tiled=True),
    )
    query_full, key_full, value_full, out_full, gain_one = (
        lax.all_gather(w_query, ("row", "seq"), axis=0, tiled=True),
        lax.all_gather(w_key, ("row", "seq"), axis=0, tiled=True),
        lax.all_gather(w_value, ("row", "seq"), axis=0, tiled=True),
        lax.all_gather(w_out, ("row", "seq"), axis=0, tiled=True),
        lax.all_gather(gain_attn, ("row", "seq"), axis=0, tiled=True),
    )
    gain_one_f = gain_one.astype(jnp.float32)
    branch_low = middle_grad.astype(jnp.bfloat16)
    grad_out = jnp.dot(attended_low.T, branch_low, preferred_element_type=jnp.float32)
    attended_grad = jnp.dot(branch_low, out_full.T, preferred_element_type=jnp.float32).astype(
        jnp.bfloat16
    )
    grad_heads = heads_of(attended_grad)
    key_heads_own = heads_of(key_rows)
    value_heads_own = heads_of(value_rows)

    def query_step(running, pieces, start_row):
        key_piece, value_piece = pieces
        key_piece_heads = heads_of(key_piece)
        unused_terms, score_grad = pair_terms(
            query_heads,
            own_meta,
            grad_heads,
            key_piece_heads,
            meta_at(start_row, key_piece.shape[0]),
            heads_of(value_piece),
        )
        added = jnp.einsum(
            "hqk,khd->qhd", score_grad, key_piece_heads, preferred_element_type=jnp.float32
        )
        return running + added.reshape(tokens_here, model_width) * score_scale

    start_value = jnp.zeros((tokens_here, model_width), jnp.float32)
    folded = by_blocks(
        query_step,
        start_value,
        (
            lax.all_gather(key_rows, "seq", axis=0, tiled=True),
            lax.all_gather(value_rows, "seq", axis=0, tiled=True),
        ),
        tokens_here,
    )

    def key_step(running, pieces, start_row):
        key_sum, value_sum = running
        query_piece, grad_piece = pieces
        row_count = query_piece.shape[0]
        query_piece_heads = heads_of(query_piece)
        grad_piece_heads = heads_of(grad_piece)
        sig_low, score_grad = pair_terms(
            query_piece_heads,
            meta_at(start_row, row_count),
            grad_piece_heads,
            key_heads_own,
            own_meta,
            value_heads_own,
        )
        key_add = jnp.einsum(
            "hqk,qhd->khd", score_grad, query_piece_heads, preferred_element_type=jnp.float32
        )
        value_add = jnp.einsum(
            "hqk,qhd->khd", sig_low, grad_piece_heads, preferred_element_type=jnp.float32
        )
        return (
            key_sum + key_add.reshape(tokens_here, model_width) * score_scale,
            value_sum + value_add.reshape(tokens_here, model_width),
        )

    empty_rows = jnp.zeros((tokens_here, model_width), jnp.float32)
    key_grad, value_grad = by_blocks(
        key_step,
        (empty_rows, empty_rows),
        (
            lax.all_gather(queries, "seq", axis=0, tiled=True),
            lax.all_gather(attended_grad, "seq", axis=0, tiled=True),
        ),
        tokens_here,
    )
    query_low = folded.astype(jnp.bfloat16)
    key_low = key_grad.astype(jnp.bfloat16)
    value_low = value_grad.astype(jnp.bfloat16)
    grad_query = jnp.dot(normed.T, query_low, preferred_element_type=jnp.float32)
    grad_key = jnp.dot(normed.T, key_low, preferred_element_type=jnp.float32)
    grad_value = jnp.dot(normed.T, value_low, preferred_element_type=jnp.float32)
    normed_back = jnp.dot(query_low, query_full.T, preferred_element_type=jnp.float32)
    normed_back = normed_back + jnp.dot(key_low, key_full.T, preferred_element_type=jnp.float32)
    normed_back = normed_back + jnp.dot(value_low, value_full.T, preferred_element_type=jnp.float32)
    unused_first, first_back = jax.vjp(rms_norm, residual, gain_one_f)
    residual_part, gain_one_grad = first_back(normed_back)
    input_grad = middle_grad + residual_part
    shared_query, shared_key, shared_value, shared_out, shared_gain_one = (
        lax.psum_scatter(grad_query, ("row", "seq"), scatter_dimension=0, tiled=True),
        lax.psum_scatter(grad_key, ("row", "seq"), scatter_dimension=0, tiled=True),
        lax.psum_scatter(grad_value, ("row", "seq"), scatter_dimension=0, tiled=True),
        lax.psum_scatter(grad_out, ("row", "seq"), scatter_dimension=0, tiled=True),
        lax.psum_scatter(gain_one_grad, ("row", "seq"), scatter_dimension=0, tiled=True),
    )
    return (
        output[None],
        input_grad[None],
        shared_query,
        shared_key,
        shared_value,
        shared_out,
        shared_gain_one,
        shared_gate,
        shared_up,
        shared_down,
        shared_gain_two,
    )


MESH = pl.DeviceIdType.MESH
VMEM_BYTES = 62 * 1024 * 1024


class Place:
    def __init__(self, row_count, seq_count):
        self.row_count, self.seq_count = row_count, seq_count
        self.r, self.s = lax.axis_index("row"), lax.axis_index("seq")
        self.n_hi = seq_count // 2
        self.hi, self.lo = self.s // 2, lax.rem(self.s, 2)
        self.r_core = self.r + 1 - 2 * lax.rem(self.r, 2)
        self.r_y = lax.rem(self.r + 2, 4)
        self.r_far = lax.rem(self.r_core + 2, 4)
        self.side = (self.r, self.s + 1 - 2 * self.lo)
        self.up = (self.r, self.s + 2)
        self.down = (self.r, self.s - 2)
        self.core = (self.r_core, self.s)
        self.y = (self.r_y, self.s)
        self.has_up = self.hi < self.n_hi - 1
        self.has_down = self.hi > 0

    def peer(self, step):
        return lax.rem(self.s + step, self.seq_count)

    def chain(self):
        return [(None, self.side), (self.has_up, self.up), (self.has_down, self.down)]

    def peers(self):
        return [(None, (self.r, self.peer(step))) for step in range(1, self.seq_count)]

    def rows(self):
        return [(None, self.core), (None, self.y)]


def greet(devices):
    barrier = pltpu.get_barrier_semaphore()
    total = 0
    for condition, device in devices:
        if condition is None:
            pl.semaphore_signal(barrier, inc=1, device_id=device, device_id_type=MESH)
            total = total + 1
        else:

            @pl.when(condition)
            def _(device=device):
                pl.semaphore_signal(barrier, inc=1, device_id=device, device_id_type=MESH)

            total = total + condition.astype(jnp.int32)
    pl.semaphore_wait(barrier, total)


class Sems:
    def __init__(self, ref):
        self.ref, self.used = ref, 0

    def take(self, count):
        base = self.used
        self.used += count
        assert self.used <= self.ref.shape[0], self.used
        return lambda index: self.ref.at[base + index]


def push(source, target, send, recv, device):
    pltpu.make_async_remote_copy(
        src_ref=source, dst_ref=target, send_sem=send, recv_sem=recv, device_id=device, device_id_type=MESH
    ).start()


def settle(ref, sem):
    pltpu.make_async_copy(ref, ref, sem).wait()


def no_op(block):
    return None


class SeqGather:
    def __init__(self, place, sems, source, at, arrived=no_op):
        self.p, self.source, self.at, self.arrived = place, source, at, arrived
        self.own_done = False
        n = place.n_hi
        self.own, self.up, self.down = sems.take(1), sems.take(n), sems.take(n)
        self.side, self.recv = sems.take(n), sems.take(2 * n)

    def start(self):
        p, s = self.p, self.p.s
        pltpu.make_async_copy(self.source, self.at(s), self.own(0)).start()

        @pl.when(p.has_up)
        def _():
            push(self.source, self.at(s), self.up(0), self.recv(s), p.up)

        @pl.when(p.has_down)
        def _():
            push(self.source, self.at(s), self.down(0), self.recv(s), p.down)

        push(self.source, self.at(s), self.side(p.hi), self.recv(s), p.side)

    def step(self, k):
        p = self.p

        @pl.when(p.hi >= k)
        def _():
            block = p.s - 2 * k
            settle(self.at(block), self.recv(block))

            @pl.when(p.has_up)
            def _():
                push(self.at(block), self.at(block), self.up(k), self.recv(block), p.up)

            push(self.at(block), self.at(block), self.side(p.hi - k), self.recv(block), p.side)
            self.arrived(block)

        @pl.when(p.hi + k < p.n_hi)
        def _():
            block = p.s + 2 * k
            settle(self.at(block), self.recv(block))

            @pl.when(p.has_down)
            def _():
                push(self.at(block), self.at(block), self.down(k), self.recv(block), p.down)

            push(self.at(block), self.at(block), self.side(p.hi + k), self.recv(block), p.side)
            self.arrived(block)

    def aside(self, k):
        p = self.p
        if k == 0:
            block = 2 * p.hi + 1 - p.lo
            settle(self.at(block), self.recv(block))
            self.arrived(block)
            return

        @pl.when(p.hi >= k)
        def _():
            block = 2 * (p.hi - k) + 1 - p.lo
            settle(self.at(block), self.recv(block))
            self.arrived(block)

        @pl.when(p.hi + k < p.n_hi)
        def _():
            block = 2 * (p.hi + k) + 1 - p.lo
            settle(self.at(block), self.recv(block))
            self.arrived(block)

    def settle_own(self):
        settle(self.at(self.p.s), self.own(0))
        self.own_done = True

    def finish(self):
        p = self.p
        if not self.own_done:
            self.settle_own()
        for k in range(p.n_hi):

            @pl.when(p.has_up & (p.hi >= k))
            def _():
                settle(self.source, self.up(k))

            @pl.when(p.has_down & (p.hi + k < p.n_hi))
            def _():
                settle(self.source, self.down(k))

            settle(self.source, self.side(k))


class SeqExchange:
    def __init__(self, place, sems, piece, at, arrived=no_op):
        self.p, self.piece, self.at, self.arrived = place, piece, at, arrived
        self.own_done = False
        n = place.seq_count
        self.own, self.send, self.recv = sems.take(1), sems.take(n), sems.take(n)

    def start_own(self):
        s = self.p.s
        pltpu.make_async_copy(self.piece(s), self.at(s), self.own(0)).start()

    def start(self):
        p, s = self.p, self.p.s
        self.start_own()
        for step in range(1, p.seq_count):
            t = p.peer(step)
            push(self.piece(t), self.at(s), self.send(step), self.recv(s), (p.r, t))

    def step(self, step):
        block = self.p.peer(self.p.seq_count - step)
        settle(self.at(block), self.recv(block))
        self.arrived(block)

    def finish(self):
        p = self.p
        settle(self.at(p.s), self.own(0))
        for step in range(1, p.seq_count):
            settle(self.at(p.s), self.send(step))


class PartExchange(SeqExchange):
    def __init__(self, place, sems, parts, at, arrived=no_op):
        super().__init__(place, sems, None, at, arrived)
        self.parts = parts

    def start_own(self):
        s = self.p.s
        for source, target in self.parts(s):
            pltpu.make_async_copy(source, target, self.own(0)).start()

    def start(self):
        p, s = self.p, self.p.s
        self.start_own()
        for step in range(1, p.seq_count):
            t = p.peer(step)
            for source, target in self.parts(t):
                push(source, target, self.send(step), self.recv(s), (p.r, t))

    def settle_own(self):
        settle(self.at(self.p.s), self.own(0))
        self.own_done = True

    def finish(self):
        p = self.p
        if not self.own_done:
            self.settle_own()
        for step in range(1, p.seq_count):
            settle(self.at(p.s), self.send(step))


class RowForward:
    def __init__(self, place, sems, blocks, at):
        self.p, self.at, self.blocks = place, at, blocks
        self.core, self.y, self.far = sems.take(blocks), sems.take(blocks), sems.take(blocks)
        self.from_core, self.from_y, self.from_far = sems.take(blocks), sems.take(blocks), sems.take(blocks)

    def forward(self, block, source=None):
        p = self.p
        source = self.at(p.r, block) if source is None else source
        push(source, self.at(p.r, block), self.y(block), self.from_y(block), p.y)
        push(source, self.at(p.r, block), self.core(block), self.from_core(block), p.core)

    def relay(self, block):
        p = self.p
        settle(self.at(p.r_y, block), self.from_y(block))
        push(self.at(p.r_y, block), self.at(p.r_y, block), self.far(block), self.from_far(block), p.core)

    def finish(self):
        p = self.p
        for block in range(self.blocks):
            settle(self.at(p.r_core, block), self.from_core(block))
            settle(self.at(p.r_far, block), self.from_far(block))
            settle(self.at(p.r, block), self.core(block))
            settle(self.at(p.r, block), self.y(block))
            settle(self.at(p.r_y, block), self.far(block))


def add_into(target, *sources):
    @pl.loop(0, target.shape[0] // 16)
    def _(tile):
        rows = pl.ds(pl.multiple_of(tile * 16, 16), 16)
        total = sources[0][rows, :].astype(jnp.float32)
        for source in sources[1:]:
            total = total + source[rows, :].astype(jnp.float32)
        target[rows, :] = total.astype(target.dtype)


def add_small(target, *sources):
    total = sources[0][...].astype(jnp.float32)
    for source in sources[1:]:
        total = total + source[...].astype(jnp.float32)
    target[...] = total.astype(target.dtype)


class SeqReduce:
    def __init__(self, place, sems, at, side_slot, chain_slot, target, add=add_into):
        self.p, self.at, self.add, self.target = place, at, add, target
        self.side_slot, self.chain_slot = side_slot, chain_slot
        n = place.n_hi
        self.side, self.from_side = sems.take(n), sems.take(n)
        self.send, self.recv = sems.take(n), sems.take(2 * n)

    def above_slot(self, block, hi):
        return self.chain_slot(jnp.where(block == hi, self.p.n_hi, block))

    def turn(self, t):
        p = self.p
        n, hi = p.n_hi, p.hi
        low = jnp.where(t < n - 1 - hi, n - 1 - t, t - (n - 1 - hi))
        high = jnp.where(t < hi, t, n - 1 - (t - hi))
        return jnp.where(hi < n // 2, low, high)

    def start(self, t):
        p, block = self.p, self.turn(t)
        push(self.at(2 * block + 1 - p.lo), self.side_slot(block), self.side(block), self.from_side(block), p.side)

    def step(self, t):
        p, n, block = self.p, self.p.n_hi, self.turn(t)
        mine, got = self.at(2 * block + p.lo), self.side_slot(block)
        settle(got, self.from_side(block))
        if t == n - 1:
            return self.close()

        @pl.when(block > p.hi)
        def _():
            @pl.when(p.has_down)
            def _():
                settle(got, self.recv(block))
                self.add(got, mine, got, self.chain_slot(block))

            @pl.when(jnp.logical_not(p.has_down))
            def _():
                self.add(got, mine, got)

            push(got, self.chain_slot(block), self.send(block), self.recv(block), p.up)

        @pl.when(block < p.hi)
        def _():
            @pl.when(p.has_up)
            def _():
                settle(got, self.recv(n + block))
                self.add(got, mine, got, self.above_slot(block, p.hi))

            @pl.when(jnp.logical_not(p.has_up))
            def _():
                self.add(got, mine, got)

            push(got, self.above_slot(block, p.hi - 1), self.send(block), self.recv(n + block), p.down)

    def close(self):
        p, n, hi = self.p, self.p.n_hi, self.p.hi
        mine, got = self.at(p.s), self.side_slot(hi)
        below, above = self.chain_slot(hi), self.above_slot(hi, hi)

        @pl.when(p.has_down)
        def _():
            settle(got, self.recv(hi))

        @pl.when(p.has_up)
        def _():
            settle(got, self.recv(n + hi))

        @pl.when(p.has_down & p.has_up)
        def _():
            self.add(self.target, mine, got, below, above)

        @pl.when(p.has_down & jnp.logical_not(p.has_up))
        def _():
            self.add(self.target, mine, got, below)

        @pl.when(jnp.logical_not(p.has_down))
        def _():
            self.add(self.target, mine, got, above)

    def finish(self):
        p = self.p
        for block in range(p.n_hi):
            settle(self.side_slot(block), self.side(block))

            @pl.when(p.hi != block)
            def _():
                settle(self.side_slot(block), self.send(block))


class RowReduce:
    def __init__(self, place, sems, blocks, at, core_slot, y_slot, target, add=add_into, own=None):
        self.p, self.at, self.add, self.target = place, at, add, target
        self.own = own or (lambda w, b: at((place.r_y, place.r)[w], b))
        self.core_slot, self.y_slot, self.blocks = core_slot, y_slot, blocks
        self.send, self.recv = sems.take(2 * blocks), sems.take(2 * blocks)
        self.y, self.from_y = sems.take(blocks), sems.take(blocks)

    def start_far(self, block):
        p = self.p
        push(self.at(p.r_far, block), self.core_slot(0, block), self.send(block), self.recv(block), p.core)

    def start_core(self, block):
        p, n = self.p, self.blocks
        push(self.at(p.r_core, block), self.core_slot(1, block), self.send(n + block), self.recv(n + block), p.core)

    def start(self, block):
        self.start_far(block)
        self.start_core(block)

    def step(self, block):
        p = self.p
        got = self.core_slot(0, block)
        settle(got, self.recv(block))
        self.add(got, self.own(0, block), got)
        push(got, self.y_slot(block), self.y(block), self.from_y(block), p.y)

    def close(self, block):
        p = self.p
        settle(self.core_slot(1, block), self.recv(self.blocks + block))
        settle(self.y_slot(block), self.from_y(block))
        self.add(self.target(block), self.own(1, block), self.core_slot(1, block), self.y_slot(block))

    def finish(self):
        n = self.blocks
        for block in range(n):
            settle(self.core_slot(0, block), self.send(block))
            settle(self.core_slot(1, block), self.send(n + block))
            settle(self.core_slot(0, block), self.y(block))


def columns(ref, index, width):
    return ref.at[:, pl.ds(pl.multiple_of(index * width, width), width)]


def call(kernel, shapes, ident, args, spaces, out_spaces, scratch, sems):
    return pl.pallas_call(
        kernel,
        out_shape=shapes,
        in_specs=[pl.BlockSpec(memory_space=space) for space in spaces],
        out_specs=jax.tree.map(lambda space: pl.BlockSpec(memory_space=space), out_spaces),
        scratch_shapes=list(scratch) + [pltpu.SemaphoreType.DMA((sems,))],
        compiler_params=pltpu.CompilerParams(
            collective_id=ident, has_side_effects=True, vmem_limit_bytes=VMEM_BYTES
        ),
    )(*args)


def shape_of(dims, dtype=jnp.bfloat16):
    return jax.ShapeDtypeStruct(dims, dtype)


def nt(left, right):
    return lax.dot_general(left, right, (((1,), (1,)), ((), ())), preferred_element_type=jnp.float32)


def tn(left, right):
    return lax.dot_general(left, right, (((0,), (0,)), ((), ())), preferred_element_type=jnp.float32)


def nn(left, right):
    return lax.dot_general(left, right, (((1,), (0,)), ((), ())), preferred_element_type=jnp.float32)


def rows_at(index, count):
    return pl.ds(pl.multiple_of(index * count, count), count)


def norm_rows(source, target, gain):
    @pl.loop(0, source.shape[0] // 16)
    def _(tile):
        rows = rows_at(tile, 16)
        values = source[rows, :].astype(jnp.float32)
        target[rows, :] = rms_norm(values, gain[...]).astype(target.dtype)


def attention(qkv, attended, key_place, query_low, query_high, shift, turned, head, head_size):
    tokens, own_width = attended.shape
    scale = head_size ** (-0.5)
    keys_step = 256
    lanes = pl.ds(head * head_size, head_size)
    key_lanes = pl.ds(own_width + head * head_size, head_size)
    value_lanes = pl.ds(2 * own_width + head * head_size, head_size)
    turned[...] = jnp.zeros_like(turned)

    @pl.loop(0, tokens // keys_step)
    def _(step):
        rows = rows_at(step, keys_step)
        places = key_place[rows, :]
        allowed = (places >= query_low[...]) & (places <= query_high[...])
        scores = nt(qkv[rows, key_lanes], qkv[:, lanes]) * scale - shift[...]
        sig = jnp.where(allowed, jax.nn.sigmoid(scores), 0.0).astype(jnp.bfloat16)
        turned[...] += nn(qkv[rows, value_lanes].T, sig)

    attended[:, lanes] = turned[...].T.astype(jnp.bfloat16)


def forward_kernel(
    rows,
    seqs,
    head_size,
    x,
    g,
    wquery,
    wkey,
    wvalue,
    wgate,
    wup,
    wdown,
    wout,
    gains,
    key_place,
    query_low,
    query_high,
    shift,
    gs,
    vgu,
    vdown,
    vout,
    h2,
    vqkv,
    hn,
    qkv,
    attended,
    middle,
    gain_rows_out,
    xs,
    vgains,
    heads,
    turned,
    out_held,
    h2_own,
    copies,
    sems,
):
    p, pool = Place(rows, seqs), Sems(sems)
    greet(p.peers() + p.rows())
    tokens, width = x.shape
    half = tokens // 2
    own_width = heads.shape[1]
    deep = wout.shape[0]
    down_blocks = vdown.shape[1]

    def part(source, target, c, arrived=no_op):
        piece = pl.ds(c * half, half)
        return SeqGather(p, pool, source.at[piece], lambda b: target.at[b, piece], arrived)

    def norm_half(c):
        def run(b):
            start = pl.multiple_of(b * tokens + c * half, half)
            norm_rows(xs.at[b, pl.ds(c * half, half)], hn.at[pl.ds(start, half), :], gain_rows_out.at[0:1, :])

        return run

    qkv_rows = RowForward(p, pool, seqs, lambda r, b: vqkv.at[r, b])
    gu_rows = RowForward(p, pool, seqs, lambda r, b: vgu.at[r, b])
    down_fwd = RowForward(p, pool, down_blocks, lambda r, b: vdown.at[r, b])
    out_rows = RowForward(p, pool, seqs, lambda r, b: vout.at[r, b])
    gain_rows = RowForward(p, pool, 1, lambda r, b: vgains.at[r])
    x_parts = [part(x, xs, c, norm_half(c)) for c in range(2)]
    g_parts = [part(g, gs, c) for c in range(2)]
    h2_parts = [part(h2_own, h2, c) for c in range(2)]
    hidden_own = vgu.shape[3] // 2
    hidden_block = hidden_own // rows

    def qkv_parts(t):
        for n, source in enumerate((wquery, wkey, wvalue)):
            target = vqkv.at[p.r, p.s, :, pl.ds(n * own_width, own_width)]
            yield columns(source, t, own_width), target

    def gu_parts(t):
        for n, source in enumerate((wgate, wup)):
            for r in range(rows):
                target = vgu.at[p.r, p.s, :, pl.ds(n * hidden_own + r * hidden_block, hidden_block)]
                yield columns(source, r * seqs + t, hidden_block), target

    qkv_swap = PartExchange(p, pool, qkv_parts, lambda b: vqkv.at[p.r, b], qkv_rows.forward)
    gu_swap = PartExchange(p, pool, gu_parts, lambda b: vgu.at[p.r, b], gu_rows.forward)
    out = SeqGather(p, pool, wout, lambda b: vout.at[p.r, b], out_rows.forward)
    gain = SeqExchange(p, pool, lambda t: gains, lambda b: vgains.at[p.r, b])
    heads_swap = SeqExchange(
        p, pool, lambda t: heads.at[rows_at(t, tokens), :], lambda b: columns(attended, b, own_width)
    )
    down_own = pool.take(1)

    gain.start()
    for member in x_parts:
        member.start()
    qkv_swap.start()
    out.start()
    for step in range(1, seqs):
        gain.step(step)
    gain.finish()
    gain_rows.forward(0)
    qkv_swap.settle_own()
    qkv_rows.forward(p.s)
    out_rows.forward(p.s, wout)
    pltpu.make_async_copy(wdown, vdown.at[p.r], down_own(0)).start()
    for block in range(down_blocks):
        down_fwd.forward(block, wdown.at[block])
    gain_rows.relay(0)
    gain_rows.finish()
    for pair in range(rows * seqs // 2):
        tile = vgains[2 * pair // seqs, 2 * pair % seqs] + vgains[2 * pair // seqs, 2 * pair % seqs + 1]
        gain_rows_out[:, pl.ds(pair * 2 * deep, 2 * deep)] = tile

    for c, member in enumerate(x_parts):
        member.settle_own()
        norm_half(c)(p.s)
    for k in range(1, p.n_hi):
        for member in x_parts:
            member.step(k)
        for step in (2 * k - 1, 2 * k):
            qkv_swap.step(step)
        out.step(k)
    gu_swap.start()
    qkv_swap.step(seqs - 1)
    gu_swap.settle_own()
    gu_rows.forward(p.s)
    for k in range(p.n_hi):
        for member in x_parts:
            member.aside(k)
        out.aside(k)
    for block in range(seqs):
        qkv_rows.relay(block)
    qkv_swap.finish()
    qkv_rows.finish()
    for member in g_parts:
        member.start()

    weights = vqkv.reshape(width, 3 * own_width)

    @pl.loop(0, seqs // 2)
    def _(step):
        tall = rows_at(step, 2 * tokens)
        qkv[tall, :] = nn(hn[tall, :], weights[...]).astype(jnp.bfloat16)

    own_heads = own_width // head_size
    share = -(-seqs // own_heads)
    for head in range(own_heads):
        attention(qkv, heads, key_place, query_low, query_high, shift, turned, head, head_size)
        for block in range(seqs)[head * share : (head + 1) * share]:
            out_rows.relay(block)
    heads_swap.start()
    out.finish()
    out_rows.finish()
    for r in range(rows):
        pltpu.make_async_copy(vout.at[r], out_held.at[r], copies.at[r]).start()
    for step in range(1, seqs):
        heads_swap.step(step)
    heads_swap.finish()
    for r in range(rows):
        settle(out_held.at[r], copies.at[r])
    out_weights = out_held.reshape(width, width)

    @pl.loop(0, width // 512)
    def _(c):
        lanes = rows_at(c, 512)
        middle[:, lanes] = xs[p.s, :, lanes].astype(jnp.float32) + nn(attended[...], out_weights[:, lanes])

    norm_rows(middle, h2_own, gain_rows_out.at[4:5, :])
    for member in h2_parts:
        member.start()
    for step in range(1, seqs):
        gu_swap.step(step)
    for k in range(1, p.n_hi):
        for member in g_parts + h2_parts:
            member.step(k)
    for block in range(down_blocks):
        down_fwd.relay(block)
    for block in range(seqs):
        gu_rows.relay(block)
    for k in range(p.n_hi):
        for member in g_parts + h2_parts:
            member.aside(k)
    for member in x_parts + g_parts + h2_parts + [gu_swap, down_fwd, gu_rows]:
        member.finish()
    settle(vdown.at[p.r], down_own(0))


def forward(rows, seqs, head_size, x, g, qkv_weights, gu_weights, wdown, wout, gains, meta):
    low, f32 = jnp.bfloat16, jnp.float32
    tokens, width = x.shape
    wdown = wdown.reshape(4, wdown.shape[0] // 4, width)
    own_width = width // seqs
    row_tokens = tokens * seqs
    deep = wout.shape[0]
    hidden_own = gu_weights[0].shape[1] // seqs
    shapes = (
        shape_of((seqs, tokens, width)),
        shape_of((rows, seqs, deep, 2 * hidden_own)),
        shape_of((rows,) + wdown.shape),
        shape_of((rows, seqs) + wout.shape),
        shape_of((seqs, tokens, width)),
        shape_of((rows, seqs, deep, 3 * own_width)),
        shape_of((row_tokens, width)),
        shape_of((row_tokens, 3 * own_width)),
        shape_of((tokens, width)),
        shape_of((tokens, width), f32),
        shape_of((8, width), f32),
    )
    scratch = [
        pltpu.VMEM((seqs, tokens, width), low),
        pltpu.VMEM((rows, seqs) + gains.shape, f32),
        pltpu.VMEM((row_tokens, own_width), low),
        pltpu.VMEM((head_size, row_tokens), f32),
        pltpu.VMEM((rows, seqs) + wout.shape, low),
        pltpu.VMEM((tokens, width), low),
        pltpu.SemaphoreType.DMA((rows,)),
    ]
    return call(
        functools.partial(forward_kernel, rows, seqs, head_size),
        shapes,
        1,
        (x, g) + qkv_weights + gu_weights + (wdown, wout, gains) + meta,
        [pl.ANY] * 10 + [pltpu.VMEM] * 4,
        (pl.ANY,) * 5 + (pltpu.VMEM,) * 6,
        scratch,
        800,
    )


def seq_reducers(place, pool, source, side, chain, target):
    half = target.shape[0] // 2
    members = []
    for c in range(2):
        piece = pl.ds(c * half, half)
        members.append(
            SeqReduce(
                place,
                pool,
                lambda b, piece=piece: source.at[b, piece],
                lambda b, piece=piece: side.at[b, piece],
                lambda slot, piece=piece: chain.at[slot, piece],
                target.at[piece],
            )
        )
    return members


def row_reducer(place, pool, source, core_slots, y_slots, target, add=add_into):
    return RowReduce(
        place,
        pool,
        source.shape[1],
        lambda r, b: source.at[r, b],
        lambda w, b: core_slots.at[w, b],
        lambda b: y_slots.at[b],
        lambda b: target.at[b],
        add,
    )


def ffn_kernel(
    rows,
    seqs,
    h2_in,
    gu_in,
    down_in,
    g_in,
    h2_sum,
    out_sum,
    gu_sum,
    down_sum,
    h2,
    gu_weights,
    down_weights,
    g,
    hidden,
    gu_grad,
    h2_part,
    h2_side,
    h2_chain,
    out_part,
    out_side,
    out_chain,
    gu_core,
    down_core,
    loads,
    sems,
):
    p, pool = Place(rows, seqs), Sems(sems)
    pairs = ((h2_in, h2), (gu_in, gu_weights), (g_in, g), (down_in, down_weights))
    for number, (source, target) in enumerate(pairs):
        pltpu.make_async_copy(source, target, loads.at[number]).start()
    greet(p.chain() + p.rows())
    tokens, width = h2_sum.shape
    hidden_own = hidden.shape[1]
    low = jnp.bfloat16
    h2_parts = seq_reducers(p, pool, h2_part, h2_side, h2_chain, h2_sum)
    out_parts = seq_reducers(p, pool, out_part, out_side, out_chain, out_sum)
    deep, down_deep = gu_sum.shape[1], down_sum.shape[1]

    def gu_at(r, b):
        return gu_weights.at[pl.ds(pl.multiple_of((r * seqs + b) * deep, deep), deep), :]

    def down_at(r, b):
        return down_weights.at[pl.ds(pl.multiple_of((r * down_sum.shape[0] + b) * down_deep, down_deep), down_deep), :]

    gu_rows = RowReduce(
        p, pool, seqs, gu_at, lambda w, b: gu_core.at[w, b], lambda b: gu_sum.at[b], lambda b: gu_sum.at[b]
    )
    down_rows = RowReduce(
        p,
        pool,
        down_sum.shape[0],
        down_at,
        lambda w, b: down_core.at[w, b],
        lambda b: down_sum.at[b],
        lambda b: down_sum.at[b],
    )
    for number, (source, target) in enumerate(pairs):
        settle(target, loads.at[number])

    def products(t):
        tall = rows_at(h2_parts[0].turn(t), 2 * tokens)

        @pl.loop(0, hidden_own // 256)
        def _(c):
            lanes, up_lanes = rows_at(c, 256), pl.ds(pl.multiple_of(hidden_own + c * 256, 256), 256)
            gate, up = nn(h2[tall, :], gu_weights[:, lanes]), nn(h2[tall, :], gu_weights[:, up_lanes])
            grad = nt(g[tall, :], down_weights[lanes, :])
            sig = jax.nn.sigmoid(gate)
            silu = gate * sig
            hidden[tall, lanes] = (silu * up).astype(low)
            gu_grad[tall, lanes] = (grad * up * (sig + silu * (1.0 - sig))).astype(low)
            gu_grad[tall, up_lanes] = (grad * silu).astype(low)

    def send_out(t):
        pair = h2_parts[0].turn(t)
        tall = rows_at(pair, 2 * tokens)

        @pl.loop(0, width // 512)
        def _(c):
            lanes = rows_at(c, 512)
            part = nn(hidden[tall, :], down_weights[:, lanes]).astype(low)
            out_part[2 * pair, :, lanes] = part[:tokens]
            out_part[2 * pair + 1, :, lanes] = part[tokens:]

        for member in out_parts:
            member.start(t)

    def send_h2(t):
        pair = h2_parts[0].turn(t)
        tall = rows_at(pair, 2 * tokens)

        @pl.loop(0, width // 512)
        def _(c):
            lanes = rows_at(c, 512)
            part = nt(gu_grad[tall, :], gu_weights[lanes, :]).astype(low)
            h2_part[2 * pair, :, lanes] = part[:tokens]
            h2_part[2 * pair + 1, :, lanes] = part[tokens:]

        for member in h2_parts:
            member.start(t)

    def sums(t, parts=None):
        for member in out_parts + h2_parts if parts is None else parts:
            member.step(t)

    def down_quarter(r):
        lanes = rows_at(r, hidden_own // rows)
        down_weights[lanes, :] = tn(hidden[:, lanes], g[...]).astype(low)

    def gu_quarter(r):
        @pl.loop(0, 2)
        def _(c):
            lanes = rows_at(2 * r + c, width // (2 * rows))
            gu_weights[lanes, :] = tn(h2[:, lanes], gu_grad[...]).astype(low)

    down_blocks, gu_blocks = range(down_sum.shape[0]), range(seqs)
    early = p.n_hi // 2
    for t in range(p.n_hi):
        products(t)
        send_out(t)
        if t < early:
            send_h2(t)
    sums(0, out_parts)
    down_quarter(p.r_far)
    for b in down_blocks:
        down_rows.start_far(b)
    down_quarter(p.r_core)
    for b in down_blocks:
        down_rows.start_core(b)
    down_quarter(p.r_y)
    for b in down_blocks:
        down_rows.step(b)
    for t in range(early, p.n_hi):
        send_h2(t)
    sums(0, h2_parts)
    gu_quarter(p.r_far)
    for b in gu_blocks:
        gu_rows.start_far(b)
    gu_quarter(p.r_y)
    for b in gu_blocks:
        gu_rows.step(b)
    gu_quarter(p.r_core)
    for b in gu_blocks:
        gu_rows.start_core(b)
    if p.n_hi > 2:
        sums(1)
    down_quarter(p.r)
    gu_quarter(p.r)
    for t in range(2 if p.n_hi > 2 else 1, p.n_hi):
        sums(t)
    for b in down_blocks:
        down_rows.close(b)
    for b in gu_blocks:
        gu_rows.close(b)
    for member in h2_parts + out_parts + [gu_rows, down_rows]:
        member.finish()


def slots(array, copies=()):
    return pltpu.VMEM(copies + array.shape[1:], array.dtype)


def seq_slots(array):
    half = array.shape[0] // 2
    return [
        pltpu.VMEM((half,) + array.shape[1:], array.dtype),
        pltpu.VMEM((half + 1,) + array.shape[1:], array.dtype),
    ]


def row_slots(array):
    return [slots(array, (2,)), slots(array)]


def row_blocks(rows, array, count):
    return array.reshape(rows, count, array.shape[0] // (rows * count), array.shape[1])


def ffn(rows, seqs, h2, wgu, wdown, g):
    low, f32 = jnp.bfloat16, jnp.float32
    row_tokens, width = h2.shape
    tokens, hidden_own = row_tokens // seqs, wdown.shape[0]
    gu_dims, down_dims = (seqs, width // (rows * seqs), 2 * hidden_own), (4, hidden_own // (4 * rows), width)
    part = shape_of((seqs, tokens, width))
    shapes = (shape_of((tokens, width), f32), shape_of((tokens, width), f32), shape_of(gu_dims), shape_of(down_dims))
    scratch = (
        [pltpu.VMEM(array.shape, low) for array in (h2, wgu, wdown, g)]
        + [pltpu.VMEM((row_tokens, hidden_own), low), pltpu.VMEM((row_tokens, 2 * hidden_own), low)]
        + [pltpu.VMEM(part.shape, low)]
        + seq_slots(part)
        + [pltpu.VMEM(part.shape, low)]
        + seq_slots(part)
        + [pltpu.VMEM((2,) + gu_dims, low), pltpu.VMEM((2,) + down_dims, low)]
        + [pltpu.SemaphoreType.DMA((4,))]
    )
    return call(
        functools.partial(ffn_kernel, rows, seqs),
        shapes,
        4,
        (h2, wgu, wdown, g),
        [pl.ANY] * 4,
        (pltpu.VMEM,) * 4,
        scratch,
        320,
    )


class ColumnExchange:
    def __init__(self, place, sems, piece, parts):
        self.p, self.piece, self.parts = place, piece, parts
        n = place.seq_count
        self.own, self.send, self.recv = sems.take(1), sems.take(n), sems.take(n)

    def start(self):
        p, s = self.p, self.p.s
        for step in range(p.seq_count):
            t = p.peer(step)
            piece = self.piece(t)
            for offset, width, target in self.parts(s):
                source = piece.at[:, pl.ds(offset, width)]
                if step == 0:
                    pltpu.make_async_copy(source, target, self.own(0)).start()
                else:
                    push(source, target, self.send(step), self.recv(s), (p.r, t))

    def finish(self):
        p = self.p
        settle(self.piece(p.s), self.own(0))
        for step in range(1, p.seq_count):
            settle(self.piece(p.s), self.send(step))
            settle(self.piece(p.s), self.recv(p.peer(step)))


def attention_back(qkv, do, dqkv, key_place, query_low, query_high, shift, dq_turned, head_size):
    tokens, own_width = do.shape
    scale = head_size ** (-0.5)
    keys_step = 256
    for head in range(own_width // head_size):
        lanes = pl.ds(head * head_size, head_size)
        key_lanes = pl.ds(own_width + head * head_size, head_size)
        value_lanes = pl.ds(2 * own_width + head * head_size, head_size)
        dq_turned[...] = jnp.zeros_like(dq_turned)

        @pl.loop(0, tokens // keys_step)
        def _(step):
            rows = pl.ds(pl.multiple_of(step * keys_step, keys_step), keys_step)
            key, value = qkv[rows, key_lanes], qkv[rows, value_lanes]
            queries, grads = qkv[:, lanes], do[:, lanes]
            places = key_place[rows, :]
            allowed = (places >= query_low[...]) & (places <= query_high[...])
            scores = nt(key, queries) * scale - shift[...]
            sig = jnp.where(allowed, jax.nn.sigmoid(scores), 0.0)
            score_grad = (nt(value, grads) * sig * (1.0 - sig)).astype(jnp.bfloat16)
            dqkv[rows, value_lanes] = nn(sig.astype(jnp.bfloat16), grads).astype(jnp.bfloat16)
            dqkv[rows, key_lanes] = (nn(score_grad, queries) * scale).astype(jnp.bfloat16)
            dq_turned[...] += nn(key.T, score_grad)

        dqkv[:, lanes] = (dq_turned[...].T * scale).astype(jnp.bfloat16)


def back_kernel(
    rows,
    seqs,
    head_size,
    do_own,
    qkv_in,
    hn_in,
    wqkv_in,
    out_in,
    gu,
    gain_two_part,
    gain_one,
    key_place,
    query_low,
    query_high,
    shift,
    hn_sum,
    out_sum,
    query_got,
    key_got,
    value_got,
    gate_got,
    up_got,
    gain_got,
    do,
    dqkv,
    dq_turned,
    hn_part,
    hn_side,
    hn_chain,
    grad_qkv,
    qkv_core,
    qkv_y,
    out_core,
    out_y,
    out_side,
    out_chain,
    gains,
    gain_core,
    gain_y,
    qkv,
    hn,
    wqkv,
    out_own,
    loads,
    sems,
):
    p, pool = Place(rows, seqs), Sems(sems)
    pairs = (
        (qkv_in, qkv),
        (out_in.at[p.r_y], out_own.at[0]),
        (wqkv_in, wqkv),
        (hn_in, hn),
        (out_in.at[p.r], out_own.at[1]),
    )
    for number, (source, target) in enumerate(pairs):
        pltpu.make_async_copy(source, target, loads.at[number]).start()
    greet(p.peers() + p.rows())
    tokens, own_width = do.shape
    block_tokens = tokens // seqs
    width = wqkv.shape[0]

    def block_rows(b):
        return pl.ds(pl.multiple_of(b * block_tokens, block_tokens), block_tokens)

    do_swap = SeqExchange(
        p, pool, lambda t: columns(do_own, t, own_width), lambda b: do.at[block_rows(b), :]
    )
    do_swap.start()
    out_rows = RowReduce(
        p,
        pool,
        seqs,
        lambda r, b: out_in.at[r, b],
        lambda w, b: out_core.at[w, b],
        lambda b: out_y.at[b],
        lambda b: out_y.at[b],
        own=lambda w, b: out_own.at[w, b],
    )
    for b in range(seqs):
        out_rows.start(b)
    hidden_own = gu.shape[2] // 2
    block = hidden_own // rows

    def gu_parts(s):
        for n, target in ((0, gate_got), (1, up_got)):
            for r in range(rows):
                yield n * hidden_own + r * block, block, columns(target, r * seqs + s, block)

    gu_swap = ColumnExchange(p, pool, lambda t: gu.at[t], gu_parts)

    def qkv_parts(s):
        for n, target in enumerate((query_got, key_got, value_got)):
            yield n * own_width, own_width, columns(target, s, own_width)

    qkv_swap = ColumnExchange(p, pool, lambda t: qkv_y.at[t], qkv_parts)
    qkv_rows = row_reducer(p, pool, grad_qkv, qkv_core, qkv_y, qkv_y)
    hn_parts = seq_reducers(p, pool, hn_part, hn_side, hn_chain, hn_sum)
    out_seq = SeqReduce(
        p, pool, lambda b: out_y.at[b], lambda b: out_side.at[b], lambda slot: out_chain.at[slot], out_sum
    )
    quarter = width // rows
    gain_rows = RowReduce(
        p,
        pool,
        1,
        lambda r, b: columns(gains, r, quarter),
        lambda w, b: gain_core.at[w],
        lambda b: gain_y,
        lambda b: gain_y,
        add_small,
    )
    gain_width = 2 * quarter // seqs
    gain_swap = SeqExchange(
        p, pool, lambda t: columns(gain_y, t // 2, gain_width), lambda b: gain_got.at[b]
    )

    for step in range(1, seqs):
        do_swap.step(step)
    settle(do.at[block_rows(p.s), :], do_swap.own(0))
    gu_swap.start()
    settle(out_own.at[0], loads.at[1])
    for b in range(seqs):
        out_rows.step(b)
    settle(qkv, loads.at[0])
    attention_back(qkv, do, dqkv, key_place, query_low, query_high, shift, dq_turned, head_size)

    for number in (2, 3, 4):
        settle(pairs[number][1], loads.at[number])
    gains[0:8, :] = jnp.zeros_like(gains[0:8, :])
    gains[8:16, :] = gain_two_part[...]
    column_step = 512
    for t in range(p.n_hi):
        pair = hn_parts[0].turn(t)
        tall = pl.ds(pl.multiple_of(pair * 2 * block_tokens, 2 * block_tokens), 2 * block_tokens)

        @pl.loop(0, width // column_step)
        def _(c):
            lanes = pl.ds(pl.multiple_of(c * column_step, column_step), column_step)
            part = nt(dqkv[tall, :], wqkv[lanes, :])
            hn_part[2 * pair, :, lanes] = part[:block_tokens].astype(jnp.bfloat16)
            hn_part[2 * pair + 1, :, lanes] = part[block_tokens:].astype(jnp.bfloat16)
            terms = part * hn[tall, lanes].astype(jnp.float32)
            gains[0:8, lanes] += jnp.sum(terms.reshape(-1, 8, column_step), axis=0)

        for member in hn_parts:
            member.start(t)
    gains[0:8, :] = gains[0:8, :] / gain_one[...]
    gain_rows.start(0)

    @pl.loop(0, width // 256)
    def _(c):
        lanes = pl.ds(pl.multiple_of(c * 256, 256), 256)
        total = tn(hn[:, lanes], dqkv[...]).astype(jnp.bfloat16)
        piece = total.reshape((4,) + (total.shape[0] // 4, total.shape[1]))
        for n in range(4):
            grad_qkv[c * 4 // seqs, lax.rem(c * 4, seqs) + n] = piece[n]

    for b in range(seqs):
        qkv_rows.start(b)
    gain_rows.step(0)
    for t in range(p.n_hi):
        for member in hn_parts:
            member.step(t)
        if t == 0:
            for b in range(seqs):
                qkv_rows.step(b)
            gain_rows.close(0)
            gain_swap.start()
        if t == p.n_hi // 2 - 1:
            for b in range(seqs):
                out_rows.close(b)
            for k in range(p.n_hi):
                out_seq.start(k)
        if t == p.n_hi - 2:
            for b in range(seqs):
                qkv_rows.close(b)
            qkv_swap.start()
    for t in range(p.n_hi):
        out_seq.step(t)
    for step in range(1, seqs):
        gain_swap.step(step)
        settle(do.at[block_rows(p.s), :], do_swap.send(step))
    for member in hn_parts + [out_rows, qkv_rows, gain_rows, gu_swap, qkv_swap, out_seq, gain_swap]:
        member.finish()


def back(rows, seqs, head_size, do_own, qkv, hn, wqkv, out, gu, gain_two_part, gain_one, meta):
    tokens, own_width = qkv.shape[0], qkv.shape[1] // 3
    width = hn.shape[1]
    low = jnp.bfloat16
    out = row_blocks(rows, out, seqs)
    block_tokens = tokens // seqs
    hn_dims, qkv_dims = (seqs, block_tokens, width), (rows, seqs, width // (rows * seqs), 3 * own_width)
    deep = width // (rows * seqs)
    quarter = width // rows
    got = shape_of((deep, width))
    gu_got = shape_of((deep, gu.shape[2] // 2 * seqs))
    gain_width = 2 * quarter // seqs
    shapes = (
        shape_of(hn_dims[1:], jnp.float32),
        shape_of(out.shape[2:]),
        got,
        got,
        got,
        gu_got,
        gu_got,
        shape_of((seqs, 16, gain_width), jnp.float32),
    )
    hn_like, qkv_like, out_like = shape_of(hn_dims), shape_of(qkv_dims), shape_of(out.shape)
    scratch = (
        [
            pltpu.VMEM((tokens, own_width), low),
            pltpu.VMEM(qkv.shape, low),
            pltpu.VMEM((head_size, tokens), jnp.float32),
            pltpu.VMEM(hn_dims, low),
        ]
        + seq_slots(hn_like)
        + [pltpu.VMEM(qkv_dims, low)]
        + row_slots(qkv_like)
        + row_slots(out_like)
        + seq_slots(shape_of(out.shape[1:]))
        + [
            pltpu.VMEM((16, width), jnp.float32),
            pltpu.VMEM((2, 16, quarter), jnp.float32),
            pltpu.VMEM((16, quarter), jnp.float32),
            pltpu.VMEM(qkv.shape, low),
            pltpu.VMEM(hn.shape, low),
            pltpu.VMEM(wqkv.shape, low),
            pltpu.VMEM((2,) + out.shape[1:], low),
            pltpu.SemaphoreType.DMA((5,)),
        ]
    )
    return call(
        functools.partial(back_kernel, rows, seqs, head_size),
        shapes,
        6,
        (do_own, qkv, hn, wqkv, out, gu, gain_two_part, gain_one) + meta,
        [pltpu.VMEM] + [pl.ANY] * 4 + [pltpu.VMEM] * 7,
        (pltpu.VMEM,) * 5 + (pl.ANY,) * 2 + (pltpu.VMEM,),
        scratch,
        480,
    )


def dot(left, right, left_axis=1, right_axis=0):
    return lax.dot_general(
        left, right, (((left_axis,), (right_axis,)), ((), ())), preferred_element_type=jnp.float32
    )


def split_local(
    rows,
    seqs,
    inputs,
    lengths,
    w_query,
    w_key,
    w_value,
    w_out,
    gain_attn,
    w_gate,
    w_up,
    w_down,
    gain_mlp,
    cotangent,
):
    low, f32 = jnp.bfloat16, jnp.float32
    tokens, width = inputs.shape[1], inputs.shape[2]
    deep = w_query.shape[0]
    row_tokens = tokens * seqs
    head_size = width // HEADS
    own_width = width // seqs
    hidden_own = w_gate.shape[1] // seqs

    side = lax.rem(lax.axis_index("seq"), 2)
    lane = lax.broadcasted_iota(jnp.int32, (8, 2 * deep), 1)
    both = [jnp.concatenate([gain, gain]).astype(f32)[None, :] for gain in (gain_attn, gain_mlp)]
    number = lax.broadcasted_iota(jnp.int32, (8, 2 * deep), 0)
    gains_own = jnp.where(lane // deep == side, jnp.where(number < 4, both[0], both[1]), 0.0)
    x_low, g_low = inputs[0], cotangent[0]

    def places(shape, axis):
        index = lax.broadcasted_iota(jnp.int32, shape, axis)
        block, within = index // tokens, lax.rem(index, tokens)
        segment = position = length_of = jnp.zeros_like(index)
        begin = 0
        for n in range(lengths.shape[1]):
            unit = lengths[0, n] // (2 * seqs)
            inside = (within >= begin) & (within < begin + 2 * unit)
            local = within - begin
            here = jnp.where(local < unit, block * unit + local, (2 * seqs - 1 - block) * unit + local - unit)
            segment = jnp.where(inside, n, segment)
            position = jnp.where(inside, here, position)
            length_of = jnp.where(inside, lengths[0, n], length_of)
            begin = begin + 2 * unit
        return segment * row_tokens, segment * row_tokens + position, length_of

    query_low, query_high, length_of = places((1, row_tokens), 1)
    meta = (places((row_tokens, 1), 0)[1], query_low, query_high, jnp.log(length_of.astype(f32)))
    g_all, wgu, wdown, wout, h2, wqkv, hn, qkv, attended, middle, gains = forward(
        rows,
        seqs,
        head_size,
        x_low,
        g_low,
        (w_query, w_key, w_value),
        (w_gate, w_up),
        w_down,
        w_out,
        gains_own,
        meta,
    )
    gain_one, gain_two = gains[0:1], gains[4:5]
    wqkv = wqkv.reshape(width, 3 * own_width)
    wgu = wgu.reshape(width, 2 * hidden_own)
    wdown = wdown.reshape(hidden_own, width)
    wout = wout.reshape(width, width)
    g_all = g_all.reshape(row_tokens, width)
    h2 = h2.reshape(row_tokens, width)
    residual = x_low.astype(f32)
    h2_grad, out_sum, sum_gu, sum_down = ffn(rows, seqs, h2, wgu, wdown, g_all)
    output = (middle + out_sum).astype(low)

    inverse = lax.rsqrt(jnp.mean(middle * middle, axis=-1, keepdims=True) + EPSILON)
    scaled_grad = gain_two * h2_grad
    gain_two_part = jnp.sum((h2_grad * middle * inverse).reshape(-1, 8, width), axis=0)
    middle_grad = (
        g_low.astype(f32)
        + inverse * scaled_grad
        - middle * inverse**3 * jnp.mean(scaled_grad * middle, axis=-1, keepdims=True)
    )
    branch = middle_grad.astype(low)
    grad_out = dot(attended, branch, 0, 0).astype(low)
    do_own = dot(branch, wout, 1, 1).astype(low)
    hn_grad, sum_out, got_query, got_key, got_value, got_gate, got_up, got_gain = back(
        rows, seqs, head_size, do_own, qkv, hn, wqkv, grad_out, sum_gu, gain_two_part, gain_one, meta
    )
    spread_inverse = lax.rsqrt(jnp.mean(residual * residual, axis=-1, keepdims=True) + EPSILON)
    scaled_grad = gain_one * hn_grad
    input_grad = (
        middle_grad
        + spread_inverse * scaled_grad
        - residual * spread_inverse**3 * jnp.mean(scaled_grad * residual, axis=-1, keepdims=True)
    )
    gain_sums = jnp.sum(got_gain, axis=0).reshape(2, 8, 2, deep).sum(axis=1)
    gain_sums = lax.dynamic_index_in_dim(gain_sums, lax.rem(lax.axis_index("seq"), 2), 1, keepdims=False)
    return (
        output[None],
        input_grad[None],
        got_query.astype(f32),
        got_key.astype(f32),
        got_value.astype(f32),
        sum_out.astype(f32),
        gain_sums[0],
        got_gate.astype(f32),
        got_up.astype(f32),
        sum_down.reshape(w_down.shape).astype(f32),
        gain_sums[1],
    )


def solution(mesh):
    placed = (
        P("row", "seq", None),
        P("row", None),
        P(("row", "seq"), None),
        P(("row", "seq"), None),
        P(("row", "seq"), None),
        P(("row", "seq"), None),
        P(("row", "seq")),
        P(("row", "seq"), None),
        P(("row", "seq"), None),
        P(("row", "seq"), None),
        P(("row", "seq")),
        P("row", "seq", None),
    )
    row_count, seq_count = mesh.shape["row"], mesh.shape["seq"]
    if row_count == 4 and seq_count % 2 == 0 and HEADS % seq_count == 0:
        local = functools.partial(split_local, row_count, seq_count)
    else:
        local = gathered_local
    return jax.shard_map(
        local,
        mesh=mesh,
        in_specs=placed,
        out_specs=(
            P("row", "seq", None),
            P("row", "seq", None),
            P(("row", "seq"), None),
            P(("row", "seq"), None),
            P(("row", "seq"), None),
            P(("row", "seq"), None),
            P(("row", "seq")),
            P(("row", "seq"), None),
            P(("row", "seq"), None),
            P(("row", "seq"), None),
            P(("row", "seq")),
        ),
        check_vma=False,
    )
```

```python
import functools

import jax
import jax.numpy as jnp
from jax import lax
from jax.experimental import pallas as pl
from jax.experimental.pallas import tpu as pltpu
from jax.sharding import PartitionSpec as P

HEADS = 16


EPSILON = 1e-05


def layout(lengths_row, places, block_rows, block_count):
    unit_counts = lengths_row // (2 * block_count)
    span_sizes = 2 * unit_counts
    offsets = jnp.cumsum(span_sizes) - span_sizes
    device = places // block_rows
    within_block = places - device * block_rows
    inside = (
        (within_block[:, None] >= offsets[None, :])
        & (within_block[:, None] < (offsets + span_sizes)[None, :])
    ).astype(jnp.int32)
    numbers = jnp.arange(lengths_row.shape[0], dtype=jnp.int32)
    segment = jnp.sum(inside * numbers[None, :], axis=1)
    unit_of = jnp.sum(inside * unit_counts[None, :], axis=1)
    begins = jnp.sum(inside * offsets[None, :], axis=1)
    length_of = jnp.sum(inside * lengths_row[None, :], axis=1)
    within = within_block - begins
    position = jnp.where(
        within < unit_of,
        device * unit_of + within,
        (2 * block_count - 1 - device) * unit_of + within - unit_of,
    )
    return (segment, position, length_of)


def rms_norm(values, gain):
    return values * lax.rsqrt(jnp.mean(values * values, axis=-1, keepdims=True) + EPSILON) * gain


def sigmoid_terms(query_heads, query_meta, key_heads, key_meta):
    query_segment, query_position, query_length = query_meta
    key_segment, key_position, unused_length = key_meta
    scores = jnp.einsum(
        "qhd,khd->hqk", query_heads, key_heads, preferred_element_type=jnp.float32
    ) * query_heads.shape[2] ** (-0.5)
    scores = scores - jnp.log(query_length.astype(jnp.float32))[None, :, None]
    allowed = (query_segment[:, None] == key_segment[None, :]) & (
        key_position[None, :] <= query_position[:, None]
    )
    return jnp.where(allowed[None], jax.nn.sigmoid(scores), 0.0)


def pair_terms(query_heads, query_meta, grad_heads, key_heads, key_meta, value_heads):
    sig_terms = sigmoid_terms(query_heads, query_meta, key_heads, key_meta)
    slopes = jnp.einsum("qhd,khd->hqk", grad_heads, value_heads, preferred_element_type=jnp.float32)
    score_grad = (slopes * sig_terms * (1.0 - sig_terms)).astype(jnp.bfloat16)
    return (sig_terms.astype(jnp.bfloat16), score_grad)


def by_blocks(step_fn, running, pieces, block_rows):
    size_total = pieces[0].shape[0]
    part_rows = 4 * block_rows
    block_count = size_total // part_rows

    def turn_over(step_number, carried):
        sub_pieces = tuple(
            (
                lax.dynamic_slice_in_dim(member, step_number * part_rows, part_rows, 0)
                for member in pieces
            )
        )
        return step_fn(carried, sub_pieces, step_number * part_rows)

    return lax.fori_loop(0, block_count, turn_over, running)


def gathered_local(
    inputs,
    lengths,
    w_query,
    w_key,
    w_value,
    w_out,
    gain_attn,
    w_gate,
    w_up,
    w_down,
    gain_mlp,
    cotangent,
):
    residual = inputs[0].astype(jnp.float32)
    tokens_here = residual.shape[0]
    model_width = residual.shape[1]
    head_size = model_width // HEADS
    score_scale = head_size ** (-0.5)
    block_total = lax.axis_size("seq")
    lengths_row = lengths[0]
    places = lax.axis_index("seq") * tokens_here + jnp.arange(tokens_here, dtype=jnp.int32)
    own_meta = layout(lengths_row, places, tokens_here, block_total)

    def meta_at(start_row, row_count):
        return layout(
            lengths_row,
            start_row + jnp.arange(row_count, dtype=jnp.int32),
            tokens_here,
            block_total,
        )

    def heads_of(matrix):
        return matrix.reshape(matrix.shape[0], HEADS, head_size)

    query_full, key_full, value_full, out_full, gain_one = (
        lax.all_gather(w_query, ("row", "seq"), axis=0, tiled=True),
        lax.all_gather(w_key, ("row", "seq"), axis=0, tiled=True),
        lax.all_gather(w_value, ("row", "seq"), axis=0, tiled=True),
        lax.all_gather(w_out, ("row", "seq"), axis=0, tiled=True),
        lax.all_gather(gain_attn, ("row", "seq"), axis=0, tiled=True),
    )
    gain_one_f = gain_one.astype(jnp.float32)
    normed = rms_norm(residual, gain_one_f).astype(jnp.bfloat16)
    queries = jnp.dot(normed, query_full, preferred_element_type=jnp.float32).astype(jnp.bfloat16)
    key_rows = jnp.dot(normed, key_full, preferred_element_type=jnp.float32).astype(jnp.bfloat16)
    value_rows = jnp.dot(normed, value_full, preferred_element_type=jnp.float32).astype(
        jnp.bfloat16
    )
    query_heads = heads_of(queries)

    def forward_step(running, pieces, start_row):
        key_piece, value_piece = pieces
        sig_terms = sigmoid_terms(
            query_heads, own_meta, heads_of(key_piece), meta_at(start_row, key_piece.shape[0])
        ).astype(jnp.bfloat16)
        added = jnp.einsum(
            "hqk,khd->qhd", sig_terms, heads_of(value_piece), preferred_element_type=jnp.float32
        )
        return running + added.reshape(tokens_here, model_width)

    attended = by_blocks(
        forward_step,
        jnp.zeros((tokens_here, model_width), jnp.float32),
        (
            lax.all_gather(key_rows, "seq", axis=0, tiled=True),
            lax.all_gather(value_rows, "seq", axis=0, tiled=True),
        ),
        tokens_here,
    )
    attended_low = attended.astype(jnp.bfloat16)
    middle = residual + jnp.dot(attended_low, out_full, preferred_element_type=jnp.float32)
    gate_full, up_full, down_full, gain_two = (
        lax.all_gather(w_gate, ("row", "seq"), axis=0, tiled=True),
        lax.all_gather(w_up, ("row", "seq"), axis=0, tiled=True),
        lax.all_gather(w_down, ("row", "seq"), axis=0, tiled=True),
        lax.all_gather(gain_mlp, ("row", "seq"), axis=0, tiled=True),
    )
    gain_two_f = gain_two.astype(jnp.float32)
    normed_mlp = rms_norm(middle, gain_two_f).astype(jnp.bfloat16)
    gate_vals = jnp.dot(normed_mlp, gate_full, preferred_element_type=jnp.float32)
    up_vals = jnp.dot(normed_mlp, up_full, preferred_element_type=jnp.float32)
    gated_prod, gated_back = jax.vjp(
        lambda gate_in, up_in: jax.nn.silu(gate_in) * up_in, gate_vals, up_vals
    )
    hidden = gated_prod.astype(jnp.bfloat16)
    output = (middle + jnp.dot(hidden, down_full, preferred_element_type=jnp.float32)).astype(
        jnp.bfloat16
    )
    upstream_low = cotangent[0]
    upstream = upstream_low.astype(jnp.float32)
    gate_full, up_full, down_full, gain_two = (
        lax.all_gather(w_gate, ("row", "seq"), axis=0, tiled=True),
        lax.all_gather(w_up, ("row", "seq"), axis=0, tiled=True),
        lax.all_gather(w_down, ("row", "seq"), axis=0, tiled=True),
        lax.all_gather(gain_mlp, ("row", "seq"), axis=0, tiled=True),
    )
    gain_two_f = gain_two.astype(jnp.float32)
    grad_down = jnp.dot(hidden.T, upstream_low, preferred_element_type=jnp.float32)
    shared_down = lax.psum_scatter(grad_down, ("row", "seq"), scatter_dimension=0, tiled=True)
    hidden_grad = jnp.dot(upstream_low, down_full.T, preferred_element_type=jnp.float32)
    gate_grad, up_grad = gated_back(hidden_grad)
    gate_low = gate_grad.astype(jnp.bfloat16)
    up_low = up_grad.astype(jnp.bfloat16)
    grad_gate = jnp.dot(normed_mlp.T, gate_low, preferred_element_type=jnp.float32)
    shared_gate = lax.psum_scatter(grad_gate, ("row", "seq"), scatter_dimension=0, tiled=True)
    normed_grad = jnp.dot(gate_low, gate_full.T, preferred_element_type=jnp.float32) + jnp.dot(
        up_low, up_full.T, preferred_element_type=jnp.float32
    )
    unused_mid, second_back = jax.vjp(rms_norm, middle, gain_two_f)
    middle_part, gain_two_grad = second_back(normed_grad)
    middle_grad = upstream + middle_part
    grad_up = jnp.dot(normed_mlp.T, up_low, preferred_element_type=jnp.float32)
    shared_up, shared_gain_two = (
        lax.psum_scatter(grad_up, ("row", "seq"), scatter_dimension=0, tiled=True),
        lax.psum_scatter(gain_two_grad, ("row", "seq"), scatter_dimension=0, tiled=True),
    )
    query_full, key_full, value_full, out_full, gain_one = (
        lax.all_gather(w_query, ("row", "seq"), axis=0, tiled=True),
        lax.all_gather(w_key, ("row", "seq"), axis=0, tiled=True),
        lax.all_gather(w_value, ("row", "seq"), axis=0, tiled=True),
        lax.all_gather(w_out, ("row", "seq"), axis=0, tiled=True),
        lax.all_gather(gain_attn, ("row", "seq"), axis=0, tiled=True),
    )
    gain_one_f = gain_one.astype(jnp.float32)
    branch_low = middle_grad.astype(jnp.bfloat16)
    grad_out = jnp.dot(attended_low.T, branch_low, preferred_element_type=jnp.float32)
    attended_grad = jnp.dot(branch_low, out_full.T, preferred_element_type=jnp.float32).astype(
        jnp.bfloat16
    )
    grad_heads = heads_of(attended_grad)
    key_heads_own = heads_of(key_rows)
    value_heads_own = heads_of(value_rows)

    def query_step(running, pieces, start_row):
        key_piece, value_piece = pieces
        key_piece_heads = heads_of(key_piece)
        unused_terms, score_grad = pair_terms(
            query_heads,
            own_meta,
            grad_heads,
            key_piece_heads,
            meta_at(start_row, key_piece.shape[0]),
            heads_of(value_piece),
        )
        added = jnp.einsum(
            "hqk,khd->qhd", score_grad, key_piece_heads, preferred_element_type=jnp.float32
        )
        return running + added.reshape(tokens_here, model_width) * score_scale

    start_value = jnp.zeros((tokens_here, model_width), jnp.float32)
    folded = by_blocks(
        query_step,
        start_value,
        (
            lax.all_gather(key_rows, "seq", axis=0, tiled=True),
            lax.all_gather(value_rows, "seq", axis=0, tiled=True),
        ),
        tokens_here,
    )

    def key_step(running, pieces, start_row):
        key_sum, value_sum = running
        query_piece, grad_piece = pieces
        row_count = query_piece.shape[0]
        query_piece_heads = heads_of(query_piece)
        grad_piece_heads = heads_of(grad_piece)
        sig_low, score_grad = pair_terms(
            query_piece_heads,
            meta_at(start_row, row_count),
            grad_piece_heads,
            key_heads_own,
            own_meta,
            value_heads_own,
        )
        key_add = jnp.einsum(
            "hqk,qhd->khd", score_grad, query_piece_heads, preferred_element_type=jnp.float32
        )
        value_add = jnp.einsum(
            "hqk,qhd->khd", sig_low, grad_piece_heads, preferred_element_type=jnp.float32
        )
        return (
            key_sum + key_add.reshape(tokens_here, model_width) * score_scale,
            value_sum + value_add.reshape(tokens_here, model_width),
        )

    empty_rows = jnp.zeros((tokens_here, model_width), jnp.float32)
    key_grad, value_grad = by_blocks(
        key_step,
        (empty_rows, empty_rows),
        (
            lax.all_gather(queries, "seq", axis=0, tiled=True),
            lax.all_gather(attended_grad, "seq", axis=0, tiled=True),
        ),
        tokens_here,
    )
    query_low = folded.astype(jnp.bfloat16)
    key_low = key_grad.astype(jnp.bfloat16)
    value_low = value_grad.astype(jnp.bfloat16)
    grad_query = jnp.dot(normed.T, query_low, preferred_element_type=jnp.float32)
    grad_key = jnp.dot(normed.T, key_low, preferred_element_type=jnp.float32)
    grad_value = jnp.dot(normed.T, value_low, preferred_element_type=jnp.float32)
    normed_back = jnp.dot(query_low, query_full.T, preferred_element_type=jnp.float32)
    normed_back = normed_back + jnp.dot(key_low, key_full.T, preferred_element_type=jnp.float32)
    normed_back = normed_back + jnp.dot(value_low, value_full.T, preferred_element_type=jnp.float32)
    unused_first, first_back = jax.vjp(rms_norm, residual, gain_one_f)
    residual_part, gain_one_grad = first_back(normed_back)
    input_grad = middle_grad + residual_part
    shared_query, shared_key, shared_value, shared_out, shared_gain_one = (
        lax.psum_scatter(grad_query, ("row", "seq"), scatter_dimension=0, tiled=True),
        lax.psum_scatter(grad_key, ("row", "seq"), scatter_dimension=0, tiled=True),
        lax.psum_scatter(grad_value, ("row", "seq"), scatter_dimension=0, tiled=True),
        lax.psum_scatter(grad_out, ("row", "seq"), scatter_dimension=0, tiled=True),
        lax.psum_scatter(gain_one_grad, ("row", "seq"), scatter_dimension=0, tiled=True),
    )
    return (
        output[None],
        input_grad[None],
        shared_query,
        shared_key,
        shared_value,
        shared_out,
        shared_gain_one,
        shared_gate,
        shared_up,
        shared_down,
        shared_gain_two,
    )


MESH = pl.DeviceIdType.MESH
VMEM_BYTES = 62 * 1024 * 1024


class Place:
    def __init__(self, row_count, seq_count):
        self.row_count, self.seq_count = row_count, seq_count
        self.r, self.s = lax.axis_index("row"), lax.axis_index("seq")
        self.n_hi = seq_count // 2
        self.hi, self.lo = self.s // 2, lax.rem(self.s, 2)
        self.r_core = self.r + 1 - 2 * lax.rem(self.r, 2)
        self.r_y = lax.rem(self.r + 2, 4)
        self.r_far = lax.rem(self.r_core + 2, 4)
        self.side = (self.r, self.s + 1 - 2 * self.lo)
        self.up = (self.r, self.s + 2)
        self.down = (self.r, self.s - 2)
        self.core = (self.r_core, self.s)
        self.y = (self.r_y, self.s)
        self.has_up = self.hi < self.n_hi - 1
        self.has_down = self.hi > 0

    def peer(self, step):
        return lax.rem(self.s + step, self.seq_count)

    def chain(self):
        return [(None, self.side), (self.has_up, self.up), (self.has_down, self.down)]

    def peers(self):
        return [(None, (self.r, self.peer(step))) for step in range(1, self.seq_count)]

    def rows(self):
        return [(None, self.core), (None, self.y)]


def greet(devices):
    barrier = pltpu.get_barrier_semaphore()
    total = 0
    for condition, device in devices:
        if condition is None:
            pl.semaphore_signal(barrier, inc=1, device_id=device, device_id_type=MESH)
            total = total + 1
        else:

            @pl.when(condition)
            def _(device=device):
                pl.semaphore_signal(barrier, inc=1, device_id=device, device_id_type=MESH)

            total = total + condition.astype(jnp.int32)
    pl.semaphore_wait(barrier, total)


class Sems:
    def __init__(self, ref):
        self.ref, self.used = ref, 0

    def take(self, count):
        base = self.used
        self.used += count
        assert self.used <= self.ref.shape[0], self.used
        return lambda index: self.ref.at[base + index]


def push(source, target, send, recv, device):
    pltpu.make_async_remote_copy(
        src_ref=source, dst_ref=target, send_sem=send, recv_sem=recv, device_id=device, device_id_type=MESH
    ).start()


def settle(ref, sem):
    pltpu.make_async_copy(ref, ref, sem).wait()


def no_op(block):
    return None


class Stores:
    def __init__(self, sems):
        self.sems, self.open = sems, []

    def start(self, source, target):
        sem = self.sems.take(1)(0)
        pltpu.make_async_copy(source, target, sem).start()
        self.open.append((target, sem))

    def finish(self):
        for target, sem in self.open:
            settle(target, sem)


class SeqGather:
    def __init__(self, place, sems, source, at, arrived=no_op, arrived_aside=None):
        self.p, self.source, self.at, self.arrived = place, source, at, arrived
        self.arrived_aside = arrived_aside or arrived
        self.own_done = False
        n = place.n_hi
        self.own, self.up, self.down = sems.take(1), sems.take(n), sems.take(n)
        self.side, self.recv = sems.take(n), sems.take(2 * n)

    def start(self):
        p, s = self.p, self.p.s
        pltpu.make_async_copy(self.source, self.at(s), self.own(0)).start()

        @pl.when(p.has_up)
        def _():
            push(self.source, self.at(s), self.up(0), self.recv(s), p.up)

        @pl.when(p.has_down)
        def _():
            push(self.source, self.at(s), self.down(0), self.recv(s), p.down)

        push(self.source, self.at(s), self.side(p.hi), self.recv(s), p.side)

    def step(self, k):
        p = self.p

        @pl.when(p.hi >= k)
        def _():
            block = p.s - 2 * k
            settle(self.at(block), self.recv(block))

            @pl.when(p.has_up)
            def _():
                push(self.at(block), self.at(block), self.up(k), self.recv(block), p.up)

            push(self.at(block), self.at(block), self.side(p.hi - k), self.recv(block), p.side)
            self.arrived(block)

        @pl.when(p.hi + k < p.n_hi)
        def _():
            block = p.s + 2 * k
            settle(self.at(block), self.recv(block))

            @pl.when(p.has_down)
            def _():
                push(self.at(block), self.at(block), self.down(k), self.recv(block), p.down)

            push(self.at(block), self.at(block), self.side(p.hi + k), self.recv(block), p.side)
            self.arrived(block)

    def aside(self, k):
        p = self.p
        if k == 0:
            block = 2 * p.hi + 1 - p.lo
            settle(self.at(block), self.recv(block))
            self.arrived_aside(block)
            return

        @pl.when(p.hi >= k)
        def _():
            block = 2 * (p.hi - k) + 1 - p.lo
            settle(self.at(block), self.recv(block))
            self.arrived_aside(block)

        @pl.when(p.hi + k < p.n_hi)
        def _():
            block = 2 * (p.hi + k) + 1 - p.lo
            settle(self.at(block), self.recv(block))
            self.arrived_aside(block)

    def settle_own(self):
        settle(self.at(self.p.s), self.own(0))
        self.own_done = True

    def finish(self):
        p = self.p
        if not self.own_done:
            self.settle_own()
        for k in range(p.n_hi):

            @pl.when(p.has_up & (p.hi >= k))
            def _():
                settle(self.source, self.up(k))

            @pl.when(p.has_down & (p.hi + k < p.n_hi))
            def _():
                settle(self.source, self.down(k))

            settle(self.source, self.side(k))


class SeqExchange:
    def __init__(self, place, sems, piece, at, arrived=no_op):
        self.p, self.piece, self.at, self.arrived = place, piece, at, arrived
        self.own_done = False
        n = place.seq_count
        self.own, self.send, self.recv = sems.take(1), sems.take(n), sems.take(n)

    def start_own(self):
        s = self.p.s
        pltpu.make_async_copy(self.piece(s), self.at(s), self.own(0)).start()

    def start(self):
        p, s = self.p, self.p.s
        self.start_own()
        for step in range(1, p.seq_count):
            t = p.peer(step)
            push(self.piece(t), self.at(s), self.send(step), self.recv(s), (p.r, t))

    def step(self, step):
        block = self.p.peer(self.p.seq_count - step)
        settle(self.at(block), self.recv(block))
        self.arrived(block)

    def finish(self):
        p = self.p
        settle(self.at(p.s), self.own(0))
        for step in range(1, p.seq_count):
            settle(self.at(p.s), self.send(step))


class PartExchange(SeqExchange):
    def __init__(self, place, sems, parts, at, arrived=no_op):
        super().__init__(place, sems, None, at, arrived)
        self.parts = parts

    def start_own(self):
        s = self.p.s
        for source, target in self.parts(s):
            pltpu.make_async_copy(source, target, self.own(0)).start()

    def start(self):
        p, s = self.p, self.p.s
        self.start_own()
        for step in range(1, p.seq_count):
            t = p.peer(step)
            for source, target in self.parts(t):
                push(source, target, self.send(step), self.recv(s), (p.r, t))

    def settle_own(self):
        settle(self.at(self.p.s), self.own(0))
        self.own_done = True

    def finish(self):
        p = self.p
        if not self.own_done:
            self.settle_own()
        for step in range(1, p.seq_count):
            settle(self.at(p.s), self.send(step))


class RowForward:
    def __init__(self, place, sems, blocks, at):
        self.p, self.at, self.blocks = place, at, blocks
        self.core, self.y, self.far = sems.take(blocks), sems.take(blocks), sems.take(blocks)
        self.from_core, self.from_y, self.from_far = sems.take(blocks), sems.take(blocks), sems.take(blocks)

    def forward(self, block, source=None):
        p = self.p
        source = self.at(p.r, block) if source is None else source
        push(source, self.at(p.r, block), self.y(block), self.from_y(block), p.y)
        push(source, self.at(p.r, block), self.core(block), self.from_core(block), p.core)

    def relay(self, block):
        p = self.p
        settle(self.at(p.r_y, block), self.from_y(block))
        push(self.at(p.r_y, block), self.at(p.r_y, block), self.far(block), self.from_far(block), p.core)

    def finish(self):
        p = self.p
        for block in range(self.blocks):
            settle(self.at(p.r_core, block), self.from_core(block))
            settle(self.at(p.r_far, block), self.from_far(block))
            settle(self.at(p.r, block), self.core(block))
            settle(self.at(p.r, block), self.y(block))
            settle(self.at(p.r_y, block), self.far(block))


def add_into(target, *sources):
    @pl.loop(0, target.shape[0] // 16)
    def _(tile):
        rows = pl.ds(pl.multiple_of(tile * 16, 16), 16)
        total = sources[0][rows, :].astype(jnp.float32)
        for source in sources[1:]:
            total = total + source[rows, :].astype(jnp.float32)
        target[rows, :] = total.astype(target.dtype)


def add_small(target, *sources):
    total = sources[0][...].astype(jnp.float32)
    for source in sources[1:]:
        total = total + source[...].astype(jnp.float32)
    target[...] = total.astype(target.dtype)


class SeqReduce:
    def __init__(self, place, sems, at, side_slot, chain_slot, target, add=add_into):
        self.p, self.at, self.add, self.target = place, at, add, target
        self.side_slot, self.chain_slot = side_slot, chain_slot
        n = place.n_hi
        self.side, self.from_side = sems.take(n), sems.take(n)
        self.send, self.recv = sems.take(n), sems.take(2 * n)

    def above_slot(self, block, hi):
        return self.chain_slot(jnp.where(block == hi, self.p.n_hi, block))

    def turn(self, t):
        p = self.p
        n, hi = p.n_hi, p.hi
        low = jnp.where(t < n - 1 - hi, n - 1 - t, t - (n - 1 - hi))
        high = jnp.where(t < hi, t, n - 1 - (t - hi))
        return jnp.where(hi < n // 2, low, high)

    def start(self, t):
        p, block = self.p, self.turn(t)
        push(self.at(2 * block + 1 - p.lo), self.side_slot(block), self.side(block), self.from_side(block), p.side)

    def step(self, t):
        p, n, block = self.p, self.p.n_hi, self.turn(t)
        mine, got = self.at(2 * block + p.lo), self.side_slot(block)
        settle(got, self.from_side(block))
        if t == n - 1:
            return self.close()

        @pl.when(block > p.hi)
        def _():
            @pl.when(p.has_down)
            def _():
                settle(got, self.recv(block))
                self.add(got, mine, got, self.chain_slot(block))

            @pl.when(jnp.logical_not(p.has_down))
            def _():
                self.add(got, mine, got)

            push(got, self.chain_slot(block), self.send(block), self.recv(block), p.up)

        @pl.when(block < p.hi)
        def _():
            @pl.when(p.has_up)
            def _():
                settle(got, self.recv(n + block))
                self.add(got, mine, got, self.above_slot(block, p.hi))

            @pl.when(jnp.logical_not(p.has_up))
            def _():
                self.add(got, mine, got)

            push(got, self.above_slot(block, p.hi - 1), self.send(block), self.recv(n + block), p.down)

    def close(self):
        p, n, hi = self.p, self.p.n_hi, self.p.hi
        mine, got = self.at(p.s), self.side_slot(hi)
        below, above = self.chain_slot(hi), self.above_slot(hi, hi)

        @pl.when(p.has_down)
        def _():
            settle(got, self.recv(hi))

        @pl.when(p.has_up)
        def _():
            settle(got, self.recv(n + hi))

        @pl.when(p.has_down & p.has_up)
        def _():
            self.add(self.target, mine, got, below, above)

        @pl.when(p.has_down & jnp.logical_not(p.has_up))
        def _():
            self.add(self.target, mine, got, below)

        @pl.when(jnp.logical_not(p.has_down))
        def _():
            self.add(self.target, mine, got, above)

    def finish(self):
        p = self.p
        for block in range(p.n_hi):
            settle(self.side_slot(block), self.side(block))

            @pl.when(p.hi != block)
            def _():
                settle(self.side_slot(block), self.send(block))


class RowReduce:
    def __init__(self, place, sems, blocks, at, core_slot, y_slot, target, add=add_into, own=None):
        self.p, self.at, self.add, self.target = place, at, add, target
        self.own = own or (lambda w, b: at((place.r_y, place.r)[w], b))
        self.core_slot, self.y_slot, self.blocks = core_slot, y_slot, blocks
        self.send, self.recv = sems.take(2 * blocks), sems.take(2 * blocks)
        self.y, self.from_y = sems.take(blocks), sems.take(blocks)

    def start_far(self, block):
        p = self.p
        push(self.at(p.r_far, block), self.core_slot(0, block), self.send(block), self.recv(block), p.core)

    def start_core(self, block):
        p, n = self.p, self.blocks
        push(self.at(p.r_core, block), self.core_slot(1, block), self.send(n + block), self.recv(n + block), p.core)

    def start(self, block):
        self.start_far(block)
        self.start_core(block)

    def step(self, block):
        p = self.p
        got = self.core_slot(0, block)
        settle(got, self.recv(block))
        self.add(got, self.own(0, block), got)
        push(got, self.y_slot(block), self.y(block), self.from_y(block), p.y)

    def close(self, block):
        p = self.p
        settle(self.core_slot(1, block), self.recv(self.blocks + block))
        settle(self.y_slot(block), self.from_y(block))
        self.add(self.target(block), self.own(1, block), self.core_slot(1, block), self.y_slot(block))

    def finish(self):
        n = self.blocks
        for block in range(n):
            settle(self.core_slot(0, block), self.send(block))
            settle(self.core_slot(1, block), self.send(n + block))
            settle(self.core_slot(0, block), self.y(block))


def columns(ref, index, width):
    return ref.at[:, pl.ds(pl.multiple_of(index * width, width), width)]


def call(kernel, shapes, ident, args, spaces, out_spaces, scratch, sems):
    return pl.pallas_call(
        kernel,
        out_shape=shapes,
        in_specs=[pl.BlockSpec(memory_space=space) for space in spaces],
        out_specs=jax.tree.map(lambda space: pl.BlockSpec(memory_space=space), out_spaces),
        scratch_shapes=list(scratch) + [pltpu.SemaphoreType.DMA((sems,))],
        compiler_params=pltpu.CompilerParams(
            collective_id=ident, has_side_effects=True, vmem_limit_bytes=VMEM_BYTES
        ),
    )(*args)


def shape_of(dims, dtype=jnp.bfloat16):
    return jax.ShapeDtypeStruct(dims, dtype)


def nt(left, right):
    return lax.dot_general(left, right, (((1,), (1,)), ((), ())), preferred_element_type=jnp.float32)


def tn(left, right):
    return lax.dot_general(left, right, (((0,), (0,)), ((), ())), preferred_element_type=jnp.float32)


def nn(left, right):
    return lax.dot_general(left, right, (((1,), (0,)), ((), ())), preferred_element_type=jnp.float32)


def rows_at(index, count):
    return pl.ds(pl.multiple_of(index * count, count), count)


def norm_rows(source, target, gain):
    @pl.loop(0, source.shape[0] // 16)
    def _(tile):
        rows = rows_at(tile, 16)
        values = source[rows, :].astype(jnp.float32)
        target[rows, :] = rms_norm(values, gain[...]).astype(target.dtype)


def places(lengths, shape, axis, tokens, seqs):
    row_tokens = tokens * seqs
    index = lax.broadcasted_iota(jnp.int32, shape, axis)
    block, within = index // tokens, lax.rem(index, tokens)
    segment = position = length_of = jnp.zeros_like(index)
    begin = 0
    for n in range(lengths.shape[1]):
        length = lengths[0, n]
        unit = length // (2 * seqs)
        inside = (within >= begin) & (within < begin + 2 * unit)
        local = within - begin
        here = jnp.where(local < unit, block * unit + local, (2 * seqs - 1 - block) * unit + local - unit)
        segment = jnp.where(inside, n, segment)
        position = jnp.where(inside, here, position)
        length_of = jnp.where(inside, length, length_of)
        begin = begin + 2 * unit
    return segment * row_tokens, segment * row_tokens + position, length_of


def fill_meta(lengths, key_place, query_low, query_high, shift, tokens, seqs):
    key_place[...] = places(lengths, key_place.shape, 0, tokens, seqs)[1]
    low, high, length_of = places(lengths, query_low.shape, 1, tokens, seqs)
    query_low[...] = low
    query_high[...] = high
    shift[...] = jnp.log(length_of.astype(jnp.float32))


def meta_scratch(row_tokens):
    return [
        pltpu.VMEM((row_tokens, 1), jnp.int32),
        pltpu.VMEM((1, row_tokens), jnp.int32),
        pltpu.VMEM((1, row_tokens), jnp.int32),
        pltpu.VMEM((1, row_tokens), jnp.float32),
    ]


def attention(qkv, attended, key_place, query_low, query_high, shift, turned, head, head_size):
    tokens, own_width = attended.shape
    scale = head_size ** (-0.5)
    keys_step = 256
    lanes = pl.ds(head * head_size, head_size)
    key_lanes = pl.ds(own_width + head * head_size, head_size)
    value_lanes = pl.ds(2 * own_width + head * head_size, head_size)
    turned[...] = jnp.zeros_like(turned)

    @pl.loop(0, tokens // keys_step)
    def _(step):
        rows = rows_at(step, keys_step)
        places = key_place[rows, :]
        allowed = (places >= query_low[...]) & (places <= query_high[...])
        scores = nt(qkv[rows, key_lanes], qkv[:, lanes]) * scale - shift[...]
        sig = jnp.where(allowed, jax.nn.sigmoid(scores), 0.0).astype(jnp.bfloat16)
        turned[...] += nn(qkv[rows, value_lanes].T, sig)

    attended[:, lanes] = turned[...].T.astype(jnp.bfloat16)


def forward_kernel(
    rows,
    seqs,
    head_size,
    x,
    g,
    wquery,
    wkey,
    wvalue,
    wgate,
    wup,
    wdown,
    wout,
    gains,
    lengths,
    gs,
    vgu,
    vdown,
    vout,
    h2,
    vqkv_kept,
    hn_kept,
    qkv_kept,
    attended_kept,
    middle_kept,
    gain_rows_out,
    vqkv,
    hn,
    qkv,
    attended,
    middle,
    xs,
    vgains,
    heads,
    turned,
    out_held,
    h2_own,
    key_place,
    query_low,
    query_high,
    shift,
    copies,
    sems,
):
    p, pool = Place(rows, seqs), Sems(sems)
    greet(p.peers() + p.rows())
    tokens, width = x.shape
    half = tokens // 2
    own_width = heads.shape[1]
    deep = wout.shape[0]
    down_blocks = vdown.shape[1]

    def part(source, target, c, arrived_aside=None):
        piece = pl.ds(c * half, half)
        return SeqGather(p, pool, source.at[piece], lambda b: target.at[b, piece], no_op, arrived_aside)

    def norm_half(c):
        def run(block):
            for b in (block, block + 1 - 2 * lax.rem(block, 2)):
                start = pl.multiple_of(b * tokens + c * half, half)
                norm_rows(xs.at[b, pl.ds(c * half, half)], hn.at[pl.ds(start, half), :], gain_rows_out.at[0:1, :])

        return run

    qkv_rows = RowForward(p, pool, seqs, lambda r, b: vqkv.at[r, b])
    gu_rows = RowForward(p, pool, seqs, lambda r, b: vgu.at[r, b])
    down_fwd = RowForward(p, pool, down_blocks, lambda r, b: vdown.at[r, b])
    out_rows = RowForward(p, pool, seqs, lambda r, b: vout.at[r, b])
    gain_rows = RowForward(p, pool, 1, lambda r, b: vgains.at[r])
    x_parts = [part(x, xs, c, norm_half(c)) for c in range(2)]
    g_parts = [part(g, gs, c) for c in range(2)]
    h2_parts = [part(h2_own, h2, c) for c in range(2)]
    hidden_own = vgu.shape[3] // 2
    hidden_block = hidden_own // rows

    def qkv_parts(t):
        for n, source in enumerate((wquery, wkey, wvalue)):
            target = vqkv.at[p.r, p.s, :, pl.ds(n * own_width, own_width)]
            yield columns(source, t, own_width), target

    def gu_parts(t):
        for n, source in enumerate((wgate, wup)):
            for r in range(rows):
                target = vgu.at[p.r, p.s, :, pl.ds(n * hidden_own + r * hidden_block, hidden_block)]
                yield columns(source, r * seqs + t, hidden_block), target

    qkv_swap = PartExchange(p, pool, qkv_parts, lambda b: vqkv.at[p.r, b], qkv_rows.forward)
    gu_swap = PartExchange(p, pool, gu_parts, lambda b: vgu.at[p.r, b], gu_rows.forward)
    out = SeqGather(p, pool, wout, lambda b: vout.at[p.r, b], out_rows.forward)
    gain = SeqExchange(p, pool, lambda t: gains, lambda b: vgains.at[p.r, b])
    heads_swap = SeqExchange(
        p, pool, lambda t: heads.at[rows_at(t, tokens), :], lambda b: columns(attended, b, own_width)
    )
    stores = Stores(pool)

    gain.start()
    for member in x_parts:
        member.start()
    qkv_swap.start()
    out.start()
    for step in range(1, seqs):
        gain.step(step)
    gain.finish()
    gain_rows.forward(0)
    qkv_swap.settle_own()
    qkv_rows.forward(p.s)
    out_rows.forward(p.s, wout)
    stores.start(wdown, vdown.at[p.r])
    for block in range(down_blocks):
        down_fwd.forward(block, wdown.at[block])
    gain_rows.relay(0)
    gain_rows.finish()
    for pair in range(rows * seqs // 2):
        tile = vgains[2 * pair // seqs, 2 * pair % seqs] + vgains[2 * pair // seqs, 2 * pair % seqs + 1]
        gain_rows_out[:, pl.ds(pair * 2 * deep, 2 * deep)] = tile

    fill_meta(lengths, key_place, query_low, query_high, shift, tokens, seqs)
    for member in x_parts:
        member.settle_own()
    for k in range(1, p.n_hi):
        for member in x_parts:
            member.step(k)
    for step in range(1, seqs):
        qkv_swap.step(step)
    for k in range(1, p.n_hi):
        out.step(k)
    gu_swap.start()
    gu_swap.settle_own()
    gu_rows.forward(p.s)
    for k in range(p.n_hi):
        for member in x_parts:
            member.aside(k)
    for member in g_parts:
        member.start()
    for block in range(seqs):
        qkv_rows.relay(block)
    for k in range(p.n_hi):
        out.aside(k)
    qkv_swap.finish()
    qkv_rows.finish()
    stores.start(hn, hn_kept)
    stores.start(vqkv, vqkv_kept)

    weights = vqkv.reshape(width, 3 * own_width)

    @pl.loop(0, seqs // 2)
    def _(step):
        tall = rows_at(step, 2 * tokens)
        qkv[tall, :] = nn(hn[tall, :], weights[...]).astype(jnp.bfloat16)

    stores.start(qkv, qkv_kept)
    own_heads = own_width // head_size
    for head in range(own_heads):
        attention(qkv, heads, key_place, query_low, query_high, shift, turned, head, head_size)
    heads_swap.start()
    for block in range(seqs):
        out_rows.relay(block)
    for member in g_parts:
        member.step(1)
    out.finish()
    out_rows.finish()
    for r in range(rows):
        pltpu.make_async_copy(vout.at[r], out_held.at[r], copies.at[r]).start()
    for step in range(1, seqs):
        heads_swap.step(step)
    heads_swap.finish()
    for r in range(rows):
        settle(out_held.at[r], copies.at[r])
    out_weights = out_held.reshape(width, width)

    @pl.loop(0, width // 512)
    def _(c):
        lanes = rows_at(c, 512)
        middle[:, lanes] = xs[p.s, :, lanes].astype(jnp.float32) + nn(attended[...], out_weights[:, lanes])

    norm_rows(middle, h2_own, gain_rows_out.at[4:5, :])
    stores.start(attended, attended_kept)
    stores.start(middle, middle_kept)
    for member in h2_parts:
        member.start()
    for step in range(1, seqs):
        gu_swap.step(step)
    for k in range(2, p.n_hi):
        for member in g_parts:
            member.step(k)
        for member in h2_parts:
            member.step(k - 1)
    for member in h2_parts:
        member.step(p.n_hi - 1)
    for block in range(down_blocks):
        down_fwd.relay(block)
    for block in range(seqs):
        gu_rows.relay(block)
    for k in range(p.n_hi):
        for member in g_parts + h2_parts:
            member.aside(k)
    for member in x_parts + g_parts + h2_parts + [gu_swap, down_fwd, gu_rows]:
        member.finish()
    stores.finish()


def forward(rows, seqs, head_size, x, g, qkv_weights, gu_weights, wdown, wout, gains, lengths):
    low, f32 = jnp.bfloat16, jnp.float32
    tokens, width = x.shape
    wdown = wdown.reshape(4, wdown.shape[0] // 4, width)
    own_width = width // seqs
    row_tokens = tokens * seqs
    deep = wout.shape[0]
    hidden_own = gu_weights[0].shape[1] // seqs
    shapes = (
        shape_of((seqs, tokens, width)),
        shape_of((rows, seqs, deep, 2 * hidden_own)),
        shape_of((rows,) + wdown.shape),
        shape_of((rows, seqs) + wout.shape),
        shape_of((seqs, tokens, width)),
        shape_of((rows, seqs, deep, 3 * own_width)),
        shape_of((row_tokens, width)),
        shape_of((row_tokens, 3 * own_width)),
        shape_of((tokens, width)),
        shape_of((tokens, width), f32),
        shape_of((8, width), f32),
    )
    scratch = [pltpu.VMEM(member.shape, member.dtype) for member in shapes[5:10]] + [
        pltpu.VMEM((seqs, tokens, width), low),
        pltpu.VMEM((rows, seqs) + gains.shape, f32),
        pltpu.VMEM((row_tokens, own_width), low),
        pltpu.VMEM((head_size, row_tokens), f32),
        pltpu.VMEM((rows, seqs) + wout.shape, low),
        pltpu.VMEM((tokens, width), low),
        *meta_scratch(row_tokens),
        pltpu.SemaphoreType.DMA((rows,)),
    ]
    return call(
        functools.partial(forward_kernel, rows, seqs, head_size),
        shapes,
        1,
        (x, g) + qkv_weights + gu_weights + (wdown, wout, gains, lengths),
        [pltpu.VMEM] * 10 + [pltpu.SMEM],
        (pl.ANY,) * 10 + (pltpu.VMEM,),
        scratch,
        800,
    )


def seq_reducers(place, pool, source, side, chain, target):
    half = target.shape[0] // 2
    members = []
    for c in range(2):
        piece = pl.ds(c * half, half)
        members.append(
            SeqReduce(
                place,
                pool,
                lambda b, piece=piece: source.at[b, piece],
                lambda b, piece=piece: side.at[b, piece],
                lambda slot, piece=piece: chain.at[slot, piece],
                target.at[piece],
            )
        )
    return members


def row_reducer(place, pool, source, core_slots, y_slots, target, add=add_into):
    return RowReduce(
        place,
        pool,
        source.shape[1],
        lambda r, b: source.at[r, b],
        lambda w, b: core_slots.at[w, b],
        lambda b: y_slots.at[b],
        lambda b: target.at[b],
        add,
    )


def ffn_kernel(
    rows,
    seqs,
    h2_in,
    gu_in,
    down_in,
    g_in,
    h2_kept,
    out_kept,
    gu_kept,
    down_kept,
    h2_sum,
    out_sum,
    gu_sum,
    down_sum,
    h2,
    gu_weights,
    down_weights,
    g,
    hidden,
    gu_grad,
    h2_part,
    h2_side,
    h2_chain,
    out_part,
    out_side,
    out_chain,
    gu_core,
    down_core,
    loads,
    sems,
):
    p, pool = Place(rows, seqs), Sems(sems)
    pairs = ((h2_in, h2), (gu_in, gu_weights), (g_in, g), (down_in, down_weights))
    for number, (source, target) in enumerate(pairs):
        pltpu.make_async_copy(source, target, loads.at[number]).start()
    greet(p.chain() + p.rows())
    tokens, width = h2_sum.shape
    hidden_own = hidden.shape[1]
    low = jnp.bfloat16
    h2_parts = seq_reducers(p, pool, h2_part, h2_side, h2_chain, h2_sum)
    out_parts = seq_reducers(p, pool, out_part, out_side, out_chain, out_sum)
    deep, down_deep = gu_sum.shape[1], down_sum.shape[1]

    def gu_at(r, b):
        return gu_weights.at[pl.ds(pl.multiple_of((r * seqs + b) * deep, deep), deep), :]

    def down_at(r, b):
        return down_weights.at[pl.ds(pl.multiple_of((r * down_sum.shape[0] + b) * down_deep, down_deep), down_deep), :]

    gu_rows = RowReduce(
        p, pool, seqs, gu_at, lambda w, b: gu_core.at[w, b], lambda b: gu_sum.at[b], lambda b: gu_sum.at[b]
    )
    down_rows = RowReduce(
        p,
        pool,
        down_sum.shape[0],
        down_at,
        lambda w, b: down_core.at[w, b],
        lambda b: down_sum.at[b],
        lambda b: down_sum.at[b],
    )
    for number, (source, target) in enumerate(pairs):
        settle(target, loads.at[number])

    def products(t):
        tall = rows_at(h2_parts[0].turn(t), 2 * tokens)

        @pl.loop(0, hidden_own // 256)
        def _(c):
            lanes, up_lanes = rows_at(c, 256), pl.ds(pl.multiple_of(hidden_own + c * 256, 256), 256)
            gate, up = nn(h2[tall, :], gu_weights[:, lanes]), nn(h2[tall, :], gu_weights[:, up_lanes])
            grad = nt(g[tall, :], down_weights[lanes, :])
            sig = jax.nn.sigmoid(gate)
            silu = gate * sig
            hidden[tall, lanes] = (silu * up).astype(low)
            gu_grad[tall, lanes] = (grad * up * (sig + silu * (1.0 - sig))).astype(low)
            gu_grad[tall, up_lanes] = (grad * silu).astype(low)

    def send_out(t):
        pair = h2_parts[0].turn(t)
        tall = rows_at(pair, 2 * tokens)

        @pl.loop(0, width // 512)
        def _(c):
            lanes = rows_at(c, 512)
            part = nn(hidden[tall, :], down_weights[:, lanes]).astype(low)
            out_part[2 * pair, :, lanes] = part[:tokens]
            out_part[2 * pair + 1, :, lanes] = part[tokens:]

        for member in out_parts:
            member.start(t)

    def send_h2(t):
        pair = h2_parts[0].turn(t)
        tall = rows_at(pair, 2 * tokens)

        @pl.loop(0, width // 512)
        def _(c):
            lanes = rows_at(c, 512)
            part = nt(gu_grad[tall, :], gu_weights[lanes, :]).astype(low)
            h2_part[2 * pair, :, lanes] = part[:tokens]
            h2_part[2 * pair + 1, :, lanes] = part[tokens:]

        for member in h2_parts:
            member.start(t)

    def sums(t, parts=None):
        for member in out_parts + h2_parts if parts is None else parts:
            member.step(t)

    def down_quarter(r):
        lanes = rows_at(r, hidden_own // rows)
        down_weights[lanes, :] = tn(hidden[:, lanes], g[...]).astype(low)

    def gu_quarter(r):
        @pl.loop(0, 2)
        def _(c):
            lanes = rows_at(2 * r + c, width // (2 * rows))
            gu_weights[lanes, :] = tn(h2[:, lanes], gu_grad[...]).astype(low)

    down_blocks, gu_blocks = range(down_sum.shape[0]), range(seqs)
    early = p.n_hi // 2
    for t in range(p.n_hi):
        products(t)
        send_out(t)
        if t < early:
            send_h2(t)
    sums(0, out_parts)
    down_quarter(p.r_far)
    for b in down_blocks:
        down_rows.start_far(b)
    down_quarter(p.r_core)
    for b in down_blocks:
        down_rows.start_core(b)
    down_quarter(p.r_y)
    for b in down_blocks:
        down_rows.step(b)
    for t in range(early, p.n_hi):
        send_h2(t)
    sums(0, h2_parts)
    gu_quarter(p.r_far)
    for b in gu_blocks:
        gu_rows.start_far(b)
    gu_quarter(p.r_y)
    for b in gu_blocks:
        gu_rows.step(b)
    gu_quarter(p.r_core)
    for b in gu_blocks:
        gu_rows.start_core(b)
    if p.n_hi > 2:
        sums(1)
    down_quarter(p.r)
    gu_quarter(p.r)
    for t in range(2 if p.n_hi > 2 else 1, p.n_hi):
        sums(t)
    stores = Stores(pool)
    stores.start(out_sum, out_kept)
    stores.start(h2_sum, h2_kept)
    for b in down_blocks:
        down_rows.close(b)
        stores.start(down_sum.at[b], down_kept.at[b])
    for b in gu_blocks:
        gu_rows.close(b)
        stores.start(gu_sum.at[b], gu_kept.at[b])
    for member in h2_parts + out_parts + [gu_rows, down_rows, stores]:
        member.finish()


def slots(array, copies=()):
    return pltpu.VMEM(copies + array.shape[1:], array.dtype)


def seq_slots(array):
    half = array.shape[0] // 2
    return [
        pltpu.VMEM((half,) + array.shape[1:], array.dtype),
        pltpu.VMEM((half + 1,) + array.shape[1:], array.dtype),
    ]


def row_slots(array):
    return [slots(array, (2,)), slots(array)]


def row_blocks(rows, array, count):
    return array.reshape(rows, count, array.shape[0] // (rows * count), array.shape[1])


def ffn(rows, seqs, h2, wgu, wdown, g):
    low, f32 = jnp.bfloat16, jnp.float32
    row_tokens, width = h2.shape
    tokens, hidden_own = row_tokens // seqs, wdown.shape[0]
    gu_dims, down_dims = (seqs, width // (rows * seqs), 2 * hidden_own), (4, hidden_own // (4 * rows), width)
    part = shape_of((seqs, tokens, width))
    shapes = (shape_of((tokens, width), f32), shape_of((tokens, width), f32), shape_of(gu_dims), shape_of(down_dims))
    scratch = (
        [pltpu.VMEM(member.shape, member.dtype) for member in shapes]
        + [pltpu.VMEM(array.shape, low) for array in (h2, wgu, wdown, g)]
        + [pltpu.VMEM((row_tokens, hidden_own), low), pltpu.VMEM((row_tokens, 2 * hidden_own), low)]
        + [pltpu.VMEM(part.shape, low)]
        + seq_slots(part)
        + [pltpu.VMEM(part.shape, low)]
        + seq_slots(part)
        + [pltpu.VMEM((2,) + gu_dims, low), pltpu.VMEM((2,) + down_dims, low)]
        + [pltpu.SemaphoreType.DMA((4,))]
    )
    return call(
        functools.partial(ffn_kernel, rows, seqs),
        shapes,
        4,
        (h2, wgu, wdown, g),
        [pl.ANY] * 4,
        (pl.ANY,) * 4,
        scratch,
        320,
    )


class ColumnExchange:
    def __init__(self, place, sems, piece, parts):
        self.p, self.piece, self.parts = place, piece, parts
        n = place.seq_count
        self.own, self.send, self.recv = sems.take(1), sems.take(n), sems.take(n)

    def start(self, first=0, last=None):
        p, s = self.p, self.p.s
        for step in range(first, p.seq_count if last is None else last):
            t = p.peer(step)
            piece = self.piece(t)
            for offset, width, target in self.parts(s):
                source = piece.at[:, pl.ds(offset, width)]
                if step == 0:
                    pltpu.make_async_copy(source, target, self.own(0)).start()
                else:
                    push(source, target, self.send(step), self.recv(s), (p.r, t))

    def finish(self):
        p = self.p
        settle(self.piece(p.s), self.own(0))
        for step in range(1, p.seq_count):
            settle(self.piece(p.s), self.send(step))
            settle(self.piece(p.s), self.recv(p.peer(step)))


def attention_back(qkv, do, dqkv, key_place, query_low, query_high, shift, dq_turned, head_size):
    tokens, own_width = do.shape
    scale = head_size ** (-0.5)
    keys_step = 256
    for head in range(own_width // head_size):
        lanes = pl.ds(head * head_size, head_size)
        key_lanes = pl.ds(own_width + head * head_size, head_size)
        value_lanes = pl.ds(2 * own_width + head * head_size, head_size)
        dq_turned[...] = jnp.zeros_like(dq_turned)

        @pl.loop(0, tokens // keys_step)
        def _(step):
            rows = pl.ds(pl.multiple_of(step * keys_step, keys_step), keys_step)
            key, value = qkv[rows, key_lanes], qkv[rows, value_lanes]
            queries, grads = qkv[:, lanes], do[:, lanes]
            places = key_place[rows, :]
            allowed = (places >= query_low[...]) & (places <= query_high[...])
            scores = nt(key, queries) * scale - shift[...]
            sig = jnp.where(allowed, jax.nn.sigmoid(scores), 0.0)
            score_grad = (nt(value, grads) * sig * (1.0 - sig)).astype(jnp.bfloat16)
            dqkv[rows, value_lanes] = nn(sig.astype(jnp.bfloat16), grads).astype(jnp.bfloat16)
            dqkv[rows, key_lanes] = (nn(score_grad, queries) * scale).astype(jnp.bfloat16)
            dq_turned[...] += nn(key.T, score_grad)

        dqkv[:, lanes] = (dq_turned[...].T * scale).astype(jnp.bfloat16)


def middle_back(middle, h2_grad, g, gain, middle_grad, branch, gain_part):
    gain_part[...] = jnp.zeros_like(gain_part)

    @pl.loop(0, middle.shape[0] // 16)
    def _(tile):
        rows = rows_at(tile, 16)
        values, grads = middle[rows, :], h2_grad[rows, :]
        inverse = lax.rsqrt(jnp.mean(values * values, axis=-1, keepdims=True) + EPSILON)
        terms = grads * values * inverse
        gain_part[...] += terms[:8] + terms[8:]
        scaled = gain[...] * grads
        total = (
            g[rows, :].astype(jnp.float32)
            + inverse * scaled
            - values * inverse**3 * jnp.mean(scaled * values, axis=-1, keepdims=True)
        )
        middle_grad[rows, :] = total
        branch[rows, :] = total.astype(branch.dtype)


def back_kernel(
    rows,
    seqs,
    head_size,
    middle,
    h2_grad,
    g,
    attended,
    gain_values,
    lengths,
    gu,
    wout_in,
    qkv_in,
    hn_in,
    wqkv_in,
    hn_sum,
    out_sum,
    query_got,
    key_got,
    value_got,
    gate_got,
    up_got,
    gain_got,
    middle_kept,
    do,
    dqkv,
    dq_turned,
    hn_side,
    hn_chain,
    grad_qkv,
    qkv_core,
    qkv_y,
    out_core,
    out_y,
    out_side,
    out_chain,
    gains,
    gain_core,
    gain_y,
    qkv,
    hn,
    wqkv,
    wout,
    out,
    do_own,
    branch,
    middle_grad,
    key_place,
    query_low,
    query_high,
    shift,
    loads,
    sems,
):
    p, pool = Place(rows, seqs), Sems(sems)
    pairs = ((wout_in, wout), (qkv_in, qkv), (wqkv_in, wqkv), (hn_in, hn))
    for number, (source, target) in enumerate(pairs):
        pltpu.make_async_copy(source, target, loads.at[number]).start()
    greet(p.peers() + p.rows())
    stores = Stores(pool)
    tokens, own_width = do.shape
    block_tokens = tokens // seqs
    width = wqkv.shape[0]
    hn_part = wout.at[pl.ds(0, tokens), :].reshape(seqs, block_tokens, width)

    def block_rows(b):
        return pl.ds(pl.multiple_of(b * block_tokens, block_tokens), block_tokens)

    do_swap = SeqExchange(
        p, pool, lambda t: columns(do_own, t, own_width), lambda b: do.at[block_rows(b), :]
    )
    deep = width // (rows * seqs)
    out_rows = RowReduce(
        p,
        pool,
        seqs,
        lambda r, b: out.at[pl.ds(pl.multiple_of((r * seqs + b) * deep, deep), deep), :],
        lambda w, b: out_core.at[w, b],
        lambda b: out_y.at[b],
        lambda b: out_y.at[b],
    )
    hidden_own = gu.shape[2] // 2
    block = hidden_own // rows

    def gu_parts(s):
        for n, target in ((0, gate_got), (1, up_got)):
            for r in range(rows):
                yield n * hidden_own + r * block, block, columns(target, r * seqs + s, block)

    gu_swap = ColumnExchange(p, pool, lambda t: gu.at[t], gu_parts)

    def qkv_parts(s):
        for n, target in enumerate((query_got, key_got, value_got)):
            yield n * own_width, own_width, columns(target, s, own_width)

    qkv_swap = ColumnExchange(p, pool, lambda t: qkv_y.at[t], qkv_parts)
    qkv_rows = row_reducer(p, pool, grad_qkv, qkv_core, qkv_y, qkv_y)
    hn_parts = seq_reducers(p, pool, hn_part, hn_side, hn_chain, hn_sum)
    out_seq = SeqReduce(
        p, pool, lambda b: out_y.at[b], lambda b: out_side.at[b], lambda slot: out_chain.at[slot], out_sum
    )
    quarter = width // rows
    gain_rows = RowReduce(
        p,
        pool,
        1,
        lambda r, b: columns(gains, r, quarter),
        lambda w, b: gain_core.at[w],
        lambda b: gain_y,
        lambda b: gain_y,
        add_small,
    )
    gain_width = 2 * quarter // seqs
    gain_swap = SeqExchange(
        p, pool, lambda t: columns(gain_y, t // 2, gain_width), lambda b: gain_got.at[b]
    )

    gu_swap.start(0, 3)
    middle_back(middle, h2_grad, g, gain_values.at[4:5, :], middle_grad, branch, gains.at[8:16, :])
    stores.start(middle_grad, middle_kept)
    settle(wout, loads.at[0])

    @pl.loop(0, width // 512)
    def _(c):
        lanes = rows_at(c, 512)
        do_own[:, lanes] = nt(branch[...], wout[lanes, :]).astype(jnp.bfloat16)

    do_swap.start()

    def out_quarter(r):
        @pl.loop(0, 2)
        def _(c):
            lanes = rows_at(2 * r + c, width // (2 * rows))
            out[lanes, :] = tn(attended[:, lanes], branch[...]).astype(jnp.bfloat16)

    out_quarter(p.r_far)
    for b in range(seqs):
        out_rows.start_far(b)
    out_quarter(p.r_y)
    out_quarter(p.r_core)
    for b in range(seqs):
        out_rows.start_core(b)
    fill_meta(lengths, key_place, query_low, query_high, shift, block_tokens, seqs)
    for b in range(seqs):
        out_rows.step(b)
    for step in range(1, seqs):
        do_swap.step(step)
    settle(do.at[block_rows(p.s), :], do_swap.own(0))
    gu_swap.start(3, seqs)
    out_quarter(p.r)
    settle(qkv, loads.at[1])
    attention_back(qkv, do, dqkv, key_place, query_low, query_high, shift, dq_turned, head_size)

    for number in (2, 3):
        settle(pairs[number][1], loads.at[number])
    gains[0:8, :] = jnp.zeros_like(gains[0:8, :])
    column_step = 512
    for t in range(p.n_hi):
        pair = hn_parts[0].turn(t)
        tall = pl.ds(pl.multiple_of(pair * 2 * block_tokens, 2 * block_tokens), 2 * block_tokens)

        @pl.loop(0, width // column_step)
        def _(c):
            lanes = pl.ds(pl.multiple_of(c * column_step, column_step), column_step)
            part = nt(dqkv[tall, :], wqkv[lanes, :])
            hn_part[2 * pair, :, lanes] = part[:block_tokens].astype(jnp.bfloat16)
            hn_part[2 * pair + 1, :, lanes] = part[block_tokens:].astype(jnp.bfloat16)
            terms = part * hn[tall, lanes].astype(jnp.float32)
            gains[0:8, lanes] += jnp.sum(terms.reshape(-1, 8, column_step), axis=0)

        for member in hn_parts:
            member.start(t)
    gains[0:8, :] = gains[0:8, :] / gain_values[0:1, :]
    gain_rows.start(0)

    @pl.loop(0, width // 256)
    def _(c):
        lanes = pl.ds(pl.multiple_of(c * 256, 256), 256)
        total = tn(hn[:, lanes], dqkv[...]).astype(jnp.bfloat16)
        piece = total.reshape((4,) + (total.shape[0] // 4, total.shape[1]))
        for n in range(4):
            grad_qkv[c * 4 // seqs, lax.rem(c * 4, seqs) + n] = piece[n]

    for b in range(seqs):
        qkv_rows.start(b)
    gain_rows.step(0)
    for t in range(p.n_hi):
        for member in hn_parts:
            member.step(t)
        if t == 0:
            for b in range(seqs):
                qkv_rows.step(b)
            gain_rows.close(0)
            gain_swap.start()
        if t == p.n_hi // 2 - 1:
            for b in range(seqs):
                out_rows.close(b)
            for k in range(p.n_hi):
                out_seq.start(k)
        if t == p.n_hi - 2:
            for b in range(seqs):
                qkv_rows.close(b)
            qkv_swap.start()
    for t in range(p.n_hi):
        out_seq.step(t)
    for step in range(1, seqs):
        gain_swap.step(step)
        settle(do.at[block_rows(p.s), :], do_swap.send(step))
    for member in hn_parts + [out_rows, qkv_rows, gain_rows, gu_swap, qkv_swap, out_seq, gain_swap, stores]:
        member.finish()


def back(rows, seqs, head_size, middle, h2_grad, g, attended, gain_values, lengths, gu, wout, qkv, hn, wqkv):
    tokens, own_width = qkv.shape[0], qkv.shape[1] // 3
    width = hn.shape[1]
    low, f32 = jnp.bfloat16, jnp.float32
    block_tokens = tokens // seqs
    deep = width // (rows * seqs)
    quarter = width // rows
    hn_dims, qkv_dims = (seqs, block_tokens, width), (rows, seqs, deep, 3 * own_width)
    got = shape_of((deep, width))
    gu_got = shape_of((deep, gu.shape[2] // 2 * seqs))
    gain_width = 2 * quarter // seqs
    shapes = (
        shape_of(hn_dims[1:], f32),
        got,
        got,
        got,
        got,
        gu_got,
        gu_got,
        shape_of((seqs, 16, gain_width), f32),
        shape_of(hn_dims[1:], f32),
    )
    qkv_like, out_like = shape_of(qkv_dims), shape_of((rows, seqs, deep, width))
    scratch = (
        [
            pltpu.VMEM((tokens, own_width), low),
            pltpu.VMEM(qkv.shape, low),
            pltpu.VMEM((head_size, tokens), f32),
        ]
        + seq_slots(shape_of(hn_dims))
        + [pltpu.VMEM(qkv_dims, low)]
        + row_slots(qkv_like)
        + row_slots(out_like)
        + seq_slots(shape_of(out_like.shape[1:]))
        + [pltpu.VMEM((16, width), f32), pltpu.VMEM((2, 16, quarter), f32), pltpu.VMEM((16, quarter), f32)]
        + [pltpu.VMEM(array.shape, low) for array in (qkv, hn, wqkv, wout)]
        + [pltpu.VMEM((width, width), low)]
        + [pltpu.VMEM(hn_dims[1:], low), pltpu.VMEM(hn_dims[1:], low), pltpu.VMEM(hn_dims[1:], f32)]
        + meta_scratch(tokens)
        + [pltpu.SemaphoreType.DMA((4,))]
    )
    return call(
        functools.partial(back_kernel, rows, seqs, head_size),
        shapes,
        6,
        (middle, h2_grad, g, attended, gain_values, lengths, gu, wout, qkv, hn, wqkv),
        [pltpu.VMEM] * 5 + [pltpu.SMEM, pltpu.VMEM] + [pl.ANY] * 4,
        (pltpu.VMEM,) * 5 + (pl.ANY,) * 2 + (pltpu.VMEM, pl.ANY),
        scratch,
        480,
    )


def dot(left, right, left_axis=1, right_axis=0):
    return lax.dot_general(
        left, right, (((left_axis,), (right_axis,)), ((), ())), preferred_element_type=jnp.float32
    )


def split_local(
    rows,
    seqs,
    inputs,
    lengths,
    w_query,
    w_key,
    w_value,
    w_out,
    gain_attn,
    w_gate,
    w_up,
    w_down,
    gain_mlp,
    cotangent,
):
    low, f32 = jnp.bfloat16, jnp.float32
    tokens, width = inputs.shape[1], inputs.shape[2]
    deep = w_query.shape[0]
    row_tokens = tokens * seqs
    head_size = width // HEADS
    own_width = width // seqs
    hidden_own = w_gate.shape[1] // seqs

    side = lax.rem(lax.axis_index("seq"), 2)
    lane = lax.broadcasted_iota(jnp.int32, (8, 2 * deep), 1)
    both = [jnp.concatenate([gain, gain]).astype(f32)[None, :] for gain in (gain_attn, gain_mlp)]
    number = lax.broadcasted_iota(jnp.int32, (8, 2 * deep), 0)
    gains_own = jnp.where(lane // deep == side, jnp.where(number < 4, both[0], both[1]), 0.0)
    x_low, g_low = inputs[0], cotangent[0]

    g_all, wgu, wdown, wout, h2, wqkv, hn, qkv, attended, middle, gains = forward(
        rows,
        seqs,
        head_size,
        x_low,
        g_low,
        (w_query, w_key, w_value),
        (w_gate, w_up),
        w_down,
        w_out,
        gains_own,
        lengths,
    )
    gain_one = gains[0:1]
    wqkv = wqkv.reshape(width, 3 * own_width)
    wgu = wgu.reshape(width, 2 * hidden_own)
    wdown = wdown.reshape(hidden_own, width)
    wout = wout.reshape(width, width)
    g_all = g_all.reshape(row_tokens, width)
    h2 = h2.reshape(row_tokens, width)
    residual = x_low.astype(f32)
    h2_grad, out_sum, sum_gu, sum_down = ffn(rows, seqs, h2, wgu, wdown, g_all)
    output = (middle + out_sum).astype(low)

    hn_grad, sum_out, got_query, got_key, got_value, got_gate, got_up, got_gain, middle_grad = back(
        rows, seqs, head_size, middle, h2_grad, g_low, attended, gains, lengths, sum_gu, wout, qkv, hn, wqkv
    )
    spread_inverse = lax.rsqrt(jnp.mean(residual * residual, axis=-1, keepdims=True) + EPSILON)
    scaled_grad = gain_one * hn_grad
    input_grad = (
        middle_grad
        + spread_inverse * scaled_grad
        - residual * spread_inverse**3 * jnp.mean(scaled_grad * residual, axis=-1, keepdims=True)
    )
    gain_sums = jnp.sum(got_gain, axis=0).reshape(2, 8, 2, deep).sum(axis=1)
    gain_sums = lax.dynamic_index_in_dim(gain_sums, lax.rem(lax.axis_index("seq"), 2), 1, keepdims=False)
    return (
        output[None],
        input_grad[None],
        got_query.astype(f32),
        got_key.astype(f32),
        got_value.astype(f32),
        sum_out.astype(f32),
        gain_sums[0],
        got_gate.astype(f32),
        got_up.astype(f32),
        sum_down.reshape(w_down.shape).astype(f32),
        gain_sums[1],
    )


def solution(mesh):
    placed = (
        P("row", "seq", None),
        P("row", None),
        P(("row", "seq"), None),
        P(("row", "seq"), None),
        P(("row", "seq"), None),
        P(("row", "seq"), None),
        P(("row", "seq")),
        P(("row", "seq"), None),
        P(("row", "seq"), None),
        P(("row", "seq"), None),
        P(("row", "seq")),
        P("row", "seq", None),
    )
    row_count, seq_count = mesh.shape["row"], mesh.shape["seq"]
    if row_count == 4 and seq_count % 2 == 0 and HEADS % seq_count == 0:
        local = functools.partial(split_local, row_count, seq_count)
    else:
        local = gathered_local
    return jax.shard_map(
        local,
        mesh=mesh,
        in_specs=placed,
        out_specs=(
            P("row", "seq", None),
            P("row", "seq", None),
            P(("row", "seq"), None),
            P(("row", "seq"), None),
            P(("row", "seq"), None),
            P(("row", "seq"), None),
            P(("row", "seq")),
            P(("row", "seq"), None),
            P(("row", "seq"), None),
            P(("row", "seq"), None),
            P(("row", "seq")),
        ),
        check_vma=False,
    )
```

```python
import functools

import jax
import jax.numpy as jnp
from jax import lax
from jax.experimental import pallas as pl
from jax.experimental.pallas import tpu as pltpu
from jax.sharding import PartitionSpec as P

HEADS = 16


EPSILON = 1e-05


def layout(lengths_row, places, block_rows, block_count):
    unit_counts = lengths_row // (2 * block_count)
    span_sizes = 2 * unit_counts
    offsets = jnp.cumsum(span_sizes) - span_sizes
    device = places // block_rows
    within_block = places - device * block_rows
    inside = (
        (within_block[:, None] >= offsets[None, :])
        & (within_block[:, None] < (offsets + span_sizes)[None, :])
    ).astype(jnp.int32)
    numbers = jnp.arange(lengths_row.shape[0], dtype=jnp.int32)
    segment = jnp.sum(inside * numbers[None, :], axis=1)
    unit_of = jnp.sum(inside * unit_counts[None, :], axis=1)
    begins = jnp.sum(inside * offsets[None, :], axis=1)
    length_of = jnp.sum(inside * lengths_row[None, :], axis=1)
    within = within_block - begins
    position = jnp.where(
        within < unit_of,
        device * unit_of + within,
        (2 * block_count - 1 - device) * unit_of + within - unit_of,
    )
    return (segment, position, length_of)


def rms_norm(values, gain):
    return values * lax.rsqrt(jnp.mean(values * values, axis=-1, keepdims=True) + EPSILON) * gain


def sigmoid_terms(query_heads, query_meta, key_heads, key_meta):
    query_segment, query_position, query_length = query_meta
    key_segment, key_position, unused_length = key_meta
    scores = jnp.einsum(
        "qhd,khd->hqk", query_heads, key_heads, preferred_element_type=jnp.float32
    ) * query_heads.shape[2] ** (-0.5)
    scores = scores - jnp.log(query_length.astype(jnp.float32))[None, :, None]
    allowed = (query_segment[:, None] == key_segment[None, :]) & (
        key_position[None, :] <= query_position[:, None]
    )
    return jnp.where(allowed[None], jax.nn.sigmoid(scores), 0.0)


def pair_terms(query_heads, query_meta, grad_heads, key_heads, key_meta, value_heads):
    sig_terms = sigmoid_terms(query_heads, query_meta, key_heads, key_meta)
    slopes = jnp.einsum("qhd,khd->hqk", grad_heads, value_heads, preferred_element_type=jnp.float32)
    score_grad = (slopes * sig_terms * (1.0 - sig_terms)).astype(jnp.bfloat16)
    return (sig_terms.astype(jnp.bfloat16), score_grad)


def by_blocks(step_fn, running, pieces, block_rows):
    size_total = pieces[0].shape[0]
    part_rows = 4 * block_rows
    block_count = size_total // part_rows

    def turn_over(step_number, carried):
        sub_pieces = tuple(
            (
                lax.dynamic_slice_in_dim(member, step_number * part_rows, part_rows, 0)
                for member in pieces
            )
        )
        return step_fn(carried, sub_pieces, step_number * part_rows)

    return lax.fori_loop(0, block_count, turn_over, running)


def gathered_local(
    inputs,
    lengths,
    w_query,
    w_key,
    w_value,
    w_out,
    gain_attn,
    w_gate,
    w_up,
    w_down,
    gain_mlp,
    cotangent,
):
    residual = inputs[0].astype(jnp.float32)
    tokens_here = residual.shape[0]
    model_width = residual.shape[1]
    head_size = model_width // HEADS
    score_scale = head_size ** (-0.5)
    block_total = lax.axis_size("seq")
    lengths_row = lengths[0]
    places = lax.axis_index("seq") * tokens_here + jnp.arange(tokens_here, dtype=jnp.int32)
    own_meta = layout(lengths_row, places, tokens_here, block_total)

    def meta_at(start_row, row_count):
        return layout(
            lengths_row,
            start_row + jnp.arange(row_count, dtype=jnp.int32),
            tokens_here,
            block_total,
        )

    def heads_of(matrix):
        return matrix.reshape(matrix.shape[0], HEADS, head_size)

    query_full, key_full, value_full, out_full, gain_one = (
        lax.all_gather(w_query, ("row", "seq"), axis=0, tiled=True),
        lax.all_gather(w_key, ("row", "seq"), axis=0, tiled=True),
        lax.all_gather(w_value, ("row", "seq"), axis=0, tiled=True),
        lax.all_gather(w_out, ("row", "seq"), axis=0, tiled=True),
        lax.all_gather(gain_attn, ("row", "seq"), axis=0, tiled=True),
    )
    gain_one_f = gain_one.astype(jnp.float32)
    normed = rms_norm(residual, gain_one_f).astype(jnp.bfloat16)
    queries = jnp.dot(normed, query_full, preferred_element_type=jnp.float32).astype(jnp.bfloat16)
    key_rows = jnp.dot(normed, key_full, preferred_element_type=jnp.float32).astype(jnp.bfloat16)
    value_rows = jnp.dot(normed, value_full, preferred_element_type=jnp.float32).astype(
        jnp.bfloat16
    )
    query_heads = heads_of(queries)

    def forward_step(running, pieces, start_row):
        key_piece, value_piece = pieces
        sig_terms = sigmoid_terms(
            query_heads, own_meta, heads_of(key_piece), meta_at(start_row, key_piece.shape[0])
        ).astype(jnp.bfloat16)
        added = jnp.einsum(
            "hqk,khd->qhd", sig_terms, heads_of(value_piece), preferred_element_type=jnp.float32
        )
        return running + added.reshape(tokens_here, model_width)

    attended = by_blocks(
        forward_step,
        jnp.zeros((tokens_here, model_width), jnp.float32),
        (
            lax.all_gather(key_rows, "seq", axis=0, tiled=True),
            lax.all_gather(value_rows, "seq", axis=0, tiled=True),
        ),
        tokens_here,
    )
    attended_low = attended.astype(jnp.bfloat16)
    middle = residual + jnp.dot(attended_low, out_full, preferred_element_type=jnp.float32)
    gate_full, up_full, down_full, gain_two = (
        lax.all_gather(w_gate, ("row", "seq"), axis=0, tiled=True),
        lax.all_gather(w_up, ("row", "seq"), axis=0, tiled=True),
        lax.all_gather(w_down, ("row", "seq"), axis=0, tiled=True),
        lax.all_gather(gain_mlp, ("row", "seq"), axis=0, tiled=True),
    )
    gain_two_f = gain_two.astype(jnp.float32)
    normed_mlp = rms_norm(middle, gain_two_f).astype(jnp.bfloat16)
    gate_vals = jnp.dot(normed_mlp, gate_full, preferred_element_type=jnp.float32)
    up_vals = jnp.dot(normed_mlp, up_full, preferred_element_type=jnp.float32)
    gated_prod, gated_back = jax.vjp(
        lambda gate_in, up_in: jax.nn.silu(gate_in) * up_in, gate_vals, up_vals
    )
    hidden = gated_prod.astype(jnp.bfloat16)
    output = (middle + jnp.dot(hidden, down_full, preferred_element_type=jnp.float32)).astype(
        jnp.bfloat16
    )
    upstream_low = cotangent[0]
    upstream = upstream_low.astype(jnp.float32)
    gate_full, up_full, down_full, gain_two = (
        lax.all_gather(w_gate, ("row", "seq"), axis=0, tiled=True),
        lax.all_gather(w_up, ("row", "seq"), axis=0, tiled=True),
        lax.all_gather(w_down, ("row", "seq"), axis=0, tiled=True),
        lax.all_gather(gain_mlp, ("row", "seq"), axis=0, tiled=True),
    )
    gain_two_f = gain_two.astype(jnp.float32)
    grad_down = jnp.dot(hidden.T, upstream_low, preferred_element_type=jnp.float32)
    shared_down = lax.psum_scatter(grad_down, ("row", "seq"), scatter_dimension=0, tiled=True)
    hidden_grad = jnp.dot(upstream_low, down_full.T, preferred_element_type=jnp.float32)
    gate_grad, up_grad = gated_back(hidden_grad)
    gate_low = gate_grad.astype(jnp.bfloat16)
    up_low = up_grad.astype(jnp.bfloat16)
    grad_gate = jnp.dot(normed_mlp.T, gate_low, preferred_element_type=jnp.float32)
    shared_gate = lax.psum_scatter(grad_gate, ("row", "seq"), scatter_dimension=0, tiled=True)
    normed_grad = jnp.dot(gate_low, gate_full.T, preferred_element_type=jnp.float32) + jnp.dot(
        up_low, up_full.T, preferred_element_type=jnp.float32
    )
    unused_mid, second_back = jax.vjp(rms_norm, middle, gain_two_f)
    middle_part, gain_two_grad = second_back(normed_grad)
    middle_grad = upstream + middle_part
    grad_up = jnp.dot(normed_mlp.T, up_low, preferred_element_type=jnp.float32)
    shared_up, shared_gain_two = (
        lax.psum_scatter(grad_up, ("row", "seq"), scatter_dimension=0, tiled=True),
        lax.psum_scatter(gain_two_grad, ("row", "seq"), scatter_dimension=0, tiled=True),
    )
    query_full, key_full, value_full, out_full, gain_one = (
        lax.all_gather(w_query, ("row", "seq"), axis=0, tiled=True),
        lax.all_gather(w_key, ("row", "seq"), axis=0, tiled=True),
        lax.all_gather(w_value, ("row", "seq"), axis=0, tiled=True),
        lax.all_gather(w_out, ("row", "seq"), axis=0, tiled=True),
        lax.all_gather(gain_attn, ("row", "seq"), axis=0, tiled=True),
    )
    gain_one_f = gain_one.astype(jnp.float32)
    branch_low = middle_grad.astype(jnp.bfloat16)
    grad_out = jnp.dot(attended_low.T, branch_low, preferred_element_type=jnp.float32)
    attended_grad = jnp.dot(branch_low, out_full.T, preferred_element_type=jnp.float32).astype(
        jnp.bfloat16
    )
    grad_heads = heads_of(attended_grad)
    key_heads_own = heads_of(key_rows)
    value_heads_own = heads_of(value_rows)

    def query_step(running, pieces, start_row):
        key_piece, value_piece = pieces
        key_piece_heads = heads_of(key_piece)
        unused_terms, score_grad = pair_terms(
            query_heads,
            own_meta,
            grad_heads,
            key_piece_heads,
            meta_at(start_row, key_piece.shape[0]),
            heads_of(value_piece),
        )
        added = jnp.einsum(
            "hqk,khd->qhd", score_grad, key_piece_heads, preferred_element_type=jnp.float32
        )
        return running + added.reshape(tokens_here, model_width) * score_scale

    start_value = jnp.zeros((tokens_here, model_width), jnp.float32)
    folded = by_blocks(
        query_step,
        start_value,
        (
            lax.all_gather(key_rows, "seq", axis=0, tiled=True),
            lax.all_gather(value_rows, "seq", axis=0, tiled=True),
        ),
        tokens_here,
    )

    def key_step(running, pieces, start_row):
        key_sum, value_sum = running
        query_piece, grad_piece = pieces
        row_count = query_piece.shape[0]
        query_piece_heads = heads_of(query_piece)
        grad_piece_heads = heads_of(grad_piece)
        sig_low, score_grad = pair_terms(
            query_piece_heads,
            meta_at(start_row, row_count),
            grad_piece_heads,
            key_heads_own,
            own_meta,
            value_heads_own,
        )
        key_add = jnp.einsum(
            "hqk,qhd->khd", score_grad, query_piece_heads, preferred_element_type=jnp.float32
        )
        value_add = jnp.einsum(
            "hqk,qhd->khd", sig_low, grad_piece_heads, preferred_element_type=jnp.float32
        )
        return (
            key_sum + key_add.reshape(tokens_here, model_width) * score_scale,
            value_sum + value_add.reshape(tokens_here, model_width),
        )

    empty_rows = jnp.zeros((tokens_here, model_width), jnp.float32)
    key_grad, value_grad = by_blocks(
        key_step,
        (empty_rows, empty_rows),
        (
            lax.all_gather(queries, "seq", axis=0, tiled=True),
            lax.all_gather(attended_grad, "seq", axis=0, tiled=True),
        ),
        tokens_here,
    )
    query_low = folded.astype(jnp.bfloat16)
    key_low = key_grad.astype(jnp.bfloat16)
    value_low = value_grad.astype(jnp.bfloat16)
    grad_query = jnp.dot(normed.T, query_low, preferred_element_type=jnp.float32)
    grad_key = jnp.dot(normed.T, key_low, preferred_element_type=jnp.float32)
    grad_value = jnp.dot(normed.T, value_low, preferred_element_type=jnp.float32)
    normed_back = jnp.dot(query_low, query_full.T, preferred_element_type=jnp.float32)
    normed_back = normed_back + jnp.dot(key_low, key_full.T, preferred_element_type=jnp.float32)
    normed_back = normed_back + jnp.dot(value_low, value_full.T, preferred_element_type=jnp.float32)
    unused_first, first_back = jax.vjp(rms_norm, residual, gain_one_f)
    residual_part, gain_one_grad = first_back(normed_back)
    input_grad = middle_grad + residual_part
    shared_query, shared_key, shared_value, shared_out, shared_gain_one = (
        lax.psum_scatter(grad_query, ("row", "seq"), scatter_dimension=0, tiled=True),
        lax.psum_scatter(grad_key, ("row", "seq"), scatter_dimension=0, tiled=True),
        lax.psum_scatter(grad_value, ("row", "seq"), scatter_dimension=0, tiled=True),
        lax.psum_scatter(grad_out, ("row", "seq"), scatter_dimension=0, tiled=True),
        lax.psum_scatter(gain_one_grad, ("row", "seq"), scatter_dimension=0, tiled=True),
    )
    return (
        output[None],
        input_grad[None],
        shared_query,
        shared_key,
        shared_value,
        shared_out,
        shared_gain_one,
        shared_gate,
        shared_up,
        shared_down,
        shared_gain_two,
    )


MESH = pl.DeviceIdType.MESH
VMEM_BYTES = 62 * 1024 * 1024


class Place:
    def __init__(self, row_count, seq_count):
        self.row_count, self.seq_count = row_count, seq_count
        self.r, self.s = lax.axis_index("row"), lax.axis_index("seq")
        self.n_hi = seq_count // 2
        self.hi, self.lo = self.s // 2, lax.rem(self.s, 2)
        self.r_core = self.r + 1 - 2 * lax.rem(self.r, 2)
        self.r_y = lax.rem(self.r + 2, 4)
        self.r_far = lax.rem(self.r_core + 2, 4)
        self.side = (self.r, self.s + 1 - 2 * self.lo)
        self.up = (self.r, self.s + 2)
        self.down = (self.r, self.s - 2)
        self.core = (self.r_core, self.s)
        self.y = (self.r_y, self.s)
        self.has_up = self.hi < self.n_hi - 1
        self.has_down = self.hi > 0

    def peer(self, step):
        return lax.rem(self.s + step, self.seq_count)

    def chain(self):
        return [(None, self.side), (self.has_up, self.up), (self.has_down, self.down)]

    def peers(self):
        return [(None, (self.r, self.peer(step))) for step in range(1, self.seq_count)]

    def rows(self):
        return [(None, self.core), (None, self.y)]


def greet(devices):
    barrier = pltpu.get_barrier_semaphore()
    total = 0
    for condition, device in devices:
        if condition is None:
            pl.semaphore_signal(barrier, inc=1, device_id=device, device_id_type=MESH)
            total = total + 1
        else:

            @pl.when(condition)
            def _(device=device):
                pl.semaphore_signal(barrier, inc=1, device_id=device, device_id_type=MESH)

            total = total + condition.astype(jnp.int32)
    pl.semaphore_wait(barrier, total)


class Sems:
    def __init__(self, ref):
        self.ref, self.used = ref, 0

    def take(self, count):
        base = self.used
        self.used += count
        assert self.used <= self.ref.shape[0], self.used
        return lambda index: self.ref.at[base + index]


def push(source, target, send, recv, device):
    pltpu.make_async_remote_copy(
        src_ref=source, dst_ref=target, send_sem=send, recv_sem=recv, device_id=device, device_id_type=MESH
    ).start()


def settle(ref, sem):
    pltpu.make_async_copy(ref, ref, sem).wait()


def no_op(block):
    return None


class Stores:
    def __init__(self, sems):
        self.sems, self.open = sems, []

    def start(self, source, target):
        sem = self.sems.take(1)(0)
        pltpu.make_async_copy(source, target, sem).start()
        self.open.append((target, sem))

    def finish(self):
        for target, sem in self.open:
            settle(target, sem)


class SeqGather:
    def __init__(self, place, sems, source, at, arrived=no_op, arrived_aside=None):
        self.p, self.source, self.at, self.arrived = place, source, at, arrived
        self.arrived_aside = arrived_aside or arrived
        self.own_done = False
        n = place.n_hi
        self.own, self.up, self.down = sems.take(1), sems.take(n), sems.take(n)
        self.side, self.recv = sems.take(n), sems.take(2 * n)

    def start(self):
        p, s = self.p, self.p.s
        pltpu.make_async_copy(self.source, self.at(s), self.own(0)).start()

        @pl.when(p.has_up)
        def _():
            push(self.source, self.at(s), self.up(0), self.recv(s), p.up)

        @pl.when(p.has_down)
        def _():
            push(self.source, self.at(s), self.down(0), self.recv(s), p.down)

        push(self.source, self.at(s), self.side(p.hi), self.recv(s), p.side)

    def step(self, k):
        p = self.p

        @pl.when(p.hi >= k)
        def _():
            block = p.s - 2 * k
            settle(self.at(block), self.recv(block))

            @pl.when(p.has_up)
            def _():
                push(self.at(block), self.at(block), self.up(k), self.recv(block), p.up)

            push(self.at(block), self.at(block), self.side(p.hi - k), self.recv(block), p.side)
            self.arrived(block)

        @pl.when(p.hi + k < p.n_hi)
        def _():
            block = p.s + 2 * k
            settle(self.at(block), self.recv(block))

            @pl.when(p.has_down)
            def _():
                push(self.at(block), self.at(block), self.down(k), self.recv(block), p.down)

            push(self.at(block), self.at(block), self.side(p.hi + k), self.recv(block), p.side)
            self.arrived(block)

    def aside(self, k):
        p = self.p
        if k == 0:
            block = 2 * p.hi + 1 - p.lo
            settle(self.at(block), self.recv(block))
            self.arrived_aside(block)
            return

        @pl.when(p.hi >= k)
        def _():
            block = 2 * (p.hi - k) + 1 - p.lo
            settle(self.at(block), self.recv(block))
            self.arrived_aside(block)

        @pl.when(p.hi + k < p.n_hi)
        def _():
            block = 2 * (p.hi + k) + 1 - p.lo
            settle(self.at(block), self.recv(block))
            self.arrived_aside(block)

    def settle_own(self):
        settle(self.at(self.p.s), self.own(0))
        self.own_done = True

    def finish(self):
        p = self.p
        if not self.own_done:
            self.settle_own()
        for k in range(p.n_hi):

            @pl.when(p.has_up & (p.hi >= k))
            def _():
                settle(self.source, self.up(k))

            @pl.when(p.has_down & (p.hi + k < p.n_hi))
            def _():
                settle(self.source, self.down(k))

            settle(self.source, self.side(k))


class SeqExchange:
    def __init__(self, place, sems, piece, at, arrived=no_op):
        self.p, self.piece, self.at, self.arrived = place, piece, at, arrived
        self.own_done = False
        n = place.seq_count
        self.own, self.send, self.recv = sems.take(1), sems.take(n), sems.take(n)

    def start_own(self):
        s = self.p.s
        pltpu.make_async_copy(self.piece(s), self.at(s), self.own(0)).start()

    def start(self):
        p, s = self.p, self.p.s
        self.start_own()
        for step in range(1, p.seq_count):
            t = p.peer(step)
            push(self.piece(t), self.at(s), self.send(step), self.recv(s), (p.r, t))

    def step(self, step):
        block = self.p.peer(self.p.seq_count - step)
        settle(self.at(block), self.recv(block))
        self.arrived(block)

    def finish(self):
        p = self.p
        settle(self.at(p.s), self.own(0))
        for step in range(1, p.seq_count):
            settle(self.at(p.s), self.send(step))


class PartExchange(SeqExchange):
    def __init__(self, place, sems, parts, at, arrived=no_op):
        super().__init__(place, sems, None, at, arrived)
        self.parts = parts

    def start_own(self):
        s = self.p.s
        for source, target in self.parts(s):
            pltpu.make_async_copy(source, target, self.own(0)).start()

    def start(self):
        p, s = self.p, self.p.s
        self.start_own()
        for step in range(1, p.seq_count):
            t = p.peer(step)
            for source, target in self.parts(t):
                push(source, target, self.send(step), self.recv(s), (p.r, t))

    def settle_own(self):
        settle(self.at(self.p.s), self.own(0))
        self.own_done = True

    def finish(self):
        p = self.p
        if not self.own_done:
            self.settle_own()
        for step in range(1, p.seq_count):
            settle(self.at(p.s), self.send(step))


class RowForward:
    def __init__(self, place, sems, blocks, at):
        self.p, self.at, self.blocks = place, at, blocks
        self.core, self.y, self.far = sems.take(blocks), sems.take(blocks), sems.take(blocks)
        self.from_core, self.from_y, self.from_far = sems.take(blocks), sems.take(blocks), sems.take(blocks)

    def forward(self, block, source=None):
        p = self.p
        source = self.at(p.r, block) if source is None else source
        push(source, self.at(p.r, block), self.y(block), self.from_y(block), p.y)
        push(source, self.at(p.r, block), self.core(block), self.from_core(block), p.core)

    def relay(self, block):
        p = self.p
        settle(self.at(p.r_y, block), self.from_y(block))
        push(self.at(p.r_y, block), self.at(p.r_y, block), self.far(block), self.from_far(block), p.core)

    def finish(self):
        p = self.p
        for block in range(self.blocks):
            settle(self.at(p.r_core, block), self.from_core(block))
            settle(self.at(p.r_far, block), self.from_far(block))
            settle(self.at(p.r, block), self.core(block))
            settle(self.at(p.r, block), self.y(block))
            settle(self.at(p.r_y, block), self.far(block))


def add_into(target, *sources):
    @pl.loop(0, target.shape[0] // 16)
    def _(tile):
        rows = pl.ds(pl.multiple_of(tile * 16, 16), 16)
        total = sources[0][rows, :].astype(jnp.float32)
        for source in sources[1:]:
            total = total + source[rows, :].astype(jnp.float32)
        target[rows, :] = total.astype(target.dtype)


def add_small(target, *sources):
    total = sources[0][...].astype(jnp.float32)
    for source in sources[1:]:
        total = total + source[...].astype(jnp.float32)
    target[...] = total.astype(target.dtype)


class SeqReduce:
    def __init__(self, place, sems, at, side_slot, chain_slot, target, add=add_into):
        self.p, self.at, self.add, self.target = place, at, add, target
        self.side_slot, self.chain_slot = side_slot, chain_slot
        n = place.n_hi
        self.side, self.from_side = sems.take(n), sems.take(n)
        self.send, self.recv = sems.take(n), sems.take(2 * n)

    def above_slot(self, block, hi):
        return self.chain_slot(jnp.where(block == hi, self.p.n_hi, block))

    def turn(self, t):
        p = self.p
        n, hi = p.n_hi, p.hi
        low = jnp.where(t < n - 1 - hi, n - 1 - t, t - (n - 1 - hi))
        high = jnp.where(t < hi, t, n - 1 - (t - hi))
        return jnp.where(hi < n // 2, low, high)

    def start(self, t):
        p, block = self.p, self.turn(t)
        push(self.at(2 * block + 1 - p.lo), self.side_slot(block), self.side(block), self.from_side(block), p.side)

    def step(self, t):
        p, n, block = self.p, self.p.n_hi, self.turn(t)
        mine, got = self.at(2 * block + p.lo), self.side_slot(block)
        settle(got, self.from_side(block))
        if t == n - 1:
            return self.close()

        @pl.when(block > p.hi)
        def _():
            @pl.when(p.has_down)
            def _():
                settle(got, self.recv(block))
                self.add(got, mine, got, self.chain_slot(block))

            @pl.when(jnp.logical_not(p.has_down))
            def _():
                self.add(got, mine, got)

            push(got, self.chain_slot(block), self.send(block), self.recv(block), p.up)

        @pl.when(block < p.hi)
        def _():
            @pl.when(p.has_up)
            def _():
                settle(got, self.recv(n + block))
                self.add(got, mine, got, self.above_slot(block, p.hi))

            @pl.when(jnp.logical_not(p.has_up))
            def _():
                self.add(got, mine, got)

            push(got, self.above_slot(block, p.hi - 1), self.send(block), self.recv(n + block), p.down)

    def close(self):
        p, n, hi = self.p, self.p.n_hi, self.p.hi
        mine, got = self.at(p.s), self.side_slot(hi)
        below, above = self.chain_slot(hi), self.above_slot(hi, hi)

        @pl.when(p.has_down)
        def _():
            settle(got, self.recv(hi))

        @pl.when(p.has_up)
        def _():
            settle(got, self.recv(n + hi))

        @pl.when(p.has_down & p.has_up)
        def _():
            self.add(self.target, mine, got, below, above)

        @pl.when(p.has_down & jnp.logical_not(p.has_up))
        def _():
            self.add(self.target, mine, got, below)

        @pl.when(jnp.logical_not(p.has_down))
        def _():
            self.add(self.target, mine, got, above)

    def finish(self):
        p = self.p
        for block in range(p.n_hi):
            settle(self.side_slot(block), self.side(block))

            @pl.when(p.hi != block)
            def _():
                settle(self.side_slot(block), self.send(block))


class RowReduce:
    def __init__(self, place, sems, blocks, at, core_slot, y_slot, target, add=add_into, own=None):
        self.p, self.at, self.add, self.target = place, at, add, target
        self.own = own or (lambda w, b: at((place.r_y, place.r)[w], b))
        self.core_slot, self.y_slot, self.blocks = core_slot, y_slot, blocks
        self.send, self.recv = sems.take(2 * blocks), sems.take(2 * blocks)
        self.y, self.from_y = sems.take(blocks), sems.take(blocks)

    def start_far(self, block):
        p = self.p
        push(self.at(p.r_far, block), self.core_slot(0, block), self.send(block), self.recv(block), p.core)

    def start_core(self, block):
        p, n = self.p, self.blocks
        push(self.at(p.r_core, block), self.core_slot(1, block), self.send(n + block), self.recv(n + block), p.core)

    def start(self, block):
        self.start_far(block)
        self.start_core(block)

    def step(self, block):
        p = self.p
        got = self.core_slot(0, block)
        settle(got, self.recv(block))
        self.add(got, self.own(0, block), got)
        push(got, self.y_slot(block), self.y(block), self.from_y(block), p.y)

    def close(self, block):
        p = self.p
        settle(self.core_slot(1, block), self.recv(self.blocks + block))
        settle(self.y_slot(block), self.from_y(block))
        self.add(self.target(block), self.own(1, block), self.core_slot(1, block), self.y_slot(block))

    def finish(self):
        n = self.blocks
        for block in range(n):
            settle(self.core_slot(0, block), self.send(block))
            settle(self.core_slot(1, block), self.send(n + block))
            settle(self.core_slot(0, block), self.y(block))


def columns(ref, index, width):
    return ref.at[:, pl.ds(pl.multiple_of(index * width, width), width)]


def call(kernel, shapes, ident, args, spaces, out_spaces, scratch, sems):
    return pl.pallas_call(
        kernel,
        out_shape=shapes,
        in_specs=[pl.BlockSpec(memory_space=space) for space in spaces],
        out_specs=jax.tree.map(lambda space: pl.BlockSpec(memory_space=space), out_spaces),
        scratch_shapes=list(scratch) + [pltpu.SemaphoreType.DMA((sems,))],
        compiler_params=pltpu.CompilerParams(
            collective_id=ident, has_side_effects=True, vmem_limit_bytes=VMEM_BYTES
        ),
    )(*args)


def shape_of(dims, dtype=jnp.bfloat16):
    return jax.ShapeDtypeStruct(dims, dtype)


def nt(left, right):
    return lax.dot_general(left, right, (((1,), (1,)), ((), ())), preferred_element_type=jnp.float32)


def tn(left, right):
    return lax.dot_general(left, right, (((0,), (0,)), ((), ())), preferred_element_type=jnp.float32)


def nn(left, right):
    return lax.dot_general(left, right, (((1,), (0,)), ((), ())), preferred_element_type=jnp.float32)


def rows_at(index, count):
    return pl.ds(pl.multiple_of(index * count, count), count)


def norm_rows(source, target, gain):
    @pl.loop(0, source.shape[0] // 16)
    def _(tile):
        rows = rows_at(tile, 16)
        values = source[rows, :].astype(jnp.float32)
        target[rows, :] = rms_norm(values, gain[...]).astype(target.dtype)


def places(lengths, shape, axis, tokens, seqs):
    row_tokens = tokens * seqs
    index = lax.broadcasted_iota(jnp.int32, shape, axis)
    block, within = index // tokens, lax.rem(index, tokens)
    segment = position = length_of = jnp.zeros_like(index)
    begin = 0
    for n in range(lengths.shape[1]):
        length = lengths[0, n]
        unit = length // (2 * seqs)
        inside = (within >= begin) & (within < begin + 2 * unit)
        local = within - begin
        here = jnp.where(local < unit, block * unit + local, (2 * seqs - 1 - block) * unit + local - unit)
        segment = jnp.where(inside, n, segment)
        position = jnp.where(inside, here, position)
        length_of = jnp.where(inside, length, length_of)
        begin = begin + 2 * unit
    return segment * row_tokens, segment * row_tokens + position, length_of


def fill_meta(lengths, key_place, query_low, query_high, shift, tokens, seqs):
    key_place[...] = places(lengths, key_place.shape, 0, tokens, seqs)[1]
    low, high, length_of = places(lengths, query_low.shape, 1, tokens, seqs)
    query_low[...] = low
    query_high[...] = high
    shift[...] = jnp.log(length_of.astype(jnp.float32))


def meta_scratch(row_tokens):
    return [
        pltpu.VMEM((row_tokens, 1), jnp.int32),
        pltpu.VMEM((1, row_tokens), jnp.int32),
        pltpu.VMEM((1, row_tokens), jnp.int32),
        pltpu.VMEM((1, row_tokens), jnp.float32),
    ]


def attention(qkv, attended, key_place, query_low, query_high, shift, turned, head, head_size):
    tokens, own_width = attended.shape
    scale = head_size ** (-0.5)
    keys_step = 256
    lanes = pl.ds(head * head_size, head_size)
    key_lanes = pl.ds(own_width + head * head_size, head_size)
    value_lanes = pl.ds(2 * own_width + head * head_size, head_size)
    turned[...] = jnp.zeros_like(turned)

    @pl.loop(0, tokens // keys_step)
    def _(step):
        rows = rows_at(step, keys_step)
        places = key_place[rows, :]
        allowed = (places >= query_low[...]) & (places <= query_high[...])
        scores = nt(qkv[rows, key_lanes], qkv[:, lanes]) * scale - shift[...]
        sig = jnp.where(allowed, jax.nn.sigmoid(scores), 0.0).astype(jnp.bfloat16)
        turned[...] += nn(qkv[rows, value_lanes].T, sig)

    attended[:, lanes] = turned[...].T.astype(jnp.bfloat16)


def forward_kernel(
    rows,
    seqs,
    head_size,
    x,
    g,
    wquery,
    wkey,
    wvalue,
    wgate,
    wup,
    wdown,
    wout,
    gains,
    lengths,
    gs,
    vgu,
    vdown,
    vout,
    h2,
    vqkv_kept,
    hn_kept,
    qkv_kept,
    attended_kept,
    middle_kept,
    gain_rows_out,
    vqkv,
    hn,
    qkv,
    attended,
    middle,
    xs,
    vgains,
    heads,
    turned,
    out_held,
    h2_own,
    key_place,
    query_low,
    query_high,
    shift,
    copies,
    sems,
):
    p, pool = Place(rows, seqs), Sems(sems)
    greet(p.peers() + p.rows())
    tokens, width = x.shape
    half = tokens // 2
    own_width = heads.shape[1]
    deep = wout.shape[0]
    down_blocks = vdown.shape[1]

    def part(source, target, c, arrived_aside=None):
        piece = pl.ds(c * half, half)
        return SeqGather(p, pool, source.at[piece], lambda b: target.at[b, piece], no_op, arrived_aside)

    def norm_half(c):
        def run(block):
            for b in (block, block + 1 - 2 * lax.rem(block, 2)):
                start = pl.multiple_of(b * tokens + c * half, half)
                norm_rows(xs.at[b, pl.ds(c * half, half)], hn.at[pl.ds(start, half), :], gain_rows_out.at[0:1, :])

        return run

    qkv_rows = RowForward(p, pool, seqs, lambda r, b: vqkv.at[r, b])
    gu_rows = RowForward(p, pool, seqs, lambda r, b: vgu.at[r, b])
    down_fwd = RowForward(p, pool, down_blocks, lambda r, b: vdown.at[r, b])
    out_rows = RowForward(p, pool, seqs, lambda r, b: vout.at[r, b])
    gain_rows = RowForward(p, pool, 1, lambda r, b: vgains.at[r])
    x_parts = [part(x, xs, c, norm_half(c)) for c in range(2)]
    g_parts = [part(g, gs, c) for c in range(2)]
    h2_parts = [part(h2_own, h2, c) for c in range(2)]
    hidden_own = vgu.shape[3] // 2
    hidden_block = hidden_own // rows

    def qkv_parts(t):
        for n, source in enumerate((wquery, wkey, wvalue)):
            target = vqkv.at[p.r, p.s, :, pl.ds(n * own_width, own_width)]
            yield columns(source, t, own_width), target

    def gu_parts(t):
        for n, source in enumerate((wgate, wup)):
            for r in range(rows):
                target = vgu.at[p.r, p.s, :, pl.ds(n * hidden_own + r * hidden_block, hidden_block)]
                yield columns(source, r * seqs + t, hidden_block), target

    qkv_swap = PartExchange(p, pool, qkv_parts, lambda b: vqkv.at[p.r, b], qkv_rows.forward)
    gu_swap = PartExchange(p, pool, gu_parts, lambda b: vgu.at[p.r, b], gu_rows.forward)
    out = SeqGather(p, pool, wout, lambda b: vout.at[p.r, b], out_rows.forward)
    gain = SeqExchange(p, pool, lambda t: gains, lambda b: vgains.at[p.r, b])
    heads_swap = SeqExchange(
        p, pool, lambda t: heads.at[rows_at(t, tokens), :], lambda b: columns(attended, b, own_width)
    )
    stores = Stores(pool)

    gain.start()
    for member in x_parts:
        member.start()
    qkv_swap.start()
    out.start()
    for step in range(1, seqs):
        gain.step(step)
    gain.finish()
    gain_rows.forward(0)
    qkv_swap.settle_own()
    qkv_rows.forward(p.s)
    out_rows.forward(p.s, wout)
    stores.start(wdown, vdown.at[p.r])
    for block in range(down_blocks):
        down_fwd.forward(block, wdown.at[block])
    gain_rows.relay(0)
    gain_rows.finish()
    for pair in range(rows * seqs // 2):
        tile = vgains[2 * pair // seqs, 2 * pair % seqs] + vgains[2 * pair // seqs, 2 * pair % seqs + 1]
        gain_rows_out[:, pl.ds(pair * 2 * deep, 2 * deep)] = tile

    fill_meta(lengths, key_place, query_low, query_high, shift, tokens, seqs)
    for member in x_parts:
        member.settle_own()
    for k in range(1, p.n_hi):
        for member in x_parts:
            member.step(k)
    for step in range(1, seqs):
        qkv_swap.step(step)
    for k in range(1, p.n_hi):
        out.step(k)
    gu_swap.start()
    gu_swap.settle_own()
    gu_rows.forward(p.s)
    for k in range(p.n_hi):
        for member in x_parts:
            member.aside(k)
    for member in g_parts:
        member.start()
    for block in range(seqs):
        qkv_rows.relay(block)
    for k in range(p.n_hi):
        out.aside(k)
    qkv_swap.finish()
    qkv_rows.finish()
    stores.start(hn, hn_kept)
    stores.start(vqkv, vqkv_kept)

    weights = vqkv.reshape(width, 3 * own_width)

    @pl.loop(0, seqs // 2)
    def _(step):
        tall = rows_at(step, 2 * tokens)
        qkv[tall, :] = nn(hn[tall, :], weights[...]).astype(jnp.bfloat16)

    stores.start(qkv, qkv_kept)
    own_heads = own_width // head_size
    for head in range(own_heads):
        attention(qkv, heads, key_place, query_low, query_high, shift, turned, head, head_size)
    heads_swap.start()
    for block in range(seqs):
        out_rows.relay(block)
    for member in g_parts:
        member.step(1)
    out.finish()
    out_rows.finish()
    for r in range(rows):
        pltpu.make_async_copy(vout.at[r], out_held.at[r], copies.at[r]).start()
    for step in range(1, seqs):
        heads_swap.step(step)
    heads_swap.finish()
    for r in range(rows):
        settle(out_held.at[r], copies.at[r])
    out_weights = out_held.reshape(width, width)

    @pl.loop(0, width // 512)
    def _(c):
        lanes = rows_at(c, 512)
        middle[:, lanes] = xs[p.s, :, lanes].astype(jnp.float32) + nn(attended[...], out_weights[:, lanes])

    norm_rows(middle, h2_own, gain_rows_out.at[4:5, :])
    stores.start(attended, attended_kept)
    stores.start(middle, middle_kept)
    for member in h2_parts:
        member.start()
    for step in range(1, seqs):
        gu_swap.step(step)
    for k in range(2, p.n_hi):
        for member in g_parts:
            member.step(k)
        for member in h2_parts:
            member.step(k - 1)
    for member in h2_parts:
        member.step(p.n_hi - 1)
    for block in range(down_blocks):
        down_fwd.relay(block)
    for block in range(seqs):
        gu_rows.relay(block)
    for k in range(p.n_hi):
        for member in g_parts + h2_parts:
            member.aside(k)
    for member in x_parts + g_parts + h2_parts + [gu_swap, down_fwd, gu_rows]:
        member.finish()
    stores.finish()


def forward(rows, seqs, head_size, x, g, qkv_weights, gu_weights, wdown, wout, gains, lengths):
    low, f32 = jnp.bfloat16, jnp.float32
    tokens, width = x.shape
    wdown = wdown.reshape(4, wdown.shape[0] // 4, width)
    own_width = width // seqs
    row_tokens = tokens * seqs
    deep = wout.shape[0]
    hidden_own = gu_weights[0].shape[1] // seqs
    shapes = (
        shape_of((seqs, tokens, width)),
        shape_of((rows, seqs, deep, 2 * hidden_own)),
        shape_of((rows,) + wdown.shape),
        shape_of((rows, seqs) + wout.shape),
        shape_of((seqs, tokens, width)),
        shape_of((rows, seqs, deep, 3 * own_width)),
        shape_of((row_tokens, width)),
        shape_of((row_tokens, 3 * own_width)),
        shape_of((tokens, width)),
        shape_of((tokens, width), f32),
        shape_of((8, width), f32),
    )
    scratch = [pltpu.VMEM(member.shape, member.dtype) for member in shapes[5:10]] + [
        pltpu.VMEM((seqs, tokens, width), low),
        pltpu.VMEM((rows, seqs) + gains.shape, f32),
        pltpu.VMEM((row_tokens, own_width), low),
        pltpu.VMEM((head_size, row_tokens), f32),
        pltpu.VMEM((rows, seqs) + wout.shape, low),
        pltpu.VMEM((tokens, width), low),
        *meta_scratch(row_tokens),
        pltpu.SemaphoreType.DMA((rows,)),
    ]
    return call(
        functools.partial(forward_kernel, rows, seqs, head_size),
        shapes,
        1,
        (x, g) + qkv_weights + gu_weights + (wdown, wout, gains, lengths),
        [pltpu.VMEM] * 10 + [pltpu.SMEM],
        (pl.ANY,) * 10 + (pltpu.VMEM,),
        scratch,
        800,
    )


def seq_reducers(place, pool, source, side, chain, target):
    half = target.shape[0] // 2
    members = []
    for c in range(2):
        piece = pl.ds(c * half, half)
        members.append(
            SeqReduce(
                place,
                pool,
                lambda b, piece=piece: source.at[b, piece],
                lambda b, piece=piece: side.at[b, piece],
                lambda slot, piece=piece: chain.at[slot, piece],
                target.at[piece],
            )
        )
    return members


def row_reducer(place, pool, source, core_slots, y_slots, target, add=add_into):
    return RowReduce(
        place,
        pool,
        source.shape[1],
        lambda r, b: source.at[r, b],
        lambda w, b: core_slots.at[w, b],
        lambda b: y_slots.at[b],
        lambda b: target.at[b],
        add,
    )


def ffn_kernel(
    rows,
    seqs,
    h2_in,
    gu_in,
    down_in,
    g_in,
    h2_kept,
    out_kept,
    gu_kept,
    down_kept,
    h2_sum,
    out_sum,
    gu_sum,
    down_sum,
    h2,
    gu_weights,
    down_weights,
    g,
    hidden,
    gu_grad,
    h2_part,
    h2_side,
    h2_chain,
    out_part,
    out_side,
    out_chain,
    gu_core,
    down_core,
    loads,
    sems,
):
    p, pool = Place(rows, seqs), Sems(sems)
    pairs = ((h2_in, h2), (gu_in, gu_weights), (g_in, g), (down_in, down_weights))
    for number, (source, target) in enumerate(pairs):
        pltpu.make_async_copy(source, target, loads.at[number]).start()
    greet(p.chain() + p.rows())
    tokens, width = h2_sum.shape
    hidden_own = hidden.shape[1]
    low = jnp.bfloat16
    h2_parts = seq_reducers(p, pool, h2_part, h2_side, h2_chain, h2_sum)
    out_parts = seq_reducers(p, pool, out_part, out_side, out_chain, out_sum)
    deep, down_deep = gu_sum.shape[1], down_sum.shape[1]

    def gu_at(r, b):
        return gu_weights.at[pl.ds(pl.multiple_of((r * seqs + b) * deep, deep), deep), :]

    def down_at(r, b):
        return down_weights.at[pl.ds(pl.multiple_of((r * down_sum.shape[0] + b) * down_deep, down_deep), down_deep), :]

    gu_rows = RowReduce(
        p, pool, seqs, gu_at, lambda w, b: gu_core.at[w, b], lambda b: gu_sum.at[b], lambda b: gu_sum.at[b]
    )
    down_rows = RowReduce(
        p,
        pool,
        down_sum.shape[0],
        down_at,
        lambda w, b: down_core.at[w, b],
        lambda b: down_sum.at[b],
        lambda b: down_sum.at[b],
    )
    for number, (source, target) in enumerate(pairs):
        settle(target, loads.at[number])

    def products(t):
        tall = rows_at(h2_parts[0].turn(t), 2 * tokens)

        @pl.loop(0, hidden_own // 256)
        def _(c):
            lanes, up_lanes = rows_at(c, 256), pl.ds(pl.multiple_of(hidden_own + c * 256, 256), 256)
            gate, up = nn(h2[tall, :], gu_weights[:, lanes]), nn(h2[tall, :], gu_weights[:, up_lanes])
            grad = nt(g[tall, :], down_weights[lanes, :])
            sig = jax.nn.sigmoid(gate)
            silu = gate * sig
            hidden[tall, lanes] = (silu * up).astype(low)
            gu_grad[tall, lanes] = (grad * up * (sig + silu * (1.0 - sig))).astype(low)
            gu_grad[tall, up_lanes] = (grad * silu).astype(low)

    def send_out(t):
        pair = h2_parts[0].turn(t)
        tall = rows_at(pair, 2 * tokens)

        @pl.loop(0, width // 512)
        def _(c):
            lanes = rows_at(c, 512)
            part = nn(hidden[tall, :], down_weights[:, lanes]).astype(low)
            out_part[2 * pair, :, lanes] = part[:tokens]
            out_part[2 * pair + 1, :, lanes] = part[tokens:]

        for member in out_parts:
            member.start(t)

    def send_h2(t):
        pair = h2_parts[0].turn(t)
        tall = rows_at(pair, 2 * tokens)

        @pl.loop(0, width // 512)
        def _(c):
            lanes = rows_at(c, 512)
            part = nt(gu_grad[tall, :], gu_weights[lanes, :]).astype(low)
            h2_part[2 * pair, :, lanes] = part[:tokens]
            h2_part[2 * pair + 1, :, lanes] = part[tokens:]

        for member in h2_parts:
            member.start(t)

    def sums(t, parts=None):
        for member in out_parts + h2_parts if parts is None else parts:
            member.step(t)

    def down_quarter(r):
        lanes = rows_at(r, hidden_own // rows)
        down_weights[lanes, :] = tn(hidden[:, lanes], g[...]).astype(low)

    def gu_quarter(r):
        @pl.loop(0, 2)
        def _(c):
            lanes = rows_at(2 * r + c, width // (2 * rows))
            gu_weights[lanes, :] = tn(h2[:, lanes], gu_grad[...]).astype(low)

    down_blocks, gu_blocks = range(down_sum.shape[0]), range(seqs)
    early = p.n_hi // 2
    for t in range(p.n_hi):
        products(t)
        send_out(t)
        if t < early:
            send_h2(t)
    sums(0, out_parts)
    down_quarter(p.r_far)
    for b in down_blocks:
        down_rows.start_far(b)
    down_quarter(p.r_core)
    for b in down_blocks:
        down_rows.start_core(b)
    down_quarter(p.r_y)
    for b in down_blocks:
        down_rows.step(b)
    for t in range(early, p.n_hi):
        send_h2(t)
    sums(0, h2_parts)
    gu_quarter(p.r_far)
    for b in gu_blocks:
        gu_rows.start_far(b)
    gu_quarter(p.r_y)
    for b in gu_blocks:
        gu_rows.step(b)
    gu_quarter(p.r_core)
    for b in gu_blocks:
        gu_rows.start_core(b)
    if p.n_hi > 2:
        sums(1)
    down_quarter(p.r)
    gu_quarter(p.r)
    for t in range(2 if p.n_hi > 2 else 1, p.n_hi):
        sums(t)
    stores = Stores(pool)
    stores.start(out_sum, out_kept)
    stores.start(h2_sum, h2_kept)
    for b in down_blocks:
        down_rows.close(b)
        stores.start(down_sum.at[b], down_kept.at[b])
    for b in gu_blocks:
        gu_rows.close(b)
        stores.start(gu_sum.at[b], gu_kept.at[b])
    for member in h2_parts + out_parts + [gu_rows, down_rows, stores]:
        member.finish()


def slots(array, copies=()):
    return pltpu.VMEM(copies + array.shape[1:], array.dtype)


def seq_slots(array):
    half = array.shape[0] // 2
    return [
        pltpu.VMEM((half,) + array.shape[1:], array.dtype),
        pltpu.VMEM((half + 1,) + array.shape[1:], array.dtype),
    ]


def row_slots(array):
    return [slots(array, (2,)), slots(array)]


def row_blocks(rows, array, count):
    return array.reshape(rows, count, array.shape[0] // (rows * count), array.shape[1])


def ffn(rows, seqs, h2, wgu, wdown, g):
    low, f32 = jnp.bfloat16, jnp.float32
    row_tokens, width = h2.shape
    tokens, hidden_own = row_tokens // seqs, wdown.shape[0]
    gu_dims, down_dims = (seqs, width // (rows * seqs), 2 * hidden_own), (4, hidden_own // (4 * rows), width)
    part = shape_of((seqs, tokens, width))
    shapes = (shape_of((tokens, width), f32), shape_of((tokens, width), f32), shape_of(gu_dims), shape_of(down_dims))
    scratch = (
        [pltpu.VMEM(member.shape, member.dtype) for member in shapes]
        + [pltpu.VMEM(array.shape, low) for array in (h2, wgu, wdown, g)]
        + [pltpu.VMEM((row_tokens, hidden_own), low), pltpu.VMEM((row_tokens, 2 * hidden_own), low)]
        + [pltpu.VMEM(part.shape, low)]
        + seq_slots(part)
        + [pltpu.VMEM(part.shape, low)]
        + seq_slots(part)
        + [pltpu.VMEM((2,) + gu_dims, low), pltpu.VMEM((2,) + down_dims, low)]
        + [pltpu.SemaphoreType.DMA((4,))]
    )
    return call(
        functools.partial(ffn_kernel, rows, seqs),
        shapes,
        4,
        (h2, wgu, wdown, g),
        [pl.ANY] * 4,
        (pl.ANY,) * 4,
        scratch,
        320,
    )


class ColumnExchange:
    def __init__(self, place, sems, piece, parts):
        self.p, self.piece, self.parts = place, piece, parts
        n = place.seq_count
        self.own, self.send, self.recv = sems.take(1), sems.take(n), sems.take(n)

    def start(self, first=0, last=None):
        p, s = self.p, self.p.s
        for step in range(first, p.seq_count if last is None else last):
            t = p.peer(step)
            piece = self.piece(t)
            for offset, width, target in self.parts(s):
                source = piece.at[:, pl.ds(offset, width)]
                if step == 0:
                    pltpu.make_async_copy(source, target, self.own(0)).start()
                else:
                    push(source, target, self.send(step), self.recv(s), (p.r, t))

    def finish(self):
        p = self.p
        settle(self.piece(p.s), self.own(0))
        for step in range(1, p.seq_count):
            settle(self.piece(p.s), self.send(step))
            settle(self.piece(p.s), self.recv(p.peer(step)))


def attention_back(qkv, do, dqkv, key_place, query_low, query_high, shift, dq_turned, head_size):
    tokens, own_width = do.shape
    scale = head_size ** (-0.5)
    keys_step = 256
    for head in range(own_width // head_size):
        lanes = pl.ds(head * head_size, head_size)
        key_lanes = pl.ds(own_width + head * head_size, head_size)
        value_lanes = pl.ds(2 * own_width + head * head_size, head_size)
        dq_turned[...] = jnp.zeros_like(dq_turned)

        @pl.loop(0, tokens // keys_step)
        def _(step):
            rows = pl.ds(pl.multiple_of(step * keys_step, keys_step), keys_step)
            key, value = qkv[rows, key_lanes], qkv[rows, value_lanes]
            queries, grads = qkv[:, lanes], do[:, lanes]
            places = key_place[rows, :]
            allowed = (places >= query_low[...]) & (places <= query_high[...])
            scores = nt(key, queries) * scale - shift[...]
            sig = jnp.where(allowed, jax.nn.sigmoid(scores), 0.0)
            score_grad = (nt(value, grads) * sig * (1.0 - sig)).astype(jnp.bfloat16)
            dqkv[rows, value_lanes] = nn(sig.astype(jnp.bfloat16), grads).astype(jnp.bfloat16)
            dqkv[rows, key_lanes] = (nn(score_grad, queries) * scale).astype(jnp.bfloat16)
            dq_turned[...] += nn(key.T, score_grad)

        dqkv[:, lanes] = (dq_turned[...].T * scale).astype(jnp.bfloat16)


def middle_back(middle, h2_grad, g, gain, middle_grad, branch, gain_part):
    gain_part[...] = jnp.zeros_like(gain_part)

    @pl.loop(0, middle.shape[0] // 16)
    def _(tile):
        rows = rows_at(tile, 16)
        values, grads = middle[rows, :], h2_grad[rows, :]
        inverse = lax.rsqrt(jnp.mean(values * values, axis=-1, keepdims=True) + EPSILON)
        terms = grads * values * inverse
        gain_part[...] += terms[:8] + terms[8:]
        scaled = gain[...] * grads
        total = (
            g[rows, :].astype(jnp.float32)
            + inverse * scaled
            - values * inverse**3 * jnp.mean(scaled * values, axis=-1, keepdims=True)
        )
        middle_grad[rows, :] = total
        branch[rows, :] = total.astype(branch.dtype)


def back_kernel(
    rows,
    seqs,
    head_size,
    middle,
    h2_grad,
    g,
    attended,
    gain_values,
    lengths,
    gu,
    wout_in,
    qkv_in,
    hn_in,
    wqkv_in,
    hn_sum,
    out_sum,
    query_got,
    key_got,
    value_got,
    gate_got,
    up_got,
    gain_got,
    middle_kept,
    do,
    dqkv,
    dq_turned,
    hn_side,
    hn_chain,
    grad_qkv,
    qkv_core,
    qkv_y,
    out_core,
    out_y,
    out_side,
    out_chain,
    gains,
    gain_core,
    gain_y,
    qkv,
    hn,
    wqkv,
    wout,
    out,
    do_own,
    branch,
    middle_grad,
    key_place,
    query_low,
    query_high,
    shift,
    loads,
    sems,
):
    p, pool = Place(rows, seqs), Sems(sems)
    pairs = ((wout_in, wout), (qkv_in, qkv), (wqkv_in, wqkv), (hn_in, hn))
    for number, (source, target) in enumerate(pairs):
        pltpu.make_async_copy(source, target, loads.at[number]).start()
    greet(p.peers() + p.rows())
    stores = Stores(pool)
    tokens, own_width = do.shape
    block_tokens = tokens // seqs
    width = wqkv.shape[0]
    hn_part = wout.at[pl.ds(0, tokens), :].reshape(seqs, block_tokens, width)

    def block_rows(b):
        return pl.ds(pl.multiple_of(b * block_tokens, block_tokens), block_tokens)

    do_swap = SeqExchange(
        p, pool, lambda t: columns(do_own, t, own_width), lambda b: do.at[block_rows(b), :]
    )
    deep = width // (rows * seqs)
    out_rows = RowReduce(
        p,
        pool,
        seqs,
        lambda r, b: out.at[pl.ds(pl.multiple_of((r * seqs + b) * deep, deep), deep), :],
        lambda w, b: out_core.at[w, b],
        lambda b: out_y.at[b],
        lambda b: out_y.at[b],
    )
    hidden_own = gu.shape[2] // 2
    block = hidden_own // rows

    def gu_parts(s):
        for n, target in ((0, gate_got), (1, up_got)):
            for r in range(rows):
                yield n * hidden_own + r * block, block, columns(target, r * seqs + s, block)

    gu_swap = ColumnExchange(p, pool, lambda t: gu.at[t], gu_parts)

    def qkv_parts(s):
        for n, target in enumerate((query_got, key_got, value_got)):
            yield n * own_width, own_width, columns(target, s, own_width)

    qkv_swap = ColumnExchange(p, pool, lambda t: qkv_y.at[t], qkv_parts)
    qkv_rows = row_reducer(p, pool, grad_qkv, qkv_core, qkv_y, qkv_y)
    hn_parts = seq_reducers(p, pool, hn_part, hn_side, hn_chain, hn_sum)
    out_seq = SeqReduce(
        p, pool, lambda b: out_y.at[b], lambda b: out_side.at[b], lambda slot: out_chain.at[slot], out_sum
    )
    quarter = width // rows
    gain_rows = RowReduce(
        p,
        pool,
        1,
        lambda r, b: columns(gains, r, quarter),
        lambda w, b: gain_core.at[w],
        lambda b: gain_y,
        lambda b: gain_y,
        add_small,
    )
    gain_width = 2 * quarter // seqs
    gain_swap = SeqExchange(
        p, pool, lambda t: columns(gain_y, t // 2, gain_width), lambda b: gain_got.at[b]
    )

    gu_swap.start(0, 3)
    middle_back(middle, h2_grad, g, gain_values.at[4:5, :], middle_grad, branch, gains.at[8:16, :])
    stores.start(middle_grad, middle_kept)
    settle(wout, loads.at[0])

    @pl.loop(0, width // 512)
    def _(c):
        lanes = rows_at(c, 512)
        do_own[:, lanes] = nt(branch[...], wout[lanes, :]).astype(jnp.bfloat16)

    do_swap.start()

    def out_quarter(r):
        @pl.loop(0, 2)
        def _(c):
            lanes = rows_at(2 * r + c, width // (2 * rows))
            out[lanes, :] = tn(attended[:, lanes], branch[...]).astype(jnp.bfloat16)

    out_quarter(p.r_far)
    for b in range(seqs):
        out_rows.start_far(b)
    out_quarter(p.r_y)
    out_quarter(p.r_core)
    for b in range(seqs):
        out_rows.start_core(b)
    fill_meta(lengths, key_place, query_low, query_high, shift, block_tokens, seqs)
    for b in range(seqs):
        out_rows.step(b)
    for step in range(1, seqs):
        do_swap.step(step)
    settle(do.at[block_rows(p.s), :], do_swap.own(0))
    gu_swap.start(3, seqs)
    out_quarter(p.r)
    settle(qkv, loads.at[1])
    attention_back(qkv, do, dqkv, key_place, query_low, query_high, shift, dq_turned, head_size)

    for number in (2, 3):
        settle(pairs[number][1], loads.at[number])
    gains[0:8, :] = jnp.zeros_like(gains[0:8, :])
    column_step = 512
    for t in range(p.n_hi):
        pair = hn_parts[0].turn(t)
        tall = pl.ds(pl.multiple_of(pair * 2 * block_tokens, 2 * block_tokens), 2 * block_tokens)

        @pl.loop(0, width // column_step)
        def _(c):
            lanes = pl.ds(pl.multiple_of(c * column_step, column_step), column_step)
            part = nt(dqkv[tall, :], wqkv[lanes, :])
            hn_part[2 * pair, :, lanes] = part[:block_tokens].astype(jnp.bfloat16)
            hn_part[2 * pair + 1, :, lanes] = part[block_tokens:].astype(jnp.bfloat16)
            terms = part * hn[tall, lanes].astype(jnp.float32)
            gains[0:8, lanes] += jnp.sum(terms.reshape(-1, 8, column_step), axis=0)

        for member in hn_parts:
            member.start(t)
    gains[0:8, :] = gains[0:8, :] / gain_values[0:1, :]
    gain_rows.start(0)

    @pl.loop(0, width // 256)
    def _(c):
        lanes = pl.ds(pl.multiple_of(c * 256, 256), 256)
        total = tn(hn[:, lanes], dqkv[...]).astype(jnp.bfloat16)
        piece = total.reshape((4,) + (total.shape[0] // 4, total.shape[1]))
        for n in range(4):
            grad_qkv[c * 4 // seqs, lax.rem(c * 4, seqs) + n] = piece[n]

    for b in range(seqs):
        qkv_rows.start(b)
    gain_rows.step(0)
    for t in range(p.n_hi):
        for member in hn_parts:
            member.step(t)
        if t == 0:
            for b in range(seqs):
                qkv_rows.step(b)
            gain_rows.close(0)
            gain_swap.start()
        if t == p.n_hi // 2 - 1:
            for b in range(seqs):
                out_rows.close(b)
            for k in range(p.n_hi):
                out_seq.start(k)
        if t == p.n_hi - 2:
            for b in range(seqs):
                qkv_rows.close(b)
            qkv_swap.start()
    for t in range(p.n_hi):
        out_seq.step(t)
    for step in range(1, seqs):
        gain_swap.step(step)
        settle(do.at[block_rows(p.s), :], do_swap.send(step))
    for member in hn_parts + [out_rows, qkv_rows, gain_rows, gu_swap, qkv_swap, out_seq, gain_swap, stores]:
        member.finish()


def back(rows, seqs, head_size, middle, h2_grad, g, attended, gain_values, lengths, gu, wout, qkv, hn, wqkv):
    tokens, own_width = qkv.shape[0], qkv.shape[1] // 3
    width = hn.shape[1]
    low, f32 = jnp.bfloat16, jnp.float32
    block_tokens = tokens // seqs
    deep = width // (rows * seqs)
    quarter = width // rows
    hn_dims, qkv_dims = (seqs, block_tokens, width), (rows, seqs, deep, 3 * own_width)
    got = shape_of((deep, width))
    gu_got = shape_of((deep, gu.shape[2] // 2 * seqs))
    gain_width = 2 * quarter // seqs
    shapes = (
        shape_of(hn_dims[1:], f32),
        got,
        got,
        got,
        got,
        gu_got,
        gu_got,
        shape_of((seqs, 16, gain_width), f32),
        shape_of(hn_dims[1:], f32),
    )
    qkv_like, out_like = shape_of(qkv_dims), shape_of((rows, seqs, deep, width))
    scratch = (
        [
            pltpu.VMEM((tokens, own_width), low),
            pltpu.VMEM(qkv.shape, low),
            pltpu.VMEM((head_size, tokens), f32),
        ]
        + seq_slots(shape_of(hn_dims))
        + [pltpu.VMEM(qkv_dims, low)]
        + row_slots(qkv_like)
        + row_slots(out_like)
        + seq_slots(shape_of(out_like.shape[1:]))
        + [pltpu.VMEM((16, width), f32), pltpu.VMEM((2, 16, quarter), f32), pltpu.VMEM((16, quarter), f32)]
        + [pltpu.VMEM(array.shape, low) for array in (qkv, hn, wqkv, wout)]
        + [pltpu.VMEM((width, width), low)]
        + [pltpu.VMEM(hn_dims[1:], low), pltpu.VMEM(hn_dims[1:], low), pltpu.VMEM(hn_dims[1:], f32)]
        + meta_scratch(tokens)
        + [pltpu.SemaphoreType.DMA((4,))]
    )
    return call(
        functools.partial(back_kernel, rows, seqs, head_size),
        shapes,
        6,
        (middle, h2_grad, g, attended, gain_values, lengths, gu, wout, qkv, hn, wqkv),
        [pltpu.VMEM] * 5 + [pltpu.SMEM, pltpu.VMEM] + [pl.ANY] * 4,
        (pltpu.VMEM,) * 5 + (pl.ANY,) * 2 + (pltpu.VMEM, pl.ANY),
        scratch,
        480,
    )


def ending_kernel(
    middle, out_sum, middle_grad, hn_grad, x, gain, query, key, value, out, gate, up, down, *results
):
    output, input_grad = results[:2]
    for source, target in zip((query, key, value, out, gate, up, down), results[2:]):
        target[...] = source[...].astype(target.dtype)
    output[...] = (middle[...] + out_sum[...]).astype(output.dtype)
    values = x[...].astype(jnp.float32)
    inverse = lax.rsqrt(jnp.mean(values * values, axis=-1, keepdims=True) + EPSILON)
    scaled = gain[...] * hn_grad[...]
    input_grad[...] = (
        middle_grad[...]
        + inverse * scaled
        - values * inverse**3 * jnp.mean(scaled * values, axis=-1, keepdims=True)
    )


def ending(middle, out_sum, middle_grad, hn_grad, x, gain, gradients):
    steps = 4
    f32 = jnp.float32

    def blocks(array):
        return pl.BlockSpec((array.shape[0] // steps, array.shape[1]), lambda n: (n, 0))

    args = (middle, out_sum, middle_grad, hn_grad, x)
    shapes = (shape_of(middle.shape), shape_of(middle.shape, f32)) + tuple(
        shape_of(member.shape, f32) for member in gradients
    )
    return pl.pallas_call(
        ending_kernel,
        grid=(steps,),
        out_shape=shapes,
        in_specs=[blocks(member) for member in args]
        + [pl.BlockSpec(gain.shape, lambda n: (0, 0))]
        + [blocks(member) for member in gradients],
        out_specs=tuple(blocks(member) for member in shapes),
        compiler_params=pltpu.CompilerParams(vmem_limit_bytes=VMEM_BYTES),
    )(*args, gain, *gradients)


def split_local(
    rows,
    seqs,
    inputs,
    lengths,
    w_query,
    w_key,
    w_value,
    w_out,
    gain_attn,
    w_gate,
    w_up,
    w_down,
    gain_mlp,
    cotangent,
):
    low, f32 = jnp.bfloat16, jnp.float32
    tokens, width = inputs.shape[1], inputs.shape[2]
    deep = w_query.shape[0]
    row_tokens = tokens * seqs
    head_size = width // HEADS
    own_width = width // seqs
    hidden_own = w_gate.shape[1] // seqs

    side = lax.rem(lax.axis_index("seq"), 2)
    lane = lax.broadcasted_iota(jnp.int32, (8, 2 * deep), 1)
    both = [jnp.concatenate([gain, gain]).astype(f32)[None, :] for gain in (gain_attn, gain_mlp)]
    number = lax.broadcasted_iota(jnp.int32, (8, 2 * deep), 0)
    gains_own = jnp.where(lane // deep == side, jnp.where(number < 4, both[0], both[1]), 0.0)
    x_low, g_low = inputs[0], cotangent[0]

    g_all, wgu, wdown, wout, h2, wqkv, hn, qkv, attended, middle, gains = forward(
        rows,
        seqs,
        head_size,
        x_low,
        g_low,
        (w_query, w_key, w_value),
        (w_gate, w_up),
        w_down,
        w_out,
        gains_own,
        lengths,
    )
    gain_one = gains[0:1]
    wqkv = wqkv.reshape(width, 3 * own_width)
    wgu = wgu.reshape(width, 2 * hidden_own)
    wdown = wdown.reshape(hidden_own, width)
    wout = wout.reshape(width, width)
    g_all = g_all.reshape(row_tokens, width)
    h2 = h2.reshape(row_tokens, width)
    h2_grad, out_sum, sum_gu, sum_down = ffn(rows, seqs, h2, wgu, wdown, g_all)

    hn_grad, sum_out, got_query, got_key, got_value, got_gate, got_up, got_gain, middle_grad = back(
        rows, seqs, head_size, middle, h2_grad, g_low, attended, gains, lengths, sum_gu, wout, qkv, hn, wqkv
    )
    gradients = (got_query, got_key, got_value, sum_out, got_gate, got_up, sum_down.reshape(w_down.shape))
    output, input_grad, *gradients = ending(middle, out_sum, middle_grad, hn_grad, x_low, gain_one, gradients)
    gain_sums = jnp.sum(got_gain, axis=0).reshape(2, 8, 2, deep).sum(axis=1)
    gain_sums = lax.dynamic_index_in_dim(gain_sums, lax.rem(lax.axis_index("seq"), 2), 1, keepdims=False)
    grad_query, grad_key, grad_value, grad_out, grad_gate, grad_up, grad_down = gradients
    return (
        output[None],
        input_grad[None],
        grad_query,
        grad_key,
        grad_value,
        grad_out,
        gain_sums[0],
        grad_gate,
        grad_up,
        grad_down,
        gain_sums[1],
    )


def solution(mesh):
    placed = (
        P("row", "seq", None),
        P("row", None),
        P(("row", "seq"), None),
        P(("row", "seq"), None),
        P(("row", "seq"), None),
        P(("row", "seq"), None),
        P(("row", "seq")),
        P(("row", "seq"), None),
        P(("row", "seq"), None),
        P(("row", "seq"), None),
        P(("row", "seq")),
        P("row", "seq", None),
    )
    row_count, seq_count = mesh.shape["row"], mesh.shape["seq"]
    if row_count == 4 and seq_count % 2 == 0 and HEADS % seq_count == 0:
        local = functools.partial(split_local, row_count, seq_count)
    else:
        local = gathered_local
    return jax.shard_map(
        local,
        mesh=mesh,
        in_specs=placed,
        out_specs=(
            P("row", "seq", None),
            P("row", "seq", None),
            P(("row", "seq"), None),
            P(("row", "seq"), None),
            P(("row", "seq"), None),
            P(("row", "seq"), None),
            P(("row", "seq")),
            P(("row", "seq"), None),
            P(("row", "seq"), None),
            P(("row", "seq"), None),
            P(("row", "seq")),
        ),
        check_vma=False,
    )
```

```python
import functools

import jax
import jax.numpy as jnp
from jax import lax
from jax.experimental import pallas as pl
from jax.experimental.pallas import tpu as pltpu
from jax.sharding import PartitionSpec as P

HEADS = 16


EPSILON = 1e-05


def layout(lengths_row, places, block_rows, block_count):
    unit_counts = lengths_row // (2 * block_count)
    span_sizes = 2 * unit_counts
    offsets = jnp.cumsum(span_sizes) - span_sizes
    device = places // block_rows
    within_block = places - device * block_rows
    inside = (
        (within_block[:, None] >= offsets[None, :])
        & (within_block[:, None] < (offsets + span_sizes)[None, :])
    ).astype(jnp.int32)
    numbers = jnp.arange(lengths_row.shape[0], dtype=jnp.int32)
    segment = jnp.sum(inside * numbers[None, :], axis=1)
    unit_of = jnp.sum(inside * unit_counts[None, :], axis=1)
    begins = jnp.sum(inside * offsets[None, :], axis=1)
    length_of = jnp.sum(inside * lengths_row[None, :], axis=1)
    within = within_block - begins
    position = jnp.where(
        within < unit_of,
        device * unit_of + within,
        (2 * block_count - 1 - device) * unit_of + within - unit_of,
    )
    return (segment, position, length_of)


def rms_norm(values, gain):
    return values * lax.rsqrt(jnp.mean(values * values, axis=-1, keepdims=True) + EPSILON) * gain


def sigmoid_terms(query_heads, query_meta, key_heads, key_meta):
    query_segment, query_position, query_length = query_meta
    key_segment, key_position, unused_length = key_meta
    scores = jnp.einsum(
        "qhd,khd->hqk", query_heads, key_heads, preferred_element_type=jnp.float32
    ) * query_heads.shape[2] ** (-0.5)
    scores = scores - jnp.log(query_length.astype(jnp.float32))[None, :, None]
    allowed = (query_segment[:, None] == key_segment[None, :]) & (
        key_position[None, :] <= query_position[:, None]
    )
    return jnp.where(allowed[None], jax.nn.sigmoid(scores), 0.0)


def pair_terms(query_heads, query_meta, grad_heads, key_heads, key_meta, value_heads):
    sig_terms = sigmoid_terms(query_heads, query_meta, key_heads, key_meta)
    slopes = jnp.einsum("qhd,khd->hqk", grad_heads, value_heads, preferred_element_type=jnp.float32)
    score_grad = (slopes * sig_terms * (1.0 - sig_terms)).astype(jnp.bfloat16)
    return (sig_terms.astype(jnp.bfloat16), score_grad)


def by_blocks(step_fn, running, pieces, block_rows):
    size_total = pieces[0].shape[0]
    part_rows = 4 * block_rows
    block_count = size_total // part_rows

    def turn_over(step_number, carried):
        sub_pieces = tuple(
            (
                lax.dynamic_slice_in_dim(member, step_number * part_rows, part_rows, 0)
                for member in pieces
            )
        )
        return step_fn(carried, sub_pieces, step_number * part_rows)

    return lax.fori_loop(0, block_count, turn_over, running)


def gathered_local(
    inputs,
    lengths,
    w_query,
    w_key,
    w_value,
    w_out,
    gain_attn,
    w_gate,
    w_up,
    w_down,
    gain_mlp,
    cotangent,
):
    residual = inputs[0].astype(jnp.float32)
    tokens_here = residual.shape[0]
    model_width = residual.shape[1]
    head_size = model_width // HEADS
    score_scale = head_size ** (-0.5)
    block_total = lax.axis_size("seq")
    lengths_row = lengths[0]
    places = lax.axis_index("seq") * tokens_here + jnp.arange(tokens_here, dtype=jnp.int32)
    own_meta = layout(lengths_row, places, tokens_here, block_total)

    def meta_at(start_row, row_count):
        return layout(
            lengths_row,
            start_row + jnp.arange(row_count, dtype=jnp.int32),
            tokens_here,
            block_total,
        )

    def heads_of(matrix):
        return matrix.reshape(matrix.shape[0], HEADS, head_size)

    query_full, key_full, value_full, out_full, gain_one = (
        lax.all_gather(w_query, ("row", "seq"), axis=0, tiled=True),
        lax.all_gather(w_key, ("row", "seq"), axis=0, tiled=True),
        lax.all_gather(w_value, ("row", "seq"), axis=0, tiled=True),
        lax.all_gather(w_out, ("row", "seq"), axis=0, tiled=True),
        lax.all_gather(gain_attn, ("row", "seq"), axis=0, tiled=True),
    )
    gain_one_f = gain_one.astype(jnp.float32)
    normed = rms_norm(residual, gain_one_f).astype(jnp.bfloat16)
    queries = jnp.dot(normed, query_full, preferred_element_type=jnp.float32).astype(jnp.bfloat16)
    key_rows = jnp.dot(normed, key_full, preferred_element_type=jnp.float32).astype(jnp.bfloat16)
    value_rows = jnp.dot(normed, value_full, preferred_element_type=jnp.float32).astype(
        jnp.bfloat16
    )
    query_heads = heads_of(queries)

    def forward_step(running, pieces, start_row):
        key_piece, value_piece = pieces
        sig_terms = sigmoid_terms(
            query_heads, own_meta, heads_of(key_piece), meta_at(start_row, key_piece.shape[0])
        ).astype(jnp.bfloat16)
        added = jnp.einsum(
            "hqk,khd->qhd", sig_terms, heads_of(value_piece), preferred_element_type=jnp.float32
        )
        return running + added.reshape(tokens_here, model_width)

    attended = by_blocks(
        forward_step,
        jnp.zeros((tokens_here, model_width), jnp.float32),
        (
            lax.all_gather(key_rows, "seq", axis=0, tiled=True),
            lax.all_gather(value_rows, "seq", axis=0, tiled=True),
        ),
        tokens_here,
    )
    attended_low = attended.astype(jnp.bfloat16)
    middle = residual + jnp.dot(attended_low, out_full, preferred_element_type=jnp.float32)
    gate_full, up_full, down_full, gain_two = (
        lax.all_gather(w_gate, ("row", "seq"), axis=0, tiled=True),
        lax.all_gather(w_up, ("row", "seq"), axis=0, tiled=True),
        lax.all_gather(w_down, ("row", "seq"), axis=0, tiled=True),
        lax.all_gather(gain_mlp, ("row", "seq"), axis=0, tiled=True),
    )
    gain_two_f = gain_two.astype(jnp.float32)
    normed_mlp = rms_norm(middle, gain_two_f).astype(jnp.bfloat16)
    gate_vals = jnp.dot(normed_mlp, gate_full, preferred_element_type=jnp.float32)
    up_vals = jnp.dot(normed_mlp, up_full, preferred_element_type=jnp.float32)
    gated_prod, gated_back = jax.vjp(
        lambda gate_in, up_in: jax.nn.silu(gate_in) * up_in, gate_vals, up_vals
    )
    hidden = gated_prod.astype(jnp.bfloat16)
    output = (middle + jnp.dot(hidden, down_full, preferred_element_type=jnp.float32)).astype(
        jnp.bfloat16
    )
    upstream_low = cotangent[0]
    upstream = upstream_low.astype(jnp.float32)
    gate_full, up_full, down_full, gain_two = (
        lax.all_gather(w_gate, ("row", "seq"), axis=0, tiled=True),
        lax.all_gather(w_up, ("row", "seq"), axis=0, tiled=True),
        lax.all_gather(w_down, ("row", "seq"), axis=0, tiled=True),
        lax.all_gather(gain_mlp, ("row", "seq"), axis=0, tiled=True),
    )
    gain_two_f = gain_two.astype(jnp.float32)
    grad_down = jnp.dot(hidden.T, upstream_low, preferred_element_type=jnp.float32)
    shared_down = lax.psum_scatter(grad_down, ("row", "seq"), scatter_dimension=0, tiled=True)
    hidden_grad = jnp.dot(upstream_low, down_full.T, preferred_element_type=jnp.float32)
    gate_grad, up_grad = gated_back(hidden_grad)
    gate_low = gate_grad.astype(jnp.bfloat16)
    up_low = up_grad.astype(jnp.bfloat16)
    grad_gate = jnp.dot(normed_mlp.T, gate_low, preferred_element_type=jnp.float32)
    shared_gate = lax.psum_scatter(grad_gate, ("row", "seq"), scatter_dimension=0, tiled=True)
    normed_grad = jnp.dot(gate_low, gate_full.T, preferred_element_type=jnp.float32) + jnp.dot(
        up_low, up_full.T, preferred_element_type=jnp.float32
    )
    unused_mid, second_back = jax.vjp(rms_norm, middle, gain_two_f)
    middle_part, gain_two_grad = second_back(normed_grad)
    middle_grad = upstream + middle_part
    grad_up = jnp.dot(normed_mlp.T, up_low, preferred_element_type=jnp.float32)
    shared_up, shared_gain_two = (
        lax.psum_scatter(grad_up, ("row", "seq"), scatter_dimension=0, tiled=True),
        lax.psum_scatter(gain_two_grad, ("row", "seq"), scatter_dimension=0, tiled=True),
    )
    query_full, key_full, value_full, out_full, gain_one = (
        lax.all_gather(w_query, ("row", "seq"), axis=0, tiled=True),
        lax.all_gather(w_key, ("row", "seq"), axis=0, tiled=True),
        lax.all_gather(w_value, ("row", "seq"), axis=0, tiled=True),
        lax.all_gather(w_out, ("row", "seq"), axis=0, tiled=True),
        lax.all_gather(gain_attn, ("row", "seq"), axis=0, tiled=True),
    )
    gain_one_f = gain_one.astype(jnp.float32)
    branch_low = middle_grad.astype(jnp.bfloat16)
    grad_out = jnp.dot(attended_low.T, branch_low, preferred_element_type=jnp.float32)
    attended_grad = jnp.dot(branch_low, out_full.T, preferred_element_type=jnp.float32).astype(
        jnp.bfloat16
    )
    grad_heads = heads_of(attended_grad)
    key_heads_own = heads_of(key_rows)
    value_heads_own = heads_of(value_rows)

    def query_step(running, pieces, start_row):
        key_piece, value_piece = pieces
        key_piece_heads = heads_of(key_piece)
        unused_terms, score_grad = pair_terms(
            query_heads,
            own_meta,
            grad_heads,
            key_piece_heads,
            meta_at(start_row, key_piece.shape[0]),
            heads_of(value_piece),
        )
        added = jnp.einsum(
            "hqk,khd->qhd", score_grad, key_piece_heads, preferred_element_type=jnp.float32
        )
        return running + added.reshape(tokens_here, model_width) * score_scale

    start_value = jnp.zeros((tokens_here, model_width), jnp.float32)
    folded = by_blocks(
        query_step,
        start_value,
        (
            lax.all_gather(key_rows, "seq", axis=0, tiled=True),
            lax.all_gather(value_rows, "seq", axis=0, tiled=True),
        ),
        tokens_here,
    )

    def key_step(running, pieces, start_row):
        key_sum, value_sum = running
        query_piece, grad_piece = pieces
        row_count = query_piece.shape[0]
        query_piece_heads = heads_of(query_piece)
        grad_piece_heads = heads_of(grad_piece)
        sig_low, score_grad = pair_terms(
            query_piece_heads,
            meta_at(start_row, row_count),
            grad_piece_heads,
            key_heads_own,
            own_meta,
            value_heads_own,
        )
        key_add = jnp.einsum(
            "hqk,qhd->khd", score_grad, query_piece_heads, preferred_element_type=jnp.float32
        )
        value_add = jnp.einsum(
            "hqk,qhd->khd", sig_low, grad_piece_heads, preferred_element_type=jnp.float32
        )
        return (
            key_sum + key_add.reshape(tokens_here, model_width) * score_scale,
            value_sum + value_add.reshape(tokens_here, model_width),
        )

    empty_rows = jnp.zeros((tokens_here, model_width), jnp.float32)
    key_grad, value_grad = by_blocks(
        key_step,
        (empty_rows, empty_rows),
        (
            lax.all_gather(queries, "seq", axis=0, tiled=True),
            lax.all_gather(attended_grad, "seq", axis=0, tiled=True),
        ),
        tokens_here,
    )
    query_low = folded.astype(jnp.bfloat16)
    key_low = key_grad.astype(jnp.bfloat16)
    value_low = value_grad.astype(jnp.bfloat16)
    grad_query = jnp.dot(normed.T, query_low, preferred_element_type=jnp.float32)
    grad_key = jnp.dot(normed.T, key_low, preferred_element_type=jnp.float32)
    grad_value = jnp.dot(normed.T, value_low, preferred_element_type=jnp.float32)
    normed_back = jnp.dot(query_low, query_full.T, preferred_element_type=jnp.float32)
    normed_back = normed_back + jnp.dot(key_low, key_full.T, preferred_element_type=jnp.float32)
    normed_back = normed_back + jnp.dot(value_low, value_full.T, preferred_element_type=jnp.float32)
    unused_first, first_back = jax.vjp(rms_norm, residual, gain_one_f)
    residual_part, gain_one_grad = first_back(normed_back)
    input_grad = middle_grad + residual_part
    shared_query, shared_key, shared_value, shared_out, shared_gain_one = (
        lax.psum_scatter(grad_query, ("row", "seq"), scatter_dimension=0, tiled=True),
        lax.psum_scatter(grad_key, ("row", "seq"), scatter_dimension=0, tiled=True),
        lax.psum_scatter(grad_value, ("row", "seq"), scatter_dimension=0, tiled=True),
        lax.psum_scatter(grad_out, ("row", "seq"), scatter_dimension=0, tiled=True),
        lax.psum_scatter(gain_one_grad, ("row", "seq"), scatter_dimension=0, tiled=True),
    )
    return (
        output[None],
        input_grad[None],
        shared_query,
        shared_key,
        shared_value,
        shared_out,
        shared_gain_one,
        shared_gate,
        shared_up,
        shared_down,
        shared_gain_two,
    )


MESH = pl.DeviceIdType.MESH
VMEM_BYTES = 62 * 1024 * 1024


class Place:
    def __init__(self, row_count, seq_count):
        self.row_count, self.seq_count = row_count, seq_count
        self.r, self.s = lax.axis_index("row"), lax.axis_index("seq")
        self.n_hi = seq_count // 2
        self.hi, self.lo = self.s // 2, lax.rem(self.s, 2)
        self.r_core = self.r + 1 - 2 * lax.rem(self.r, 2)
        self.r_y = lax.rem(self.r + 2, 4)
        self.r_far = lax.rem(self.r_core + 2, 4)
        self.side = (self.r, self.s + 1 - 2 * self.lo)
        self.up = (self.r, self.s + 2)
        self.down = (self.r, self.s - 2)
        self.core = (self.r_core, self.s)
        self.y = (self.r_y, self.s)
        self.has_up = self.hi < self.n_hi - 1
        self.has_down = self.hi > 0

    def peer(self, step):
        return lax.rem(self.s + step, self.seq_count)

    def chain(self):
        return [(None, self.side), (self.has_up, self.up), (self.has_down, self.down)]

    def peers(self):
        return [(None, (self.r, self.peer(step))) for step in range(1, self.seq_count)]

    def rows(self):
        return [(None, self.core), (None, self.y)]


def greet(devices):
    barrier = pltpu.get_barrier_semaphore()
    total = 0
    for condition, device in devices:
        if condition is None:
            pl.semaphore_signal(barrier, inc=1, device_id=device, device_id_type=MESH)
            total = total + 1
        else:

            @pl.when(condition)
            def _(device=device):
                pl.semaphore_signal(barrier, inc=1, device_id=device, device_id_type=MESH)

            total = total + condition.astype(jnp.int32)
    pl.semaphore_wait(barrier, total)


class Sems:
    def __init__(self, ref):
        self.ref, self.used = ref, 0

    def take(self, count):
        base = self.used
        self.used += count
        assert self.used <= self.ref.shape[0], self.used
        return lambda index: self.ref.at[base + index]


def push(source, target, send, recv, device):
    pltpu.make_async_remote_copy(
        src_ref=source, dst_ref=target, send_sem=send, recv_sem=recv, device_id=device, device_id_type=MESH
    ).start()


def settle(ref, sem):
    pltpu.make_async_copy(ref, ref, sem).wait()


def no_op(block):
    return None


class Stores:
    def __init__(self, sems):
        self.sems, self.open = sems, []

    def start(self, source, target):
        sem = self.sems.take(1)(0)
        pltpu.make_async_copy(source, target, sem).start()
        self.open.append((target, sem))

    def finish(self):
        for target, sem in self.open:
            settle(target, sem)


class SeqGather:
    def __init__(self, place, sems, source, at, arrived=no_op, arrived_aside=None):
        self.p, self.source, self.at, self.arrived = place, source, at, arrived
        self.arrived_aside = arrived_aside or arrived
        self.own_done = False
        n = place.n_hi
        self.own, self.up, self.down = sems.take(1), sems.take(n), sems.take(n)
        self.side, self.recv = sems.take(n), sems.take(2 * n)

    def start(self):
        p, s = self.p, self.p.s
        pltpu.make_async_copy(self.source, self.at(s), self.own(0)).start()

        @pl.when(p.has_up)
        def _():
            push(self.source, self.at(s), self.up(0), self.recv(s), p.up)

        @pl.when(p.has_down)
        def _():
            push(self.source, self.at(s), self.down(0), self.recv(s), p.down)

        push(self.source, self.at(s), self.side(p.hi), self.recv(s), p.side)

    def step(self, k):
        p = self.p

        @pl.when(p.hi >= k)
        def _():
            block = p.s - 2 * k
            settle(self.at(block), self.recv(block))

            @pl.when(p.has_up)
            def _():
                push(self.at(block), self.at(block), self.up(k), self.recv(block), p.up)

            push(self.at(block), self.at(block), self.side(p.hi - k), self.recv(block), p.side)
            self.arrived(block)

        @pl.when(p.hi + k < p.n_hi)
        def _():
            block = p.s + 2 * k
            settle(self.at(block), self.recv(block))

            @pl.when(p.has_down)
            def _():
                push(self.at(block), self.at(block), self.down(k), self.recv(block), p.down)

            push(self.at(block), self.at(block), self.side(p.hi + k), self.recv(block), p.side)
            self.arrived(block)

    def aside(self, k):
        p = self.p
        if k == 0:
            block = 2 * p.hi + 1 - p.lo
            settle(self.at(block), self.recv(block))
            self.arrived_aside(block)
            return

        @pl.when(p.hi >= k)
        def _():
            block = 2 * (p.hi - k) + 1 - p.lo
            settle(self.at(block), self.recv(block))
            self.arrived_aside(block)

        @pl.when(p.hi + k < p.n_hi)
        def _():
            block = 2 * (p.hi + k) + 1 - p.lo
            settle(self.at(block), self.recv(block))
            self.arrived_aside(block)

    def settle_own(self):
        settle(self.at(self.p.s), self.own(0))
        self.own_done = True

    def finish(self):
        p = self.p
        if not self.own_done:
            self.settle_own()
        for k in range(p.n_hi):

            @pl.when(p.has_up & (p.hi >= k))
            def _():
                settle(self.source, self.up(k))

            @pl.when(p.has_down & (p.hi + k < p.n_hi))
            def _():
                settle(self.source, self.down(k))

            settle(self.source, self.side(k))


class SeqExchange:
    def __init__(self, place, sems, piece, at, arrived=no_op):
        self.p, self.piece, self.at, self.arrived = place, piece, at, arrived
        self.own_done = False
        n = place.seq_count
        self.own, self.send, self.recv = sems.take(1), sems.take(n), sems.take(n)

    def start_own(self):
        s = self.p.s
        pltpu.make_async_copy(self.piece(s), self.at(s), self.own(0)).start()

    def start_one(self, step):
        p, s = self.p, self.p.s
        t = p.peer(step)
        push(self.piece(t), self.at(s), self.send(step), self.recv(s), (p.r, t))

    def start(self):
        self.start_own()
        for step in range(1, self.p.seq_count):
            self.start_one(step)

    def step(self, step):
        block = self.p.peer(self.p.seq_count - step)
        settle(self.at(block), self.recv(block))
        self.arrived(block)

    def finish(self):
        p = self.p
        settle(self.at(p.s), self.own(0))
        for step in range(1, p.seq_count):
            settle(self.at(p.s), self.send(step))


class PartExchange(SeqExchange):
    def __init__(self, place, sems, parts, at, arrived=no_op):
        super().__init__(place, sems, None, at, arrived)
        self.parts = parts

    def start_own(self):
        s = self.p.s
        for source, target in self.parts(s):
            pltpu.make_async_copy(source, target, self.own(0)).start()

    def start(self):
        p, s = self.p, self.p.s
        self.start_own()
        for step in range(1, p.seq_count):
            t = p.peer(step)
            for source, target in self.parts(t):
                push(source, target, self.send(step), self.recv(s), (p.r, t))

    def settle_own(self):
        settle(self.at(self.p.s), self.own(0))
        self.own_done = True

    def finish(self):
        p = self.p
        if not self.own_done:
            self.settle_own()
        for step in range(1, p.seq_count):
            settle(self.at(p.s), self.send(step))


class RowForward:
    def __init__(self, place, sems, blocks, at):
        self.p, self.at, self.blocks = place, at, blocks
        self.core, self.y, self.far = sems.take(blocks), sems.take(blocks), sems.take(blocks)
        self.from_core, self.from_y, self.from_far = sems.take(blocks), sems.take(blocks), sems.take(blocks)

    def forward(self, block, source=None):
        p = self.p
        source = self.at(p.r, block) if source is None else source
        push(source, self.at(p.r, block), self.y(block), self.from_y(block), p.y)
        push(source, self.at(p.r, block), self.core(block), self.from_core(block), p.core)

    def relay(self, block):
        p = self.p
        settle(self.at(p.r_y, block), self.from_y(block))
        push(self.at(p.r_y, block), self.at(p.r_y, block), self.far(block), self.from_far(block), p.core)

    def finish(self):
        p = self.p
        for block in range(self.blocks):
            settle(self.at(p.r_core, block), self.from_core(block))
            settle(self.at(p.r_far, block), self.from_far(block))
            settle(self.at(p.r, block), self.core(block))
            settle(self.at(p.r, block), self.y(block))
            settle(self.at(p.r_y, block), self.far(block))


def add_into(target, *sources):
    @pl.loop(0, target.shape[0] // 16)
    def _(tile):
        rows = pl.ds(pl.multiple_of(tile * 16, 16), 16)
        total = sources[0][rows, :].astype(jnp.float32)
        for source in sources[1:]:
            total = total + source[rows, :].astype(jnp.float32)
        target[rows, :] = total.astype(target.dtype)


def add_small(target, *sources):
    total = sources[0][...].astype(jnp.float32)
    for source in sources[1:]:
        total = total + source[...].astype(jnp.float32)
    target[...] = total.astype(target.dtype)


class SeqReduce:
    def __init__(self, place, sems, at, side_slot, chain_slot, target, add=add_into):
        self.p, self.at, self.add, self.target = place, at, add, target
        self.side_slot, self.chain_slot = side_slot, chain_slot
        n = place.n_hi
        self.side, self.from_side = sems.take(n), sems.take(n)
        self.send, self.recv = sems.take(n), sems.take(2 * n)

    def above_slot(self, block, hi):
        return self.chain_slot(jnp.where(block == hi, self.p.n_hi, block))

    def turn(self, t):
        return self.turn_of(self.p, t)

    @staticmethod
    def turn_of(p, t):
        n, hi = p.n_hi, p.hi
        low = jnp.where(t < n - 1 - hi, n - 1 - t, t - (n - 1 - hi))
        high = jnp.where(t < hi, t, n - 1 - (t - hi))
        return jnp.where(hi < n // 2, low, high)

    def start(self, t):
        p, block = self.p, self.turn(t)
        push(self.at(2 * block + 1 - p.lo), self.side_slot(block), self.side(block), self.from_side(block), p.side)

    def step(self, t):
        p, n, block = self.p, self.p.n_hi, self.turn(t)
        mine, got = self.at(2 * block + p.lo), self.side_slot(block)
        settle(got, self.from_side(block))
        if t == n - 1:
            return self.close()

        @pl.when(block > p.hi)
        def _():
            @pl.when(p.has_down)
            def _():
                settle(got, self.recv(block))
                self.add(got, mine, got, self.chain_slot(block))

            @pl.when(jnp.logical_not(p.has_down))
            def _():
                self.add(got, mine, got)

            push(got, self.chain_slot(block), self.send(block), self.recv(block), p.up)

        @pl.when(block < p.hi)
        def _():
            @pl.when(p.has_up)
            def _():
                settle(got, self.recv(n + block))
                self.add(got, mine, got, self.above_slot(block, p.hi))

            @pl.when(jnp.logical_not(p.has_up))
            def _():
                self.add(got, mine, got)

            push(got, self.above_slot(block, p.hi - 1), self.send(block), self.recv(n + block), p.down)

    def close(self):
        p, n, hi = self.p, self.p.n_hi, self.p.hi
        mine, got = self.at(p.s), self.side_slot(hi)
        below, above = self.chain_slot(hi), self.above_slot(hi, hi)

        @pl.when(p.has_down)
        def _():
            settle(got, self.recv(hi))

        @pl.when(p.has_up)
        def _():
            settle(got, self.recv(n + hi))

        @pl.when(p.has_down & p.has_up)
        def _():
            self.add(self.target, mine, got, below, above)

        @pl.when(p.has_down & jnp.logical_not(p.has_up))
        def _():
            self.add(self.target, mine, got, below)

        @pl.when(jnp.logical_not(p.has_down))
        def _():
            self.add(self.target, mine, got, above)

    def finish(self):
        p = self.p
        for block in range(p.n_hi):
            settle(self.side_slot(block), self.side(block))

            @pl.when(p.hi != block)
            def _():
                settle(self.side_slot(block), self.send(block))


class RowReduce:
    def __init__(self, place, sems, blocks, at, core_slot, y_slot, target, add=add_into, own=None):
        self.p, self.at, self.add, self.target = place, at, add, target
        self.own = own or (lambda w, b: at((place.r_y, place.r)[w], b))
        self.core_slot, self.y_slot, self.blocks = core_slot, y_slot, blocks
        self.send, self.recv = sems.take(2 * blocks), sems.take(2 * blocks)
        self.y, self.from_y = sems.take(blocks), sems.take(blocks)

    def start_far(self, block):
        p = self.p
        push(self.at(p.r_far, block), self.core_slot(0, block), self.send(block), self.recv(block), p.core)

    def start_core(self, block):
        p, n = self.p, self.blocks
        push(self.at(p.r_core, block), self.core_slot(1, block), self.send(n + block), self.recv(n + block), p.core)

    def start(self, block):
        self.start_far(block)
        self.start_core(block)

    def step(self, block):
        p = self.p
        got = self.core_slot(0, block)
        settle(got, self.recv(block))
        self.add(got, self.own(0, block), got)
        push(got, self.y_slot(block), self.y(block), self.from_y(block), p.y)

    def close(self, block):
        p = self.p
        settle(self.core_slot(1, block), self.recv(self.blocks + block))
        settle(self.y_slot(block), self.from_y(block))
        self.add(self.target(block), self.own(1, block), self.core_slot(1, block), self.y_slot(block))

    def finish(self):
        n = self.blocks
        for block in range(n):
            settle(self.core_slot(0, block), self.send(block))
            settle(self.core_slot(1, block), self.send(n + block))
            settle(self.core_slot(0, block), self.y(block))


def columns(ref, index, width):
    return ref.at[:, pl.ds(pl.multiple_of(index * width, width), width)]


def call(kernel, shapes, ident, args, spaces, out_spaces, scratch, sems):
    return pl.pallas_call(
        kernel,
        out_shape=shapes,
        in_specs=[pl.BlockSpec(memory_space=space) for space in spaces],
        out_specs=jax.tree.map(lambda space: pl.BlockSpec(memory_space=space), out_spaces),
        scratch_shapes=list(scratch) + [pltpu.SemaphoreType.DMA((sems,))],
        compiler_params=pltpu.CompilerParams(
            collective_id=ident, has_side_effects=True, vmem_limit_bytes=VMEM_BYTES
        ),
    )(*args)


def shape_of(dims, dtype=jnp.bfloat16):
    return jax.ShapeDtypeStruct(dims, dtype)


def nt(left, right):
    return lax.dot_general(left, right, (((1,), (1,)), ((), ())), preferred_element_type=jnp.float32)


def tn(left, right):
    return lax.dot_general(left, right, (((0,), (0,)), ((), ())), preferred_element_type=jnp.float32)


def nn(left, right):
    return lax.dot_general(left, right, (((1,), (0,)), ((), ())), preferred_element_type=jnp.float32)


def rows_at(index, count):
    return pl.ds(pl.multiple_of(index * count, count), count)


def norm_rows(source, target, gain):
    @pl.loop(0, source.shape[0] // 16)
    def _(tile):
        rows = rows_at(tile, 16)
        values = source[rows, :].astype(jnp.float32)
        target[rows, :] = rms_norm(values, gain[...]).astype(target.dtype)


def places(lengths, shape, axis, tokens, seqs):
    row_tokens = tokens * seqs
    index = lax.broadcasted_iota(jnp.int32, shape, axis)
    block, within = index // tokens, lax.rem(index, tokens)
    segment = position = length_of = jnp.zeros_like(index)
    begin = 0
    for n in range(lengths.shape[1]):
        length = lengths[0, n]
        unit = length // (2 * seqs)
        inside = (within >= begin) & (within < begin + 2 * unit)
        local = within - begin
        here = jnp.where(local < unit, block * unit + local, (2 * seqs - 1 - block) * unit + local - unit)
        segment = jnp.where(inside, n, segment)
        position = jnp.where(inside, here, position)
        length_of = jnp.where(inside, length, length_of)
        begin = begin + 2 * unit
    return segment * row_tokens, segment * row_tokens + position, length_of


def fill_meta(lengths, key_place, query_low, query_high, shift, tokens, seqs):
    key_place[...] = places(lengths, key_place.shape, 0, tokens, seqs)[1]
    low, high, length_of = places(lengths, query_low.shape, 1, tokens, seqs)
    query_low[...] = low
    query_high[...] = high
    shift[...] = jnp.log(length_of.astype(jnp.float32))


def meta_scratch(row_tokens):
    return [
        pltpu.VMEM((row_tokens, 1), jnp.int32),
        pltpu.VMEM((1, row_tokens), jnp.int32),
        pltpu.VMEM((1, row_tokens), jnp.int32),
        pltpu.VMEM((1, row_tokens), jnp.float32),
    ]


def attention(qkv, attended, key_place, query_low, query_high, shift, turned, head, head_size):
    tokens, own_width = attended.shape
    scale = head_size ** (-0.5)
    keys_step = 256
    lanes = pl.ds(head * head_size, head_size)
    key_lanes = pl.ds(own_width + head * head_size, head_size)
    value_lanes = pl.ds(2 * own_width + head * head_size, head_size)
    turned[...] = jnp.zeros_like(turned)

    @pl.loop(0, tokens // keys_step)
    def _(step):
        rows = rows_at(step, keys_step)
        places = key_place[rows, :]
        allowed = (places >= query_low[...]) & (places <= query_high[...])
        scores = nt(qkv[rows, key_lanes], qkv[:, lanes]) * scale - shift[...]
        sig = jnp.where(allowed, jax.nn.sigmoid(scores), 0.0).astype(jnp.bfloat16)
        turned[...] += nn(qkv[rows, value_lanes].T, sig)

    attended[:, lanes] = turned[...].T.astype(jnp.bfloat16)


def forward_kernel(
    rows,
    seqs,
    head_size,
    x,
    g,
    wquery,
    wkey,
    wvalue,
    wgate,
    wup,
    wdown,
    wout,
    gains,
    lengths,
    gs,
    vgu,
    vdown,
    vout,
    h2,
    vqkv_kept,
    hn_kept,
    qkv_kept,
    attended_kept,
    middle_kept,
    gain_rows_out,
    vqkv,
    hn,
    qkv,
    attended,
    middle,
    xs,
    vgains,
    heads,
    turned,
    out_held,
    h2_own,
    key_place,
    query_low,
    query_high,
    shift,
    copies,
    sems,
):
    p, pool = Place(rows, seqs), Sems(sems)
    greet(p.peers() + p.rows())
    tokens, width = x.shape
    half = tokens // 2
    own_width = heads.shape[1]
    deep = wout.shape[0]
    down_blocks = vdown.shape[1]

    def part(source, target, c, arrived_aside=None):
        piece = pl.ds(c * half, half)
        return SeqGather(p, pool, source.at[piece], lambda b: target.at[b, piece], no_op, arrived_aside)

    def norm_half(c):
        def run(block):
            for b in (block, block + 1 - 2 * lax.rem(block, 2)):
                start = pl.multiple_of(b * tokens + c * half, half)
                norm_rows(xs.at[b, pl.ds(c * half, half)], hn.at[pl.ds(start, half), :], gain_rows_out.at[0:1, :])

        return run

    qkv_rows = RowForward(p, pool, seqs, lambda r, b: vqkv.at[r, b])
    gu_rows = RowForward(p, pool, seqs, lambda r, b: vgu.at[r, b])
    down_fwd = RowForward(p, pool, down_blocks, lambda r, b: vdown.at[r, b])
    out_rows = RowForward(p, pool, seqs, lambda r, b: vout.at[r, b])
    gain_rows = RowForward(p, pool, 1, lambda r, b: vgains.at[r])
    x_parts = [part(x, xs, c, norm_half(c)) for c in range(2)]
    g_parts = [part(g, gs, c) for c in range(2)]
    h2_parts = [part(h2_own, h2, c) for c in range(2)]
    hidden_own = vgu.shape[3] // 2
    hidden_block = hidden_own // rows

    def qkv_parts(t):
        for n, source in enumerate((wquery, wkey, wvalue)):
            target = vqkv.at[p.r, p.s, :, pl.ds(n * own_width, own_width)]
            yield columns(source, t, own_width), target

    def gu_parts(t):
        for n, source in enumerate((wgate, wup)):
            for r in range(rows):
                target = vgu.at[p.r, p.s, :, pl.ds(n * hidden_own + r * hidden_block, hidden_block)]
                yield columns(source, r * seqs + t, hidden_block), target

    qkv_swap = PartExchange(p, pool, qkv_parts, lambda b: vqkv.at[p.r, b], qkv_rows.forward)
    gu_swap = PartExchange(p, pool, gu_parts, lambda b: vgu.at[p.r, b], gu_rows.forward)
    out = SeqGather(p, pool, wout, lambda b: vout.at[p.r, b], out_rows.forward)
    gain = SeqExchange(p, pool, lambda t: gains, lambda b: vgains.at[p.r, b])
    heads_swap = SeqExchange(
        p, pool, lambda t: heads.at[rows_at(t, tokens), :], lambda b: columns(attended, b, own_width)
    )
    stores = Stores(pool)

    gain.start()
    for member in x_parts:
        member.start()
    qkv_swap.start()
    out.start()
    for step in range(1, seqs):
        gain.step(step)
    gain.finish()
    gain_rows.forward(0)
    qkv_swap.settle_own()
    qkv_rows.forward(p.s)
    out_rows.forward(p.s, wout)
    stores.start(wdown, vdown.at[p.r])
    for block in range(down_blocks):
        down_fwd.forward(block, wdown.at[block])
    gain_rows.relay(0)
    gain_rows.finish()
    for pair in range(rows * seqs // 2):
        tile = vgains[2 * pair // seqs, 2 * pair % seqs] + vgains[2 * pair // seqs, 2 * pair % seqs + 1]
        gain_rows_out[:, pl.ds(pair * 2 * deep, 2 * deep)] = tile

    fill_meta(lengths, key_place, query_low, query_high, shift, tokens, seqs)
    for member in x_parts:
        member.settle_own()
    for k in range(1, p.n_hi):
        for member in x_parts:
            member.step(k)
    for step in range(1, seqs):
        qkv_swap.step(step)
    for k in range(1, p.n_hi):
        out.step(k)
    gu_swap.start()
    gu_swap.settle_own()
    gu_rows.forward(p.s)
    for k in range(p.n_hi):
        for member in x_parts:
            member.aside(k)
    for member in g_parts:
        member.start()
    for block in range(seqs):
        qkv_rows.relay(block)
    for k in range(p.n_hi):
        out.aside(k)
    qkv_swap.finish()
    qkv_rows.finish()
    stores.start(hn, hn_kept)
    stores.start(vqkv, vqkv_kept)

    weights = vqkv.reshape(width, 3 * own_width)

    @pl.loop(0, seqs // 2)
    def _(step):
        tall = rows_at(step, 2 * tokens)
        qkv[tall, :] = nn(hn[tall, :], weights[...]).astype(jnp.bfloat16)

    stores.start(qkv, qkv_kept)
    own_heads = own_width // head_size
    for head in range(own_heads):
        attention(qkv, heads, key_place, query_low, query_high, shift, turned, head, head_size)
    heads_swap.start()
    for block in range(seqs):
        out_rows.relay(block)
    for member in g_parts:
        member.step(1)
    out.finish()
    out_rows.finish()
    for r in range(rows):
        pltpu.make_async_copy(vout.at[r], out_held.at[r], copies.at[r]).start()
    for step in range(1, seqs):
        heads_swap.step(step)
    heads_swap.finish()
    for r in range(rows):
        settle(out_held.at[r], copies.at[r])
    out_weights = out_held.reshape(width, width)

    @pl.loop(0, width // 512)
    def _(c):
        lanes = rows_at(c, 512)
        middle[:, lanes] = xs[p.s, :, lanes].astype(jnp.float32) + nn(attended[...], out_weights[:, lanes])

    norm_rows(middle, h2_own, gain_rows_out.at[4:5, :])
    stores.start(attended, attended_kept)
    stores.start(middle, middle_kept)
    for member in h2_parts:
        member.start()
    for step in range(1, seqs):
        gu_swap.step(step)
    for k in range(2, p.n_hi):
        for member in g_parts:
            member.step(k)
        for member in h2_parts:
            member.step(k - 1)
    for member in h2_parts:
        member.step(p.n_hi - 1)
    for block in range(down_blocks):
        down_fwd.relay(block)
    for block in range(seqs):
        gu_rows.relay(block)
    for k in range(p.n_hi):
        for member in g_parts + h2_parts:
            member.aside(k)
    for member in x_parts + g_parts + h2_parts + [gu_swap, down_fwd, gu_rows]:
        member.finish()
    stores.finish()


def forward(rows, seqs, head_size, x, g, qkv_weights, gu_weights, wdown, wout, gains, lengths):
    low, f32 = jnp.bfloat16, jnp.float32
    tokens, width = x.shape
    wdown = wdown.reshape(4, wdown.shape[0] // 4, width)
    own_width = width // seqs
    row_tokens = tokens * seqs
    deep = wout.shape[0]
    hidden_own = gu_weights[0].shape[1] // seqs
    shapes = (
        shape_of((seqs, tokens, width)),
        shape_of((rows, seqs, deep, 2 * hidden_own)),
        shape_of((rows,) + wdown.shape),
        shape_of((rows, seqs) + wout.shape),
        shape_of((seqs, tokens, width)),
        shape_of((rows, seqs, deep, 3 * own_width)),
        shape_of((row_tokens, width)),
        shape_of((row_tokens, 3 * own_width)),
        shape_of((tokens, width)),
        shape_of((tokens, width), f32),
        shape_of((8, width), f32),
    )
    scratch = [pltpu.VMEM(member.shape, member.dtype) for member in shapes[5:10]] + [
        pltpu.VMEM((seqs, tokens, width), low),
        pltpu.VMEM((rows, seqs) + gains.shape, f32),
        pltpu.VMEM((row_tokens, own_width), low),
        pltpu.VMEM((head_size, row_tokens), f32),
        pltpu.VMEM((rows, seqs) + wout.shape, low),
        pltpu.VMEM((tokens, width), low),
        *meta_scratch(row_tokens),
        pltpu.SemaphoreType.DMA((rows,)),
    ]
    return call(
        functools.partial(forward_kernel, rows, seqs, head_size),
        shapes,
        1,
        (x, g) + qkv_weights + gu_weights + (wdown, wout, gains, lengths),
        [pltpu.VMEM] * 10 + [pltpu.SMEM],
        (pl.ANY,) * 10 + (pltpu.VMEM,),
        scratch,
        800,
    )


def seq_reducers(place, pool, source, side, chain, target):
    half = target.shape[0] // 2
    members = []
    for c in range(2):
        piece = pl.ds(c * half, half)
        members.append(
            SeqReduce(
                place,
                pool,
                lambda b, piece=piece: source.at[b, piece],
                lambda b, piece=piece: side.at[b, piece],
                lambda slot, piece=piece: chain.at[slot, piece],
                target.at[piece],
            )
        )
    return members


def row_reducer(place, pool, source, core_slots, y_slots, target, add=add_into):
    return RowReduce(
        place,
        pool,
        source.shape[1],
        lambda r, b: source.at[r, b],
        lambda w, b: core_slots.at[w, b],
        lambda b: y_slots.at[b],
        lambda b: target.at[b],
        add,
    )


def ffn_kernel(
    rows,
    seqs,
    h2_in,
    gu_in,
    down_in,
    g_in,
    h2_kept,
    out_kept,
    gu_kept,
    down_kept,
    h2_sum,
    out_sum,
    gu_sum,
    down_sum,
    h2,
    gu_weights,
    down_weights,
    g,
    hidden,
    gu_grad,
    h2_part,
    h2_side,
    h2_chain,
    out_part,
    out_side,
    out_chain,
    gu_core,
    down_core,
    loads,
    sems,
):
    p, pool = Place(rows, seqs), Sems(sems)
    tokens, width = h2_sum.shape
    turns = [SeqReduce.turn_of(p, t) for t in range(p.n_hi)]
    talls = [rows_at(turn, 2 * tokens) for turn in turns]
    pairs = [(gu_in, gu_weights), (down_in, down_weights)]
    for tall in talls:
        pairs += [(h2_in.at[tall, :], h2.at[tall, :]), (g_in.at[tall, :], g.at[tall, :])]
    for number in [2, 0, 3, *(1, *range(4, len(pairs)))]:
        source, target = pairs[number]
        pltpu.make_async_copy(source, target, loads.at[number]).start()
    greet(p.chain() + p.rows())
    hidden_own = hidden.shape[1]
    low = jnp.bfloat16
    h2_parts = seq_reducers(p, pool, h2_part, h2_side, h2_chain, h2_sum)
    out_parts = seq_reducers(p, pool, out_part, out_side, out_chain, out_sum)
    deep, down_deep = gu_sum.shape[1], down_sum.shape[1]

    def gu_at(r, b):
        return gu_weights.at[pl.ds(pl.multiple_of((r * seqs + b) * deep, deep), deep), :]

    def down_at(r, b):
        return down_weights.at[pl.ds(pl.multiple_of((r * down_sum.shape[0] + b) * down_deep, down_deep), down_deep), :]

    gu_rows = RowReduce(
        p, pool, seqs, gu_at, lambda w, b: gu_core.at[w, b], lambda b: gu_sum.at[b], lambda b: gu_sum.at[b]
    )
    down_rows = RowReduce(
        p,
        pool,
        down_sum.shape[0],
        down_at,
        lambda w, b: down_core.at[w, b],
        lambda b: down_sum.at[b],
        lambda b: down_sum.at[b],
    )
    for number in range(2):
        settle(pairs[number][1], loads.at[number])

    def products(t):
        for number in (2 + 2 * t, 3 + 2 * t):
            settle(pairs[number][1], loads.at[number])
        tall = rows_at(h2_parts[0].turn(t), 2 * tokens)

        @pl.loop(0, hidden_own // 256)
        def _(c):
            lanes, up_lanes = rows_at(c, 256), pl.ds(pl.multiple_of(hidden_own + c * 256, 256), 256)
            gate, up = nn(h2[tall, :], gu_weights[:, lanes]), nn(h2[tall, :], gu_weights[:, up_lanes])
            grad = nt(g[tall, :], down_weights[lanes, :])
            sig = jax.nn.sigmoid(gate)
            silu = gate * sig
            hidden[tall, lanes] = (silu * up).astype(low)
            gu_grad[tall, lanes] = (grad * up * (sig + silu * (1.0 - sig))).astype(low)
            gu_grad[tall, up_lanes] = (grad * silu).astype(low)

    def send_out(t):
        pair = h2_parts[0].turn(t)
        tall = rows_at(pair, 2 * tokens)

        @pl.loop(0, width // 512)
        def _(c):
            lanes = rows_at(c, 512)
            part = nn(hidden[tall, :], down_weights[:, lanes]).astype(low)
            out_part[2 * pair, :, lanes] = part[:tokens]
            out_part[2 * pair + 1, :, lanes] = part[tokens:]

        for member in out_parts:
            member.start(t)

    def send_h2(t):
        pair = h2_parts[0].turn(t)
        tall = rows_at(pair, 2 * tokens)

        @pl.loop(0, width // 512)
        def _(c):
            lanes = rows_at(c, 512)
            part = nt(gu_grad[tall, :], gu_weights[lanes, :]).astype(low)
            h2_part[2 * pair, :, lanes] = part[:tokens]
            h2_part[2 * pair + 1, :, lanes] = part[tokens:]

        for member in h2_parts:
            member.start(t)

    def sums(t, parts=None):
        for member in out_parts + h2_parts if parts is None else parts:
            member.step(t)

    def down_quarter(r):
        lanes = rows_at(r, hidden_own // rows)
        down_weights[lanes, :] = tn(hidden[:, lanes], g[...]).astype(low)

    def gu_quarter(r):
        @pl.loop(0, 2)
        def _(c):
            lanes = rows_at(2 * r + c, width // (2 * rows))
            gu_weights[lanes, :] = tn(h2[:, lanes], gu_grad[...]).astype(low)

    down_blocks, gu_blocks = range(down_sum.shape[0]), range(seqs)
    early = p.n_hi // 2
    for t in range(p.n_hi):
        products(t)
        send_out(t)
        if t < early:
            send_h2(t)
    sums(0, out_parts)
    down_quarter(p.r_far)
    for b in down_blocks:
        down_rows.start_far(b)
    down_quarter(p.r_core)
    for b in down_blocks:
        down_rows.start_core(b)
    down_quarter(p.r_y)
    for b in down_blocks:
        down_rows.step(b)
    for t in range(early, p.n_hi):
        send_h2(t)
    sums(0, h2_parts)
    gu_quarter(p.r_far)
    for b in gu_blocks:
        gu_rows.start_far(b)
    gu_quarter(p.r_y)
    for b in gu_blocks:
        gu_rows.step(b)
    gu_quarter(p.r_core)
    for b in gu_blocks:
        gu_rows.start_core(b)
    if p.n_hi > 2:
        sums(1)
    down_quarter(p.r)
    gu_quarter(p.r)
    for t in range(2 if p.n_hi > 2 else 1, p.n_hi):
        sums(t)
    stores = Stores(pool)
    stores.start(out_sum, out_kept)
    stores.start(h2_sum, h2_kept)
    for b in down_blocks:
        down_rows.close(b)
        stores.start(down_sum.at[b], down_kept.at[b])
    for b in gu_blocks:
        gu_rows.close(b)
        stores.start(gu_sum.at[b], gu_kept.at[b])
    for member in h2_parts + out_parts + [gu_rows, down_rows, stores]:
        member.finish()


def slots(array, copies=()):
    return pltpu.VMEM(copies + array.shape[1:], array.dtype)


def seq_slots(array):
    half = array.shape[0] // 2
    return [
        pltpu.VMEM((half,) + array.shape[1:], array.dtype),
        pltpu.VMEM((half + 1,) + array.shape[1:], array.dtype),
    ]


def row_slots(array):
    return [slots(array, (2,)), slots(array)]


def row_blocks(rows, array, count):
    return array.reshape(rows, count, array.shape[0] // (rows * count), array.shape[1])


def ffn(rows, seqs, h2, wgu, wdown, g):
    low, f32 = jnp.bfloat16, jnp.float32
    row_tokens, width = h2.shape
    tokens, hidden_own = row_tokens // seqs, wdown.shape[0]
    gu_dims, down_dims = (seqs, width // (rows * seqs), 2 * hidden_own), (4, hidden_own // (4 * rows), width)
    part = shape_of((seqs, tokens, width))
    shapes = (shape_of((tokens, width), f32), shape_of((tokens, width), f32), shape_of(gu_dims), shape_of(down_dims))
    scratch = (
        [pltpu.VMEM(member.shape, member.dtype) for member in shapes]
        + [pltpu.VMEM(array.shape, low) for array in (h2, wgu, wdown, g)]
        + [pltpu.VMEM((row_tokens, hidden_own), low), pltpu.VMEM((row_tokens, 2 * hidden_own), low)]
        + [pltpu.VMEM(part.shape, low)]
        + seq_slots(part)
        + [pltpu.VMEM(part.shape, low)]
        + seq_slots(part)
        + [pltpu.VMEM((2,) + gu_dims, low), pltpu.VMEM((2,) + down_dims, low)]
        + [pltpu.SemaphoreType.DMA((2 + seqs,))]
    )
    return call(
        functools.partial(ffn_kernel, rows, seqs),
        shapes,
        4,
        (h2, wgu, wdown, g),
        [pl.ANY] * 4,
        (pl.ANY,) * 4,
        scratch,
        320,
    )


class ColumnExchange:
    def __init__(self, place, sems, piece, parts):
        self.p, self.piece, self.parts = place, piece, parts
        n = place.seq_count
        self.own, self.send, self.recv = sems.take(1), sems.take(n), sems.take(n)

    def start(self, first=0, last=None):
        p, s = self.p, self.p.s
        for step in range(first, p.seq_count if last is None else last):
            t = p.peer(step)
            piece = self.piece(t)
            for offset, width, target in self.parts(s):
                source = piece.at[:, pl.ds(offset, width)]
                if step == 0:
                    pltpu.make_async_copy(source, target, self.own(0)).start()
                else:
                    push(source, target, self.send(step), self.recv(s), (p.r, t))

    def finish(self):
        p = self.p
        settle(self.piece(p.s), self.own(0))
        for step in range(1, p.seq_count):
            settle(self.piece(p.s), self.send(step))
            settle(self.piece(p.s), self.recv(p.peer(step)))


def attention_back(qkv, do, dqkv, key_place, query_low, query_high, shift, dq_turned, head_size):
    tokens, own_width = do.shape
    scale = head_size ** (-0.5)
    keys_step = 256
    for head in range(own_width // head_size):
        lanes = pl.ds(head * head_size, head_size)
        key_lanes = pl.ds(own_width + head * head_size, head_size)
        value_lanes = pl.ds(2 * own_width + head * head_size, head_size)
        dq_turned[...] = jnp.zeros_like(dq_turned)

        @pl.loop(0, tokens // keys_step)
        def _(step):
            rows = pl.ds(pl.multiple_of(step * keys_step, keys_step), keys_step)
            key, value = qkv[rows, key_lanes], qkv[rows, value_lanes]
            queries, grads = qkv[:, lanes], do[:, lanes]
            places = key_place[rows, :]
            allowed = (places >= query_low[...]) & (places <= query_high[...])
            scores = nt(key, queries) * scale - shift[...]
            sig = jnp.where(allowed, jax.nn.sigmoid(scores), 0.0)
            score_grad = (nt(value, grads) * sig * (1.0 - sig)).astype(jnp.bfloat16)
            dqkv[rows, value_lanes] = nn(sig.astype(jnp.bfloat16), grads).astype(jnp.bfloat16)
            dqkv[rows, key_lanes] = (nn(score_grad, queries) * scale).astype(jnp.bfloat16)
            dq_turned[...] += nn(key.T, score_grad)

        dqkv[:, lanes] = (dq_turned[...].T * scale).astype(jnp.bfloat16)


def middle_back(middle, h2_grad, g, gain, middle_grad, branch, gain_part):
    gain_part[...] = jnp.zeros_like(gain_part)

    @pl.loop(0, middle.shape[0] // 16)
    def _(tile):
        rows = rows_at(tile, 16)
        values, grads = middle[rows, :], h2_grad[rows, :]
        inverse = lax.rsqrt(jnp.mean(values * values, axis=-1, keepdims=True) + EPSILON)
        terms = grads * values * inverse
        gain_part[...] += terms[:8] + terms[8:]
        scaled = gain[...] * grads
        total = (
            g[rows, :].astype(jnp.float32)
            + inverse * scaled
            - values * inverse**3 * jnp.mean(scaled * values, axis=-1, keepdims=True)
        )
        middle_grad[rows, :] = total
        branch[rows, :] = total.astype(branch.dtype)


def back_kernel(
    rows,
    seqs,
    head_size,
    middle,
    h2_grad,
    g,
    attended,
    gain_values,
    lengths,
    gu,
    wout_in,
    qkv_in,
    hn_in,
    wqkv_in,
    hn_sum,
    out_sum,
    query_got,
    key_got,
    value_got,
    gate_got,
    up_got,
    gain_got,
    middle_kept,
    do,
    dqkv,
    dq_turned,
    hn_side,
    hn_chain,
    grad_qkv,
    qkv_core,
    qkv_y,
    out_core,
    out_y,
    out_side,
    out_chain,
    gains,
    gain_core,
    gain_y,
    qkv,
    hn,
    wqkv,
    wout,
    out,
    do_own,
    branch,
    middle_grad,
    key_place,
    query_low,
    query_high,
    shift,
    loads,
    sems,
):
    p, pool = Place(rows, seqs), Sems(sems)
    pairs = ((wout_in, wout), (qkv_in, qkv), (wqkv_in, wqkv), (hn_in, hn))
    for number, (source, target) in enumerate(pairs):
        pltpu.make_async_copy(source, target, loads.at[number]).start()
    greet(p.peers() + p.rows())
    stores = Stores(pool)
    tokens, own_width = do.shape
    block_tokens = tokens // seqs
    width = wqkv.shape[0]
    hn_part = wout.at[pl.ds(0, tokens), :].reshape(seqs, block_tokens, width)

    def block_rows(b):
        return pl.ds(pl.multiple_of(b * block_tokens, block_tokens), block_tokens)

    do_swap = SeqExchange(
        p, pool, lambda t: columns(do_own, t, own_width), lambda b: do.at[block_rows(b), :]
    )
    deep = width // (rows * seqs)
    out_rows = RowReduce(
        p,
        pool,
        seqs,
        lambda r, b: out.at[pl.ds(pl.multiple_of((r * seqs + b) * deep, deep), deep), :],
        lambda w, b: out_core.at[w, b],
        lambda b: out_y.at[b],
        lambda b: out_y.at[b],
    )
    hidden_own = gu.shape[2] // 2
    block = hidden_own // rows

    def gu_parts(s):
        for n, target in ((0, gate_got), (1, up_got)):
            for r in range(rows):
                yield n * hidden_own + r * block, block, columns(target, r * seqs + s, block)

    gu_swap = ColumnExchange(p, pool, lambda t: gu.at[t], gu_parts)

    def qkv_parts(s):
        for n, target in enumerate((query_got, key_got, value_got)):
            yield n * own_width, own_width, columns(target, s, own_width)

    qkv_swap = ColumnExchange(p, pool, lambda t: qkv_y.at[t], qkv_parts)
    qkv_rows = row_reducer(p, pool, grad_qkv, qkv_core, qkv_y, qkv_y)
    hn_parts = seq_reducers(p, pool, hn_part, hn_side, hn_chain, hn_sum)
    out_seq = SeqReduce(
        p, pool, lambda b: out_y.at[b], lambda b: out_side.at[b], lambda slot: out_chain.at[slot], out_sum
    )
    quarter = width // rows
    gain_rows = RowReduce(
        p,
        pool,
        1,
        lambda r, b: columns(gains, r, quarter),
        lambda w, b: gain_core.at[w],
        lambda b: gain_y,
        lambda b: gain_y,
        add_small,
    )
    gain_width = 2 * quarter // seqs
    gain_swap = SeqExchange(
        p, pool, lambda t: columns(gain_y, t // 2, gain_width), lambda b: gain_got.at[b]
    )

    gu_swap.start(0, 3)
    middle_back(middle, h2_grad, g, gain_values.at[4:5, :], middle_grad, branch, gains.at[8:16, :])
    stores.start(middle_grad, middle_kept)
    settle(wout, loads.at[0])

    for step in [*range(1, seqs), 0]:
        lanes = rows_at(p.peer(step), own_width)
        do_own[:, lanes] = nt(branch[...], wout[lanes, :]).astype(jnp.bfloat16)
        do_swap.start_one(step) if step else do_swap.start_own()

    def out_quarter(r):
        @pl.loop(0, 2)
        def _(c):
            lanes = rows_at(2 * r + c, width // (2 * rows))
            out[lanes, :] = tn(attended[:, lanes], branch[...]).astype(jnp.bfloat16)

    out_quarter(p.r_far)
    for b in range(seqs):
        out_rows.start_far(b)
    out_quarter(p.r_y)
    out_quarter(p.r_core)
    for b in range(seqs):
        out_rows.start_core(b)
    fill_meta(lengths, key_place, query_low, query_high, shift, block_tokens, seqs)
    for b in range(seqs):
        out_rows.step(b)
    for step in range(1, seqs):
        do_swap.step(step)
    settle(do.at[block_rows(p.s), :], do_swap.own(0))
    gu_swap.start(3, seqs)
    out_quarter(p.r)
    settle(qkv, loads.at[1])
    attention_back(qkv, do, dqkv, key_place, query_low, query_high, shift, dq_turned, head_size)

    for number in (2, 3):
        settle(pairs[number][1], loads.at[number])
    gains[0:8, :] = jnp.zeros_like(gains[0:8, :])
    column_step = 512
    for t in range(p.n_hi):
        pair = hn_parts[0].turn(t)
        tall = pl.ds(pl.multiple_of(pair * 2 * block_tokens, 2 * block_tokens), 2 * block_tokens)

        @pl.loop(0, width // column_step)
        def _(c):
            lanes = pl.ds(pl.multiple_of(c * column_step, column_step), column_step)
            part = nt(dqkv[tall, :], wqkv[lanes, :])
            hn_part[2 * pair, :, lanes] = part[:block_tokens].astype(jnp.bfloat16)
            hn_part[2 * pair + 1, :, lanes] = part[block_tokens:].astype(jnp.bfloat16)
            terms = part * hn[tall, lanes].astype(jnp.float32)
            gains[0:8, lanes] += jnp.sum(terms.reshape(-1, 8, column_step), axis=0)

        for member in hn_parts:
            member.start(t)
    gains[0:8, :] = gains[0:8, :] / gain_values[0:1, :]
    gain_rows.start(0)

    @pl.loop(0, width // 256)
    def _(c):
        lanes = pl.ds(pl.multiple_of(c * 256, 256), 256)
        total = tn(hn[:, lanes], dqkv[...]).astype(jnp.bfloat16)
        piece = total.reshape((4,) + (total.shape[0] // 4, total.shape[1]))
        for n in range(4):
            grad_qkv[c * 4 // seqs, lax.rem(c * 4, seqs) + n] = piece[n]

    for b in range(seqs):
        qkv_rows.start(b)
    gain_rows.step(0)
    for t in range(p.n_hi):
        for member in hn_parts:
            member.step(t)
        if t == 0:
            for b in range(seqs):
                qkv_rows.step(b)
            gain_rows.close(0)
            gain_swap.start()
        if t == p.n_hi // 2 - 1:
            for b in range(seqs):
                out_rows.close(b)
            for k in range(p.n_hi):
                out_seq.start(k)
        if t == p.n_hi - 2:
            for b in range(seqs):
                qkv_rows.close(b)
            qkv_swap.start()
    for t in range(p.n_hi):
        out_seq.step(t)
    for step in range(1, seqs):
        gain_swap.step(step)
        settle(do.at[block_rows(p.s), :], do_swap.send(step))
    for member in hn_parts + [out_rows, qkv_rows, gain_rows, gu_swap, qkv_swap, out_seq, gain_swap, stores]:
        member.finish()


def back(rows, seqs, head_size, middle, h2_grad, g, attended, gain_values, lengths, gu, wout, qkv, hn, wqkv):
    tokens, own_width = qkv.shape[0], qkv.shape[1] // 3
    width = hn.shape[1]
    low, f32 = jnp.bfloat16, jnp.float32
    block_tokens = tokens // seqs
    deep = width // (rows * seqs)
    quarter = width // rows
    hn_dims, qkv_dims = (seqs, block_tokens, width), (rows, seqs, deep, 3 * own_width)
    got = shape_of((deep, width))
    gu_got = shape_of((deep, gu.shape[2] // 2 * seqs))
    gain_width = 2 * quarter // seqs
    shapes = (
        shape_of(hn_dims[1:], f32),
        got,
        got,
        got,
        got,
        gu_got,
        gu_got,
        shape_of((seqs, 16, gain_width), f32),
        shape_of(hn_dims[1:], f32),
    )
    qkv_like, out_like = shape_of(qkv_dims), shape_of((rows, seqs, deep, width))
    scratch = (
        [
            pltpu.VMEM((tokens, own_width), low),
            pltpu.VMEM(qkv.shape, low),
            pltpu.VMEM((head_size, tokens), f32),
        ]
        + seq_slots(shape_of(hn_dims))
        + [pltpu.VMEM(qkv_dims, low)]
        + row_slots(qkv_like)
        + row_slots(out_like)
        + seq_slots(shape_of(out_like.shape[1:]))
        + [pltpu.VMEM((16, width), f32), pltpu.VMEM((2, 16, quarter), f32), pltpu.VMEM((16, quarter), f32)]
        + [pltpu.VMEM(array.shape, low) for array in (qkv, hn, wqkv, wout)]
        + [pltpu.VMEM((width, width), low)]
        + [pltpu.VMEM(hn_dims[1:], low), pltpu.VMEM(hn_dims[1:], low), pltpu.VMEM(hn_dims[1:], f32)]
        + meta_scratch(tokens)
        + [pltpu.SemaphoreType.DMA((4,))]
    )
    return call(
        functools.partial(back_kernel, rows, seqs, head_size),
        shapes,
        6,
        (middle, h2_grad, g, attended, gain_values, lengths, gu, wout, qkv, hn, wqkv),
        [pltpu.VMEM] * 5 + [pltpu.SMEM, pltpu.VMEM] + [pl.ANY] * 4,
        (pltpu.VMEM,) * 5 + (pl.ANY,) * 2 + (pltpu.VMEM, pl.ANY),
        scratch,
        480,
    )


def ending_kernel(
    middle, out_sum, middle_grad, hn_grad, x, gain, query, key, value, out, gate, up, down, *results
):
    output, input_grad = results[:2]
    for source, target in zip((query, key, value, out, gate, up, down), results[2:]):
        target[...] = source[...].astype(target.dtype)
    output[...] = (middle[...] + out_sum[...]).astype(output.dtype)
    values = x[...].astype(jnp.float32)
    inverse = lax.rsqrt(jnp.mean(values * values, axis=-1, keepdims=True) + EPSILON)
    scaled = gain[0:1, :] * hn_grad[...]
    input_grad[...] = (
        middle_grad[...]
        + inverse * scaled
        - values * inverse**3 * jnp.mean(scaled * values, axis=-1, keepdims=True)
    )


def ending(middle, out_sum, middle_grad, hn_grad, x, gain, gradients):
    steps = 4
    f32 = jnp.float32

    def blocks(array):
        return pl.BlockSpec((array.shape[0] // steps, array.shape[1]), lambda n: (n, 0))

    args = (middle, out_sum, middle_grad, hn_grad, x)
    shapes = (shape_of(middle.shape), shape_of(middle.shape, f32)) + tuple(
        shape_of(member.shape, f32) for member in gradients
    )
    return pl.pallas_call(
        ending_kernel,
        grid=(steps,),
        out_shape=shapes,
        in_specs=[blocks(member) for member in args]
        + [pl.BlockSpec(gain.shape, lambda n: (0, 0))]
        + [blocks(member) for member in gradients],
        out_specs=tuple(blocks(member) for member in shapes),
        compiler_params=pltpu.CompilerParams(vmem_limit_bytes=VMEM_BYTES),
    )(*args, gain, *gradients)


def split_local(
    rows,
    seqs,
    inputs,
    lengths,
    w_query,
    w_key,
    w_value,
    w_out,
    gain_attn,
    w_gate,
    w_up,
    w_down,
    gain_mlp,
    cotangent,
):
    low, f32 = jnp.bfloat16, jnp.float32
    tokens, width = inputs.shape[1], inputs.shape[2]
    deep = w_query.shape[0]
    row_tokens = tokens * seqs
    head_size = width // HEADS
    own_width = width // seqs
    hidden_own = w_gate.shape[1] // seqs

    side = lax.rem(lax.axis_index("seq"), 2)
    lane = lax.broadcasted_iota(jnp.int32, (8, 2 * deep), 1)
    both = [jnp.concatenate([gain, gain]).astype(f32)[None, :] for gain in (gain_attn, gain_mlp)]
    number = lax.broadcasted_iota(jnp.int32, (8, 2 * deep), 0)
    gains_own = jnp.where(lane // deep == side, jnp.where(number < 4, both[0], both[1]), 0.0)
    x_low, g_low = inputs[0], cotangent[0]

    g_all, wgu, wdown, wout, h2, wqkv, hn, qkv, attended, middle, gains = forward(
        rows,
        seqs,
        head_size,
        x_low,
        g_low,
        (w_query, w_key, w_value),
        (w_gate, w_up),
        w_down,
        w_out,
        gains_own,
        lengths,
    )
    wqkv = wqkv.reshape(width, 3 * own_width)
    wgu = wgu.reshape(width, 2 * hidden_own)
    wdown = wdown.reshape(hidden_own, width)
    wout = wout.reshape(width, width)
    g_all = g_all.reshape(row_tokens, width)
    h2 = h2.reshape(row_tokens, width)
    h2_grad, out_sum, sum_gu, sum_down = ffn(rows, seqs, h2, wgu, wdown, g_all)

    hn_grad, sum_out, got_query, got_key, got_value, got_gate, got_up, got_gain, middle_grad = back(
        rows, seqs, head_size, middle, h2_grad, g_low, attended, gains, lengths, sum_gu, wout, qkv, hn, wqkv
    )
    gradients = (got_query, got_key, got_value, sum_out, got_gate, got_up, sum_down.reshape(w_down.shape))
    output, input_grad, *gradients = ending(middle, out_sum, middle_grad, hn_grad, x_low, gains, gradients)
    gain_sums = jnp.sum(got_gain, axis=0).reshape(2, 8, 2, deep).sum(axis=1)
    gain_sums = lax.dynamic_index_in_dim(gain_sums, lax.rem(lax.axis_index("seq"), 2), 1, keepdims=False)
    grad_query, grad_key, grad_value, grad_out, grad_gate, grad_up, grad_down = gradients
    return (
        output[None],
        input_grad[None],
        grad_query,
        grad_key,
        grad_value,
        grad_out,
        gain_sums[0],
        grad_gate,
        grad_up,
        grad_down,
        gain_sums[1],
    )


def solution(mesh):
    placed = (
        P("row", "seq", None),
        P("row", None),
        P(("row", "seq"), None),
        P(("row", "seq"), None),
        P(("row", "seq"), None),
        P(("row", "seq"), None),
        P(("row", "seq")),
        P(("row", "seq"), None),
        P(("row", "seq"), None),
        P(("row", "seq"), None),
        P(("row", "seq")),
        P("row", "seq", None),
    )
    row_count, seq_count = mesh.shape["row"], mesh.shape["seq"]
    if row_count == 4 and seq_count % 2 == 0 and HEADS % seq_count == 0:
        local = functools.partial(split_local, row_count, seq_count)
    else:
        local = gathered_local
    return jax.shard_map(
        local,
        mesh=mesh,
        in_specs=placed,
        out_specs=(
            P("row", "seq", None),
            P("row", "seq", None),
            P(("row", "seq"), None),
            P(("row", "seq"), None),
            P(("row", "seq"), None),
            P(("row", "seq"), None),
            P(("row", "seq")),
            P(("row", "seq"), None),
            P(("row", "seq"), None),
            P(("row", "seq"), None),
            P(("row", "seq")),
        ),
        check_vma=False,
    )
```
